32 devices in a mesh: stream: 4 (over y, x), blk: 8 (over z, core).
Axes of the slice: x: 2, y: 2, z: 4, core: 2. Of those that a mesh axis runs over, the one named last changes fastest.
Arguments:
- latents: bfloat16 [16384, 1152], P(('stream', 'blk')), may hold values from -6 to 6
- skip_input: bfloat16 [16384, 1152], P(('stream', 'blk')), may hold values from -6 to 6
- cond_tokens: bfloat16 [64, 2, 1152], P('stream'), may hold values from -6 to 6
- extra_length: int32 [4, 16], P('stream'), may hold values from 1 to 129, 1040 in all within a row
- skip_weight: bfloat16 [2304, 1152], P('blk'), may hold values from -0.125 to 0.125
- skip_bias: bfloat16 [1152], P('blk'), may hold values from -1.75 to 1.75
- first_gain: bfloat16 [1152], P('blk'), may hold values from 0.25 to 1.75
- first_shift: bfloat16 [1152], P('blk'), may hold values from -1.75 to 1.75
- joint_weight: bfloat16 [1152, 3456], P('blk'), may hold values from -0.1875 to 0.1875
- out_weight: bfloat16 [1152, 1152], P('blk'), may hold values from -1.5 to 1.5
- out_bias: bfloat16 [1152], P('blk'), may hold values from -1.75 to 1.75
- second_gain: bfloat16 [1152], P('blk'), may hold values from 0.25 to 1.75
- second_shift: bfloat16 [1152], P('blk'), may hold values from -1.75 to 1.75
- up_weight: bfloat16 [1152, 4608], P('blk'), may hold values from -0.1875 to 0.1875
- up_bias: bfloat16 [4608], P('blk'), may hold values from -1.75 to 1.75
- down_weight: bfloat16 [4608, 1152], P('blk'), may hold values from -0.09375 to 0.09375
- down_bias: bfloat16 [1152], P('blk'), may hold values from -1.75 to 1.75
- cotangent: bfloat16 [16384, 1152], P(('stream', 'blk')), may hold values from -6 to 6
Outputs:
- output_tokens: bfloat16 [16384, 1152], P(('stream', 'blk'))
- latents_grad: bfloat16 [16384, 1152], P(('stream', 'blk'))
- skip_grad: bfloat16 [16384, 1152], P(('stream', 'blk'))
- cond_grad: bfloat16 [64, 2, 1152], P('stream')
- grad_skip_weight: float32 [2304, 1152], P('blk')
- grad_skip_bias: float32 [1152], P('blk')
- grad_first_gain: float32 [1152], P('blk')
- grad_first_shift: float32 [1152], P('blk')
- grad_joint_weight: float32 [1152, 3456], P('blk')
- grad_out_weight: float32 [1152, 1152], P('blk')
- grad_out_bias: float32 [1152], P('blk')
- grad_second_gain: float32 [1152], P('blk')
- grad_second_shift: float32 [1152], P('blk')
- grad_up_weight: float32 [1152, 4608], P('blk')
- grad_up_bias: float32 [4608], P('blk')
- grad_down_weight: float32 [4608, 1152], P('blk')
- grad_down_bias: float32 [1152], P('blk')
The draws below stay inside these ranges and needn't reach their ends.
Inputs may be any that keep to these rules, and one draw needn't show every extreme that they name: In each stream the item lengths extra_length + 191 sum to 4096, and one item has exactly 320 tokens.
All inputs are finite; a program needn't handle non-finite values.
Results may differ from the reference program's by a relative error of at most 0.02.
Values may be sent and summed in bfloat16 or wider, within the bound.
A program may use at most 256 MiB of HBM per device.

```python
import math
import jax
import jax.numpy as jnp
import numpy as np
from jax import lax

D = 1152
HEADS = 16
HEAD = 72
FF = 4608
TOK_DEV = 512
LEN_MIN = 192
STREAMS = 4
STREAM_TOK = 4096
TOKENS = 16384
ITEMS = 16
EXTRA_MOST = 129
EXTRA_TOTAL = 1040
N_STREAM = 4
N_BLK = 8


def levels(stream_key, dims, cuts, smallest, top_value):
    factor_of, own = 1.0, jax.random.fold_in(stream_key, 6)
    for dim, shards_of in cuts:
        draws = jnp.exp(jax.random.uniform(jax.random.fold_in(own, dim), (shards_of,), jnp.float32, smallest / len(cuts), top_value / len(cuts)))
        factor_of = factor_of * jnp.repeat(draws, dims[dim] // shards_of).reshape([-1 if axis == dim else 1 for axis in range(len(dims))])
    return factor_of


def length_profile(amount, total, reach, slope):
    portions = [(1 << 20) // math.isqrt(grade ** slope) + 1 for grade in range(2, amount + 1)]
    surplus, holding = total - reach - (amount - 1), [1] * (amount - 1)
    while surplus > 0:
        free = [i for i in range(amount - 1) if holding[i] < reach]
        mass, budget = sum([portions[i] for i in free]), surplus
        for i in free:
            addition = min(reach - holding[i], max(1, budget * portions[i] // mass), surplus)
            holding[i] = holding[i] + addition
            surplus = surplus - addition
    return np.array([reach] + holding)


def ragged(rng, amount, total, bound, slope):
    if amount == 2:
        one = jax.random.randint(rng, (), max(1, total - bound), min(bound, total - 1) + 1)
        return jnp.stack([one, total - one])
    lengths = jnp.asarray(length_profile(amount, total, bound, slope), jnp.int32)
    twos = (amount - 1) // 2
    giver, receiver = lengths[1:1 + 2 * twos:2], lengths[2:2 + 2 * twos:2]
    slack = jnp.minimum(giver - 1, bound - receiver)
    shifted = jax.random.randint(jax.random.fold_in(rng, 1), (twos,), 0, 1 << 20) % (slack + 1)
    lengths = lengths.at[1:1 + 2 * twos:2].set(giver - shifted).at[2:2 + 2 * twos:2].set(receiver + shifted)
    return lengths[jax.random.permutation(jax.random.fold_in(rng, 2), amount)]


def normal_values(rng, extent, width, reach, split=(), kind=jnp.bfloat16):
    values = jax.random.normal(rng, extent, jnp.float32) * width
    if len(split) > 0:
        values = levels(rng, extent, split, -0.22, 0.18) * values
    return jnp.clip(values, min=-reach, max=reach).astype(kind)


def setup_inputs(seed: int = 0) -> dict:
    splits = jax.random.split(jax.random.key(seed), 19)
    latents = normal_values(splits[0], (TOKENS, D), 1.0, 6.0, ((0, 32),))
    skip_input = normal_values(splits[1], (TOKENS, D), 1.0, 6.0, ((0, 32),))
    cond_tokens = normal_values(splits[2], (STREAMS * ITEMS, 2, D), 1.0, 6.0, ((0, 4),))
    extra_length = jax.vmap(lambda own: ragged(own, ITEMS, EXTRA_TOTAL, EXTRA_MOST, 0))(jax.random.split(splits[3], STREAMS)).reshape((STREAMS, ITEMS)).astype(jnp.int32)
    skip_weight = normal_values(splits[4], (2 * D, D), (2 * D) ** -0.5, 0.125, ((0, 8),))
    skip_bias = normal_values(splits[5], (D,), 0.3, 1.75, ((0, 8),))
    first_gain = jnp.clip(1.0 + 0.15 * jax.random.normal(splits[6], (D,), jnp.float32), 0.25, 1.75).astype(jnp.bfloat16)
    first_shift = normal_values(splits[7], (D,), 0.3, 1.75, ((0, 8),))
    joint_weight = normal_values(splits[8], (D, 3 * D), D ** -0.5, 0.1875, ((0, 8),))
    out_weight = normal_values(splits[9], (D, D), (D // 64) ** -0.5, 1.5, ((0, 8),))
    out_bias = normal_values(splits[10], (D,), 0.3, 1.75, ((0, 8),))
    second_gain = jnp.clip(1.0 + 0.15 * jax.random.normal(splits[11], (D,), jnp.float32), 0.25, 1.75).astype(jnp.bfloat16)
    second_shift = normal_values(splits[12], (D,), 0.3, 1.75, ((0, 8),))
    up_weight = normal_values(splits[13], (D, FF), D ** -0.5, 0.1875, ((0, 8),))
    up_bias = normal_values(splits[14], (FF,), 0.3, 1.75, ((0, 8),))
    down_weight = normal_values(splits[15], (FF, D), FF ** -0.5, 0.09375, ((0, 8),))
    down_bias = normal_values(splits[16], (D,), 0.3, 1.75, ((0, 8),))
    cotangent = normal_values(splits[17], (TOKENS, D), 1.0, 6.0, ((0, 32),))
    return dict(latents=latents, skip_input=skip_input, cond_tokens=cond_tokens, extra_length=extra_length, skip_weight=skip_weight, skip_bias=skip_bias, first_gain=first_gain, first_shift=first_shift, joint_weight=joint_weight, out_weight=out_weight, out_bias=out_bias, second_gain=second_gain, second_shift=second_shift, up_weight=up_weight, up_bias=up_bias, down_weight=down_weight, down_bias=down_bias, cotangent=cotangent)


@jax.custom_vjp
def low(v):
    return lax.optimization_barrier(v.astype(jnp.bfloat16)).astype(jnp.float32)

@jax.custom_vjp
def low_back(v):
    return v

def low_keep(v):
    return (low(v), None)

def low_pass(kept, grad):
    return (grad,)

def back_keep(v):
    return (v, None)

def back_low(kept, grad):
    return (low(grad),)
low.defvjp(low_keep, low_pass)
low_back.defvjp(back_keep, back_low)
EXACT = lax.Precision.HIGHEST

def matmul(left, right):
    return jnp.dot(left, right, precision=EXACT)

def layer_norm(values, gain, shift):
    center = values - lax.optimization_barrier(jnp.mean(values, axis=-1, keepdims=True))
    spread = lax.optimization_barrier(jnp.mean(center * center, axis=-1, keepdims=True))
    return center * lax.rsqrt(spread + 1e-05) * gain + shift

def segments_of(extra):
    ends = jnp.cumsum(extra.astype(jnp.int32) + (LEN_MIN - 1)).astype(jnp.int32)
    places = jnp.arange(STREAM_TOK, dtype=jnp.int32)
    return lax.optimization_barrier(jnp.sum((ends[None, :] <= places[:, None]).astype(jnp.int32), axis=1)).astype(jnp.int32)

def attend_block(parts, cond_keys, cond_values, cond_segments):
    query, key_prev, key_here, value_prev, value_here, seg_query, seg_prev = parts
    keys = jnp.concatenate([key_prev, key_here, cond_keys], 0)
    values = jnp.concatenate([value_prev, value_here, cond_values], 0)
    seg_keys = jnp.concatenate([seg_prev, seg_query, cond_segments], 0)
    rows = query.shape[0]
    head_query = query.reshape(rows, HEADS, HEAD)
    head_key = keys.reshape(keys.shape[0], HEADS, HEAD)
    head_value = values.reshape(values.shape[0], HEADS, HEAD)
    scores = low_back(jnp.einsum('qhd,khd->hqk', head_query, head_key, precision=EXACT) * HEAD ** (-0.5))
    allowed = seg_query[:, None] == seg_keys[None, :]
    scores = jnp.where(allowed[None], scores, -1e+30)
    top = lax.optimization_barrier(jnp.max(scores, axis=-1, keepdims=True))
    expo = jnp.exp(scores - top)
    probs = low(expo / lax.optimization_barrier(jnp.sum(expo, axis=-1, keepdims=True)))
    mixed = jnp.einsum('hqk,khd->qhd', probs, head_value, precision=EXACT)
    return mixed.reshape(rows, HEADS * HEAD)

def block_forward(tokens, skipped, conds, segments, params):
    skip_weight, skip_bias, first_gain, first_shift, joint_weight, out_weight, out_bias, second_gain, second_shift, up_weight, up_bias, down_weight, down_bias = params
    base = low_back(matmul(jnp.concatenate([tokens, skipped], 1), skip_weight) + skip_bias)
    first = low(layer_norm(base, first_gain, first_shift))
    triple = low_back(low(matmul(first, joint_weight)))
    cond_first = low(layer_norm(conds, first_gain, first_shift))
    cond_pair = low_back(low(matmul(cond_first, joint_weight[:, D:])))
    query = triple[:, :D]
    key = triple[:, D:2 * D]
    value = triple[:, 2 * D:]
    padding = jnp.zeros((TOK_DEV, D), jnp.float32)
    key_prev = jnp.concatenate([padding, key[:STREAM_TOK - TOK_DEV]], 0)
    value_prev = jnp.concatenate([padding, value[:STREAM_TOK - TOK_DEV]], 0)
    seg_prev = jnp.concatenate([jnp.full((TOK_DEV,), -1, jnp.int32), segments[:STREAM_TOK - TOK_DEV]], 0)
    cond_segments = (jnp.arange(2 * ITEMS, dtype=jnp.int32) // 2).astype(jnp.int32)
    cond_keys = cond_pair[:, :D]
    cond_values = cond_pair[:, D:]

    def shaped(array):
        return array.reshape((N_BLK, TOK_DEV) + array.shape[1:])

    def one_block(parts):
        return attend_block(parts, cond_keys, cond_values, cond_segments)
    mixed = lax.map(jax.checkpoint(one_block), tuple((shaped(a) for a in (query, key_prev, key, value_prev, value, segments, seg_prev))))
    attended = low_back(low(mixed.reshape(STREAM_TOK, D)))
    middle = base + low_back(matmul(attended, out_weight) + out_bias)
    second = low(layer_norm(middle, second_gain, second_shift))
    before = low_back(matmul(second, up_weight) + up_bias)
    hidden = low(jax.nn.gelu(before, approximate=False))
    return middle + low_back(matmul(hidden, down_weight) + down_bias)

def reference(latents, skip_input, cond_tokens, extra_length, skip_weight, skip_bias, first_gain, first_shift, joint_weight, out_weight, out_bias, second_gain, second_shift, up_weight, up_bias, down_weight, down_bias, cotangent):
    params = tuple((p.astype(jnp.float32) for p in (skip_weight, skip_bias, first_gain, first_shift, joint_weight, out_weight, out_bias, second_gain, second_shift, up_weight, up_bias, down_weight, down_bias)))
    streams = (latents.astype(jnp.float32).reshape(N_STREAM, STREAM_TOK, D), skip_input.astype(jnp.float32).reshape(N_STREAM, STREAM_TOK, D), cond_tokens.astype(jnp.float32).reshape(N_STREAM, 2 * ITEMS, D), extra_length, cotangent.astype(jnp.float32).reshape(N_STREAM, STREAM_TOK, D))

    def one_stream(total, parts):
        tokens, skipped, conds, extra, incoming = parts
        segments = segments_of(extra)

        def forward(a, b, c, weights):
            return block_forward(a, b, c, segments, weights)
        result, pull = jax.vjp(forward, tokens, skipped, conds, params)
        grads = pull(incoming)
        total = jax.tree.map(lambda s, g: s + g, total, grads[3])
        return (total, (result, grads[0], grads[1], grads[2]))
    zero = jax.tree.map(jnp.zeros_like, params)
    total, outs = lax.scan(one_stream, zero, streams)
    result, tokens_grad, skipped_grad, conds_grad = outs
    return (result.reshape(TOKENS, D).astype(jnp.bfloat16), tokens_grad.reshape(TOKENS, D).astype(jnp.bfloat16), skipped_grad.reshape(TOKENS, D).astype(jnp.bfloat16), conds_grad.reshape(N_STREAM * ITEMS, 2, D).astype(jnp.bfloat16), total[0], total[1], total[2], total[3], total[4], total[5], total[6], total[7], total[8], total[9], total[10], total[11], total[12])
```

```python
from functools import partial

import jax
import jax.numpy as jnp
from jax import lax
from jax.experimental import pallas as pl
from jax.experimental.pallas import tpu as pltpu
from jax.sharding import PartitionSpec as P

HEADS = 16
HEAD = 72
LEN_MIN = 192

MESH = pl.DeviceIdType.MESH
ANY = pl.BlockSpec(memory_space=pl.ANY)
WIDTH = 1152
PART = 144
SMALL = (16, 128)


class Place:
    def __init__(self):
        self.s = lax.axis_index("stream")
        self.b = lax.axis_index("blk")
        self.x = lax.rem(self.s, 2)
        self.y = lax.div(self.s, 2)
        self.c = lax.rem(self.b, 2)
        self.zz = lax.div(self.b, 2)

    def flip(self, bit):
        return 1 - bit

    def other(self, k):
        low, high = lax.rem(self.zz, 2), lax.div(self.zz, 2)
        return 2 * (1 - high if k & 2 else high) + (1 - low if k & 1 else low)

    def source(self, k):
        zz = self.zz
        table = ((1, 0, 3, 2), (2, 2, 1, 1), (3, 3, 0, 0))[k - 1]
        return jnp.where(zz < 2, jnp.where(zz == 0, table[0], table[1]), jnp.where(zz == 2, table[2], table[3]))

    def at(self, x=None, y=None, zz=None, c=None):
        x = self.x if x is None else x
        y = self.y if y is None else y
        zz = self.zz if zz is None else zz
        c = self.c if c is None else c
        return (2 * y + x, 2 * zz + c)


def greet(place):
    barrier = pltpu.get_barrier_semaphore()
    near = [
        place.at(x=1 - place.x),
        place.at(y=1 - place.y),
        place.at(c=1 - place.c),
    ] + [place.at(zz=place.other(k)) for k in (1, 2, 3)]
    for device in near:
        pl.semaphore_signal(barrier, inc=1, device_id=device, device_id_type=MESH)
    pl.semaphore_wait(barrier, len(near))


def remote(src, dst, send, recv, device):
    return pltpu.make_async_remote_copy(
        src_ref=src, dst_ref=dst, send_sem=send, recv_sem=recv, device_id=device, device_id_type=MESH
    )


def piece(kind, ref, b, x, y):
    if kind == "cols":
        return ref.at[b, :, pl.ds(pl.multiple_of((2 * y + x) * WIDTH, 128), WIDTH)]
    if kind == "rows":
        return ref.at[b, pl.ds(pl.multiple_of((2 * y + x) * PART, 16), PART)]
    low, size = (0, 80) if y == 0 else (80, 64)
    return ref.at[b, pl.ds(pl.multiple_of(x * PART + low, 16), size)]


KINDS = ("half", "cols", "cols", "rows")


class Gather:
    SEMS = [pltpu.SemaphoreType.DMA((4, 6, 4, 2)), pltpu.SemaphoreType.DMA((12,)), pltpu.SemaphoreType.DMA((2, 8))]

    def __init__(self, place, shards, outs, scratch):
        self.place = place
        self.small_in, self.skip_in, self.joint_in, self.out_in, self.up_in, self.down_in = shards
        self.small = outs[0]
        self.outs = outs[1:]
        self.sems, self.local_sems, self.small_sems = scratch[:3]
        self.stage = scratch[3:]
        self.sent = []

    def copy(self, t, x, y, zz, c, stage, k, device):
        ref = piece(KINDS[t], self.outs[t], 2 * zz + c, x, y)
        return remote(ref, ref, self.sems.at[t, stage, k, 0], self.sems.at[t, stage, k, 1], device)

    def each_y(self, t, run):
        if KINDS[t] != "half":
            run(self.place.y)
            return
        for value in (0, 1):
            pl.when(self.place.y == value)(lambda value=value: run(value))

    STAGE = [
        pltpu.VMEM((2 * PART, WIDTH), jnp.bfloat16),
        pltpu.VMEM((PART, 4 * WIDTH), jnp.bfloat16),
        pltpu.VMEM((PART, 4 * WIDTH), jnp.bfloat16),
        pltpu.VMEM((4 * PART, WIDTH), jnp.bfloat16),
    ]

    def locals(self, t):
        if t == 1:
            return [
                (self.joint_in, self.stage[1].at[:, pl.ds(0, 3 * WIDTH)]),
                (self.out_in, self.stage[1].at[:, pl.ds(3 * WIDTH, WIDTH)]),
            ]
        return [({0: self.skip_in, 2: self.up_in, 3: self.down_in}[t], self.stage[t])]

    def own_start(self, t):
        for i, (src, dst) in enumerate(self.locals(t)):
            pltpu.make_async_copy(src, dst, self.local_sems.at[2 * t + i]).start()

    def own_keep(self, t):
        return pltpu.make_async_copy(self.stage[t], self.outs[t].at[self.place.b], self.local_sems.at[8 + t])

    def own_done(self, t):
        for i, (src, dst) in enumerate(self.locals(t)):
            pltpu.make_async_copy(src, dst, self.local_sems.at[2 * t + i]).wait()
        self.own_keep(t).start()

    def own_copy(self, t, c):
        ref = self.outs[t].at[2 * self.place.zz + c]
        src = self.stage[t]
        sems = self.sems.at[t, 4, 0]
        return remote(src, ref, sems.at[0], sems.at[1], self.place.at(c=1 - self.place.c))

    def small_start(self):
        p = self.place
        for i, device in enumerate([p.at(zz=p.other(k)) for k in (1, 2, 3)] + [p.at(c=1 - p.c)]):
            remote(self.small_in, self.small.at[p.b], self.small_sems.at[0, i], self.small_sems.at[1, i], device).start()
        pltpu.make_async_copy(self.small_in, self.small.at[p.b], self.small_sems.at[0, 7]).start()

    def small_pass(self):
        p = self.place
        for i, k in enumerate((1, 2, 3)):
            ref = self.small.at[2 * p.other(k) + p.c]
            remote(ref, ref, self.small_sems.at[0, i], self.small_sems.at[1, i], p.at()).wait_recv()
            remote(ref, ref, self.small_sems.at[0, 4 + i], self.small_sems.at[1, 4 + i], p.at(c=1 - p.c)).start()

    def small_done(self):
        p = self.place
        for i, k in enumerate((0, 1, 2, 3)):
            ref = self.small.at[2 * p.other(k) + 1 - p.c]
            remote(ref, ref, self.small_sems.at[0, 3 + i], self.small_sems.at[1, 3 + i], p.at()).wait_recv()
        for i in range(7):
            remote(self.small_in, self.small_in, self.small_sems.at[0, i], self.small_sems.at[1, i], p.at()).wait_send()
        pltpu.make_async_copy(self.small_in, self.small.at[p.b], self.small_sems.at[0, 7]).wait()

    def stage_piece(self, t, y):
        x = self.place.x
        q = 2 * y + x
        if KINDS[t] == "cols":
            return self.stage[t].at[:, pl.ds(pl.multiple_of(q * WIDTH, 128), WIDTH)]
        if KINDS[t] == "rows":
            return self.stage[t].at[pl.ds(pl.multiple_of(q * PART, 16), PART)]
        low, size = (0, 80) if y == 0 else (80, 64)
        return self.stage[t].at[pl.ds(pl.multiple_of(x * PART + low, 16), size)]

    def z_copies(self, t, y, zz, start, own=False):
        p = self.place
        for step, send in ((1, 0), (-1, 5)):
            go = (zz <= p.zz) & (p.zz < 3) if step == 1 else (zz >= p.zz) & (p.zz > 0)
            ref = piece(KINDS[t], self.outs[t], 2 * zz + p.c, p.x, y)

            @pl.when(go)
            def _():
                copy = remote(self.stage_piece(t, y) if own else ref, ref, self.sems.at[t, send, zz, 0], self.sems.at[t, 0, zz, 1], p.at(zz=p.zz + step))
                copy.start() if start else copy.wait_send()

    def z_start(self, t):
        p = self.place
        self.each_y(t, lambda y: self.z_copies(t, y, p.zz, True, True))
        self.own_copy(t, p.c).start()

    def z_done(self, t, k):
        p = self.place
        zz = p.source(k)

        def run(y):
            self.copy(t, p.x, y, zz, p.c, 0, zz, p.at()).wait_recv()
            self.copy(t, p.x, y, zz, p.c, 1, k, p.at(x=1 - p.x)).start()
            self.copy(t, p.x, y, zz, p.c, 2, k, p.at(y=1 - p.y)).start()
            self.z_copies(t, y, zz, True)

        self.each_y(t, run)

    def by_x(self, t, k):
        return k == 1 or (k == 2 and t % 2 == 0)

    def xy_done(self, t, k):
        p = self.place

        def run(y):
            zz = p.source(k)
            self.copy(t, 1 - p.x, y, zz, p.c, 1, k, p.at()).wait_recv()
            if self.by_x(t, k):
                self.copy(t, 1 - p.x, y, zz, p.c, 3, k, p.at(y=1 - p.y)).start()
            self.copy(t, p.x, 1 - y, zz, p.c, 2, k, p.at()).wait_recv()
            if not self.by_x(t, k):
                self.copy(t, p.x, 1 - y, zz, p.c, 3, k, p.at(x=1 - p.x)).start()

        self.each_y(t, run)

    def diag_done(self, t, k):
        p = self.place

        def run(y):
            zz = p.source(k)
            self.copy(t, 1 - p.x, 1 - y, zz, p.c, 3, k, p.at()).wait_recv()

        self.each_y(t, run)
        self.pair_copy(t, k, p.c).start()

    def pair_copy(self, t, k, c):
        ref = self.outs[t].at[2 * self.place.source(k) + c]
        sems = self.sems.at[t, 4, k]
        return remote(ref, ref, sems.at[0], sems.at[1], self.place.at(c=1 - self.place.c))

    def ready(self, t):
        p = self.place
        self.own_copy(t, 1 - p.c).wait_recv()
        for k in (1, 2, 3):
            self.pair_copy(t, k, 1 - p.c).wait_recv()

    def all_sent(self, t):
        p = self.place
        self.own_copy(t, p.c).wait_send()
        self.own_keep(t).wait()

        def run(y):
            self.z_copies(t, y, p.zz, False, True)
            for k in (1, 2, 3):
                zz = p.source(k)
                self.z_copies(t, y, zz, False)
                self.copy(t, p.x, y, zz, p.c, 1, k, p.at()).wait_send()
                self.copy(t, p.x, y, zz, p.c, 2, k, p.at()).wait_send()
                if self.by_x(t, k):
                    self.copy(t, 1 - p.x, y, zz, p.c, 3, k, p.at()).wait_send()
                else:
                    self.copy(t, p.x, 1 - y, zz, p.c, 3, k, p.at()).wait_send()

        self.each_y(t, run)
        for k in (1, 2, 3):
            self.pair_copy(t, k, p.c).wait_send()


def gather_kernel(*refs):
    shards, outs, scratch = refs[:6], refs[6:11], refs[11:]
    place = Place()
    g = Gather(place, shards, outs, scratch)
    for t in range(4):
        g.own_start(t)
    greet(place)
    g.small_start()
    g.own_done(0)
    g.z_start(0)
    g.small_pass()
    for t in range(4):
        for k in (1, 2, 3):
            g.z_done(t, k)
        if t + 1 < 4:
            g.own_done(t + 1)
            g.z_start(t + 1)
        if t > 0:
            for k in (1, 2, 3):
                g.diag_done(t - 1, k)
        for k in (1, 2, 3):
            g.xy_done(t, k)
    for k in (1, 2, 3):
        g.diag_done(3, k)
    g.small_done()
    for t in range(4):
        g.ready(t)
        g.all_sent(t)


def gather_weights(small, skip, joint, out, up, down):
    bf16 = jnp.bfloat16
    return pl.pallas_call(
        gather_kernel,
        out_shape=[
            jax.ShapeDtypeStruct((8, *SMALL), bf16),
            jax.ShapeDtypeStruct((8, 2 * PART, WIDTH), bf16),
            jax.ShapeDtypeStruct((8, PART, 4 * WIDTH), bf16),
            jax.ShapeDtypeStruct((8, PART, 4 * WIDTH), bf16),
            jax.ShapeDtypeStruct((8, 4 * PART, WIDTH), bf16),
        ],
        in_specs=[ANY] * 6,
        out_specs=[ANY] * 5,
        scratch_shapes=Gather.SEMS + Gather.STAGE,
        compiler_params=pltpu.CompilerParams(collective_id=0, has_side_effects=True),
    )(small, skip, joint, out, up, down)


def add_units(out, *ins):
    @pl.loop(0, out.shape[0] // 16)
    def _(i):
        rows = pl.ds(pl.multiple_of(i * 16, 16), 16)
        total = ins[0][rows].astype(jnp.float32)
        for ref in ins[1:]:
            total += ref[rows].astype(jnp.float32)
        out[rows] = total.astype(out.dtype)


SIZES = (80, PART, PART, PART)


class Reduce:
    SEMS = [
        pltpu.SemaphoreType.DMA((4, 4, 2, 3)),
        pltpu.SemaphoreType.DMA((4, 4, 2)),
        pltpu.SemaphoreType.DMA((4, 4, 2)),
        pltpu.SemaphoreType.DMA((4, 4, 2)),
    ]
    BUFFERS = [
        pltpu.VMEM(lead + (size, WIDTH), jnp.bfloat16)
        for size in SIZES
        for lead in ((4, 2), (4, 2), (4,), (4,), ())
    ]

    def __init__(self, place, parts, outs, scratch):
        self.place, self.parts, self.outs = place, parts, outs
        self.sem1, self.sem2, self.sem3, self.sem4 = scratch[:4]
        bufs = scratch[4:]
        self.stage, self.land1, self.land2, self.land3, self.fin = (
            [bufs[5 * t + i] for t in range(4)] for i in range(5)
        )

    def piece(self, t, zz, x, y):
        ref = self.parts[t]
        if KINDS[t] == "cols":
            return ref.at[zz, :, pl.ds(pl.multiple_of((2 * y + x) * WIDTH, 128), WIDTH)]
        if KINDS[t] == "rows":
            return ref.at[zz, pl.ds(pl.multiple_of((2 * y + x) * PART, 16), PART)]
        return ref.at[zz, pl.ds(pl.multiple_of(x * PART + 64 * y, 16), 80)]

    def first(self, t, zz, j):
        p = self.place
        if zz < 2:
            src, device = self.piece(t, zz, 1 - p.x, j), p.at(x=1 - p.x)
        else:
            src, device = self.piece(t, zz, j, 1 - p.y), p.at(y=1 - p.y)
        sems = self.sem1.at[t, zz, j]
        return remote(src, self.land1[t].at[zz, j], sems.at[0], sems.at[1], device)

    def load(self, t, zz, j):
        p = self.place
        src = self.piece(t, zz, p.x, j) if zz < 2 else self.piece(t, zz, j, p.y)
        return pltpu.make_async_copy(src, self.stage[t].at[zz, j], self.sem1.at[t, zz, j, 2])

    def start(self, t):
        for zz in (0, 2, 1, 3):
            for j in (0, 1):
                self.first(t, zz, j).start()
                self.load(t, zz, j).start()

    def second(self, t, zz):
        p = self.place
        keep = p.y if zz < 2 else p.x
        device = p.at(y=1 - p.y) if zz < 2 else p.at(x=1 - p.x)
        sems = self.sem2.at[t, zz]
        return remote(self.stage[t].at[zz, 1 - keep], self.land2[t].at[zz], sems.at[0], sems.at[1], device)

    def pass_on(self, t):
        p = self.place
        for zz in (0, 2, 1, 3):
            keep = p.y if zz < 2 else p.x
            for j in (0, 1):
                self.load(t, zz, j).wait()
                self.first(t, zz, j).wait_recv()
            mine = self.stage[t].at[zz, 1 - keep]
            add_units(mine, mine, self.land1[t].at[zz, 1 - keep])
            self.second(t, zz).start()

    def third(self, t, zz, slot):
        p = self.place
        keep = p.y if zz < 2 else p.x
        return remote(
            self.stage[t].at[zz, keep], self.land3[t].at[slot], self.sem3.at[t, zz, 0], self.sem3.at[t, slot, 1],
            p.at(zz=zz),
        )

    def to_chip(self, t):
        p = self.place
        for zz in (0, 2, 1, 3):
            keep = p.y if zz < 2 else p.x
            self.second(t, zz).wait_recv()
            mine = self.stage[t].at[zz, keep]
            add_units(mine, mine, self.land1[t].at[zz, keep], self.land2[t].at[zz])

            @pl.when(zz != p.zz)
            def _():
                self.third(t, zz, p.zz).start()

            @pl.when(zz == p.zz)
            def _():
                add_units(self.fin[t], mine)

    def share(self, t, k):
        p = self.place
        x = 1 - p.x if k & 1 else p.x
        y = 1 - p.y if k & 2 else p.y
        return p.at(x=x, y=y), self.sem4.at[t, k]

    def result(self, t, x, y):
        ref = self.outs[t]
        if KINDS[t] == "cols":
            return ref.at[:, pl.ds(pl.multiple_of((2 * y + x) * WIDTH, 128), WIDTH)]
        if KINDS[t] == "rows":
            return ref.at[pl.ds(pl.multiple_of((2 * y + x) * PART, 16), PART)]
        low, size = (0, 80) if y == 0 else (80, 64)
        return ref.at[pl.ds(pl.multiple_of(x * PART + low, 16), size)]

    def fin_part(self, t, y):
        if KINDS[t] != "half":
            return self.fin[t]
        return self.fin[t] if y == 0 else self.fin[t].at[pl.ds(16, 64)]

    def each_y(self, t, run):
        if KINDS[t] != "half":
            run(self.place.y)
            return
        for value in (0, 1):
            pl.when(self.place.y == value)(lambda value=value: run(value))

    def spread(self, t, start):
        p = self.place

        def run(y):
            src, dst = self.fin_part(t, y), self.result(t, p.x, y)
            for k in (1, 2, 3):
                device, sems = self.share(t, k)
                copy = remote(src, dst, sems.at[0], sems.at[1], device)
                copy.start() if start else copy.wait_send()
            keep = pltpu.make_async_copy(src, dst, self.sem4.at[t, 0, 0])
            keep.start() if start else keep.wait()

        self.each_y(t, run)

    def finish(self, t):
        p = self.place
        for k in (1, 2, 3):
            ref = self.land3[t].at[p.other(k)]
            remote(ref, ref, self.sem3.at[t, p.zz, 0], self.sem3.at[t, p.other(k), 1], p.at()).wait_recv()
        add_units(self.fin[t], self.fin[t], *[self.land3[t].at[p.other(k)] for k in (1, 2, 3)])
        self.spread(t, True)

    def done(self, t):
        p = self.place
        for zz in range(4):
            for j in (0, 1):
                self.first(t, zz, j).wait_send()
            self.second(t, zz).wait_send()

            @pl.when(zz != p.zz)
            def _():
                self.third(t, zz, p.zz).wait_send()

        self.spread(t, False)

        def run(y):
            for k in (1, 2, 3):
                ref = self.result(t, 1 - p.x if k & 1 else p.x, 1 - y if k & 2 else y)
                sems = self.sem4.at[t, k]
                remote(ref, ref, sems.at[0], sems.at[1], p.at()).wait_recv()

        self.each_y(t, run)


class Little:
    SCRATCH = [
        pltpu.VMEM((8, *SMALL), jnp.float32),
        pltpu.VMEM((4, *SMALL), jnp.float32),
        pltpu.VMEM((4, *SMALL), jnp.float32),
        pltpu.VMEM((4, *SMALL), jnp.float32),
        pltpu.VMEM((4, *SMALL), jnp.float32),
        pltpu.VMEM((4, *SMALL), jnp.float32),
        pltpu.VMEM(SMALL, jnp.float32),
        pltpu.VMEM((32, WIDTH), jnp.float32),
        pltpu.VMEM((32, WIDTH), jnp.float32),
        pltpu.VMEM((32, WIDTH), jnp.float32),
        pltpu.VMEM((4, 32, WIDTH), jnp.float32),
        pltpu.VMEM((32, WIDTH), jnp.bfloat16),
        pltpu.SemaphoreType.DMA((16, 2)),
    ]

    def __init__(self, place, small, cond, small_out, cond_out, scratch):
        self.place, self.ins, self.outs = place, (small, cond), (small_out, cond_out)
        self.part, self.pair, self.x_in, self.sum1, self.y_in, self.z_in, self.total = scratch[:7]
        self.mine, self.cond_pair, self.cond_sum, self.cond_in, self.cond_out = scratch[7:12]
        self.sems = scratch[12]

    def copy(self, i, src, dst, device, j=None):
        return remote(src, dst, self.sems.at[i, 0], self.sems.at[i if j is None else j, 1], device)

    def load(self):
        for i, (src, dst) in enumerate(((self.ins[0], self.part), (self.ins[1], self.mine))):
            pltpu.make_async_copy(src, dst, self.sems.at[14 + i, 0]).start()
        for i, (src, dst) in enumerate(((self.ins[0], self.part), (self.ins[1], self.mine))):
            pltpu.make_async_copy(src, dst, self.sems.at[14 + i, 0]).wait()

    def small_pair(self, zz):
        p = self.place
        return self.copy(zz, self.part.at[2 * zz + 1 - p.c], self.pair.at[zz], p.at(c=1 - p.c))

    def run_pair(self):
        p = self.place
        for zz in range(4):
            self.small_pair(zz).start()
        cond = self.copy(4, self.mine, self.cond_pair, p.at(c=1 - p.c))
        cond.start()
        for zz in range(4):
            self.small_pair(zz).wait()
            self.pair[zz] += self.part[2 * zz + p.c]
        cond.wait()
        self.cond_sum[...] = self.mine[...] + self.cond_pair[...]
        self.copy(5, self.pair, self.x_in, p.at(x=1 - p.x)).start()
        for k in (1, 2, 3):
            self.copy(6 + k, self.cond_sum, self.cond_in.at[p.zz], p.at(zz=p.other(k))).start()
        self.cond_in[p.zz] = self.cond_sum[...]

    def run_x(self):
        p = self.place
        self.copy(5, self.pair, self.x_in, p.at(x=1 - p.x)).wait()
        self.sum1[...] = self.pair[...] + self.x_in[...]
        self.copy(6, self.sum1, self.y_in, p.at(y=1 - p.y)).start()

    def run_y(self):
        p = self.place
        self.copy(6, self.sum1, self.y_in, p.at(y=1 - p.y)).wait()
        self.sum1[...] += self.y_in[...]
        for k in (1, 2, 3):
            self.copy(9 + k, self.sum1.at[p.other(k)], self.z_in.at[p.zz], p.at(zz=p.other(k))).start()
        self.z_in[p.zz] = self.sum1[p.zz]

    def run_z(self):
        p = self.place
        for k in (1, 2, 3):
            self.copy(9 + k, self.sum1.at[p.other(k)], self.z_in.at[p.zz], p.at(zz=p.other(k))).wait()
            self.copy(6 + k, self.cond_sum, self.cond_in.at[p.zz], p.at(zz=p.other(k))).wait()
        self.total[...] = (self.z_in[0] + self.z_in[1]) + (self.z_in[2] + self.z_in[3])
        cond = (self.cond_in[0] + self.cond_in[1]) + (self.cond_in[2] + self.cond_in[3])
        self.cond_out[...] = cond.astype(jnp.bfloat16)
        pairs = ((self.total, self.outs[0]), (self.cond_out, self.outs[1]))
        for i, (src, dst) in enumerate(pairs):
            pltpu.make_async_copy(src, dst, self.sems.at[14 + i, 0]).start()
        for i, (src, dst) in enumerate(pairs):
            pltpu.make_async_copy(src, dst, self.sems.at[14 + i, 0]).wait()


N_RED = len(Reduce.SEMS) + len(Reduce.BUFFERS)


def reduce_kernel(*refs):
    parts, small, cond, outs, small_out, cond_out = refs[:4], refs[4], refs[5], refs[6:10], refs[10], refs[11]
    scratch = refs[12:]
    place = Place()
    r = Reduce(place, parts, outs, scratch[:N_RED])
    little = Little(place, small, cond, small_out, cond_out, scratch[N_RED:])
    greet(place)
    order = (3, 2, 1, 0)
    r.start(order[0])
    little.load()
    little.run_pair()
    little.run_x()
    little.run_y()
    for i, t in enumerate(order):
        r.pass_on(t)
        if i < 3:
            r.start(order[i + 1])
        if i > 0:
            r.finish(order[i - 1])
        r.to_chip(t)
    r.finish(order[3])
    little.run_z()
    for t in order:
        r.done(t)


def reduce_grads(parts, small, cond):
    bf16 = jnp.bfloat16
    return pl.pallas_call(
        reduce_kernel,
        out_shape=[
            jax.ShapeDtypeStruct((2 * PART, WIDTH), bf16),
            jax.ShapeDtypeStruct((PART, 4 * WIDTH), bf16),
            jax.ShapeDtypeStruct((PART, 4 * WIDTH), bf16),
            jax.ShapeDtypeStruct((4 * PART, WIDTH), bf16),
            jax.ShapeDtypeStruct(SMALL, jnp.float32),
            jax.ShapeDtypeStruct((32, WIDTH), bf16),
        ],
        in_specs=[ANY] * 6,
        out_specs=[ANY] * 6,
        scratch_shapes=Reduce.SEMS + Reduce.BUFFERS + Little.SCRATCH,
        compiler_params=pltpu.CompilerParams(collective_id=1, has_side_effects=True, vmem_limit_bytes=58 << 20),
    )(*parts, small, cond)


HALO = 320
COND = 32
TILES = ((0, 0), (256, 256))
LOG2E = 1.4426950408889634


def nt(a, b):
    return lax.dot_general(a, b, (((1,), (1,)), ((), ())), preferred_element_type=jnp.float32)


def tn(a, b):
    return lax.dot_general(a, b, (((0,), (0,)), ((), ())), preferred_element_type=jnp.float32)


def nn(a, b):
    return jnp.dot(a, b, preferred_element_type=jnp.float32)


def make_bias(seg_q, seg_k, bias):
    bias[...] = jnp.where(seg_q[...] == seg_k[...], 0.0, -1e30)


def head(h):
    return slice(HEAD * h, HEAD * (h + 1))


def attend_kernel(query, pairs, seg_q, seg_k, attended, logsum, heads_q, heads_k, heads_v, heads_o, bias):
    make_bias(seg_q, seg_k, bias)
    for h in range(HEADS):
        heads_q[h] = query[:, head(h)]
        heads_k[h] = pairs[:, head(h)]
        heads_v[h] = pairs[:, HEADS * HEAD + HEAD * h : HEADS * HEAD + HEAD * (h + 1)]

    @pl.loop(0, HEADS)
    def _(h):
        for row, low in TILES:
            rows, keys = pl.ds(row, 256), pl.ds(low, HALO + 512 + COND - low)
            scores = nt(heads_q[h, rows], heads_k[h, keys]) * (HEAD**-0.5 * LOG2E) + bias[rows, keys]
            top = jnp.max(scores, axis=1, keepdims=True)
            expo = jnp.exp2(scores - top)
            total = jnp.sum(expo, axis=1, keepdims=True)
            mixed = nn(expo.astype(jnp.bfloat16), heads_v[h, keys])
            heads_o[h, rows] = (mixed / total).astype(jnp.bfloat16)
            logsum[h, rows] = top + jnp.log2(total)

    for h in range(HEADS):
        attended[:, head(h)] = heads_o[h]


def vmem(shape, dtype):
    return pltpu.VMEM(shape, dtype)


def attend(query, pairs, seg_q, seg_k):
    rows, keys = query.shape[0], pairs.shape[0]
    bf16 = jnp.bfloat16
    return pl.pallas_call(
        attend_kernel,
        out_shape=[
            jax.ShapeDtypeStruct((rows, HEADS * HEAD), bf16),
            jax.ShapeDtypeStruct((HEADS, rows, 1), jnp.float32),
        ],
        scratch_shapes=[
            vmem((HEADS, rows, HEAD), bf16),
            vmem((HEADS, keys, HEAD), bf16),
            vmem((HEADS, keys, HEAD), bf16),
            vmem((HEADS, rows, HEAD), bf16),
            vmem((rows, keys), jnp.float32),
        ],
        compiler_params=pltpu.CompilerParams(vmem_limit_bytes=50 << 20),
    )(query, pairs, seg_q, seg_k)


def attend_back_kernel(
    query, pairs, attended, grad, logsum, seg_q, seg_k, d_query, d_pairs,
    heads_q, heads_k, heads_v, heads_o, heads_g, heads_dk, heads_dv, sum_k, sum_v, bias,
):
    make_bias(seg_q, seg_k, bias)
    for h in range(HEADS):
        heads_q[h] = query[:, head(h)]
        heads_k[h] = pairs[:, head(h)]
        heads_v[h] = pairs[:, HEADS * HEAD + HEAD * h : HEADS * HEAD + HEAD * (h + 1)]
        heads_o[h] = attended[:, head(h)]
        heads_g[h] = grad[:, head(h)]
    scale = HEAD**-0.5

    @pl.loop(0, HEADS)
    def _(h):
        for row, low in TILES:
            rows, keys = pl.ds(row, 256), pl.ds(low, HALO + 512 + COND - low)
            q, k, v, g = heads_q[h, rows], heads_k[h, keys], heads_v[h, keys], heads_g[h, rows]
            scores = nt(q, k) * (scale * LOG2E) + bias[rows, keys]
            probs = jnp.exp2(scores - logsum[h, rows])
            d_probs = nt(g, v)
            inner = jnp.sum(g.astype(jnp.float32) * heads_o[h, rows].astype(jnp.float32), axis=1, keepdims=True)
            d_scores = (probs * (d_probs - inner)).astype(jnp.bfloat16)
            d_k, d_v = tn(d_scores, q), tn(probs.astype(jnp.bfloat16), g)
            if row == 0:
                sum_k[...] = d_k
                sum_v[...] = d_v
            else:
                sum_k[keys] += d_k
                sum_v[keys] += d_v
            heads_o[h, rows] = (nn(d_scores, k) * scale).astype(jnp.bfloat16)
        heads_dk[h] = (sum_k[...] * scale).astype(jnp.bfloat16)
        heads_dv[h] = sum_v[...].astype(jnp.bfloat16)

    for h in range(HEADS):
        d_query[:, head(h)] = heads_o[h]
        d_pairs[:, head(h)] = heads_dk[h]
        d_pairs[:, HEADS * HEAD + HEAD * h : HEADS * HEAD + HEAD * (h + 1)] = heads_dv[h]


def attend_back(query, pairs, attended, grad, logsum, seg_q, seg_k):
    rows, keys = query.shape[0], pairs.shape[0]
    bf16 = jnp.bfloat16
    small, large = (HEADS, rows, HEAD), (HEADS, keys, HEAD)
    return pl.pallas_call(
        attend_back_kernel,
        out_shape=[
            jax.ShapeDtypeStruct((rows, HEADS * HEAD), bf16),
            jax.ShapeDtypeStruct((keys, 2 * HEADS * HEAD), bf16),
        ],
        scratch_shapes=[
            vmem(small, bf16), vmem(large, bf16), vmem(large, bf16), vmem(small, bf16), vmem(small, bf16),
            vmem(large, bf16), vmem(large, bf16),
            vmem((keys, HEAD), jnp.float32), vmem((keys, HEAD), jnp.float32),
            vmem((rows, keys), jnp.float32),
        ],
        compiler_params=pltpu.CompilerParams(vmem_limit_bytes=58 << 20),
    )(query, pairs, attended, grad, logsum, seg_q, seg_k)


def item_ends(extra_length):
    lengths = extra_length[0] + (LEN_MIN - 1)
    count = lengths.shape[0]
    upto = lax.iota(jnp.int32, count)[None, :] <= lax.iota(jnp.int32, count)[:, None]
    return jnp.sum(jnp.where(upto, lengths[None, :], 0), axis=1)


def norm_parts(values):
    center = values - jnp.mean(values, axis=-1, keepdims=True)
    spread = jnp.mean(center * center, axis=-1, keepdims=True)
    rstd = lax.rsqrt(spread + 1e-05)
    return center * rstd, rstd


def norm_back(unit, rstd, gain, grad):
    scaled = grad * gain
    first = jnp.mean(scaled, axis=-1, keepdims=True)
    second = jnp.mean(scaled * unit, axis=-1, keepdims=True)
    return rstd * (scaled - first - unit * second), jnp.sum(grad * unit, axis=0), jnp.sum(grad, axis=0)


def quick(
    latents, skip_input, cond_tokens, extra_length, skip_weight, skip_bias, first_gain, first_shift, joint_weight,
    out_weight, out_bias, second_gain, second_shift, up_weight, up_bias, down_weight, down_bias, cotangent,
):
    f32, bf16 = jnp.float32, jnp.bfloat16
    vectors = (skip_bias, first_gain, first_shift, out_bias, second_gain, second_shift, down_bias, up_bias)
    packed = jnp.concatenate(vectors + (jnp.zeros((SMALL[0] * SMALL[1] - 11 * PART,), bf16),)).reshape(SMALL)
    small, skip_all, joint_all, up_all, down_all = gather_weights(
        packed, skip_weight, joint_weight, out_weight, up_weight, down_weight
    )
    small = small.reshape(8, SMALL[0] * SMALL[1])
    skip_offset, gain_first, shift_first, out_offset, gain_second, shift_second, down_offset = (
        v.reshape(WIDTH).astype(f32) for v in jnp.split(small[:, : 7 * PART], 7, axis=1)
    )
    up_offset = small[:, 7 * PART : 11 * PART].reshape(4 * WIDTH).astype(f32)
    skip_matrix = skip_all.reshape(2 * WIDTH, WIDTH)
    joint_out = joint_all.reshape(WIDTH, 4 * WIDTH)
    joint_matrix, out_matrix = joint_out[:, : 3 * WIDTH], joint_out[:, 3 * WIDTH :]
    up_matrix = up_all.reshape(WIDTH, 4 * WIDTH)
    down_matrix = down_all.reshape(4 * WIDTH, WIDTH)

    rows, width = latents.shape
    here = lax.axis_index("blk")
    ends = item_ends(extra_length)
    places = here * rows + lax.iota(jnp.int32, HALO + rows) - HALO
    items = jnp.where(places >= 0, jnp.sum((ends[None, :] <= places[:, None]).astype(jnp.int32), axis=1), -1)
    seg_q = items[HALO:, None]
    seg_k = jnp.concatenate([items, lax.iota(jnp.int32, COND) // 2])[None, :]

    base = nn(latents, skip_matrix[:width]) + nn(skip_input, skip_matrix[width:]) + skip_offset
    first_unit, first_rstd = norm_parts(base)
    first_in = (first_unit * gain_first + shift_first).astype(bf16)
    triple = nn(first_in, joint_matrix).astype(bf16)
    cond_flat = cond_tokens.reshape(-1, width).astype(f32)
    cond_unit, cond_rstd = norm_parts(cond_flat)
    cond_in = (cond_unit * gain_first + shift_first).astype(bf16)
    cond_pair = nn(cond_in, joint_matrix[:, width:]).astype(bf16)
    halo = lax.ppermute(triple[rows - HALO :, width:], "blk", [(i, i + 1) for i in range(7)])
    query, pairs = triple[:, :width], jnp.concatenate([halo, triple[:, width:], cond_pair], 0)
    attended, logsum = attend(query, pairs, seg_q, seg_k)
    middle = base + nn(attended, out_matrix) + out_offset
    second_unit, second_rstd = norm_parts(middle)
    second_in = (second_unit * gain_second + shift_second).astype(bf16)
    before = nn(second_in, up_matrix) + up_offset
    inside = 0.5 * (1.0 + lax.erf(before * 2**-0.5))
    slope = (inside + before * jnp.exp(-0.5 * before * before) * (2 * jnp.pi) ** -0.5).astype(bf16)
    hidden = (before * inside).astype(bf16)
    hidden, slope = lax.optimization_barrier((hidden, slope))
    output = middle + nn(hidden, down_matrix) + down_offset

    core = lax.rem(here, 2)

    def chip(grad):
        halves = grad.astype(bf16).reshape(4, 2, -1, grad.shape[1])
        mine = lax.dynamic_index_in_dim(halves, core, 1, keepdims=False)
        other = lax.dynamic_index_in_dim(halves, 1 - core, 1, keepdims=False)
        received = lax.ppermute(other, "blk", [(i, i ^ 1) for i in range(8)])
        return (mine.astype(f32) + received.astype(f32)).astype(bf16)

    g = cotangent.astype(f32)
    sum_down = jnp.sum(g, axis=0)
    part_down = chip(tn(hidden, cotangent))
    d_before = (nt(cotangent, down_matrix) * slope.astype(f32)).astype(bf16)
    sum_up = jnp.sum(d_before.astype(f32), axis=0)
    part_up = chip(tn(second_in, d_before))
    d_second = nt(d_before, up_matrix)
    d_norm, sum_gain_second, sum_shift_second = norm_back(second_unit, second_rstd, gain_second, d_second)
    d_middle = g + d_norm
    d_branch = d_middle.astype(bf16)
    sum_out = jnp.sum(d_branch.astype(f32), axis=0)
    part_out = tn(attended, d_branch)
    d_attended = nt(d_branch, out_matrix).astype(bf16)
    d_query, d_pairs = attend_back(query, pairs, attended, d_attended, logsum, seg_q, seg_k)
    returned = lax.ppermute(d_pairs[:HALO], "blk", [(i + 1, i) for i in range(7)])
    own = d_pairs[HALO : HALO + rows].astype(f32) + jnp.pad(returned.astype(f32), ((rows - HALO, 0), (0, 0)))
    d_triple = jnp.concatenate([d_query, own.astype(bf16)], 1)
    d_cond = d_pairs[HALO + rows :]
    cond_rows = jnp.concatenate([jnp.zeros((COND, width), bf16), d_cond], 1)
    part_joint = tn(first_in, d_triple) + tn(cond_in, cond_rows)
    part_joint_out = chip(jnp.concatenate([part_joint, part_out], 1))
    d_first = nt(d_triple, joint_matrix)
    d_norm, sum_gain_first, sum_shift_first = norm_back(first_unit, first_rstd, gain_first, d_first)
    d_cond_in = nt(d_cond, joint_matrix[:, width:])
    d_cond_flat, sum_gain_cond, sum_shift_cond = norm_back(cond_unit, cond_rstd, gain_first, d_cond_in)
    d_base = (d_middle + d_norm).astype(bf16)
    sum_skip = jnp.sum(d_base.astype(f32), axis=0)
    part_skip = chip(jnp.concatenate([tn(latents, d_base), tn(skip_input, d_base)], 0))
    d_joined = nt(d_base, skip_matrix).astype(bf16)

    sums = (
        sum_skip, sum_gain_first + sum_gain_cond, sum_shift_first + sum_shift_cond, sum_out, sum_gain_second,
        sum_shift_second, sum_down, sum_up,
    )
    flat = jnp.concatenate([v.reshape(8, -1) for v in sums], axis=1)
    flat = jnp.pad(flat, ((0, 0), (0, SMALL[0] * SMALL[1] - flat.shape[1]))).reshape(8, *SMALL)
    skip_sum, joint_out_sum, up_sum, down_sum, small_sum, cond_sum = reduce_grads(
        (part_skip, part_joint_out, part_up, part_down), flat, d_cond_flat
    )
    small_sum = small_sum.reshape(-1)
    v = jnp.split(small_sum[: 7 * PART], 7)
    return (
        output.astype(bf16),
        d_joined[:, :width],
        d_joined[:, width:],
        cond_sum.reshape(cond_tokens.shape),
        skip_sum.astype(f32),
        v[0],
        v[1],
        v[2],
        joint_out_sum[:, : 3 * WIDTH].astype(f32),
        joint_out_sum[:, 3 * WIDTH :].astype(f32),
        v[3],
        v[4],
        v[5],
        up_sum.astype(f32),
        small_sum[7 * PART : 11 * PART],
        down_sum.astype(f32),
        v[6],
    )


def shifted(value, axis, steps):
    count = lax.axis_size(axis)
    leading, last = (max(0, -steps), min(count, count - steps))
    return lax.ppermute(value, axis, [(source, source + steps) for source in range(leading, last)])


def layer_norm(values, gain, shift):
    center = values - jnp.mean(values, axis=-1, keepdims=True)
    spread = jnp.mean(center * center, axis=-1, keepdims=True)
    return center * lax.rsqrt(spread + 1e-05) * gain + shift


def contract_rows(left, right):
    return lax.dot_general(
        left, right, (((0,), (0,)), ((), ())), preferred_element_type=jnp.float32
    )


def contract_cols(left, right):
    return lax.dot_general(
        left, right, (((1,), (1,)), ((), ())), preferred_element_type=jnp.float32
    )


def segment_ids(ends, places):
    inside = jnp.sum((ends[None, :] <= places[:, None]).astype(jnp.int32), axis=1)
    return jnp.where(places >= 0, inside, -1)


def split_heads(block):
    return block.reshape(block.shape[0], HEADS, HEAD).transpose(1, 0, 2)


def merge_heads(block):
    return block.transpose(1, 0, 2).reshape(block.shape[1], HEADS * HEAD)


def masked_scores(query, keys, allowed):
    scores = contract_cols(query, keys) * HEAD ** (-0.5)
    return jnp.where(allowed, scores, -1e30)


def plain(
    latents,
    skip_input,
    cond_tokens,
    extra_length,
    skip_weight,
    skip_bias,
    first_gain,
    first_shift,
    joint_weight,
    out_weight,
    out_bias,
    second_gain,
    second_shift,
    up_weight,
    up_bias,
    down_weight,
    down_bias,
    cotangent,
):
    whole = (
        lax.all_gather(skip_weight, "blk", axis=0, tiled=True),
        lax.all_gather(skip_bias, "blk", axis=0, tiled=True),
        lax.all_gather(first_gain, "blk", axis=0, tiled=True),
        lax.all_gather(first_shift, "blk", axis=0, tiled=True),
        lax.all_gather(joint_weight, "blk", axis=0, tiled=True),
        lax.all_gather(out_weight, "blk", axis=0, tiled=True),
        lax.all_gather(out_bias, "blk", axis=0, tiled=True),
        lax.all_gather(second_gain, "blk", axis=0, tiled=True),
        lax.all_gather(second_shift, "blk", axis=0, tiled=True),
        lax.all_gather(up_weight, "blk", axis=0, tiled=True),
        lax.all_gather(up_bias, "blk", axis=0, tiled=True),
        lax.all_gather(down_weight, "blk", axis=0, tiled=True),
        lax.all_gather(down_bias, "blk", axis=0, tiled=True),
    )
    (
        skip_matrix,
        skip_offset,
        gain_first,
        shift_first,
        joint_matrix,
        out_matrix,
        out_offset,
        gain_second,
        shift_second,
        up_matrix,
        up_offset,
        down_matrix,
        down_offset,
    ) = whole
    rows = latents.shape[0]
    width = latents.shape[1]
    scale = HEAD ** (-0.5)
    joined = jnp.concatenate([latents, skip_input], 1)
    base = jnp.dot(joined, skip_matrix, preferred_element_type=jnp.float32) + skip_offset
    first_in = layer_norm(base, gain_first, shift_first).astype(jnp.bfloat16)
    triple = jnp.dot(first_in, joint_matrix, preferred_element_type=jnp.float32).astype(
        jnp.bfloat16
    )
    query = triple[:, :width]
    pair_here = triple[:, width:]
    pair_left = shifted(pair_here, "blk", 1)
    cond_flat = cond_tokens.reshape(-1, width).astype(jnp.float32)
    cond_in = layer_norm(cond_flat, gain_first, shift_first).astype(jnp.bfloat16)
    cond_pair = jnp.dot(
        cond_in, joint_matrix[:, width:], preferred_element_type=jnp.float32
    ).astype(jnp.bfloat16)
    pairs = jnp.concatenate([pair_left, pair_here, cond_pair], 0)
    ends = item_ends(extra_length)
    here = lax.axis_index("blk")
    places = here * rows + lax.iota(jnp.int32, rows)
    seg_here = segment_ids(ends, places)
    seg_left = segment_ids(ends, places - rows)
    cond_seg = lax.iota(jnp.int32, cond_pair.shape[0]) // 2
    allowed = seg_here[:, None] == jnp.concatenate([seg_left, seg_here, cond_seg])[None, :]
    head_query = split_heads(query)
    head_key = split_heads(pairs[:, :width])
    head_value = split_heads(pairs[:, width:])

    def head_forward(parts):
        query_one, key_one, value_one = parts
        scores = masked_scores(query_one, key_one, allowed)
        top = jnp.max(scores, axis=1, keepdims=True)
        expo = jnp.exp(scores - top)
        total = jnp.sum(expo, axis=1, keepdims=True)
        probs = (expo / total).astype(jnp.bfloat16)
        mixed = jnp.dot(probs, value_one, preferred_element_type=jnp.float32)
        return (mixed, (top + jnp.log(total))[:, 0])

    mixed, logsum = lax.map(head_forward, (head_query, head_key, head_value))
    attended = merge_heads(mixed).astype(jnp.bfloat16)
    middle = base + jnp.dot(attended, out_matrix, preferred_element_type=jnp.float32) + out_offset
    second_in = layer_norm(middle, gain_second, shift_second).astype(jnp.bfloat16)
    before = jnp.dot(second_in, up_matrix, preferred_element_type=jnp.float32) + up_offset
    hidden = jax.nn.gelu(before, approximate=False).astype(jnp.bfloat16)
    output = middle + jnp.dot(hidden, down_matrix, preferred_element_type=jnp.float32) + down_offset
    again = (
        lax.all_gather(skip_weight, "blk", axis=0, tiled=True),
        lax.all_gather(skip_bias, "blk", axis=0, tiled=True),
        lax.all_gather(first_gain, "blk", axis=0, tiled=True),
        lax.all_gather(first_shift, "blk", axis=0, tiled=True),
        lax.all_gather(joint_weight, "blk", axis=0, tiled=True),
        lax.all_gather(out_weight, "blk", axis=0, tiled=True),
        lax.all_gather(out_bias, "blk", axis=0, tiled=True),
        lax.all_gather(second_gain, "blk", axis=0, tiled=True),
        lax.all_gather(second_shift, "blk", axis=0, tiled=True),
        lax.all_gather(up_weight, "blk", axis=0, tiled=True),
        lax.all_gather(up_bias, "blk", axis=0, tiled=True),
        lax.all_gather(down_weight, "blk", axis=0, tiled=True),
        lax.all_gather(down_bias, "blk", axis=0, tiled=True),
    )
    (
        skip_matrix,
        skip_offset,
        gain_first,
        shift_first,
        joint_matrix,
        out_matrix,
        out_offset,
        gain_second,
        shift_second,
        up_matrix,
        up_offset,
        down_matrix,
        down_offset,
    ) = again
    incoming = cotangent.astype(jnp.float32)
    grad_down_offset = jnp.sum(incoming, axis=0)
    grad_down_matrix = contract_rows(hidden, cotangent)
    d_hidden = contract_cols(cotangent, down_matrix)
    gelu_value, gelu_pull = jax.vjp(partial(jax.nn.gelu, approximate=False), before)
    d_before = gelu_pull(d_hidden)[0].astype(jnp.bfloat16)
    grad_up_offset = jnp.sum(d_before.astype(jnp.float32), axis=0)
    grad_up_matrix = contract_rows(second_in, d_before)
    d_second = contract_cols(d_before, up_matrix)
    norm_value, norm_pull = jax.vjp(
        layer_norm, middle, gain_second.astype(jnp.float32), shift_second.astype(jnp.float32)
    )
    d_middle_norm, grad_gain_second, grad_shift_second = norm_pull(d_second)
    d_middle = incoming + d_middle_norm
    d_branch = d_middle.astype(jnp.bfloat16)
    grad_out_offset = jnp.sum(d_branch.astype(jnp.float32), axis=0)
    grad_out_matrix = contract_rows(attended, d_branch)
    d_attended = contract_cols(d_branch, out_matrix).astype(jnp.bfloat16)

    def head_backward(parts):
        query_one, key_one, value_one, grad_one, logsum_one = parts
        scores = masked_scores(query_one, key_one, allowed)
        probs = jnp.exp(scores - logsum_one[:, None])
        d_probs = contract_cols(grad_one, value_one)
        inner = jnp.sum(probs * d_probs, axis=1, keepdims=True)
        d_scores = (probs * (d_probs - inner)).astype(jnp.bfloat16)
        d_query_one = jnp.dot(d_scores, key_one, preferred_element_type=jnp.float32) * scale
        d_key_one = contract_rows(d_scores, query_one) * scale
        d_value_one = contract_rows(probs.astype(jnp.bfloat16), grad_one)
        return (d_query_one, d_key_one, d_value_one)

    d_query_heads, d_key_heads, d_value_heads = lax.map(
        head_backward, (head_query, head_key, head_value, split_heads(d_attended), logsum)
    )
    d_query = merge_heads(d_query_heads)
    d_pairs = jnp.concatenate([merge_heads(d_key_heads), merge_heads(d_value_heads)], 1)
    d_left = d_pairs[:rows]
    d_own = d_pairs[rows : 2 * rows]
    d_cond_part = d_pairs[2 * rows :]
    d_returned = shifted(d_left.astype(jnp.bfloat16), "blk", -1).astype(d_left.dtype)
    d_cond_total = lax.psum(d_cond_part.astype(jnp.bfloat16), "blk")
    d_triple = jnp.concatenate([d_query, d_own + d_returned], 1).astype(jnp.bfloat16)
    leading = (here == 0).astype(jnp.float32)
    cond_term = contract_rows(cond_in, d_cond_total) * leading
    grad_joint_matrix = contract_rows(first_in, d_triple) + jnp.concatenate(
        [jnp.zeros((width, width), jnp.float32), cond_term], 1
    )
    d_first = contract_cols(d_triple, joint_matrix)
    d_cond_in = contract_cols(d_cond_total, joint_matrix[:, width:])
    first_value, first_pull = jax.vjp(
        layer_norm, base, gain_first.astype(jnp.float32), shift_first.astype(jnp.float32)
    )
    d_base_norm, grad_gain_tokens, grad_shift_tokens = first_pull(d_first)
    cond_value, cond_pull = jax.vjp(
        layer_norm, cond_flat, gain_first.astype(jnp.float32), shift_first.astype(jnp.float32)
    )
    d_cond_flat, grad_gain_cond, grad_shift_cond = cond_pull(d_cond_in)
    grad_gain_first = grad_gain_tokens + leading * grad_gain_cond
    grad_shift_first = grad_shift_tokens + leading * grad_shift_cond
    d_base = (d_middle + d_base_norm).astype(jnp.bfloat16)
    grad_skip_offset = jnp.sum(d_base.astype(jnp.float32), axis=0)
    grad_skip_matrix = contract_rows(joined, d_base)
    d_joined = contract_cols(d_base, skip_matrix)
    shares = (
        lax.psum_scatter(
            grad_skip_matrix.astype(jnp.bfloat16), "blk", scatter_dimension=0, tiled=True
        ).astype(jnp.float32),
        lax.psum_scatter(
            grad_skip_offset.astype(jnp.bfloat16), "blk", scatter_dimension=0, tiled=True
        ).astype(jnp.float32),
        lax.psum_scatter(
            grad_gain_first.astype(jnp.bfloat16), "blk", scatter_dimension=0, tiled=True
        ).astype(jnp.float32),
        lax.psum_scatter(
            grad_shift_first.astype(jnp.bfloat16), "blk", scatter_dimension=0, tiled=True
        ).astype(jnp.float32),
        lax.psum_scatter(
            grad_joint_matrix.astype(jnp.bfloat16), "blk", scatter_dimension=0, tiled=True
        ).astype(jnp.float32),
        lax.psum_scatter(
            grad_out_matrix.astype(jnp.bfloat16), "blk", scatter_dimension=0, tiled=True
        ).astype(jnp.float32),
        lax.psum_scatter(
            grad_out_offset.astype(jnp.bfloat16), "blk", scatter_dimension=0, tiled=True
        ).astype(jnp.float32),
        lax.psum_scatter(
            grad_gain_second.astype(jnp.bfloat16), "blk", scatter_dimension=0, tiled=True
        ).astype(jnp.float32),
        lax.psum_scatter(
            grad_shift_second.astype(jnp.bfloat16), "blk", scatter_dimension=0, tiled=True
        ).astype(jnp.float32),
        lax.psum_scatter(
            grad_up_matrix.astype(jnp.bfloat16), "blk", scatter_dimension=0, tiled=True
        ).astype(jnp.float32),
        lax.psum_scatter(
            grad_up_offset.astype(jnp.bfloat16), "blk", scatter_dimension=0, tiled=True
        ).astype(jnp.float32),
        lax.psum_scatter(
            grad_down_matrix.astype(jnp.bfloat16), "blk", scatter_dimension=0, tiled=True
        ).astype(jnp.float32),
        lax.psum_scatter(
            grad_down_offset.astype(jnp.bfloat16), "blk", scatter_dimension=0, tiled=True
        ).astype(jnp.float32),
    )
    (
        share_skip,
        share_skip_offset,
        share_gain_first,
        share_shift_first,
        share_joint,
        share_out,
        share_out_offset,
        share_gain_second,
        share_shift_second,
        share_up,
        share_up_offset,
        share_down,
        share_down_offset,
    ) = shares
    summed = (
        lax.psum(share_skip.astype(jnp.bfloat16), "stream").astype(jnp.float32),
        lax.psum(share_skip_offset.astype(jnp.bfloat16), "stream").astype(jnp.float32),
        lax.psum(share_gain_first.astype(jnp.bfloat16), "stream").astype(jnp.float32),
        lax.psum(share_shift_first.astype(jnp.bfloat16), "stream").astype(jnp.float32),
        lax.psum(share_joint.astype(jnp.bfloat16), "stream").astype(jnp.float32),
        lax.psum(share_out.astype(jnp.bfloat16), "stream").astype(jnp.float32),
        lax.psum(share_out_offset.astype(jnp.bfloat16), "stream").astype(jnp.float32),
        lax.psum(share_gain_second.astype(jnp.bfloat16), "stream").astype(jnp.float32),
        lax.psum(share_shift_second.astype(jnp.bfloat16), "stream").astype(jnp.float32),
        lax.psum(share_up.astype(jnp.bfloat16), "stream").astype(jnp.float32),
        lax.psum(share_up_offset.astype(jnp.bfloat16), "stream").astype(jnp.float32),
        lax.psum(share_down.astype(jnp.bfloat16), "stream").astype(jnp.float32),
        lax.psum(share_down_offset.astype(jnp.bfloat16), "stream").astype(jnp.float32),
    )
    return (
        output.astype(jnp.bfloat16),
        d_joined[:, :width].astype(jnp.bfloat16),
        d_joined[:, width:].astype(jnp.bfloat16),
        d_cond_flat.reshape(cond_tokens.shape).astype(jnp.bfloat16),
        summed[0],
        summed[1],
        summed[2],
        summed[3],
        summed[4],
        summed[5],
        summed[6],
        summed[7],
        summed[8],
        summed[9],
        summed[10],
        summed[11],
        summed[12],
    )


def solution(mesh):
    placed = (
        P(("stream", "blk"), None),
        P(("stream", "blk"), None),
        P("stream", None, None),
        P("stream", None),
        P("blk", None),
        P("blk"),
        P("blk"),
        P("blk"),
        P("blk", None),
        P("blk", None),
        P("blk"),
        P("blk"),
        P("blk"),
        P("blk", None),
        P("blk"),
        P("blk", None),
        P("blk"),
        P(("stream", "blk"), None),
    )
    fits = mesh.shape["stream"] == 4 and mesh.shape["blk"] == 8
    return jax.shard_map(
        quick if fits else plain,
        mesh=mesh,
        in_specs=placed,
        out_specs=(
            P(("stream", "blk"), None),
            P(("stream", "blk"), None),
            P(("stream", "blk"), None),
            P("stream", None, None),
            P("blk", None),
            P("blk"),
            P("blk"),
            P("blk"),
            P("blk", None),
            P("blk", None),
            P("blk"),
            P("blk"),
            P("blk"),
            P("blk", None),
            P("blk"),
            P("blk", None),
            P("blk"),
        ),
        check_vma=False,
    )
```

```python
import functools
from functools import partial

import jax
import jax.numpy as jnp
from jax import lax
from jax.experimental import pallas as pl
from jax.experimental.pallas import tpu as pltpu
from jax.sharding import PartitionSpec as P

HEADS = 16
HEAD = 72
LEN_MIN = 192

MESH = pl.DeviceIdType.MESH
ANY = pl.BlockSpec(memory_space=pl.ANY)
WIDTH = 1152
PART = 144
SMALL = (16, 128)


class Place:
    def __init__(self):
        self.s = lax.axis_index("stream")
        self.b = lax.axis_index("blk")
        self.x = lax.rem(self.s, 2)
        self.y = lax.div(self.s, 2)
        self.c = lax.rem(self.b, 2)
        self.zz = lax.div(self.b, 2)

    def flip(self, bit):
        return 1 - bit

    def other(self, k):
        low, high = lax.rem(self.zz, 2), lax.div(self.zz, 2)
        return 2 * (1 - high if k & 2 else high) + (1 - low if k & 1 else low)

    def source(self, k):
        zz = self.zz
        table = ((1, 0, 3, 2), (2, 2, 1, 1), (3, 3, 0, 0))[k - 1]
        return jnp.where(zz < 2, jnp.where(zz == 0, table[0], table[1]), jnp.where(zz == 2, table[2], table[3]))

    def at(self, x=None, y=None, zz=None, c=None):
        x = self.x if x is None else x
        y = self.y if y is None else y
        zz = self.zz if zz is None else zz
        c = self.c if c is None else c
        return (2 * y + x, 2 * zz + c)


def greet(place):
    barrier = pltpu.get_barrier_semaphore()
    near = [
        place.at(x=1 - place.x),
        place.at(y=1 - place.y),
        place.at(c=1 - place.c),
    ] + [place.at(zz=place.other(k)) for k in (1, 2, 3)]
    for device in near:
        pl.semaphore_signal(barrier, inc=1, device_id=device, device_id_type=MESH)
    pl.semaphore_wait(barrier, len(near))


def remote(src, dst, send, recv, device):
    return pltpu.make_async_remote_copy(
        src_ref=src, dst_ref=dst, send_sem=send, recv_sem=recv, device_id=device, device_id_type=MESH
    )


def piece(kind, ref, b, x, y):
    if kind == "cols":
        return ref.at[b, :, pl.ds(pl.multiple_of((2 * y + x) * WIDTH, 128), WIDTH)]
    if kind == "rows":
        return ref.at[b, pl.ds(pl.multiple_of((2 * y + x) * PART, 16), PART)]
    low, size = (0, 80) if y == 0 else (80, 64)
    return ref.at[b, pl.ds(pl.multiple_of(x * PART + low, 16), size)]


KINDS = ("half", "cols", "cols", "rows")


class Gather:
    SEMS = [pltpu.SemaphoreType.DMA((4, 6, 4, 2)), pltpu.SemaphoreType.DMA((12,)), pltpu.SemaphoreType.DMA((2, 8))]

    def __init__(self, place, shards, outs, scratch):
        self.place = place
        self.small_in, self.skip_in, self.joint_in, self.out_in, self.up_in, self.down_in = shards
        self.small = outs[0]
        self.outs = outs[1:]
        self.sems, self.local_sems, self.small_sems = scratch[:3]
        self.stage = scratch[3:]
        self.sent = []

    def copy(self, t, x, y, zz, c, stage, k, device):
        ref = piece(KINDS[t], self.outs[t], 2 * zz + c, x, y)
        return remote(ref, ref, self.sems.at[t, stage, k, 0], self.sems.at[t, stage, k, 1], device)

    def each_y(self, t, run):
        if KINDS[t] != "half":
            run(self.place.y)
            return
        for value in (0, 1):
            pl.when(self.place.y == value)(lambda value=value: run(value))

    STAGE = [
        pltpu.VMEM((2 * PART, WIDTH), jnp.bfloat16),
        pltpu.VMEM((PART, 4 * WIDTH), jnp.bfloat16),
        pltpu.VMEM((PART, 4 * WIDTH), jnp.bfloat16),
        pltpu.VMEM((4 * PART, WIDTH), jnp.bfloat16),
    ]

    def locals(self, t):
        if t == 1:
            return [
                (self.joint_in, self.stage[1].at[:, pl.ds(0, 3 * WIDTH)]),
                (self.out_in, self.stage[1].at[:, pl.ds(3 * WIDTH, WIDTH)]),
            ]
        return [({0: self.skip_in, 2: self.up_in, 3: self.down_in}[t], self.stage[t])]

    def own_start(self, t):
        for i, (src, dst) in enumerate(self.locals(t)):
            pltpu.make_async_copy(src, dst, self.local_sems.at[2 * t + i]).start()

    def own_keep(self, t):
        return pltpu.make_async_copy(self.stage[t], self.outs[t].at[self.place.b], self.local_sems.at[8 + t])

    def own_done(self, t):
        for i, (src, dst) in enumerate(self.locals(t)):
            pltpu.make_async_copy(src, dst, self.local_sems.at[2 * t + i]).wait()
        self.own_keep(t).start()

    def own_copy(self, t, c):
        ref = self.outs[t].at[2 * self.place.zz + c]
        src = self.stage[t]
        sems = self.sems.at[t, 4, 0]
        return remote(src, ref, sems.at[0], sems.at[1], self.place.at(c=1 - self.place.c))

    def small_start(self):
        p = self.place
        for i, device in enumerate([p.at(zz=p.other(k)) for k in (1, 2, 3)] + [p.at(c=1 - p.c)]):
            remote(self.small_in, self.small.at[p.b], self.small_sems.at[0, i], self.small_sems.at[1, i], device).start()
        pltpu.make_async_copy(self.small_in, self.small.at[p.b], self.small_sems.at[0, 7]).start()

    def small_pass(self):
        p = self.place
        for i, k in enumerate((1, 2, 3)):
            ref = self.small.at[2 * p.other(k) + p.c]
            remote(ref, ref, self.small_sems.at[0, i], self.small_sems.at[1, i], p.at()).wait_recv()
            remote(ref, ref, self.small_sems.at[0, 4 + i], self.small_sems.at[1, 4 + i], p.at(c=1 - p.c)).start()

    def small_done(self):
        p = self.place
        for i, k in enumerate((0, 1, 2, 3)):
            ref = self.small.at[2 * p.other(k) + 1 - p.c]
            remote(ref, ref, self.small_sems.at[0, 3 + i], self.small_sems.at[1, 3 + i], p.at()).wait_recv()
        for i in range(7):
            remote(self.small_in, self.small_in, self.small_sems.at[0, i], self.small_sems.at[1, i], p.at()).wait_send()
        pltpu.make_async_copy(self.small_in, self.small.at[p.b], self.small_sems.at[0, 7]).wait()

    def stage_piece(self, t, y):
        x = self.place.x
        q = 2 * y + x
        if KINDS[t] == "cols":
            return self.stage[t].at[:, pl.ds(pl.multiple_of(q * WIDTH, 128), WIDTH)]
        if KINDS[t] == "rows":
            return self.stage[t].at[pl.ds(pl.multiple_of(q * PART, 16), PART)]
        low, size = (0, 80) if y == 0 else (80, 64)
        return self.stage[t].at[pl.ds(pl.multiple_of(x * PART + low, 16), size)]

    def z_copies(self, t, y, zz, start, own=False):
        p = self.place
        for step, send in ((1, 0), (-1, 5)):
            go = (zz <= p.zz) & (p.zz < 3) if step == 1 else (zz >= p.zz) & (p.zz > 0)
            ref = piece(KINDS[t], self.outs[t], 2 * zz + p.c, p.x, y)

            @pl.when(go)
            def _():
                copy = remote(self.stage_piece(t, y) if own else ref, ref, self.sems.at[t, send, zz, 0], self.sems.at[t, 0, zz, 1], p.at(zz=p.zz + step))
                copy.start() if start else copy.wait_send()

    def z_start(self, t):
        p = self.place
        self.each_y(t, lambda y: self.z_copies(t, y, p.zz, True, True))
        self.own_copy(t, p.c).start()

    def z_done(self, t, k):
        p = self.place
        zz = p.source(k)

        def run(y):
            self.copy(t, p.x, y, zz, p.c, 0, zz, p.at()).wait_recv()
            self.copy(t, p.x, y, zz, p.c, 1, k, p.at(x=1 - p.x)).start()
            self.copy(t, p.x, y, zz, p.c, 2, k, p.at(y=1 - p.y)).start()
            self.z_copies(t, y, zz, True)

        self.each_y(t, run)

    def by_x(self, t, k):
        return k == 1 or (k == 2 and t % 2 == 0)

    def xy_done(self, t, k):
        p = self.place

        def run(y):
            zz = p.source(k)
            self.copy(t, 1 - p.x, y, zz, p.c, 1, k, p.at()).wait_recv()
            if self.by_x(t, k):
                self.copy(t, 1 - p.x, y, zz, p.c, 3, k, p.at(y=1 - p.y)).start()
            self.copy(t, p.x, 1 - y, zz, p.c, 2, k, p.at()).wait_recv()
            if not self.by_x(t, k):
                self.copy(t, p.x, 1 - y, zz, p.c, 3, k, p.at(x=1 - p.x)).start()

        self.each_y(t, run)

    def diag_done(self, t, k):
        p = self.place

        def run(y):
            zz = p.source(k)
            self.copy(t, 1 - p.x, 1 - y, zz, p.c, 3, k, p.at()).wait_recv()

        self.each_y(t, run)
        self.pair_copy(t, k, p.c).start()

    def pair_copy(self, t, k, c):
        ref = self.outs[t].at[2 * self.place.source(k) + c]
        sems = self.sems.at[t, 4, k]
        return remote(ref, ref, sems.at[0], sems.at[1], self.place.at(c=1 - self.place.c))

    def ready(self, t):
        p = self.place
        self.own_copy(t, 1 - p.c).wait_recv()
        for k in (1, 2, 3):
            self.pair_copy(t, k, 1 - p.c).wait_recv()

    def all_sent(self, t):
        p = self.place
        self.own_copy(t, p.c).wait_send()
        self.own_keep(t).wait()

        def run(y):
            self.z_copies(t, y, p.zz, False, True)
            for k in (1, 2, 3):
                zz = p.source(k)
                self.z_copies(t, y, zz, False)
                self.copy(t, p.x, y, zz, p.c, 1, k, p.at()).wait_send()
                self.copy(t, p.x, y, zz, p.c, 2, k, p.at()).wait_send()
                if self.by_x(t, k):
                    self.copy(t, 1 - p.x, y, zz, p.c, 3, k, p.at()).wait_send()
                else:
                    self.copy(t, p.x, 1 - y, zz, p.c, 3, k, p.at()).wait_send()

        self.each_y(t, run)
        for k in (1, 2, 3):
            self.pair_copy(t, k, p.c).wait_send()


def gather_kernel(*refs):
    shards, outs, scratch = refs[:6], refs[6:11], refs[11:]
    place = Place()
    g = Gather(place, shards, outs, scratch)
    for t in range(4):
        g.own_start(t)
    greet(place)
    g.small_start()
    g.own_done(0)
    g.z_start(0)
    g.small_pass()
    for t in range(4):
        for k in (1, 2, 3):
            g.z_done(t, k)
        if t + 1 < 4:
            g.own_done(t + 1)
            g.z_start(t + 1)
        if t > 0:
            for k in (1, 2, 3):
                g.diag_done(t - 1, k)
        for k in (1, 2, 3):
            g.xy_done(t, k)
    for k in (1, 2, 3):
        g.diag_done(3, k)
    g.small_done()
    for t in range(4):
        g.ready(t)
        g.all_sent(t)


def gather_weights(small, skip, joint, out, up, down):
    bf16 = jnp.bfloat16
    return pl.pallas_call(
        gather_kernel,
        out_shape=[
            jax.ShapeDtypeStruct((8, *SMALL), bf16),
            jax.ShapeDtypeStruct((8, 2 * PART, WIDTH), bf16),
            jax.ShapeDtypeStruct((8, PART, 4 * WIDTH), bf16),
            jax.ShapeDtypeStruct((8, PART, 4 * WIDTH), bf16),
            jax.ShapeDtypeStruct((8, 4 * PART, WIDTH), bf16),
        ],
        in_specs=[ANY] * 6,
        out_specs=[ANY] * 5,
        scratch_shapes=Gather.SEMS + Gather.STAGE,
        compiler_params=pltpu.CompilerParams(collective_id=0, has_side_effects=True),
    )(small, skip, joint, out, up, down)


SIZES = (80, PART, PART, PART)


HALO = 320
COND = 32
TILES = ((0, 0), (256, 256))
LOG2E = 1.4426950408889634


def nt(a, b):
    return lax.dot_general(a, b, (((1,), (1,)), ((), ())), preferred_element_type=jnp.float32)


def tn(a, b):
    return lax.dot_general(a, b, (((0,), (0,)), ((), ())), preferred_element_type=jnp.float32)


def nn(a, b):
    return jnp.dot(a, b, preferred_element_type=jnp.float32)


def make_bias(seg_q, seg_k, bias):
    bias[...] = jnp.where(seg_q[...] == seg_k[...], 0.0, -1e30)


def head(h):
    return slice(HEAD * h, HEAD * (h + 1))


def attend_kernel(query, pairs, seg_q, seg_k, attended, logsum, heads_q, heads_k, heads_v, heads_o, bias):
    make_bias(seg_q, seg_k, bias)
    for h in range(HEADS):
        heads_q[h] = query[:, head(h)]
        heads_k[h] = pairs[:, head(h)]
        heads_v[h] = pairs[:, HEADS * HEAD + HEAD * h : HEADS * HEAD + HEAD * (h + 1)]

    @pl.loop(0, HEADS)
    def _(h):
        for row, low in TILES:
            rows, keys = pl.ds(row, 256), pl.ds(low, HALO + 512 + COND - low)
            scores = nt(heads_q[h, rows], heads_k[h, keys]) * (HEAD**-0.5 * LOG2E) + bias[rows, keys]
            top = jnp.max(scores, axis=1, keepdims=True)
            expo = jnp.exp2(scores - top)
            total = jnp.sum(expo, axis=1, keepdims=True)
            mixed = nn(expo.astype(jnp.bfloat16), heads_v[h, keys])
            heads_o[h, rows] = (mixed / total).astype(jnp.bfloat16)
            logsum[h, rows] = top + jnp.log2(total)

    for h in range(HEADS):
        attended[:, head(h)] = heads_o[h]


def vmem(shape, dtype):
    return pltpu.VMEM(shape, dtype)


def attend(query, pairs, seg_q, seg_k):
    rows, keys = query.shape[0], pairs.shape[0]
    bf16 = jnp.bfloat16
    return pl.pallas_call(
        attend_kernel,
        out_shape=[
            jax.ShapeDtypeStruct((rows, HEADS * HEAD), bf16),
            jax.ShapeDtypeStruct((HEADS, rows, 1), jnp.float32),
            jax.ShapeDtypeStruct((HEADS, rows, HEAD), bf16),
            jax.ShapeDtypeStruct((HEADS, keys, HEAD), bf16),
            jax.ShapeDtypeStruct((HEADS, keys, HEAD), bf16),
            jax.ShapeDtypeStruct((HEADS, rows, HEAD), bf16),
        ],
        scratch_shapes=[vmem((rows, keys), jnp.float32)],
        compiler_params=pltpu.CompilerParams(vmem_limit_bytes=50 << 20),
    )(query, pairs, seg_q, seg_k)


TOK = 512
ROWS8 = 16
ORDER = (0, 2, 1, 3)
LITTLE = (16, 256)
UNIT = (PART, WIDTH)


def add_into(out, *ins):
    @pl.loop(0, out.shape[0] // 16)
    def _(i):
        rows = pl.ds(pl.multiple_of(i * 16, 16), 16)
        total = ins[0][rows].astype(jnp.float32)
        for ref in ins[1:]:
            total += ref[rows].astype(jnp.float32)
        out[rows] = total.astype(out.dtype)


class Sum:
    SEMS = [
        pltpu.SemaphoreType.DMA((4, 4, 2, 2)),
        pltpu.SemaphoreType.DMA((4, 4, 2)),
        pltpu.SemaphoreType.DMA((4, 4, 2)),
        pltpu.SemaphoreType.DMA((4, 4, 2)),
        pltpu.SemaphoreType.DMA((23,)),
    ]
    SLOTS = [pltpu.VMEM((23, *UNIT), jnp.bfloat16), pltpu.VMEM((4, *UNIT), jnp.bfloat16)]
    LANDS = [
        jax.ShapeDtypeStruct(lead + (size, WIDTH), jnp.bfloat16)
        for size in SIZES
        for lead in ((4, 2), (4,), (4,))
    ]
    PARTS = [
        jax.ShapeDtypeStruct((8, PART, WIDTH), jnp.bfloat16),
        jax.ShapeDtypeStruct((4, PART, 4 * WIDTH), jnp.bfloat16),
        jax.ShapeDtypeStruct((4, PART, 4 * WIDTH), jnp.bfloat16),
        jax.ShapeDtypeStruct((4, 4, PART, WIDTH), jnp.bfloat16),
    ]

    def __init__(self, place, parts, lands, outs, sems, slots):
        self.place, self.parts, self.outs = place, parts, outs
        self.sem1, self.sem2, self.sem3, self.sem4, self.load_sems = sems
        self.slots, self.fins = slots
        self.land1, self.land2, self.land3 = ([lands[3 * t + i] for t in range(4)] for i in range(3))

    def slot(self, t, i):
        return self.slots.at[i, pl.ds(0, SIZES[t])]

    def fin(self, t):
        return self.fins.at[t, pl.ds(0, SIZES[t])]

    def piece(self, t, zz, x, y):
        ref = self.parts[t]
        if t == 0:
            return ref.at[2 * zz + x, pl.ds(pl.multiple_of(64 * y, 16), 80)]
        if t == 3:
            return ref.at[zz, 2 * y + x]
        return ref.at[zz, :, pl.ds(pl.multiple_of((2 * y + x) * WIDTH, 128), WIDTH)]

    def half(self, t, zz, x, y, j):
        return self.piece(t, zz, x, j) if zz < 2 else self.piece(t, zz, j, y)

    def keep(self, zz):
        return self.place.y if zz < 2 else self.place.x

    def first(self, t, zz, j):
        p = self.place
        device = p.at(x=1 - p.x) if zz < 2 else p.at(y=1 - p.y)
        sems = self.sem1.at[t, zz, j]
        src = self.half(t, zz, 1 - p.x, 1 - p.y, j)
        return remote(src, self.land1[t].at[zz, j], sems.at[0], sems.at[1], device)

    def start(self, t, zzs=ORDER):
        for zz in zzs:
            for j in (0, 1):
                self.first(t, zz, j).start()

    def load(self, t, src, i):
        return pltpu.make_async_copy(src, self.slot(t, i), self.load_sems.at[i])

    def second(self, t, zz):
        p = self.place
        device = p.at(y=1 - p.y) if zz < 2 else p.at(x=1 - p.x)
        sems = self.sem2.at[t, zz]
        return remote(self.slot(t, 2 * zz), self.land2[t].at[zz], sems.at[0], sems.at[1], device)

    def pass_on(self, t, after=None):
        p = self.place
        if after is not None:
            for zz in ORDER:
                self.second(after, zz).wait_send()

        def own(zz):
            return self.load(t, self.half(t, zz, p.x, p.y, 1 - self.keep(zz)), 2 * zz)

        def landed(zz):
            return self.load(t, self.land1[t].at[zz, 1 - self.keep(zz)], 2 * zz + 1)

        for zz in ORDER:
            own(zz).start()
        for zz in ORDER:
            for j in (0, 1):
                self.first(t, zz, j).wait_recv()
            landed(zz).start()
        for zz in ORDER:
            own(zz).wait()
            landed(zz).wait()
            add_into(self.slot(t, 2 * zz), self.slot(t, 2 * zz), self.slot(t, 2 * zz + 1))
            self.second(t, zz).start()

    def third(self, t, zz, slot):
        p = self.place
        return remote(
            self.slot(t, 8 + 3 * zz), self.land3[t].at[slot], self.sem3.at[t, zz, 0], self.sem3.at[t, slot, 1],
            p.at(zz=zz),
        )

    def third_sent(self, t):
        for zz in range(4):
            pl.when(zz != self.place.zz)(lambda zz=zz: self.third(t, zz, self.place.zz).wait_send())

    def to_chip(self, t, after=None):
        p = self.place
        if after is not None:
            self.third_sent(after)

        def load(zz, n):
            keep = self.keep(zz)
            if n == 0:
                src = self.half(t, zz, p.x, p.y, keep)
            else:
                src = self.land1[t].at[zz, keep] if n == 1 else self.land2[t].at[zz]
            return self.load(t, src, 8 + 3 * zz + n)

        for zz in ORDER:
            load(zz, 0).start()
            load(zz, 1).start()
        for zz in ORDER:
            self.second(t, zz).wait_recv()
            load(zz, 2).start()
        for zz in ORDER:
            for n in range(3):
                load(zz, n).wait()
            base = 8 + 3 * zz
            mine = self.slot(t, base)
            add_into(mine, mine, self.slot(t, base + 1), self.slot(t, base + 2))

            @pl.when(zz != p.zz)
            def _():
                self.third(t, zz, p.zz).start()

            @pl.when(zz == p.zz)
            def _():
                add_into(self.fin(t), mine)

    def result(self, t, x, y):
        ref = self.outs[t]
        if KINDS[t] == "cols":
            return ref.at[:, pl.ds(pl.multiple_of((2 * y + x) * WIDTH, 128), WIDTH)]
        if KINDS[t] == "rows":
            return ref.at[pl.ds(pl.multiple_of((2 * y + x) * PART, 16), PART)]
        low, size = (0, 80) if y == 0 else (80, 64)
        return ref.at[pl.ds(pl.multiple_of(x * PART + low, 16), size)]

    def fin_part(self, t, y):
        if KINDS[t] != "half" or y == 0:
            return self.fin(t)
        return self.fins.at[t, pl.ds(16, 64)]

    def each_y(self, t, run):
        if KINDS[t] != "half":
            run(self.place.y)
            return
        for value in (0, 1):
            pl.when(self.place.y == value)(lambda value=value: run(value))

    def spread(self, t, start):
        p = self.place

        def run(y):
            src, dst = self.fin_part(t, y), self.result(t, p.x, y)
            for k in (1, 2, 3):
                device = p.at(x=1 - p.x if k & 1 else p.x, y=1 - p.y if k & 2 else p.y)
                sems = self.sem4.at[t, k]
                copy = remote(src, dst, sems.at[0], sems.at[1], device)
                copy.start() if start else copy.wait_send()
            keep = pltpu.make_async_copy(src, dst, self.sem4.at[t, 0, 0])
            keep.start() if start else keep.wait()

        self.each_y(t, run)

    def finish(self, t):
        p = self.place
        for k in (1, 2, 3):
            ref = self.land3[t].at[p.other(k)]
            remote(ref, ref, self.sem3.at[t, p.zz, 0], self.sem3.at[t, p.other(k), 1], p.at()).wait_recv()
            self.load(t, ref, 19 + k).start()
        for k in (1, 2, 3):
            self.load(t, self.land3[t].at[p.other(k)], 19 + k).wait()
        add_into(self.fin(t), self.fin(t), *[self.slot(t, 19 + k) for k in (1, 2, 3)])
        self.spread(t, True)

    def done(self, t, last):
        p = self.place
        for zz in range(4):
            for j in (0, 1):
                self.first(t, zz, j).wait_send()
            if last:
                self.second(t, zz).wait_send()
        if last:
            self.third_sent(t)
        self.spread(t, False)

        def run(y):
            for k in (1, 2, 3):
                ref = self.result(t, 1 - p.x if k & 1 else p.x, 1 - y if k & 2 else y)
                sems = self.sem4.at[t, k]
                remote(ref, ref, sems.at[0], sems.at[1], p.at()).wait_recv()

        self.each_y(t, run)


class Vectors:
    SCRATCH = [
        pltpu.VMEM((8, *LITTLE), jnp.float32),
        pltpu.VMEM((4, *LITTLE), jnp.float32),
        pltpu.VMEM((4, *LITTLE), jnp.float32),
        pltpu.VMEM((4, *LITTLE), jnp.float32),
        pltpu.VMEM((4, *LITTLE), jnp.float32),
        pltpu.VMEM((4, *LITTLE), jnp.float32),
        pltpu.VMEM((COND, WIDTH), jnp.float32),
        pltpu.VMEM((COND, WIDTH), jnp.float32),
        pltpu.VMEM((COND, WIDTH), jnp.float32),
        pltpu.VMEM((4, COND, WIDTH), jnp.float32),
        pltpu.SemaphoreType.DMA((16, 2)),
    ]

    def __init__(self, place, small_out, cond_out, scratch):
        self.place, self.small_out, self.cond_out = place, small_out, cond_out
        self.part, self.pair, self.x_in, self.sum1, self.y_in, self.z_in = scratch[:6]
        self.mine, self.cond_pair, self.cond_sum, self.cond_in = scratch[6:10]
        self.sems = scratch[10]

    def copy(self, i, src, dst, device):
        return remote(src, dst, self.sems.at[i, 0], self.sems.at[i, 1], device)

    def small_pair(self, zz):
        p = self.place
        return self.copy(zz, self.part.at[2 * zz + 1 - p.c], self.pair.at[zz], p.at(c=1 - p.c))

    def run_pair(self):
        p = self.place
        for zz in range(4):
            self.small_pair(zz).start()
        cond = self.copy(4, self.mine, self.cond_pair, p.at(c=1 - p.c))
        cond.start()
        for zz in range(4):
            self.small_pair(zz).wait()
            self.pair[zz] += self.part[2 * zz + p.c]
        cond.wait()
        self.cond_sum[...] = self.mine[...] + self.cond_pair[...]
        self.copy(5, self.pair, self.x_in, p.at(x=1 - p.x)).start()
        for k in (1, 2, 3):
            self.copy(6 + k, self.cond_sum, self.cond_in.at[p.zz], p.at(zz=p.other(k))).start()
        self.cond_in[p.zz] = self.cond_sum[...]

    def run_x(self):
        p = self.place
        self.copy(5, self.pair, self.x_in, p.at(x=1 - p.x)).wait()
        self.sum1[...] = self.pair[...] + self.x_in[...]
        self.copy(6, self.sum1, self.y_in, p.at(y=1 - p.y)).start()

    def run_y(self):
        p = self.place
        self.copy(6, self.sum1, self.y_in, p.at(y=1 - p.y)).wait()
        self.sum1[...] += self.y_in[...]
        for k in (1, 2, 3):
            self.copy(9 + k, self.sum1.at[p.other(k)], self.z_in.at[p.zz], p.at(zz=p.other(k))).start()
        self.z_in[p.zz] = self.sum1[p.zz]

    def run_z(self):
        p = self.place
        for k in (1, 2, 3):
            self.copy(9 + k, self.sum1.at[p.other(k)], self.z_in.at[p.zz], p.at(zz=p.other(k))).wait()
            self.copy(6 + k, self.cond_sum, self.cond_in.at[p.zz], p.at(zz=p.other(k))).wait()
        self.small_out[...] = (self.z_in[0] + self.z_in[1]) + (self.z_in[2] + self.z_in[3])
        cond = (self.cond_in[0] + self.cond_in[1]) + (self.cond_in[2] + self.cond_in[3])
        self.cond_out[...] = cond.astype(jnp.bfloat16)


class Names:
    def __init__(self, names, refs):
        for (name, _), ref in zip(names, refs, strict=True):
            setattr(self, name, ref)


def hbm(shape, dtype=jnp.bfloat16):
    return jax.ShapeDtypeStruct(shape, dtype)


GROUP = 4
BACK_IN = [
    (name, ANY)
    for name in (
        "hidden_t", "slope", "cot", "second_t", "second_unit", "att_t", "q", "k", "v", "o", "logsum", "first_t",
        "first_unit", "joined_t", "w_skip", "w_joint", "w_up", "w_down", "cond_t",
    )
] + [
    (name, pl.BlockSpec(memory_space=pltpu.VMEM))
    for name in (
        "second_rstd", "first_rstd", "gain_second", "gain_first", "seg_q", "seg_k", "cond_unit", "cond_rstd"
    )
]
BACK_OUT = [
    ("d_latents", hbm((TOK, WIDTH))),
    ("d_skip", hbm((TOK, WIDTH))),
    ("g_skip", hbm((2 * PART, WIDTH))),
    ("g_joint", hbm((PART, 4 * WIDTH))),
    ("g_up", hbm((PART, 4 * WIDTH))),
    ("g_down", hbm((4 * PART, WIDTH))),
    ("hidden_t2", hbm((4, 4, PART, TOK))),
    ("second_t2", hbm((4, PART, TOK))),
    ("att_t2", hbm((4, PART, TOK))),
    ("first_t2", hbm((4, PART, TOK))),
    ("joined_t2", hbm((4, 2 * PART, TOK))),
]
BACK_SCRATCH = [
    ("cot_v", pltpu.VMEM((TOK, WIDTH), jnp.bfloat16)),
    ("cot2", pltpu.VMEM((TOK, WIDTH), jnp.bfloat16)),
    ("wide", pltpu.VMEM((4, TOK, WIDTH), jnp.bfloat16)),
    ("before2", pltpu.VMEM((4, TOK, WIDTH), jnp.bfloat16)),
    ("triple2", pltpu.VMEM((3, TOK, WIDTH), jnp.bfloat16)),
    ("branch", pltpu.VMEM((TOK, WIDTH), jnp.bfloat16)),
    ("branch2", pltpu.VMEM((TOK, WIDTH), jnp.bfloat16)),
    ("base_g", pltpu.VMEM((TOK, WIDTH), jnp.bfloat16)),
    ("base2", pltpu.VMEM((TOK, WIDTH), jnp.bfloat16)),
    ("acc", pltpu.VMEM((TOK, WIDTH), jnp.float32)),
    ("d_middle", pltpu.VMEM((TOK, WIDTH), jnp.float32)),
    ("tile", pltpu.VMEM((TOK, WIDTH), jnp.bfloat16)),
    ("weight", pltpu.VMEM((2, 8, PART, WIDTH), jnp.bfloat16)),
    ("left", pltpu.VMEM((2, 4, PART, TOK), jnp.bfloat16)),
    ("made", pltpu.VMEM((2, 4, PART, WIDTH), jnp.bfloat16)),
    ("heads_g", pltpu.VMEM((HEADS, TOK, HEAD), jnp.bfloat16)),
    ("qh", pltpu.VMEM((GROUP, TOK, HEAD), jnp.bfloat16)),
    ("oh", pltpu.VMEM((GROUP, TOK, HEAD), jnp.bfloat16)),
    ("kh", pltpu.VMEM((GROUP, HALO + TOK + COND, HEAD), jnp.bfloat16)),
    ("vh", pltpu.VMEM((GROUP, HALO + TOK + COND, HEAD), jnp.bfloat16)),
    ("lh", pltpu.VMEM((GROUP, TOK, 1), jnp.float32)),
    ("sum_k", pltpu.VMEM((HALO + TOK + COND, HEAD), jnp.float32)),
    ("sum_v", pltpu.VMEM((HALO + TOK + COND, HEAD), jnp.float32)),
    ("bias", pltpu.VMEM((TOK, HALO + TOK + COND), jnp.float32)),
    ("halo2", pltpu.VMEM((2, HALO, WIDTH), jnp.bfloat16)),
    ("d_cond", pltpu.VMEM((128, 2 * WIDTH), jnp.bfloat16)),
    ("cond_left", pltpu.VMEM((4, PART, 128), jnp.bfloat16)),
    ("sums", pltpu.VMEM((16, WIDTH), jnp.float32)),
    ("wide_sum", pltpu.VMEM((1, WIDTH), jnp.float32)),
    ("w_sems", pltpu.SemaphoreType.DMA((2,))),
    ("l_sems", pltpu.SemaphoreType.DMA((2,))),
    ("m_sems", pltpu.SemaphoreType.DMA((2,))),
    ("t_sems", pltpu.SemaphoreType.DMA((8,))),
    ("sib_sems", pltpu.SemaphoreType.DMA((32, 2))),
]
SUM_SKIP, SUM_GAIN1, SUM_SHIFT1, SUM_OUT, SUM_GAIN2, SUM_SHIFT2, SUM_DOWN, SUM_UP = range(8)


def back_greet(place):
    barrier = pltpu.get_barrier_semaphore()
    p = place
    near = [p.at(x=1 - p.x), p.at(y=1 - p.y), p.at(c=1 - p.c)] + [p.at(zz=p.other(k)) for k in (1, 2, 3)]
    for device in near:
        pl.semaphore_signal(barrier, inc=1, device_id=device, device_id_type=MESH)
    up = (p.c == 1) & (p.zz < 3)
    down = (p.c == 0) & (p.zz > 0)
    for go, device in ((up, (p.s, p.b + 1)), (down, (p.s, p.b - 1))):

        @pl.when(go)
        def _():
            pl.semaphore_signal(barrier, inc=1, device_id=device, device_id_type=MESH)

    pl.when(up | down)(lambda: pl.semaphore_wait(barrier, len(near) + 1))
    pl.when(jnp.logical_not(up | down))(lambda: pl.semaphore_wait(barrier, len(near)))


def back_kernel(*refs):
    cuts = [len(BACK_IN), len(BACK_OUT), 2, len(Sum.PARTS), len(Sum.LANDS), len(BACK_SCRATCH), len(Sum.SEMS), 2]
    pieces, at = [], 0
    for cut in cuts:
        pieces.append(refs[at : at + cut])
        at += cut
    i, o, b = Names(BACK_IN, pieces[0]), Names(BACK_OUT, pieces[1]), Names(BACK_SCRATCH, pieces[5])
    p = Place()
    total = Sum(p, pieces[3], pieces[4], (o.g_skip, o.g_joint, o.g_up, o.g_down), pieces[6], pieces[7])
    vectors = Vectors(p, *pieces[2], refs[at:])
    f32, bf16 = jnp.float32, jnp.bfloat16

    def copy(src, dst, sem):
        return pltpu.make_async_copy(src, dst, sem)

    def sib(n, src, dst):
        return remote(src, dst, b.sib_sems.at[n, 0], b.sib_sems.at[n, 1], p.at(c=1 - p.c))

    def halves(n, src, dst):
        return [sib(4 * n + zz, src.at[2 * zz + 1 - p.c], dst.at[zz]) for zz in range(4)]

    left_pairs = (
        (i.hidden_t, o.hidden_t2), (i.second_t, o.second_t2), (i.att_t, o.att_t2), (i.first_t, o.first_t2),
        (i.joined_t, o.joined_t2),
    )

    def stream(blocks, body):
        def load(n):
            return copy(blocks[n], b.weight.at[n % 2], b.w_sems.at[n % 2])

        load(0).start()
        for n in range(len(blocks)):
            if n + 1 < len(blocks):
                load(n + 1).start()
            load(n).wait()
            body(n, b.weight[n % 2].reshape(WIDTH, WIDTH))

    def column(ref, q):
        return ref.at[:, :, pl.ds(q * WIDTH, WIDTH)]

    def by_rows(size, body):
        @pl.loop(0, TOK // size)
        def _(n):
            body(pl.ds(pl.multiple_of(n * size, size), size))

    def add_sum(row, value):
        b.sums[row : row + 1, :] += value

    def colsum(value):
        return jnp.sum(value, axis=0, keepdims=True)

    def form(n, dst, own, own2, pairs, extra=None):
        result = nn(own.reshape(4 * PART, TOK), pairs[0]) + nn(own2.reshape(4 * PART, TOK), pairs[1])
        if extra is not None:
            result += extra
        slot = n % 2
        b.made[slot] = result.astype(bf16).reshape(4, PART, WIDTH)
        copy(b.made.at[slot], dst, b.m_sems.at[slot]).start()

    def formed(n, dst):
        copy(b.made.at[n % 2], dst, b.m_sems.at[n % 2]).wait()

    def load_left(own, other):
        one, two = copy(own, b.left.at[0], b.l_sems.at[0]), copy(other, b.left.at[1], b.l_sems.at[1])
        one.start()
        two.start()
        one.wait()
        two.wait()

    def send_all(copies):
        for one in copies:
            one.start()

    def recv_all(copies):
        for one in copies:
            one.wait_recv()

    cot_load = copy(i.cot, b.cot_v, b.t_sems.at[0])
    cot_load.start()
    back_greet(p)
    sib_cot = sib(20, i.cot, b.cot2)
    left_sends = [halves(n, src, dst) for n, (src, dst) in enumerate(left_pairs)]
    send_all(left_sends[0])
    sib_cot.start()
    for n in (1, 2, 3, 4):
        send_all(left_sends[n])
    b.sums[...] = jnp.zeros_like(b.sums)
    b.d_cond[2 * COND :] = jnp.zeros((128 - 2 * COND, 2 * WIDTH), bf16)
    vectors.part[...] = jnp.zeros_like(vectors.part)
    make_bias(i.seg_q, i.seg_k, b.bias)
    cot_load.wait()

    def before_sib(q):
        return sib(21 + q, b.wide.at[q], b.before2.at[q])

    def slope_load(q):
        return copy(i.slope.at[:, pl.ds(q * WIDTH, WIDTH)], b.tile, b.t_sems.at[1])

    def do_before(q, weight):
        slope_load(q).start()
        b.acc[...] = nt(b.cot_v[...], weight)
        slope_load(q).wait()
        b.wide_sum[...] = jnp.zeros_like(b.wide_sum)

        @functools.partial(by_rows, 64)
        def _(rows):
            value = (b.acc[rows] * b.tile[rows].astype(f32)).astype(bf16)
            b.wide[q, rows] = value
            b.wide_sum[...] += colsum(value.astype(f32))

        for n in range(8):
            row = 7 + n % 4
            vectors.part[2 * q + n // 4, row : row + 1, 0:PART] = b.wide_sum[:, n * PART : (n + 1) * PART]
        before_sib(q).start()

    stream([i.w_down.at[pl.ds(8 * q, 8)] for q in range(4)], do_before)

    sib_cot.wait_recv()
    down_parts = pieces[3][3]
    for n, zz in enumerate(ORDER):
        left_sends[0][zz].wait_recv()
        load_left(i.hidden_t.at[2 * zz + p.c], o.hidden_t2.at[zz])
        form(n, down_parts.at[zz], b.left[0], b.left[1], (b.cot_v[...], b.cot2[...]))
        if n > 0:
            formed(n - 1, down_parts.at[ORDER[n - 1]])
            total.start(3, (ORDER[n - 1],))
    formed(3, down_parts.at[ORDER[3]])
    total.start(3, (ORDER[3],))

    def load_lefts(n):
        own = [copy(left_pairs[n][0].at[2 * zz + p.c], b.left.at[0, zz], b.t_sems.at[4 + zz]) for zz in range(4)]
        send_all(own)
        recv_all_halves = left_sends[n]
        for one in recv_all_halves:
            one.wait_recv()
        two = copy(left_pairs[n][1], b.left.at[1], b.l_sems.at[1])
        two.start()
        for one in own:
            one.wait()
        two.wait()

    up_parts = pieces[3][2]
    load_lefts(1)
    for q in range(4):
        before_sib(q).wait_recv()
        form(q, column(up_parts, q), b.left[0], b.left[1], (b.wide[q], b.before2[q]))
        if q > 0:
            formed(q - 1, column(up_parts, q - 1))
    formed(3, column(up_parts, 3))

    def do_second(q, weight):
        value = nt(b.wide[q], weight)
        if q == 0:
            b.acc[...] = value
        else:
            b.acc[...] += value

    unit_load = copy(i.second_unit, b.tile, b.t_sems.at[1])
    unit_load.start()
    stream([column(i.w_up, q) for q in range(4)], do_second)
    unit_load.wait()

    def norm_rows(unit, rstd, gain, grad, gain_row, shift_row):
        scaled = grad * gain
        mean1 = jnp.mean(scaled, axis=1, keepdims=True)
        mean2 = jnp.mean(scaled * unit, axis=1, keepdims=True)
        add_sum(gain_row, colsum(grad * unit))
        add_sum(shift_row, colsum(grad))
        return rstd * (scaled - mean1 - unit * mean2)

    @functools.partial(by_rows, 64)
    def _(rows):
        unit = b.tile[rows].astype(f32)
        back = norm_rows(unit, i.second_rstd[rows], i.gain_second[...], b.acc[rows], SUM_GAIN2, SUM_SHIFT2)
        g = b.cot_v[rows].astype(f32)
        middle = g + back
        b.d_middle[rows] = middle
        low = middle.astype(bf16)
        b.branch[rows] = low
        add_sum(SUM_OUT, colsum(low.astype(f32)))
        add_sum(SUM_DOWN, colsum(g))

    branch_sib = sib(25, b.branch, b.branch2)
    branch_sib.start()

    def do_attended(_, weight):
        b.tile[...] = nt(b.branch[...], weight).astype(bf16)
        for h in range(HEADS):
            b.heads_g[h] = b.tile[:, head(h)]

    stream([column(i.w_joint, 3)], do_attended)

    joint_parts = pieces[3][1]
    load_lefts(2)
    branch_sib.wait_recv()
    form(0, column(joint_parts, 3), b.left[0], b.left[1], (b.branch[...], b.branch2[...]))
    formed(0, column(joint_parts, 3))

    total.pass_on(3)
    total.start(2)
    for q in range(4):
        before_sib(q).wait_send()

    scale = HEAD**-0.5
    n_keys = HALO + TOK + COND

    def group_loads(start):
        hs = pl.ds(start, GROUP)
        pairs = ((i.q, b.qh), (i.o, b.oh), (i.k, b.kh), (i.v, b.vh), (i.logsum, b.lh))
        return [copy(src.at[hs], dst, b.t_sems.at[n]) for n, (src, dst) in enumerate(pairs)]

    def group(start):
        send_all(group_loads(start))
        for one in group_loads(start):
            one.wait()

        @pl.loop(0, GROUP)
        def _(h):
            for row, low in TILES:
                rows, keys = pl.ds(row, 256), pl.ds(low, n_keys - low)
                q, k, v, g = b.qh[h, rows], b.kh[h, keys], b.vh[h, keys], b.heads_g[start + h, rows]
                scores = nt(q, k) * (scale * LOG2E) + b.bias[rows, keys]
                probs = jnp.exp2(scores - b.lh[h, rows])
                d_probs = nt(g, v)
                inner = jnp.sum(g.astype(f32) * b.oh[h, rows].astype(f32), axis=1, keepdims=True)
                d_scores = (probs * (d_probs - inner)).astype(bf16)
                d_k, d_v = tn(d_scores, q), tn(probs.astype(bf16), g)
                if row == 0:
                    b.sum_k[...] = d_k
                    b.sum_v[...] = d_v
                else:
                    b.sum_k[keys] += d_k
                    b.sum_v[keys] += d_v
                b.oh[h, rows] = (nn(d_scores, k) * scale).astype(bf16)
            b.kh[h] = (b.sum_k[...] * scale).astype(bf16)
            b.vh[h] = b.sum_v[...].astype(bf16)

        for n in range(GROUP):
            at = head(start + n)
            b.wide[0, :, at] = b.oh[n]
            for j, made in ((0, b.kh), (1, b.vh)):
                wide = slice(j * WIDTH + at.start, j * WIDTH + at.stop)
                b.before2[j, 0:HALO, at] = made[n, 0:HALO]
                b.wide[1 + j, :, at] = made[n, HALO : HALO + TOK]
                b.d_cond[0:COND, wide] = made[n, HALO + TOK :]

    group(0)
    group(4)
    total.to_chip(3)
    group(8)
    group(12)

    def halo_copy(device):
        src = b.before2.at[pl.ds(0, 2), pl.ds(0, HALO)]
        return remote(src, b.halo2, b.sib_sems.at[31, 0], b.sib_sems.at[31, 1], device)

    cond_sib = sib(30, b.d_cond.at[pl.ds(0, COND)], b.d_cond.at[pl.ds(COND, COND)])
    cond_sib.start()
    pl.when(p.b > 0)(lambda: halo_copy((p.s, p.b - 1)).start())

    def triple_sib(j):
        return sib(26 + j, b.wide.at[j], b.triple2.at[j])

    triple_sib(0).start()
    load_lefts(3)
    for zz in range(4):
        copy(i.cond_t.at[2 * zz + p.c], b.cond_left.at[zz], b.t_sems.at[zz]).start()

    @pl.when(p.b < 7)
    def _():
        halo_copy((p.s, p.b)).wait_recv()

        @pl.loop(0, HALO // 64)
        def _(n):
            low = pl.ds(pl.multiple_of(n * 64, 64), 64)
            rows = pl.ds(pl.multiple_of(n * 64 + TOK - HALO, 64), 64)
            for j in (0, 1):
                extra = b.halo2[j, low].astype(f32)
                b.wide[1 + j, rows] = (b.wide[1 + j, rows].astype(f32) + extra).astype(bf16)

    triple_sib(1).start()
    triple_sib(2).start()
    for zz in range(4):
        copy(i.cond_t.at[2 * zz + p.c], b.cond_left.at[zz], b.t_sems.at[zz]).wait()
    cond_sib.wait_recv()

    for j in range(3):
        triple_sib(j).wait_recv()
        extra = None
        if j > 0:
            extra = nn(b.cond_left[...].reshape(4 * PART, 128), b.d_cond[:, (j - 1) * WIDTH : j * WIDTH])
        form(j, column(joint_parts, j), b.left[0], b.left[1], (b.wide[j], b.triple2[j]), extra)
        if j > 0:
            formed(j - 1, column(joint_parts, j - 1))
    formed(2, column(joint_parts, 2))
    total.pass_on(2, after=3)
    total.start(1)
    total.finish(3)

    def do_first(j, weight):
        value = nt(b.wide[j], weight)
        if j == 0:
            b.acc[...] = value
        else:
            b.acc[...] += value
            cond = nt(b.d_cond[0:COND, (j - 1) * WIDTH : j * WIDTH], weight)
            if j == 1:
                vectors.mine[...] = cond
            else:
                vectors.mine[...] += cond

    unit_load = copy(i.first_unit, b.tile, b.t_sems.at[1])
    unit_load.start()
    stream([column(i.w_joint, j) for j in range(3)], do_first)
    unit_load.wait()

    @functools.partial(by_rows, 64)
    def _(rows):
        unit = b.tile[rows].astype(f32)
        back = norm_rows(unit, i.first_rstd[rows], i.gain_first[...], b.acc[rows], SUM_GAIN1, SUM_SHIFT1)
        low = (b.d_middle[rows] + back).astype(bf16)
        b.base_g[rows] = low
        add_sum(SUM_SKIP, colsum(low.astype(f32)))

    base_sib = sib(29, b.base_g, b.base2)
    base_sib.start()
    vectors.mine[...] = norm_rows(
        i.cond_unit[...], i.cond_rstd[...], i.gain_first[...], vectors.mine[...], SUM_GAIN1, SUM_SHIFT1
    )
    for row in range(7):
        for n in range(8):
            vectors.part[n, row : row + 1, 0:PART] = b.sums[row : row + 1, n * PART : (n + 1) * PART]
    vectors.run_pair()
    total.to_chip(2, after=3)

    skip_parts = pieces[3][0]
    base_sib.wait_recv()
    for n in (0, 1):
        own = [
            copy(
                i.joined_t.at[2 * (2 * n + k // 2) + p.c, pl.ds((k % 2) * PART, PART)],
                b.left.at[0, k],
                b.t_sems.at[4 + k],
            )
            for k in range(4)
        ]
        for k in (0, 1):
            left_sends[4][2 * n + k].wait_recv()
        two = [
            copy(
                o.joined_t2.at[2 * n + k // 2, pl.ds((k % 2) * PART, PART)], b.left.at[1, k], b.t_sems.at[k]
            )
            for k in range(4)
        ]
        send_all(own + two)
        for one in own + two:
            one.wait()
        form(n, skip_parts.at[pl.ds(4 * n, 4)], b.left[0], b.left[1], (b.base_g[...], b.base2[...]))
    for n in (0, 1):
        formed(n, skip_parts.at[pl.ds(4 * n, 4)])
    vectors.run_x()

    def do_joined(n, weight):
        made = (b.tile, b.branch)[n]
        made[...] = nt(b.base_g[...], weight).astype(bf16)
        copy(made, (o.d_latents, o.d_skip)[n], b.t_sems.at[n]).start()

    branch_sib.wait_send()
    stream([i.w_skip.at[pl.ds(8 * n, 8)] for n in range(2)], do_joined)
    vectors.run_y()

    total.pass_on(1, after=2)
    total.start(0)
    total.finish(2)
    total.to_chip(1, after=2)
    total.pass_on(0, after=1)
    total.finish(1)
    total.to_chip(0, after=1)
    total.finish(0)
    vectors.run_z()
    for n in (0, 1):
        copy((b.tile, b.branch)[n], (o.d_latents, o.d_skip)[n], b.t_sems.at[n]).wait()
    for group_sends in left_sends:
        for one in group_sends:
            one.wait_send()
    for one in (sib_cot, cond_sib, base_sib, triple_sib(0), triple_sib(1), triple_sib(2)):
        one.wait_send()
    pl.when(p.b > 0)(lambda: halo_copy((p.s, p.b - 1)).wait_send())
    for t in (3, 2, 1, 0):
        total.done(t, t == 0)


def backward(arrays):
    vm = pl.BlockSpec(memory_space=pltpu.VMEM)
    outs = pl.pallas_call(
        back_kernel,
        out_shape=[shape for _, shape in BACK_OUT] + [
            jax.ShapeDtypeStruct(LITTLE, jnp.float32), jax.ShapeDtypeStruct((COND, WIDTH), jnp.bfloat16)
        ] + Sum.PARTS + Sum.LANDS,
        in_specs=[spec for _, spec in BACK_IN],
        out_specs=[ANY] * len(BACK_OUT) + [vm] * 2 + [ANY] * (len(Sum.PARTS) + len(Sum.LANDS)),
        scratch_shapes=[shape for _, shape in BACK_SCRATCH] + Sum.SEMS + Sum.SLOTS + Vectors.SCRATCH,
        compiler_params=pltpu.CompilerParams(collective_id=1, has_side_effects=True, vmem_limit_bytes=60 << 20),
    )(*[arrays[name] for name, _ in BACK_IN])
    named = {name: out for (name, _), out in zip(BACK_OUT, outs)}
    return named, outs[len(BACK_OUT)], outs[len(BACK_OUT) + 1]


def item_ends(extra_length):
    lengths = extra_length[0] + (LEN_MIN - 1)
    count = lengths.shape[0]
    upto = lax.iota(jnp.int32, count)[None, :] <= lax.iota(jnp.int32, count)[:, None]
    return jnp.sum(jnp.where(upto, lengths[None, :], 0), axis=1)


def norm_parts(values):
    center = values - jnp.mean(values, axis=-1, keepdims=True)
    spread = jnp.mean(center * center, axis=-1, keepdims=True)
    rstd = lax.rsqrt(spread + 1e-05)
    return center * rstd, rstd


def quick(
    latents, skip_input, cond_tokens, extra_length, skip_weight, skip_bias, first_gain, first_shift, joint_weight,
    out_weight, out_bias, second_gain, second_shift, up_weight, up_bias, down_weight, down_bias, cotangent,
):
    f32, bf16 = jnp.float32, jnp.bfloat16
    vectors = (skip_bias, first_gain, first_shift, out_bias, second_gain, second_shift, down_bias, up_bias)
    packed = jnp.concatenate(vectors + (jnp.zeros((SMALL[0] * SMALL[1] - 11 * PART,), bf16),)).reshape(SMALL)
    small, skip_all, joint_all, up_all, down_all = gather_weights(
        packed, skip_weight, joint_weight, out_weight, up_weight, down_weight
    )
    small = small.reshape(8, SMALL[0] * SMALL[1])
    skip_offset, gain_first, shift_first, out_offset, gain_second, shift_second, down_offset = (
        v.reshape(WIDTH).astype(f32) for v in jnp.split(small[:, : 7 * PART], 7, axis=1)
    )
    up_offset = small[:, 7 * PART : 11 * PART].reshape(4 * WIDTH).astype(f32)
    skip_matrix = skip_all.reshape(2 * WIDTH, WIDTH)
    joint_out = joint_all.reshape(WIDTH, 4 * WIDTH)
    joint_matrix, out_matrix = joint_out[:, : 3 * WIDTH], joint_out[:, 3 * WIDTH :]
    up_matrix = up_all.reshape(WIDTH, 4 * WIDTH)
    down_matrix = down_all.reshape(4 * WIDTH, WIDTH)

    rows, width = latents.shape
    here = lax.axis_index("blk")
    ends = item_ends(extra_length)
    places = here * rows + lax.iota(jnp.int32, HALO + rows) - HALO
    items = jnp.where(places >= 0, jnp.sum((ends[None, :] <= places[:, None]).astype(jnp.int32), axis=1), -1)
    seg_q = items[HALO:, None]
    seg_k = jnp.concatenate([items, lax.iota(jnp.int32, COND) // 2])[None, :]

    base = nn(latents, skip_matrix[:width]) + nn(skip_input, skip_matrix[width:]) + skip_offset
    first_unit, first_rstd = norm_parts(base)
    first_in = (first_unit * gain_first + shift_first).astype(bf16)
    triple = nn(first_in, joint_matrix).astype(bf16)
    cond_flat = cond_tokens.reshape(-1, width).astype(f32)
    cond_unit, cond_rstd = norm_parts(cond_flat)
    cond_in = (cond_unit * gain_first + shift_first).astype(bf16)
    cond_pair = nn(cond_in, joint_matrix[:, width:]).astype(bf16)
    halo = lax.ppermute(triple[rows - HALO :, width:], "blk", [(i, i + 1) for i in range(7)])
    query, pairs = triple[:, :width], jnp.concatenate([halo, triple[:, width:], cond_pair], 0)
    attended, logsum, heads_q, heads_k, heads_v, heads_o = attend(query, pairs, seg_q, seg_k)
    middle = base + nn(attended, out_matrix) + out_offset
    second_unit, second_rstd = norm_parts(middle)
    second_in = (second_unit * gain_second + shift_second).astype(bf16)
    before = nn(second_in, up_matrix) + up_offset
    inside = 0.5 * (1.0 + lax.erf(before * 2**-0.5))
    slope = (inside + before * jnp.exp(-0.5 * before * before) * (2 * jnp.pi) ** -0.5).astype(bf16)
    hidden = (before * inside).astype(bf16)
    hidden, slope = lax.optimization_barrier((hidden, slope))
    output = middle + nn(hidden, down_matrix) + down_offset

    cond_t = jnp.pad(jnp.concatenate([cond_in, cond_in], 0).T, ((0, 0), (0, 128 - 2 * COND)))
    arrays = dict(
        hidden_t=hidden.T.reshape(8, 4, PART, rows),
        slope=slope,
        cot=cotangent,
        second_t=second_in.T.reshape(8, PART, rows),
        second_unit=second_unit.astype(bf16),
        att_t=attended.T.reshape(8, PART, rows),
        q=heads_q,
        k=heads_k,
        v=heads_v,
        o=heads_o,
        logsum=logsum,
        first_t=first_in.T.reshape(8, PART, rows),
        first_unit=first_unit.astype(bf16),
        joined_t=jnp.concatenate([latents.T, skip_input.T], 0).reshape(8, 2 * PART, rows),
        w_skip=skip_all.reshape(16, PART, width),
        w_joint=joint_all,
        w_up=up_all,
        w_down=down_all.reshape(32, PART, width),
        cond_t=cond_t.reshape(8, PART, 128),
        second_rstd=second_rstd,
        first_rstd=first_rstd,
        gain_second=gain_second[None],
        gain_first=gain_first[None],
        seg_q=seg_q,
        seg_k=seg_k,
        cond_unit=cond_unit,
        cond_rstd=cond_rstd,
    )
    made, vector_sums, cond_sum = backward(arrays)
    v = [vector_sums[n, :PART] for n in range(7)]
    return (
        output.astype(bf16),
        made["d_latents"],
        made["d_skip"],
        cond_sum.reshape(cond_tokens.shape),
        made["g_skip"].astype(f32),
        v[0],
        v[1],
        v[2],
        made["g_joint"][:, : 3 * WIDTH].astype(f32),
        made["g_joint"][:, 3 * WIDTH :].astype(f32),
        v[3],
        v[4],
        v[5],
        made["g_up"].astype(f32),
        vector_sums[7:11, :PART].reshape(-1),
        made["g_down"].astype(f32),
        v[6],
    )


def shifted(value, axis, steps):
    count = lax.axis_size(axis)
    leading, last = (max(0, -steps), min(count, count - steps))
    return lax.ppermute(value, axis, [(source, source + steps) for source in range(leading, last)])


def layer_norm(values, gain, shift):
    center = values - jnp.mean(values, axis=-1, keepdims=True)
    spread = jnp.mean(center * center, axis=-1, keepdims=True)
    return center * lax.rsqrt(spread + 1e-05) * gain + shift


def contract_rows(left, right):
    return lax.dot_general(
        left, right, (((0,), (0,)), ((), ())), preferred_element_type=jnp.float32
    )


def contract_cols(left, right):
    return lax.dot_general(
        left, right, (((1,), (1,)), ((), ())), preferred_element_type=jnp.float32
    )


def segment_ids(ends, places):
    inside = jnp.sum((ends[None, :] <= places[:, None]).astype(jnp.int32), axis=1)
    return jnp.where(places >= 0, inside, -1)


def split_heads(block):
    return block.reshape(block.shape[0], HEADS, HEAD).transpose(1, 0, 2)


def merge_heads(block):
    return block.transpose(1, 0, 2).reshape(block.shape[1], HEADS * HEAD)


def masked_scores(query, keys, allowed):
    scores = contract_cols(query, keys) * HEAD ** (-0.5)
    return jnp.where(allowed, scores, -1e30)


def plain(
    latents,
    skip_input,
    cond_tokens,
    extra_length,
    skip_weight,
    skip_bias,
    first_gain,
    first_shift,
    joint_weight,
    out_weight,
    out_bias,
    second_gain,
    second_shift,
    up_weight,
    up_bias,
    down_weight,
    down_bias,
    cotangent,
):
    whole = (
        lax.all_gather(skip_weight, "blk", axis=0, tiled=True),
        lax.all_gather(skip_bias, "blk", axis=0, tiled=True),
        lax.all_gather(first_gain, "blk", axis=0, tiled=True),
        lax.all_gather(first_shift, "blk", axis=0, tiled=True),
        lax.all_gather(joint_weight, "blk", axis=0, tiled=True),
        lax.all_gather(out_weight, "blk", axis=0, tiled=True),
        lax.all_gather(out_bias, "blk", axis=0, tiled=True),
        lax.all_gather(second_gain, "blk", axis=0, tiled=True),
        lax.all_gather(second_shift, "blk", axis=0, tiled=True),
        lax.all_gather(up_weight, "blk", axis=0, tiled=True),
        lax.all_gather(up_bias, "blk", axis=0, tiled=True),
        lax.all_gather(down_weight, "blk", axis=0, tiled=True),
        lax.all_gather(down_bias, "blk", axis=0, tiled=True),
    )
    (
        skip_matrix,
        skip_offset,
        gain_first,
        shift_first,
        joint_matrix,
        out_matrix,
        out_offset,
        gain_second,
        shift_second,
        up_matrix,
        up_offset,
        down_matrix,
        down_offset,
    ) = whole
    rows = latents.shape[0]
    width = latents.shape[1]
    scale = HEAD ** (-0.5)
    joined = jnp.concatenate([latents, skip_input], 1)
    base = jnp.dot(joined, skip_matrix, preferred_element_type=jnp.float32) + skip_offset
    first_in = layer_norm(base, gain_first, shift_first).astype(jnp.bfloat16)
    triple = jnp.dot(first_in, joint_matrix, preferred_element_type=jnp.float32).astype(
        jnp.bfloat16
    )
    query = triple[:, :width]
    pair_here = triple[:, width:]
    pair_left = shifted(pair_here, "blk", 1)
    cond_flat = cond_tokens.reshape(-1, width).astype(jnp.float32)
    cond_in = layer_norm(cond_flat, gain_first, shift_first).astype(jnp.bfloat16)
    cond_pair = jnp.dot(
        cond_in, joint_matrix[:, width:], preferred_element_type=jnp.float32
    ).astype(jnp.bfloat16)
    pairs = jnp.concatenate([pair_left, pair_here, cond_pair], 0)
    ends = item_ends(extra_length)
    here = lax.axis_index("blk")
    places = here * rows + lax.iota(jnp.int32, rows)
    seg_here = segment_ids(ends, places)
    seg_left = segment_ids(ends, places - rows)
    cond_seg = lax.iota(jnp.int32, cond_pair.shape[0]) // 2
    allowed = seg_here[:, None] == jnp.concatenate([seg_left, seg_here, cond_seg])[None, :]
    head_query = split_heads(query)
    head_key = split_heads(pairs[:, :width])
    head_value = split_heads(pairs[:, width:])

    def head_forward(parts):
        query_one, key_one, value_one = parts
        scores = masked_scores(query_one, key_one, allowed)
        top = jnp.max(scores, axis=1, keepdims=True)
        expo = jnp.exp(scores - top)
        total = jnp.sum(expo, axis=1, keepdims=True)
        probs = (expo / total).astype(jnp.bfloat16)
        mixed = jnp.dot(probs, value_one, preferred_element_type=jnp.float32)
        return (mixed, (top + jnp.log(total))[:, 0])

    mixed, logsum = lax.map(head_forward, (head_query, head_key, head_value))
    attended = merge_heads(mixed).astype(jnp.bfloat16)
    middle = base + jnp.dot(attended, out_matrix, preferred_element_type=jnp.float32) + out_offset
    second_in = layer_norm(middle, gain_second, shift_second).astype(jnp.bfloat16)
    before = jnp.dot(second_in, up_matrix, preferred_element_type=jnp.float32) + up_offset
    hidden = jax.nn.gelu(before, approximate=False).astype(jnp.bfloat16)
    output = middle + jnp.dot(hidden, down_matrix, preferred_element_type=jnp.float32) + down_offset
    again = (
        lax.all_gather(skip_weight, "blk", axis=0, tiled=True),
        lax.all_gather(skip_bias, "blk", axis=0, tiled=True),
        lax.all_gather(first_gain, "blk", axis=0, tiled=True),
        lax.all_gather(first_shift, "blk", axis=0, tiled=True),
        lax.all_gather(joint_weight, "blk", axis=0, tiled=True),
        lax.all_gather(out_weight, "blk", axis=0, tiled=True),
        lax.all_gather(out_bias, "blk", axis=0, tiled=True),
        lax.all_gather(second_gain, "blk", axis=0, tiled=True),
        lax.all_gather(second_shift, "blk", axis=0, tiled=True),
        lax.all_gather(up_weight, "blk", axis=0, tiled=True),
        lax.all_gather(up_bias, "blk", axis=0, tiled=True),
        lax.all_gather(down_weight, "blk", axis=0, tiled=True),
        lax.all_gather(down_bias, "blk", axis=0, tiled=True),
    )
    (
        skip_matrix,
        skip_offset,
        gain_first,
        shift_first,
        joint_matrix,
        out_matrix,
        out_offset,
        gain_second,
        shift_second,
        up_matrix,
        up_offset,
        down_matrix,
        down_offset,
    ) = again
    incoming = cotangent.astype(jnp.float32)
    grad_down_offset = jnp.sum(incoming, axis=0)
    grad_down_matrix = contract_rows(hidden, cotangent)
    d_hidden = contract_cols(cotangent, down_matrix)
    gelu_value, gelu_pull = jax.vjp(partial(jax.nn.gelu, approximate=False), before)
    d_before = gelu_pull(d_hidden)[0].astype(jnp.bfloat16)
    grad_up_offset = jnp.sum(d_before.astype(jnp.float32), axis=0)
    grad_up_matrix = contract_rows(second_in, d_before)
    d_second = contract_cols(d_before, up_matrix)
    norm_value, norm_pull = jax.vjp(
        layer_norm, middle, gain_second.astype(jnp.float32), shift_second.astype(jnp.float32)
    )
    d_middle_norm, grad_gain_second, grad_shift_second = norm_pull(d_second)
    d_middle = incoming + d_middle_norm
    d_branch = d_middle.astype(jnp.bfloat16)
    grad_out_offset = jnp.sum(d_branch.astype(jnp.float32), axis=0)
    grad_out_matrix = contract_rows(attended, d_branch)
    d_attended = contract_cols(d_branch, out_matrix).astype(jnp.bfloat16)

    def head_backward(parts):
        query_one, key_one, value_one, grad_one, logsum_one = parts
        scores = masked_scores(query_one, key_one, allowed)
        probs = jnp.exp(scores - logsum_one[:, None])
        d_probs = contract_cols(grad_one, value_one)
        inner = jnp.sum(probs * d_probs, axis=1, keepdims=True)
        d_scores = (probs * (d_probs - inner)).astype(jnp.bfloat16)
        d_query_one = jnp.dot(d_scores, key_one, preferred_element_type=jnp.float32) * scale
        d_key_one = contract_rows(d_scores, query_one) * scale
        d_value_one = contract_rows(probs.astype(jnp.bfloat16), grad_one)
        return (d_query_one, d_key_one, d_value_one)

    d_query_heads, d_key_heads, d_value_heads = lax.map(
        head_backward, (head_query, head_key, head_value, split_heads(d_attended), logsum)
    )
    d_query = merge_heads(d_query_heads)
    d_pairs = jnp.concatenate([merge_heads(d_key_heads), merge_heads(d_value_heads)], 1)
    d_left = d_pairs[:rows]
    d_own = d_pairs[rows : 2 * rows]
    d_cond_part = d_pairs[2 * rows :]
    d_returned = shifted(d_left.astype(jnp.bfloat16), "blk", -1).astype(d_left.dtype)
    d_cond_total = lax.psum(d_cond_part.astype(jnp.bfloat16), "blk")
    d_triple = jnp.concatenate([d_query, d_own + d_returned], 1).astype(jnp.bfloat16)
    leading = (here == 0).astype(jnp.float32)
    cond_term = contract_rows(cond_in, d_cond_total) * leading
    grad_joint_matrix = contract_rows(first_in, d_triple) + jnp.concatenate(
        [jnp.zeros((width, width), jnp.float32), cond_term], 1
    )
    d_first = contract_cols(d_triple, joint_matrix)
    d_cond_in = contract_cols(d_cond_total, joint_matrix[:, width:])
    first_value, first_pull = jax.vjp(
        layer_norm, base, gain_first.astype(jnp.float32), shift_first.astype(jnp.float32)
    )
    d_base_norm, grad_gain_tokens, grad_shift_tokens = first_pull(d_first)
    cond_value, cond_pull = jax.vjp(
        layer_norm, cond_flat, gain_first.astype(jnp.float32), shift_first.astype(jnp.float32)
    )
    d_cond_flat, grad_gain_cond, grad_shift_cond = cond_pull(d_cond_in)
    grad_gain_first = grad_gain_tokens + leading * grad_gain_cond
    grad_shift_first = grad_shift_tokens + leading * grad_shift_cond
    d_base = (d_middle + d_base_norm).astype(jnp.bfloat16)
    grad_skip_offset = jnp.sum(d_base.astype(jnp.float32), axis=0)
    grad_skip_matrix = contract_rows(joined, d_base)
    d_joined = contract_cols(d_base, skip_matrix)
    shares = (
        lax.psum_scatter(
            grad_skip_matrix.astype(jnp.bfloat16), "blk", scatter_dimension=0, tiled=True
        ).astype(jnp.float32),
        lax.psum_scatter(
            grad_skip_offset.astype(jnp.bfloat16), "blk", scatter_dimension=0, tiled=True
        ).astype(jnp.float32),
        lax.psum_scatter(
            grad_gain_first.astype(jnp.bfloat16), "blk", scatter_dimension=0, tiled=True
        ).astype(jnp.float32),
        lax.psum_scatter(
            grad_shift_first.astype(jnp.bfloat16), "blk", scatter_dimension=0, tiled=True
        ).astype(jnp.float32),
        lax.psum_scatter(
            grad_joint_matrix.astype(jnp.bfloat16), "blk", scatter_dimension=0, tiled=True
        ).astype(jnp.float32),
        lax.psum_scatter(
            grad_out_matrix.astype(jnp.bfloat16), "blk", scatter_dimension=0, tiled=True
        ).astype(jnp.float32),
        lax.psum_scatter(
            grad_out_offset.astype(jnp.bfloat16), "blk", scatter_dimension=0, tiled=True
        ).astype(jnp.float32),
        lax.psum_scatter(
            grad_gain_second.astype(jnp.bfloat16), "blk", scatter_dimension=0, tiled=True
        ).astype(jnp.float32),
        lax.psum_scatter(
            grad_shift_second.astype(jnp.bfloat16), "blk", scatter_dimension=0, tiled=True
        ).astype(jnp.float32),
        lax.psum_scatter(
            grad_up_matrix.astype(jnp.bfloat16), "blk", scatter_dimension=0, tiled=True
        ).astype(jnp.float32),
        lax.psum_scatter(
            grad_up_offset.astype(jnp.bfloat16), "blk", scatter_dimension=0, tiled=True
        ).astype(jnp.float32),
        lax.psum_scatter(
            grad_down_matrix.astype(jnp.bfloat16), "blk", scatter_dimension=0, tiled=True
        ).astype(jnp.float32),
        lax.psum_scatter(
            grad_down_offset.astype(jnp.bfloat16), "blk", scatter_dimension=0, tiled=True
        ).astype(jnp.float32),
    )
    (
        share_skip,
        share_skip_offset,
        share_gain_first,
        share_shift_first,
        share_joint,
        share_out,
        share_out_offset,
        share_gain_second,
        share_shift_second,
        share_up,
        share_up_offset,
        share_down,
        share_down_offset,
    ) = shares
    summed = (
        lax.psum(share_skip.astype(jnp.bfloat16), "stream").astype(jnp.float32),
        lax.psum(share_skip_offset.astype(jnp.bfloat16), "stream").astype(jnp.float32),
        lax.psum(share_gain_first.astype(jnp.bfloat16), "stream").astype(jnp.float32),
        lax.psum(share_shift_first.astype(jnp.bfloat16), "stream").astype(jnp.float32),
        lax.psum(share_joint.astype(jnp.bfloat16), "stream").astype(jnp.float32),
        lax.psum(share_out.astype(jnp.bfloat16), "stream").astype(jnp.float32),
        lax.psum(share_out_offset.astype(jnp.bfloat16), "stream").astype(jnp.float32),
        lax.psum(share_gain_second.astype(jnp.bfloat16), "stream").astype(jnp.float32),
        lax.psum(share_shift_second.astype(jnp.bfloat16), "stream").astype(jnp.float32),
        lax.psum(share_up.astype(jnp.bfloat16), "stream").astype(jnp.float32),
        lax.psum(share_up_offset.astype(jnp.bfloat16), "stream").astype(jnp.float32),
        lax.psum(share_down.astype(jnp.bfloat16), "stream").astype(jnp.float32),
        lax.psum(share_down_offset.astype(jnp.bfloat16), "stream").astype(jnp.float32),
    )
    return (
        output.astype(jnp.bfloat16),
        d_joined[:, :width].astype(jnp.bfloat16),
        d_joined[:, width:].astype(jnp.bfloat16),
        d_cond_flat.reshape(cond_tokens.shape).astype(jnp.bfloat16),
        summed[0],
        summed[1],
        summed[2],
        summed[3],
        summed[4],
        summed[5],
        summed[6],
        summed[7],
        summed[8],
        summed[9],
        summed[10],
        summed[11],
        summed[12],
    )


def solution(mesh):
    placed = (
        P(("stream", "blk"), None),
        P(("stream", "blk"), None),
        P("stream", None, None),
        P("stream", None),
        P("blk", None),
        P("blk"),
        P("blk"),
        P("blk"),
        P("blk", None),
        P("blk", None),
        P("blk"),
        P("blk"),
        P("blk"),
        P("blk", None),
        P("blk"),
        P("blk", None),
        P("blk"),
        P(("stream", "blk"), None),
    )
    fits = mesh.shape["stream"] == 4 and mesh.shape["blk"] == 8
    return jax.shard_map(
        quick if fits else plain,
        mesh=mesh,
        in_specs=placed,
        out_specs=(
            P(("stream", "blk"), None),
            P(("stream", "blk"), None),
            P(("stream", "blk"), None),
            P("stream", None, None),
            P("blk", None),
            P("blk"),
            P("blk"),
            P("blk"),
            P("blk", None),
            P("blk", None),
            P("blk"),
            P("blk"),
            P("blk"),
            P("blk", None),
            P("blk"),
            P("blk", None),
            P("blk"),
        ),
        check_vma=False,
    )
```

```python
import functools
from functools import partial

import jax
import jax.numpy as jnp
from jax import lax
from jax.experimental import pallas as pl
from jax.experimental.pallas import tpu as pltpu
from jax.sharding import PartitionSpec as P

HEADS = 16
HEAD = 72
LEN_MIN = 192

MESH = pl.DeviceIdType.MESH
ANY = pl.BlockSpec(memory_space=pl.ANY)
WIDTH = 1152
PART = 144
SMALL = (16, 256)


class Place:
    def __init__(self):
        self.s = lax.axis_index("stream")
        self.b = lax.axis_index("blk")
        self.x = lax.rem(self.s, 2)
        self.y = lax.div(self.s, 2)
        self.c = lax.rem(self.b, 2)
        self.zz = lax.div(self.b, 2)

    def other(self, k):
        low, high = lax.rem(self.zz, 2), lax.div(self.zz, 2)
        return 2 * (1 - high if k & 2 else high) + (1 - low if k & 1 else low)

    def source(self, k):
        zz = self.zz
        table = ((1, 0, 3, 2), (2, 2, 1, 1), (3, 3, 0, 0))[k - 1]
        return jnp.where(zz < 2, jnp.where(zz == 0, table[0], table[1]), jnp.where(zz == 2, table[2], table[3]))

    def at(self, x=None, y=None, zz=None, c=None):
        x = self.x if x is None else x
        y = self.y if y is None else y
        zz = self.zz if zz is None else zz
        c = self.c if c is None else c
        return (2 * y + x, 2 * zz + c)


def greet(place):
    barrier = pltpu.get_barrier_semaphore()
    p = place
    near = [p.at(x=1 - p.x), p.at(y=1 - p.y), p.at(c=1 - p.c)] + [p.at(zz=p.other(k)) for k in (1, 2, 3)]
    for device in near:
        pl.semaphore_signal(barrier, inc=1, device_id=device, device_id_type=MESH)
    up = (p.c == 1) & (p.zz < 3)
    down = (p.c == 0) & (p.zz > 0)
    for go, device in ((up, (p.s, p.b + 1)), (down, (p.s, p.b - 1))):

        @pl.when(go)
        def _():
            pl.semaphore_signal(barrier, inc=1, device_id=device, device_id_type=MESH)

    pl.when(up | down)(lambda: pl.semaphore_wait(barrier, len(near) + 1))
    pl.when(jnp.logical_not(up | down))(lambda: pl.semaphore_wait(barrier, len(near)))


def remote(src, dst, send, recv, device):
    return pltpu.make_async_remote_copy(
        src_ref=src, dst_ref=dst, send_sem=send, recv_sem=recv, device_id=device, device_id_type=MESH
    )


def block(t, ref, b):
    if t in (1, 2):
        return ref.at[b]
    size = 2 if t == 0 else 4
    return ref.at[pl.ds(b * size, size)]


def piece(t, ref, b, x, y):
    if t in (1, 2):
        return ref.at[b, :, pl.ds(pl.multiple_of((2 * y + x) * WIDTH, 128), WIDTH)]
    if t == 3:
        return ref.at[4 * b + 2 * y + x]
    low, size = (0, 80) if y == 0 else (80, 64)
    return ref.at[2 * b + x, pl.ds(low, size)]


KINDS = ("half", "cols", "cols", "rows")


class Gather:
    SEMS = [pltpu.SemaphoreType.DMA((4, 6, 4, 2)), pltpu.SemaphoreType.DMA((12,)), pltpu.SemaphoreType.DMA((2, 8))]

    def __init__(self, place, shards, outs, scratch):
        self.place = place
        self.small_in, self.skip_in, self.joint_in, self.out_in, self.up_in, self.down_in = shards
        self.small = outs[0]
        self.outs = outs[1:]
        self.sems, self.local_sems, self.small_sems = scratch[:3]
        self.stage = scratch[3:]

    def copy(self, t, x, y, zz, c, stage, k, device):
        ref = piece(t, self.outs[t], 2 * zz + c, x, y)
        return remote(ref, ref, self.sems.at[t, stage, k, 0], self.sems.at[t, stage, k, 1], device)

    def each_y(self, t, run):
        if KINDS[t] != "half":
            run(self.place.y)
            return
        for value in (0, 1):
            pl.when(self.place.y == value)(lambda value=value: run(value))

    STAGE = [
        pltpu.VMEM((2, PART, WIDTH), jnp.bfloat16),
        pltpu.VMEM((PART, 4 * WIDTH), jnp.bfloat16),
        pltpu.VMEM((PART, 4 * WIDTH), jnp.bfloat16),
        pltpu.VMEM((4, PART, WIDTH), jnp.bfloat16),
    ]

    def locals(self, t):
        if t == 1:
            return [
                (self.joint_in, self.stage[1].at[:, pl.ds(0, 3 * WIDTH)]),
                (self.out_in, self.stage[1].at[:, pl.ds(3 * WIDTH, WIDTH)]),
            ]
        return [({0: self.skip_in, 2: self.up_in, 3: self.down_in}[t], self.stage[t])]

    def own_start(self, t):
        for i, (src, dst) in enumerate(self.locals(t)):
            pltpu.make_async_copy(src, dst, self.local_sems.at[2 * t + i]).start()

    def own_keep(self, t):
        return pltpu.make_async_copy(self.stage[t], block(t, self.outs[t], self.place.b), self.local_sems.at[8 + t])

    def own_done(self, t):
        for i, (src, dst) in enumerate(self.locals(t)):
            pltpu.make_async_copy(src, dst, self.local_sems.at[2 * t + i]).wait()
        self.own_keep(t).start()

    def own_copy(self, t, c):
        ref = block(t, self.outs[t], 2 * self.place.zz + c)
        src = self.stage[t]
        sems = self.sems.at[t, 4, 0]
        return remote(src, ref, sems.at[0], sems.at[1], self.place.at(c=1 - self.place.c))

    def small_copy(self, i, src, dst, device):
        return remote(src, dst, self.small_sems.at[0, i], self.small_sems.at[1, i], device)

    def small_start(self):
        p = self.place
        for i, device in enumerate([p.at(zz=p.other(k)) for k in (1, 2, 3)] + [p.at(c=1 - p.c)]):
            self.small_copy(i, self.small_in, self.small.at[p.b], device).start()

    def small_pass(self):
        p = self.place
        for i, k in enumerate((1, 2, 3)):
            ref = self.small.at[2 * p.other(k) + p.c]
            self.small_copy(i, ref, ref, p.at()).wait_recv()
            self.small_copy(4 + i, ref, ref, p.at(c=1 - p.c)).start()

    def small_done(self):
        p = self.place
        for i, k in enumerate((0, 1, 2, 3)):
            ref = self.small.at[2 * p.other(k) + 1 - p.c]
            self.small_copy(3 + i, ref, ref, p.at()).wait_recv()
        for i in range(7):
            self.small_copy(i, self.small_in, self.small_in, p.at()).wait_send()

    def stage_piece(self, t, y):
        x = self.place.x
        if t in (1, 2):
            return self.stage[t].at[:, pl.ds(pl.multiple_of((2 * y + x) * WIDTH, 128), WIDTH)]
        if t == 3:
            return self.stage[t].at[2 * y + x]
        low, size = (0, 80) if y == 0 else (80, 64)
        return self.stage[t].at[x, pl.ds(low, size)]

    def z_copies(self, t, y, zz, start, own=False):
        p = self.place
        for step, send in ((1, 0), (-1, 5)):
            go = (zz <= p.zz) & (p.zz < 3) if step == 1 else (zz >= p.zz) & (p.zz > 0)
            ref = piece(t, self.outs[t], 2 * zz + p.c, p.x, y)

            @pl.when(go)
            def _():
                copy = remote(self.stage_piece(t, y) if own else ref, ref, self.sems.at[t, send, zz, 0], self.sems.at[t, 0, zz, 1], p.at(zz=p.zz + step))
                copy.start() if start else copy.wait_send()

    def z_start(self, t):
        p = self.place
        self.each_y(t, lambda y: self.z_copies(t, y, p.zz, True, True))
        self.own_copy(t, p.c).start()

    def z_done(self, t, k):
        p = self.place
        zz = p.source(k)

        def run(y):
            self.copy(t, p.x, y, zz, p.c, 0, zz, p.at()).wait_recv()
            self.copy(t, p.x, y, zz, p.c, 1, k, p.at(x=1 - p.x)).start()
            self.copy(t, p.x, y, zz, p.c, 2, k, p.at(y=1 - p.y)).start()
            self.z_copies(t, y, zz, True)

        self.each_y(t, run)

    def by_x(self, t, k):
        return k == 1 or (k == 2 and t % 2 == 0)

    def xy_done(self, t, k):
        p = self.place

        def run(y):
            zz = p.source(k)
            self.copy(t, 1 - p.x, y, zz, p.c, 1, k, p.at()).wait_recv()
            if self.by_x(t, k):
                self.copy(t, 1 - p.x, y, zz, p.c, 3, k, p.at(y=1 - p.y)).start()
            self.copy(t, p.x, 1 - y, zz, p.c, 2, k, p.at()).wait_recv()
            if not self.by_x(t, k):
                self.copy(t, p.x, 1 - y, zz, p.c, 3, k, p.at(x=1 - p.x)).start()

        self.each_y(t, run)

    def diag_done(self, t, k):
        p = self.place

        def run(y):
            zz = p.source(k)
            self.copy(t, 1 - p.x, 1 - y, zz, p.c, 3, k, p.at()).wait_recv()

        self.each_y(t, run)
        self.pair_copy(t, k, p.c).start()

    def pair_copy(self, t, k, c):
        ref = block(t, self.outs[t], 2 * self.place.source(k) + c)
        sems = self.sems.at[t, 4, k]
        return remote(ref, ref, sems.at[0], sems.at[1], self.place.at(c=1 - self.place.c))

    def ready(self, t):
        p = self.place
        self.own_keep(t).wait()
        self.own_copy(t, 1 - p.c).wait_recv()
        for k in (1, 2, 3):
            self.pair_copy(t, k, 1 - p.c).wait_recv()

    def all_sent(self, t):
        p = self.place
        self.own_copy(t, p.c).wait_send()

        def run(y):
            self.z_copies(t, y, p.zz, False, True)
            for k in (1, 2, 3):
                zz = p.source(k)
                self.z_copies(t, y, zz, False)
                self.copy(t, p.x, y, zz, p.c, 1, k, p.at()).wait_send()
                self.copy(t, p.x, y, zz, p.c, 2, k, p.at()).wait_send()
                if self.by_x(t, k):
                    self.copy(t, 1 - p.x, y, zz, p.c, 3, k, p.at()).wait_send()
                else:
                    self.copy(t, p.x, 1 - y, zz, p.c, 3, k, p.at()).wait_send()

        self.each_y(t, run)
        for k in (1, 2, 3):
            self.pair_copy(t, k, p.c).wait_send()


SIZES = (80, PART, PART, PART)


HALO = 320
COND = 32
TOK = 512
KEYS = HALO + TOK + COND
TILES = ((0, 0), (256, 256))
LOG2E = 1.4426950408889634


def nt(a, b):
    return lax.dot_general(a, b, (((1,), (1,)), ((), ())), preferred_element_type=jnp.float32)


def tn(a, b):
    return lax.dot_general(a, b, (((0,), (0,)), ((), ())), preferred_element_type=jnp.float32)


def nn(a, b):
    return jnp.dot(a, b, preferred_element_type=jnp.float32)


def make_bias(extra, blk, bias):
    row = lax.broadcasted_iota(jnp.int32, (TOK, 1), 0) + blk * TOK
    at = lax.broadcasted_iota(jnp.int32, (1, KEYS), 1)
    key = at + (blk * TOK - HALO)
    item_q, item_k = jnp.zeros_like(row), jnp.zeros_like(key)
    end = 0
    for n in range(extra.shape[1]):
        end = end + extra[0, n] + (LEN_MIN - 1)
        item_q += (row >= end).astype(jnp.int32)
        item_k += (key >= end).astype(jnp.int32)
    item_k = jnp.where(key >= 0, item_k, -1)
    item_k = jnp.where(at >= HALO + TOK, (at - (HALO + TOK)) >> 1, item_k)
    for low in range(0, TOK, 128):
        bias[low : low + 128] = jnp.where(item_q[low : low + 128] == item_k, 0.0, -1e30)


def head(h):
    return slice(HEAD * h, HEAD * (h + 1))


class Names:
    def __init__(self, names, refs):
        for name, ref in zip(names, refs, strict=True):
            setattr(self, name, ref)


def hbm(shape, dtype=jnp.bfloat16):
    return jax.ShapeDtypeStruct(shape, dtype)


GROUP = 4
IN_VMEM = pl.BlockSpec(memory_space=pltpu.VMEM)
IN_SMEM = pl.BlockSpec(memory_space=pltpu.SMEM)
FWD_IN = dict(
    rows=IN_VMEM, extra=IN_SMEM, cond=IN_VMEM, latents=ANY, skip_input=ANY, skip=ANY, joint=ANY, out=ANY, up=ANY, down=ANY,
)
FWD_OUT = dict(
    w_skip=hbm((16, PART, WIDTH)),
    w_joint=hbm((8, PART, 4 * WIDTH)),
    w_up=hbm((8, PART, 4 * WIDTH)),
    w_down=hbm((32, PART, WIDTH)),
    output=hbm((TOK, WIDTH)),
    hidden_t=hbm((8, 4, PART, TOK)),
    slope=hbm((TOK, 4 * WIDTH)),
    second_t=hbm((8, PART, TOK)),
    second_unit=hbm((TOK, WIDTH)),
    att_t=hbm((8, PART, TOK)),
    q=hbm((HEADS, TOK, HEAD)),
    k=hbm((HEADS, KEYS, HEAD)),
    v=hbm((HEADS, KEYS, HEAD)),
    o=hbm((HEADS, TOK, HEAD)),
    logsum=hbm((HEADS, TOK, 1), jnp.float32),
    first_t=hbm((8, PART, TOK)),
    first_unit=hbm((TOK, WIDTH)),
    joined_t=hbm((8, 2 * PART, TOK)),
)
FWD_VM = dict(
    cond_t=hbm((8, PART, 128)),
    second_rstd=hbm((TOK, 1), jnp.float32),
    first_rstd=hbm((TOK, 1), jnp.float32),
    vectors=hbm((16, WIDTH), jnp.float32),
    cond_unit=hbm((COND, WIDTH), jnp.float32),
    cond_rstd=hbm((COND, 1), jnp.float32),
)
FWD_SCRATCH = dict(
    lat=pltpu.VMEM((TOK, WIDTH), jnp.bfloat16),
    ski=pltpu.VMEM((TOK, WIDTH), jnp.bfloat16),
    weight=pltpu.VMEM((2, 8, PART, WIDTH), jnp.bfloat16),
    base=pltpu.VMEM((TOK, WIDTH), jnp.float32),
    acc=pltpu.VMEM((TOK, WIDTH), jnp.float32),
    unit=pltpu.VMEM((TOK, WIDTH), jnp.bfloat16),
    normed=pltpu.VMEM((TOK, WIDTH), jnp.bfloat16),
    pairs=pltpu.VMEM((2, TOK, WIDTH), jnp.bfloat16),
    halo=pltpu.VMEM((2, HALO, WIDTH), jnp.bfloat16),
    cond_in=pltpu.VMEM((COND, WIDTH), jnp.bfloat16),
    qh=pltpu.VMEM((HEADS, TOK, HEAD), jnp.bfloat16),
    kh=pltpu.VMEM((HEADS, KEYS, HEAD), jnp.bfloat16),
    vh=pltpu.VMEM((HEADS, KEYS, HEAD), jnp.bfloat16),
    oh=pltpu.VMEM((HEADS, TOK, HEAD), jnp.bfloat16),
    lh=pltpu.VMEM((GROUP, TOK, 1), jnp.float32),
    bias=pltpu.VMEM((TOK, KEYS), jnp.float32),
    hidden=pltpu.VMEM((4, TOK, WIDTH), jnp.bfloat16),
    turned=pltpu.VMEM((2, WIDTH, TOK), jnp.bfloat16),
    tile=pltpu.VMEM((2, TOK, WIDTH), jnp.bfloat16),
    pack=pltpu.VMEM(SMALL, jnp.float32),
    packs=pltpu.VMEM((8, *SMALL), jnp.float32),
    ups=pltpu.VMEM((4, 1, WIDTH), jnp.float32),
    w_sems=pltpu.SemaphoreType.DMA((2,)),
    t_sems=pltpu.SemaphoreType.DMA((24,)),
    halo_sems=pltpu.SemaphoreType.DMA((2,)),
)
N_GATHER = len(Gather.SEMS) + len(Gather.STAGE)


def forward_kernel(*refs):
    cuts = [len(FWD_IN), len(FWD_OUT), len(FWD_VM), len(FWD_SCRATCH), N_GATHER]
    pieces, at = [], 0
    for cut in cuts:
        pieces.append(refs[at : at + cut])
        at += cut
    i, o, vm, b = (
        Names(names, part) for names, part in zip((FWD_IN, FWD_OUT, FWD_VM, FWD_SCRATCH), pieces)
    )
    f32, bf16 = jnp.float32, jnp.bfloat16
    p = Place()
    g = Gather(
        p, (b.pack, i.skip, i.joint, i.out, i.up, i.down), (b.packs, o.w_skip, o.w_joint, o.w_up, o.w_down), pieces[4]
    )

    def copy(src, dst, sem):
        return pltpu.make_async_copy(src, dst, sem)

    def stream(blocks, body):
        def load(n):
            return copy(blocks[n], b.weight.at[n % 2], b.w_sems.at[n % 2])

        load(0).start()
        for n in range(len(blocks)):
            if n + 1 < len(blocks):
                load(n + 1).start()
            load(n).wait()
            body(n, b.weight[n % 2].reshape(WIDTH, WIDTH))

    def column(ref, q):
        return ref.at[:, :, pl.ds(q * WIDTH, WIDTH)]

    def by_rows(size, body):
        @pl.loop(0, TOK // size)
        def _(n):
            body(pl.ds(pl.multiple_of(n * size, size), size))

    def vector(n):
        return vm.vectors[n : n + 1, :]

    kept = []

    def keep(src, dst, sem):
        one = (src, dst, b.t_sems.at[sem])
        copy(*one).start()
        kept.append(one)

    def flush():
        for one in kept:
            copy(*one).wait()
        kept.clear()

    def norm(values):
        center = values - jnp.mean(values, axis=1, keepdims=True)
        rstd = lax.rsqrt(jnp.mean(center * center, axis=1, keepdims=True) + 1e-05)
        return center * rstd, rstd

    def norm_tokens(gain, shift, rstd_out):
        @functools.partial(by_rows, 64)
        def _(rows):
            unit, rstd = norm(b.base[rows])
            b.unit[rows] = unit.astype(bf16)
            rstd_out[rows] = rstd
            b.normed[rows] = (unit * gain + shift).astype(bf16)

    def turn(slot, src, dst, shape, sem):
        b.turned[slot] = src.T
        keep(b.turned.at[slot], dst, sem)

    loads = [(i.latents, b.lat, b.t_sems.at[0]), (i.skip_input, b.ski, b.t_sems.at[1])]
    for t in range(4):
        g.own_start(t)
    for one in loads:
        copy(*one).start()
    b.pack[...] = jnp.zeros(SMALL, f32)
    b.pack[0:11, 0:PART] = i.rows[...]
    b.packs[p.b] = b.pack[...]
    greet(p)
    g.small_start()
    g.own_done(0)
    g.z_start(0)
    make_bias(i.extra, p.b, b.bias)
    g.small_pass()
    for one in loads:
        copy(*one).wait()

    @pl.when(p.b == 0)
    def _():
        for n in range(HEADS):
            b.kh[n, 0:HALO] = jnp.zeros((HALO, HEAD), bf16)
            b.vh[n, 0:HALO] = jnp.zeros((HALO, HEAD), bf16)

    for k in (1, 2, 3):
        g.z_done(0, k)
    g.own_done(1)
    g.z_start(1)
    g.small_done()
    for n in range(8):
        for row in range(7):
            vm.vectors[row : row + 1, n * PART : (n + 1) * PART] = b.packs[n, row : row + 1, 0:PART]
        for j in range(4):
            at = 4 * n + j
            low = at % 8 * PART
            b.ups[at // 8, :, low : low + PART] = b.packs[n, 7 + j : 8 + j, 0:PART]
    vm.vectors[7:16, :] = jnp.zeros((9, WIDTH), f32)
    for k in (1, 2, 3):
        g.xy_done(0, k)
    g.z_done(1, 1)
    for k in (1, 2, 3):
        g.diag_done(0, k)
    g.ready(0)

    def do_base(n, weight):
        made = nn((b.lat, b.ski)[n][...], weight)
        if n == 0:
            b.base[...] = made + vector(0)
        else:
            b.base[...] += made
        g.z_done(1, 2 + n)

    stream([o.w_skip.at[pl.ds(8 * n, 8)] for n in range(2)], do_base)
    g.own_done(2)
    g.z_start(2)
    norm_tokens(vector(1), vector(2), vm.first_rstd)
    unit, rstd = norm(i.cond[...].astype(f32))
    vm.cond_unit[...] = unit
    vm.cond_rstd[...] = rstd
    cond_in = (unit * vector(1) + vector(2)).astype(bf16)
    b.cond_in[...] = cond_in
    keep(b.unit, o.first_unit, 2)
    for k in (1, 2, 3):
        g.xy_done(1, k)
    for n in range(2):
        b.turned[n] = (b.lat, b.ski)[n][...].T
        made = b.turned.at[n].reshape(8, PART, TOK)
        for k in range(4):
            keep(made.at[pl.ds(2 * k, 2)].reshape(2 * PART, TOK), o.joined_t.at[4 * n + k], 3 + 4 * n + k)
    turned = jnp.concatenate([cond_in.astype(f32)] * 2 + [jnp.zeros((128 - 2 * COND, WIDTH), f32)], 0).T
    vm.cond_t[...] = turned.astype(bf16).reshape(8, PART, 128)
    for k in (1, 2, 3):
        g.z_done(2, k)
    g.own_done(3)
    g.z_start(3)
    for k in (1, 2, 3):
        g.diag_done(1, k)
    g.ready(1)

    def halo_copy(device):
        src = b.pairs.at[:, pl.ds(TOK - HALO, HALO)]
        return remote(src, b.halo, b.halo_sems.at[0], b.halo_sems.at[1], device)

    def do_triple(n, weight):
        made = nn(b.normed[...], weight).astype(bf16)
        if n < 2:
            b.pairs[n] = made
            few = nn(b.cond_in[...], weight).astype(bf16)
            for h in range(HEADS):
                (b.kh, b.vh)[n][h, HALO + TOK :] = few[:, head(h)]
        else:
            b.tile[0] = made
        if n == 1:
            pl.when(p.b < 7)(lambda: halo_copy((p.s, p.b + 1)).start())

    stream([column(o.w_joint, n) for n in (1, 2, 0)], do_triple)
    for h in range(HEADS):
        b.qh[h] = b.tile[0, :, head(h)]
        b.kh[h, HALO : HALO + TOK] = b.pairs[0, :, head(h)]
        b.vh[h, HALO : HALO + TOK] = b.pairs[1, :, head(h)]
    flush()
    turn(0, b.normed[...], o.first_t.reshape(WIDTH, TOK), None, 2)

    @pl.when(p.b > 0)
    def _():
        halo_copy((p.s, p.b)).wait_recv()
        for h in range(HEADS):
            b.kh[h, 0:HALO] = b.halo[0, :, head(h)]
            b.vh[h, 0:HALO] = b.halo[1, :, head(h)]

    keep(b.qh, o.q, 3)
    keep(b.kh, o.k, 4)
    keep(b.vh, o.v, 5)

    def group(start):
        @pl.loop(0, GROUP)
        def _(n):
            h = start + n
            for row, low in TILES:
                rows, keys = pl.ds(row, 256), pl.ds(low, KEYS - low)
                scores = nt(b.qh[h, rows], b.kh[h, keys]) * (HEAD**-0.5 * LOG2E) + b.bias[rows, keys]
                top = jnp.max(scores, axis=1, keepdims=True)
                expo = jnp.exp2(scores - top)
                total = jnp.sum(expo, axis=1, keepdims=True)
                mixed = nn(expo.astype(bf16), b.vh[h, keys])
                b.oh[h, rows] = (mixed / total).astype(bf16)
                b.lh[n, rows] = top + jnp.log2(total)

        done = copy(b.lh, o.logsum.at[pl.ds(start, GROUP)], b.t_sems.at[6])
        done.start()
        done.wait()

    group(0)
    for k in (1, 2, 3):
        g.xy_done(2, k)
    for k in (1, 2, 3):
        g.z_done(3, k)
    group(4)
    group(8)
    group(12)
    keep(b.oh, o.o, 7)
    for h in range(HEADS):
        b.tile[0, :, head(h)] = b.oh[h]

    def do_out(_, weight):
        b.base[...] += nn(b.tile[0], weight) + vector(3)

    stream([column(o.w_joint, 3)], do_out)
    norm_tokens(vector(4), vector(5), vm.second_rstd)
    flush()
    keep(b.unit, o.second_unit, 2)
    turn(0, b.tile[0], o.att_t.reshape(WIDTH, TOK), None, 3)
    turn(1, b.normed[...], o.second_t.reshape(WIDTH, TOK), None, 4)
    for k in (1, 2, 3):
        g.diag_done(2, k)
    for k in (1, 2, 3):
        g.xy_done(3, k)
    g.ready(2)

    flush()
    hidden_t = o.hidden_t.reshape(4, WIDTH, TOK)

    def wide_keep(q):
        slot = q % 2
        return [
            copy(b.turned.at[slot], hidden_t.at[q], b.t_sems.at[8 + slot]),
            copy(b.tile.at[slot], o.slope.at[:, pl.ds(q * WIDTH, WIDTH)], b.t_sems.at[10 + slot]),
        ]

    def do_up(q, weight):
        slot = q % 2
        b.acc[...] = nn(b.normed[...], weight)
        if q >= 2:
            for one in wide_keep(q - 2):
                one.wait()

        @functools.partial(by_rows, 32)
        def _(rows):
            before = b.acc[rows] + b.ups[q]
            inside = 0.5 + 0.5 * lax.erf(before * 2**-0.5)
            bell = jnp.exp2(before * before * (-0.5 * LOG2E)) * 0.3989422804014327
            b.hidden[q, rows] = (before * inside).astype(bf16)
            b.tile[slot, rows] = (inside + before * bell).astype(bf16)

        b.turned[slot] = b.hidden[q].T
        for one in wide_keep(q):
            one.start()
        if q == 1:
            for k in (1, 2, 3):
                g.diag_done(3, k)

    stream([column(o.w_up, q) for q in range(4)], do_up)
    g.ready(3)

    def do_down(q, weight):
        made = nn(b.hidden[q], weight)
        if q == 0:
            b.base[...] += made + vector(6)
        else:
            b.base[...] += made

    stream([o.w_down.at[pl.ds(8 * q, 8)] for q in range(4)], do_down)
    b.normed[...] = b.base[...].astype(bf16)
    keep(b.normed, o.output, 2)
    for q in (2, 3):
        for one in wide_keep(q):
            one.wait()
    flush()
    pl.when(p.b < 7)(lambda: halo_copy((p.s, p.b + 1)).wait_send())
    for t in range(4):
        g.all_sent(t)


def forward(arrays):
    vm = pl.BlockSpec(memory_space=pltpu.VMEM)
    outs = pl.pallas_call(
        forward_kernel,
        out_shape=[*FWD_OUT.values(), *FWD_VM.values()],
        in_specs=[*FWD_IN.values()],
        out_specs=[ANY] * len(FWD_OUT) + [vm] * len(FWD_VM),
        scratch_shapes=[*FWD_SCRATCH.values()] + Gather.SEMS + Gather.STAGE,
        compiler_params=pltpu.CompilerParams(collective_id=0, has_side_effects=True, vmem_limit_bytes=60 << 20),
    )(*[arrays[name] for name in FWD_IN])
    return dict(zip([*FWD_OUT, *FWD_VM], outs, strict=True))


ORDER = (0, 2, 1, 3)
UNIT = (PART, WIDTH)


def add_into(out, *ins):
    @pl.loop(0, out.shape[0] // 16)
    def _(i):
        rows = pl.ds(pl.multiple_of(i * 16, 16), 16)
        total = ins[0][rows].astype(jnp.float32)
        for ref in ins[1:]:
            total += ref[rows].astype(jnp.float32)
        out[rows] = total.astype(out.dtype)


class Sum:
    SEMS = [
        pltpu.SemaphoreType.DMA((4, 4, 2, 2)),
        pltpu.SemaphoreType.DMA((4, 4, 2)),
        pltpu.SemaphoreType.DMA((4, 4, 2)),
        pltpu.SemaphoreType.DMA((4, 4, 2)),
        pltpu.SemaphoreType.DMA((23,)),
    ]
    SLOTS = [pltpu.VMEM((23, *UNIT), jnp.bfloat16), pltpu.VMEM((4, *UNIT), jnp.bfloat16)]
    LANDS = [
        jax.ShapeDtypeStruct(lead + (size, WIDTH), jnp.bfloat16)
        for size in SIZES
        for lead in ((4, 2), (4,), (4,))
    ]
    PARTS = [
        jax.ShapeDtypeStruct((8, PART, WIDTH), jnp.bfloat16),
        jax.ShapeDtypeStruct((4, PART, 4 * WIDTH), jnp.bfloat16),
        jax.ShapeDtypeStruct((4, PART, 4 * WIDTH), jnp.bfloat16),
        jax.ShapeDtypeStruct((4, 4, PART, WIDTH), jnp.bfloat16),
    ]

    def __init__(self, place, parts, lands, outs, sems, slots):
        self.place, self.parts, self.outs = place, parts, outs
        self.sem1, self.sem2, self.sem3, self.sem4, self.load_sems = sems
        self.slots, self.fins = slots
        self.land1, self.land2, self.land3 = ([lands[3 * t + i] for t in range(4)] for i in range(3))

    def slot(self, t, i):
        return self.slots.at[i, pl.ds(0, SIZES[t])]

    def fin(self, t):
        return self.fins.at[t, pl.ds(0, SIZES[t])]

    def piece(self, t, zz, x, y):
        ref = self.parts[t]
        if t == 0:
            return ref.at[2 * zz + x, pl.ds(pl.multiple_of(64 * y, 16), 80)]
        if t == 3:
            return ref.at[zz, 2 * y + x]
        return ref.at[zz, :, pl.ds(pl.multiple_of((2 * y + x) * WIDTH, 128), WIDTH)]

    def half(self, t, zz, x, y, j):
        return self.piece(t, zz, x, j) if zz < 2 else self.piece(t, zz, j, y)

    def keep(self, zz):
        return self.place.y if zz < 2 else self.place.x

    def first(self, t, zz, j):
        p = self.place
        device = p.at(x=1 - p.x) if zz < 2 else p.at(y=1 - p.y)
        sems = self.sem1.at[t, zz, j]
        src = self.half(t, zz, 1 - p.x, 1 - p.y, j)
        return remote(src, self.land1[t].at[zz, j], sems.at[0], sems.at[1], device)

    def start(self, t, zzs=ORDER):
        for zz in zzs:
            for j in (0, 1):
                self.first(t, zz, j).start()

    def load(self, t, src, i):
        return pltpu.make_async_copy(src, self.slot(t, i), self.load_sems.at[i])

    def second(self, t, zz):
        p = self.place
        device = p.at(y=1 - p.y) if zz < 2 else p.at(x=1 - p.x)
        sems = self.sem2.at[t, zz]
        return remote(self.slot(t, 2 * zz), self.land2[t].at[zz], sems.at[0], sems.at[1], device)

    def pass_on(self, t, after=None):
        p = self.place
        if after is not None:
            for zz in ORDER:
                self.second(after, zz).wait_send()

        def own(zz):
            return self.load(t, self.half(t, zz, p.x, p.y, 1 - self.keep(zz)), 2 * zz)

        def landed(zz):
            return self.load(t, self.land1[t].at[zz, 1 - self.keep(zz)], 2 * zz + 1)

        for zz in ORDER:
            own(zz).start()
        for zz in ORDER:
            for j in (0, 1):
                self.first(t, zz, j).wait_recv()
            landed(zz).start()
        for zz in ORDER:
            own(zz).wait()
            landed(zz).wait()
            add_into(self.slot(t, 2 * zz), self.slot(t, 2 * zz), self.slot(t, 2 * zz + 1))
            self.second(t, zz).start()

    def third(self, t, zz, slot):
        p = self.place
        return remote(
            self.slot(t, 8 + 3 * zz), self.land3[t].at[slot], self.sem3.at[t, zz, 0], self.sem3.at[t, slot, 1],
            p.at(zz=zz),
        )

    def third_sent(self, t):
        for zz in range(4):
            pl.when(zz != self.place.zz)(lambda zz=zz: self.third(t, zz, self.place.zz).wait_send())

    def to_chip(self, t, after=None):
        p = self.place
        if after is not None:
            self.third_sent(after)

        def load(zz, n):
            keep = self.keep(zz)
            if n == 0:
                src = self.half(t, zz, p.x, p.y, keep)
            else:
                src = self.land1[t].at[zz, keep] if n == 1 else self.land2[t].at[zz]
            return self.load(t, src, 8 + 3 * zz + n)

        for zz in ORDER:
            load(zz, 0).start()
            load(zz, 1).start()
        for zz in ORDER:
            self.second(t, zz).wait_recv()
            load(zz, 2).start()
        for zz in ORDER:
            for n in range(3):
                load(zz, n).wait()
            base = 8 + 3 * zz
            mine = self.slot(t, base)
            add_into(mine, mine, self.slot(t, base + 1), self.slot(t, base + 2))

            @pl.when(zz != p.zz)
            def _():
                self.third(t, zz, p.zz).start()

            @pl.when(zz == p.zz)
            def _():
                add_into(self.fin(t), mine)

    def result(self, t, x, y):
        ref = self.outs[t]
        if KINDS[t] == "cols":
            return ref.at[:, pl.ds(pl.multiple_of((2 * y + x) * WIDTH, 128), WIDTH)]
        if KINDS[t] == "rows":
            return ref.at[pl.ds(pl.multiple_of((2 * y + x) * PART, 16), PART)]
        low, size = (0, 80) if y == 0 else (80, 64)
        return ref.at[pl.ds(pl.multiple_of(x * PART + low, 16), size)]

    def fin_part(self, t, y):
        if KINDS[t] != "half" or y == 0:
            return self.fin(t)
        return self.fins.at[t, pl.ds(16, 64)]

    def each_y(self, t, run):
        if KINDS[t] != "half":
            run(self.place.y)
            return
        for value in (0, 1):
            pl.when(self.place.y == value)(lambda value=value: run(value))

    def spread(self, t, start):
        p = self.place

        def run(y):
            src, dst = self.fin_part(t, y), self.result(t, p.x, y)
            for k in (1, 2, 3):
                device = p.at(x=1 - p.x if k & 1 else p.x, y=1 - p.y if k & 2 else p.y)
                sems = self.sem4.at[t, k]
                copy = remote(src, dst, sems.at[0], sems.at[1], device)
                copy.start() if start else copy.wait_send()
            keep = pltpu.make_async_copy(src, dst, self.sem4.at[t, 0, 0])
            keep.start() if start else keep.wait()

        self.each_y(t, run)

    def finish(self, t):
        p = self.place
        for k in (1, 2, 3):
            ref = self.land3[t].at[p.other(k)]
            remote(ref, ref, self.sem3.at[t, p.zz, 0], self.sem3.at[t, p.other(k), 1], p.at()).wait_recv()
            self.load(t, ref, 19 + k).start()
        for k in (1, 2, 3):
            self.load(t, self.land3[t].at[p.other(k)], 19 + k).wait()
        add_into(self.fin(t), self.fin(t), *[self.slot(t, 19 + k) for k in (1, 2, 3)])
        self.spread(t, True)

    def done(self, t, last):
        p = self.place
        for zz in range(4):
            for j in (0, 1):
                self.first(t, zz, j).wait_send()
            if last:
                self.second(t, zz).wait_send()
        if last:
            self.third_sent(t)
        self.spread(t, False)

        def run(y):
            for k in (1, 2, 3):
                ref = self.result(t, 1 - p.x if k & 1 else p.x, 1 - y if k & 2 else y)
                sems = self.sem4.at[t, k]
                remote(ref, ref, sems.at[0], sems.at[1], p.at()).wait_recv()

        self.each_y(t, run)


class Vectors:
    SCRATCH = [
        pltpu.VMEM((8, *SMALL), jnp.float32),
        pltpu.VMEM((4, *SMALL), jnp.float32),
        pltpu.VMEM((4, *SMALL), jnp.float32),
        pltpu.VMEM((4, *SMALL), jnp.float32),
        pltpu.VMEM((4, *SMALL), jnp.float32),
        pltpu.VMEM((4, *SMALL), jnp.float32),
        pltpu.VMEM((COND, WIDTH), jnp.float32),
        pltpu.VMEM((COND, WIDTH), jnp.float32),
        pltpu.VMEM((COND, WIDTH), jnp.float32),
        pltpu.VMEM((4, COND, WIDTH), jnp.float32),
        pltpu.SemaphoreType.DMA((16, 2)),
    ]

    def __init__(self, place, small_out, cond_out, scratch):
        self.place, self.small_out, self.cond_out = place, small_out, cond_out
        self.part, self.pair, self.x_in, self.sum1, self.y_in, self.z_in = scratch[:6]
        self.mine, self.cond_pair, self.cond_sum, self.cond_in = scratch[6:10]
        self.sems = scratch[10]

    def copy(self, i, src, dst, device):
        return remote(src, dst, self.sems.at[i, 0], self.sems.at[i, 1], device)

    def small_pair(self, zz):
        p = self.place
        return self.copy(zz, self.part.at[2 * zz + 1 - p.c], self.pair.at[zz], p.at(c=1 - p.c))

    def pair_start(self):
        for zz in range(4):
            self.small_pair(zz).start()
        self.cond_pair_copy().start()

    def cond_pair_copy(self):
        return self.copy(4, self.mine, self.cond_pair, self.place.at(c=1 - self.place.c))

    def pair_end(self):
        p = self.place
        for zz in range(4):
            self.small_pair(zz).wait()
            self.pair[zz] += self.part[2 * zz + p.c]
        self.cond_pair_copy().wait()
        self.cond_sum[...] = self.mine[...] + self.cond_pair[...]
        self.copy(5, self.pair, self.x_in, p.at(x=1 - p.x)).start()
        for k in (1, 2, 3):
            self.copy(6 + k, self.cond_sum, self.cond_in.at[p.zz], p.at(zz=p.other(k))).start()
        self.cond_in[p.zz] = self.cond_sum[...]

    def run_x(self):
        p = self.place
        self.copy(5, self.pair, self.x_in, p.at(x=1 - p.x)).wait()
        self.sum1[...] = self.pair[...] + self.x_in[...]
        self.copy(6, self.sum1, self.y_in, p.at(y=1 - p.y)).start()

    def run_y(self):
        p = self.place
        self.copy(6, self.sum1, self.y_in, p.at(y=1 - p.y)).wait()
        self.sum1[...] += self.y_in[...]
        for k in (1, 2, 3):
            self.copy(9 + k, self.sum1.at[p.other(k)], self.z_in.at[p.zz], p.at(zz=p.other(k))).start()
        self.z_in[p.zz] = self.sum1[p.zz]

    def run_z(self):
        p = self.place
        for k in (1, 2, 3):
            self.copy(9 + k, self.sum1.at[p.other(k)], self.z_in.at[p.zz], p.at(zz=p.other(k))).wait()
            self.copy(6 + k, self.cond_sum, self.cond_in.at[p.zz], p.at(zz=p.other(k))).wait()
        self.small_out[...] = (self.z_in[0] + self.z_in[1]) + (self.z_in[2] + self.z_in[3])
        cond = (self.cond_in[0] + self.cond_in[1]) + (self.cond_in[2] + self.cond_in[3])
        self.cond_out[...] = cond.astype(jnp.bfloat16)


BACK_IN = dict(
    hidden_t=ANY, slope=ANY, cot=ANY, second_t=ANY, second_unit=ANY, att_t=ANY, q=ANY, k=ANY, v=ANY, o=ANY, logsum=ANY,
    first_t=ANY, first_unit=ANY, joined_t=ANY, w_skip=ANY, w_joint=ANY, w_up=ANY, w_down=ANY, cond_t=ANY,
    second_rstd=IN_VMEM, first_rstd=IN_VMEM, vectors=IN_VMEM, cond_unit=IN_VMEM, cond_rstd=IN_VMEM, extra=IN_SMEM,
)
BACK_OUT = dict(
    d_latents=hbm((TOK, WIDTH)),
    d_skip=hbm((TOK, WIDTH)),
    g_skip=hbm((2 * PART, WIDTH)),
    g_joint=hbm((PART, 4 * WIDTH)),
    g_up=hbm((PART, 4 * WIDTH)),
    g_down=hbm((4 * PART, WIDTH)),
    hidden_t2=hbm((4, 4, PART, TOK)),
    second_t2=hbm((4, PART, TOK)),
    att_t2=hbm((4, PART, TOK)),
    first_t2=hbm((4, PART, TOK)),
    joined_t2=hbm((4, 2 * PART, TOK)),
)
BACK_SCRATCH = dict(
    cot_v=pltpu.VMEM((TOK, WIDTH), jnp.bfloat16),
    cot2=pltpu.VMEM((TOK, WIDTH), jnp.bfloat16),
    wide=pltpu.VMEM((4, TOK, WIDTH), jnp.bfloat16),
    before2=pltpu.VMEM((4, TOK, WIDTH), jnp.bfloat16),
    triple2=pltpu.VMEM((3, TOK, WIDTH), jnp.bfloat16),
    branch=pltpu.VMEM((TOK, WIDTH), jnp.bfloat16),
    branch2=pltpu.VMEM((TOK, WIDTH), jnp.bfloat16),
    base_g=pltpu.VMEM((TOK, WIDTH), jnp.bfloat16),
    base2=pltpu.VMEM((TOK, WIDTH), jnp.bfloat16),
    acc=pltpu.VMEM((TOK, WIDTH), jnp.float32),
    d_middle=pltpu.VMEM((TOK, WIDTH), jnp.float32),
    tile=pltpu.VMEM((TOK, WIDTH), jnp.bfloat16),
    weight=pltpu.VMEM((2, 8, PART, WIDTH), jnp.bfloat16),
    left=pltpu.VMEM((2, 2, 4, PART, TOK), jnp.bfloat16),
    made=pltpu.VMEM((2, 4, PART, WIDTH), jnp.bfloat16),
    heads_g=pltpu.VMEM((HEADS, TOK, HEAD), jnp.bfloat16),
    qh=pltpu.VMEM((GROUP, TOK, HEAD), jnp.bfloat16),
    oh=pltpu.VMEM((GROUP, TOK, HEAD), jnp.bfloat16),
    kh=pltpu.VMEM((GROUP, HALO + TOK + COND, HEAD), jnp.bfloat16),
    vh=pltpu.VMEM((GROUP, HALO + TOK + COND, HEAD), jnp.bfloat16),
    lh=pltpu.VMEM((GROUP, TOK, 1), jnp.float32),
    sum_k=pltpu.VMEM((HALO + TOK + COND, HEAD), jnp.float32),
    sum_v=pltpu.VMEM((HALO + TOK + COND, HEAD), jnp.float32),
    bias=pltpu.VMEM((TOK, HALO + TOK + COND), jnp.float32),
    halo2=pltpu.VMEM((2, HALO, WIDTH), jnp.bfloat16),
    d_cond=pltpu.VMEM((128, 2 * WIDTH), jnp.bfloat16),
    cond_left=pltpu.VMEM((4, PART, 128), jnp.bfloat16),
    sums=pltpu.VMEM((16, WIDTH), jnp.float32),
    wide_sum=pltpu.VMEM((1, WIDTH), jnp.float32),
    w_sems=pltpu.SemaphoreType.DMA((2,)),
    l_sems=pltpu.SemaphoreType.DMA((2, 8)),
    m_sems=pltpu.SemaphoreType.DMA((2,)),
    t_sems=pltpu.SemaphoreType.DMA((8,)),
    sib_sems=pltpu.SemaphoreType.DMA((32, 2)),
)
SUM_SKIP, SUM_GAIN1, SUM_SHIFT1, SUM_OUT, SUM_GAIN2, SUM_SHIFT2, SUM_DOWN, SUM_UP = range(8)


def back_kernel(*refs):
    cuts = [len(BACK_IN), len(BACK_OUT), 2, len(Sum.PARTS), len(Sum.LANDS), len(BACK_SCRATCH), len(Sum.SEMS), 2]
    pieces, at = [], 0
    for cut in cuts:
        pieces.append(refs[at : at + cut])
        at += cut
    i, o, b = Names(BACK_IN, pieces[0]), Names(BACK_OUT, pieces[1]), Names(BACK_SCRATCH, pieces[5])
    p = Place()
    total = Sum(p, pieces[3], pieces[4], (o.g_skip, o.g_joint, o.g_up, o.g_down), pieces[6], pieces[7])
    vectors = Vectors(p, *pieces[2], refs[at:])
    f32, bf16 = jnp.float32, jnp.bfloat16

    def copy(src, dst, sem):
        return pltpu.make_async_copy(src, dst, sem)

    def sib(n, src, dst):
        return remote(src, dst, b.sib_sems.at[n, 0], b.sib_sems.at[n, 1], p.at(c=1 - p.c))

    def halves(n, src, dst):
        return [sib(4 * n + zz, src.at[2 * zz + 1 - p.c], dst.at[zz]) for zz in range(4)]

    left_pairs = (
        (i.hidden_t, o.hidden_t2), (i.second_t, o.second_t2), (i.att_t, o.att_t2), (i.first_t, o.first_t2),
        (i.joined_t, o.joined_t2),
    )

    def column(ref, q):
        return ref.at[:, :, pl.ds(q * WIDTH, WIDTH)]

    blocks = [i.w_down.at[pl.ds(8 * q, 8)] for q in range(4)]
    blocks += [column(i.w_up, q) for q in range(4)]
    blocks += [column(i.w_joint, q) for q in (3, 0, 1, 2)]
    blocks += [i.w_skip.at[pl.ds(8 * n, 8)] for n in range(2)]

    def load_weight(n):
        return copy(blocks[n], b.weight.at[n % 2], b.w_sems.at[n % 2])

    def stream(start, count, body):
        for n in range(start, start + count):
            if n + 1 < len(blocks):
                load_weight(n + 1).start()
            load_weight(n).wait()
            body(n - start, b.weight[n % 2].reshape(WIDTH, WIDTH))

    def by_rows(size, body):
        @pl.loop(0, TOK // size)
        def _(n):
            body(pl.ds(pl.multiple_of(n * size, size), size))

    def add_sum(row, value):
        b.sums[row : row + 1, :] += value

    def colsum(value):
        return jnp.sum(value, axis=0, keepdims=True)

    def form(n, dst, own, own2, pairs, extra=None):
        result = nn(own.reshape(4 * PART, TOK), pairs[0]) + nn(own2.reshape(4 * PART, TOK), pairs[1])
        if extra is not None:
            result += extra
        slot = n % 2
        b.made[slot] = result.astype(bf16).reshape(4, PART, WIDTH)
        copy(b.made.at[slot], dst, b.m_sems.at[slot]).start()

    def formed(n, dst):
        copy(b.made.at[n % 2], dst, b.m_sems.at[n % 2]).wait()

    def send_all(copies):
        for one in copies:
            one.start()

    def recv_all(copies):
        for one in copies:
            one.wait_recv()

    def left_copies(n):
        own, other = b.left.at[n % 2, 0], b.left.at[n % 2, 1]
        sems = b.l_sems.at[n % 2]
        if n < 4:
            zz = ORDER[n]
            pairs = [(i.hidden_t.at[2 * zz + p.c], own), (o.hidden_t2.at[zz], other)]
        elif n < 7:
            src, src2 = left_pairs[n - 3]
            pairs = [(src.at[2 * zz + p.c], own.at[zz]) for zz in range(4)] + [(src2, other)]
        else:
            pairs = []
            for k in range(4):
                zz, rows = 2 * (n - 7) + k // 2, pl.ds((k % 2) * PART, PART)
                pairs.append((i.joined_t.at[2 * zz + p.c, rows], own.at[k]))
                pairs.append((o.joined_t2.at[zz, rows], other.at[k]))
        return [copy(src, dst, sems.at[m]) for m, (src, dst) in enumerate(pairs)]

    def left_start(n):
        if n < 4:
            left_sends[0][ORDER[n]].wait_recv()
        elif n < 7:
            recv_all(left_sends[n - 3])
        else:
            recv_all(left_sends[4][2 * (n - 7) : 2 * (n - 7) + 2])
        send_all(left_copies(n))

    def left_done(n):
        for one in left_copies(n):
            one.wait()
        return b.left[n % 2, 0], b.left[n % 2, 1]

    cot_load = copy(i.cot, b.cot_v, b.t_sems.at[0])
    cot_load.start()
    load_weight(0).start()
    greet(p)
    sib_cot = sib(20, i.cot, b.cot2)
    left_sends = [halves(n, src, dst) for n, (src, dst) in enumerate(left_pairs)]
    send_all([left_sends[0][zz] for zz in ORDER])
    sib_cot.start()
    b.sums[...] = jnp.zeros_like(b.sums)
    b.d_cond[2 * COND :] = jnp.zeros((128 - 2 * COND, 2 * WIDTH), bf16)
    vectors.part[...] = jnp.zeros_like(vectors.part)
    make_bias(i.extra, p.b, b.bias)
    cot_load.wait()

    def before_sib(q):
        return sib(21 + q, b.wide.at[q], b.before2.at[q])

    def slope_load(q):
        return copy(i.slope.at[:, pl.ds(q * WIDTH, WIDTH)], b.tile, b.t_sems.at[1])

    def do_before(q, weight):
        slope_load(q).start()
        b.acc[...] = nt(b.cot_v[...], weight)
        slope_load(q).wait()
        b.wide_sum[...] = jnp.zeros_like(b.wide_sum)

        @functools.partial(by_rows, 64)
        def _(rows):
            value = (b.acc[rows] * b.tile[rows].astype(f32)).astype(bf16)
            b.wide[q, rows] = value
            b.wide_sum[...] += colsum(value.astype(f32))

        for n in range(8):
            row = 7 + n % 4
            vectors.part[2 * q + n // 4, row : row + 1, 0:PART] = b.wide_sum[:, n * PART : (n + 1) * PART]
        before_sib(q).start()

    stream(0, 4, do_before)

    for n in (1, 2, 3, 4):
        send_all(left_sends[n])

    sib_cot.wait_recv()
    down_parts = pieces[3][3]
    left_start(0)
    for n, zz in enumerate(ORDER):
        left_start(n + 1)
        form(n, down_parts.at[zz], *left_done(n), (b.cot_v[...], b.cot2[...]))
        if n > 0:
            formed(n - 1, down_parts.at[ORDER[n - 1]])
            total.start(3, (ORDER[n - 1],))

    up_parts = pieces[3][2]
    lefts = left_done(4)
    for q in range(4):
        before_sib(q).wait_recv()
        form(q, column(up_parts, q), *lefts, (b.wide[q], b.before2[q]))
        if q == 0:
            formed(3, down_parts.at[ORDER[3]])
            total.start(3, (ORDER[3],))
        else:
            formed(q - 1, column(up_parts, q - 1))
    left_start(5)

    def do_second(q, weight):
        value = nt(b.wide[q], weight)
        if q == 0:
            b.acc[...] = value
        else:
            b.acc[...] += value

    unit_load = copy(i.second_unit, b.tile, b.t_sems.at[1])
    unit_load.start()
    stream(4, 4, do_second)
    unit_load.wait()
    formed(3, column(up_parts, 3))

    def norm_rows(unit, rstd, gain, grad, gain_row, shift_row):
        scaled = grad * gain
        mean1 = jnp.mean(scaled, axis=1, keepdims=True)
        mean2 = jnp.mean(scaled * unit, axis=1, keepdims=True)
        add_sum(gain_row, colsum(grad * unit))
        add_sum(shift_row, colsum(grad))
        return rstd * (scaled - mean1 - unit * mean2)

    @functools.partial(by_rows, 64)
    def _(rows):
        unit = b.tile[rows].astype(f32)
        back = norm_rows(unit, i.second_rstd[rows], i.vectors[4:5], b.acc[rows], SUM_GAIN2, SUM_SHIFT2)
        g = b.cot_v[rows].astype(f32)
        middle = g + back
        b.d_middle[rows] = middle
        low = middle.astype(bf16)
        b.branch[rows] = low
        add_sum(SUM_OUT, colsum(low.astype(f32)))
        add_sum(SUM_DOWN, colsum(g))

    branch_sib = sib(25, b.branch, b.branch2)
    branch_sib.start()

    def do_attended(_, weight):
        b.tile[...] = nt(b.branch[...], weight).astype(bf16)
        for h in range(HEADS):
            b.heads_g[h] = b.tile[:, head(h)]

    stream(8, 1, do_attended)

    joint_parts = pieces[3][1]
    lefts = left_done(5)
    left_start(6)
    branch_sib.wait_recv()
    form(0, column(joint_parts, 3), *lefts, (b.branch[...], b.branch2[...]))

    total.pass_on(3)
    total.start(2)
    formed(0, column(joint_parts, 3))
    for q in range(4):
        before_sib(q).wait_send()

    scale = HEAD**-0.5
    n_keys = HALO + TOK + COND

    def group_loads(start):
        hs = pl.ds(start, GROUP)
        pairs = ((i.q, b.qh), (i.o, b.oh), (i.k, b.kh), (i.v, b.vh), (i.logsum, b.lh))
        return [copy(src.at[hs], dst, b.t_sems.at[n]) for n, (src, dst) in enumerate(pairs)]

    def group(start):
        send_all(group_loads(start))
        for one in group_loads(start):
            one.wait()

        @pl.loop(0, GROUP)
        def _(h):
            for row, low in TILES:
                rows, keys = pl.ds(row, 256), pl.ds(low, n_keys - low)
                q, k, v, g = b.qh[h, rows], b.kh[h, keys], b.vh[h, keys], b.heads_g[start + h, rows]
                scores = nt(q, k) * (scale * LOG2E) + b.bias[rows, keys]
                probs = jnp.exp2(scores - b.lh[h, rows])
                d_probs = nt(g, v)
                inner = jnp.sum(g.astype(f32) * b.oh[h, rows].astype(f32), axis=1, keepdims=True)
                d_scores = (probs * (d_probs - inner)).astype(bf16)
                d_k, d_v = tn(d_scores, q), tn(probs.astype(bf16), g)
                if row == 0:
                    b.sum_k[...] = d_k
                    b.sum_v[...] = d_v
                else:
                    b.sum_k[keys] += d_k
                    b.sum_v[keys] += d_v
                b.oh[h, rows] = (nn(d_scores, k) * scale).astype(bf16)
            b.kh[h] = (b.sum_k[...] * scale).astype(bf16)
            b.vh[h] = b.sum_v[...].astype(bf16)

        for n in range(GROUP):
            at = head(start + n)
            b.wide[0, :, at] = b.oh[n]
            for j, made in ((0, b.kh), (1, b.vh)):
                wide = slice(j * WIDTH + at.start, j * WIDTH + at.stop)
                b.before2[j, 0:HALO, at] = made[n, 0:HALO]
                b.wide[1 + j, :, at] = made[n, HALO : HALO + TOK]
                b.d_cond[0:COND, wide] = made[n, HALO + TOK :]

    group(0)
    group(4)
    total.to_chip(3)
    group(8)
    group(12)

    def halo_copy(device):
        src = b.before2.at[pl.ds(0, 2), pl.ds(0, HALO)]
        return remote(src, b.halo2, b.sib_sems.at[31, 0], b.sib_sems.at[31, 1], device)

    cond_sib = sib(30, b.d_cond.at[pl.ds(0, COND)], b.d_cond.at[pl.ds(COND, COND)])
    cond_sib.start()
    pl.when(p.b > 0)(lambda: halo_copy((p.s, p.b - 1)).start())

    def triple_sib(j):
        return sib(26 + j, b.wide.at[j], b.triple2.at[j])

    triple_sib(0).start()
    for zz in range(4):
        copy(i.cond_t.at[2 * zz + p.c], b.cond_left.at[zz], b.t_sems.at[4 + zz]).start()
    unit_load = copy(i.first_unit, b.tile, b.t_sems.at[1])
    unit_load.start()

    def do_first(j, weight):
        if j == 1:
            merge_halo()
        value = nt(b.wide[j], weight)
        if j == 0:
            b.acc[...] = value
        else:
            b.acc[...] += value
            cond = nt(b.d_cond[0:COND, (j - 1) * WIDTH : j * WIDTH], weight)
            if j == 1:
                vectors.mine[...] = cond
            else:
                vectors.mine[...] += cond

    def merge_halo():
        @pl.when(p.b < 7)
        def _():
            halo_copy((p.s, p.b)).wait_recv()

            @pl.loop(0, HALO // 64)
            def _(n):
                low = pl.ds(pl.multiple_of(n * 64, 64), 64)
                rows = pl.ds(pl.multiple_of(n * 64 + TOK - HALO, 64), 64)
                for j in (0, 1):
                    extra = b.halo2[j, low].astype(f32)
                    b.wide[1 + j, rows] = (b.wide[1 + j, rows].astype(f32) + extra).astype(bf16)

        triple_sib(1).start()
        triple_sib(2).start()

    stream(9, 3, do_first)
    unit_load.wait()
    total.pass_on(2, after=3)

    @functools.partial(by_rows, 64)
    def _(rows):
        unit = b.tile[rows].astype(f32)
        back = norm_rows(unit, i.first_rstd[rows], i.vectors[1:2], b.acc[rows], SUM_GAIN1, SUM_SHIFT1)
        low = (b.d_middle[rows] + back).astype(bf16)
        b.base_g[rows] = low
        add_sum(SUM_SKIP, colsum(low.astype(f32)))

    base_sib = sib(29, b.base_g, b.base2)
    base_sib.start()
    for zz in range(4):
        copy(i.cond_t.at[2 * zz + p.c], b.cond_left.at[zz], b.t_sems.at[4 + zz]).wait()
    cond_sib.wait_recv()

    lefts = left_done(6)
    left_start(7)
    for j in range(3):
        triple_sib(j).wait_recv()
        extra = None
        if j > 0:
            extra = nn(b.cond_left[...].reshape(4 * PART, 128), b.d_cond[:, (j - 1) * WIDTH : j * WIDTH])
        form(j, column(joint_parts, j), *lefts, (b.wide[j], b.triple2[j]), extra)
        if j > 0:
            formed(j - 1, column(joint_parts, j - 1))
    formed(2, column(joint_parts, 2))
    total.start(1)
    vectors.mine[...] = norm_rows(
        i.cond_unit[...], i.cond_rstd[...], i.vectors[1:2], vectors.mine[...], SUM_GAIN1, SUM_SHIFT1
    )
    for row in range(7):
        for n in range(8):
            vectors.part[n, row : row + 1, 0:PART] = b.sums[row : row + 1, n * PART : (n + 1) * PART]
    vectors.pair_start()
    total.finish(3)

    skip_parts = pieces[3][0]
    base_sib.wait_recv()
    for n in (0, 1):
        lefts = left_done(7 + n)
        if n == 0:
            left_start(8)
        form(n, skip_parts.at[pl.ds(4 * n, 4)], *lefts, (b.base_g[...], b.base2[...]))
    vectors.pair_end()
    total.to_chip(2, after=3)
    for n in (0, 1):
        formed(n, skip_parts.at[pl.ds(4 * n, 4)])

    def do_joined(n, weight):
        made = (b.tile, b.branch)[n]
        made[...] = nt(b.base_g[...], weight).astype(bf16)
        copy(made, (o.d_latents, o.d_skip)[n], b.t_sems.at[n]).start()

    branch_sib.wait_send()
    stream(12, 2, do_joined)
    vectors.run_x()

    total.pass_on(1, after=2)
    total.start(0)
    vectors.run_y()
    total.finish(2)
    total.to_chip(1, after=2)
    total.pass_on(0, after=1)
    total.finish(1)
    total.to_chip(0, after=1)
    total.finish(0)
    vectors.run_z()
    for n in (0, 1):
        copy((b.tile, b.branch)[n], (o.d_latents, o.d_skip)[n], b.t_sems.at[n]).wait()
    for group_sends in left_sends:
        for one in group_sends:
            one.wait_send()
    for one in (sib_cot, cond_sib, base_sib, triple_sib(0), triple_sib(1), triple_sib(2)):
        one.wait_send()
    pl.when(p.b > 0)(lambda: halo_copy((p.s, p.b - 1)).wait_send())
    for t in (3, 2, 1, 0):
        total.done(t, t == 0)


def backward(arrays):
    vm = pl.BlockSpec(memory_space=pltpu.VMEM)
    outs = pl.pallas_call(
        back_kernel,
        out_shape=[*BACK_OUT.values()] + [
            jax.ShapeDtypeStruct(SMALL, jnp.float32), jax.ShapeDtypeStruct((COND, WIDTH), jnp.bfloat16)
        ] + Sum.PARTS + Sum.LANDS,
        in_specs=[*BACK_IN.values()],
        out_specs=[ANY] * len(BACK_OUT) + [vm] * 2 + [ANY] * (len(Sum.PARTS) + len(Sum.LANDS)),
        scratch_shapes=[*BACK_SCRATCH.values()] + Sum.SEMS + Sum.SLOTS + Vectors.SCRATCH,
        compiler_params=pltpu.CompilerParams(collective_id=1, has_side_effects=True, vmem_limit_bytes=60 << 20),
    )(*[arrays[name] for name in BACK_IN])
    named = Names(BACK_OUT, outs[: len(BACK_OUT)])
    return named, outs[len(BACK_OUT)], outs[len(BACK_OUT) + 1]


def item_ends(extra_length):
    lengths = extra_length[0] + (LEN_MIN - 1)
    count = lengths.shape[0]
    upto = lax.iota(jnp.int32, count)[None, :] <= lax.iota(jnp.int32, count)[:, None]
    return jnp.sum(jnp.where(upto, lengths[None, :], 0), axis=1)


def quick(
    latents, skip_input, cond_tokens, extra_length, skip_weight, skip_bias, first_gain, first_shift, joint_weight,
    out_weight, out_bias, second_gain, second_shift, up_weight, up_bias, down_weight, down_bias, cotangent,
):
    f32, bf16 = jnp.float32, jnp.bfloat16
    few = (skip_bias, first_gain, first_shift, out_bias, second_gain, second_shift, down_bias)
    rows = jnp.concatenate([jnp.stack(few), up_bias.reshape(4, PART)], 0).astype(f32)
    arrays = dict(
        rows=rows,
        extra=extra_length,
        cond=cond_tokens.reshape(COND, WIDTH),
        latents=latents,
        skip_input=skip_input,
        skip=skip_weight.reshape(2, PART, WIDTH),
        joint=joint_weight,
        out=out_weight,
        up=up_weight,
        down=down_weight.reshape(4, PART, WIDTH),
        cot=cotangent,
    )
    made = forward(arrays)
    grads, sums, cond_sum = backward({**arrays, **made})
    v = [sums[n, :PART] for n in range(7)]
    return (
        made["output"],
        grads.d_latents,
        grads.d_skip,
        cond_sum.reshape(cond_tokens.shape),
        grads.g_skip.astype(f32),
        v[0],
        v[1],
        v[2],
        grads.g_joint[:, : 3 * WIDTH].astype(f32),
        grads.g_joint[:, 3 * WIDTH :].astype(f32),
        v[3],
        v[4],
        v[5],
        grads.g_up.astype(f32),
        sums[7:11, :PART].reshape(-1),
        grads.g_down.astype(f32),
        v[6],
    )


def shifted(value, axis, steps):
    count = lax.axis_size(axis)
    leading, last = (max(0, -steps), min(count, count - steps))
    return lax.ppermute(value, axis, [(source, source + steps) for source in range(leading, last)])


def layer_norm(values, gain, shift):
    center = values - jnp.mean(values, axis=-1, keepdims=True)
    spread = jnp.mean(center * center, axis=-1, keepdims=True)
    return center * lax.rsqrt(spread + 1e-05) * gain + shift


def contract_rows(left, right):
    return lax.dot_general(
        left, right, (((0,), (0,)), ((), ())), preferred_element_type=jnp.float32
    )


def contract_cols(left, right):
    return lax.dot_general(
        left, right, (((1,), (1,)), ((), ())), preferred_element_type=jnp.float32
    )


def segment_ids(ends, places):
    inside = jnp.sum((ends[None, :] <= places[:, None]).astype(jnp.int32), axis=1)
    return jnp.where(places >= 0, inside, -1)


def split_heads(block):
    return block.reshape(block.shape[0], HEADS, HEAD).transpose(1, 0, 2)


def merge_heads(block):
    return block.transpose(1, 0, 2).reshape(block.shape[1], HEADS * HEAD)


def masked_scores(query, keys, allowed):
    scores = contract_cols(query, keys) * HEAD ** (-0.5)
    return jnp.where(allowed, scores, -1e30)


def plain(
    latents,
    skip_input,
    cond_tokens,
    extra_length,
    skip_weight,
    skip_bias,
    first_gain,
    first_shift,
    joint_weight,
    out_weight,
    out_bias,
    second_gain,
    second_shift,
    up_weight,
    up_bias,
    down_weight,
    down_bias,
    cotangent,
):
    whole = (
        lax.all_gather(skip_weight, "blk", axis=0, tiled=True),
        lax.all_gather(skip_bias, "blk", axis=0, tiled=True),
        lax.all_gather(first_gain, "blk", axis=0, tiled=True),
        lax.all_gather(first_shift, "blk", axis=0, tiled=True),
        lax.all_gather(joint_weight, "blk", axis=0, tiled=True),
        lax.all_gather(out_weight, "blk", axis=0, tiled=True),
        lax.all_gather(out_bias, "blk", axis=0, tiled=True),
        lax.all_gather(second_gain, "blk", axis=0, tiled=True),
        lax.all_gather(second_shift, "blk", axis=0, tiled=True),
        lax.all_gather(up_weight, "blk", axis=0, tiled=True),
        lax.all_gather(up_bias, "blk", axis=0, tiled=True),
        lax.all_gather(down_weight, "blk", axis=0, tiled=True),
        lax.all_gather(down_bias, "blk", axis=0, tiled=True),
    )
    (
        skip_matrix,
        skip_offset,
        gain_first,
        shift_first,
        joint_matrix,
        out_matrix,
        out_offset,
        gain_second,
        shift_second,
        up_matrix,
        up_offset,
        down_matrix,
        down_offset,
    ) = whole
    rows = latents.shape[0]
    width = latents.shape[1]
    scale = HEAD ** (-0.5)
    joined = jnp.concatenate([latents, skip_input], 1)
    base = jnp.dot(joined, skip_matrix, preferred_element_type=jnp.float32) + skip_offset
    first_in = layer_norm(base, gain_first, shift_first).astype(jnp.bfloat16)
    triple = jnp.dot(first_in, joint_matrix, preferred_element_type=jnp.float32).astype(
        jnp.bfloat16
    )
    query = triple[:, :width]
    pair_here = triple[:, width:]
    pair_left = shifted(pair_here, "blk", 1)
    cond_flat = cond_tokens.reshape(-1, width).astype(jnp.float32)
    cond_in = layer_norm(cond_flat, gain_first, shift_first).astype(jnp.bfloat16)
    cond_pair = jnp.dot(
        cond_in, joint_matrix[:, width:], preferred_element_type=jnp.float32
    ).astype(jnp.bfloat16)
    pairs = jnp.concatenate([pair_left, pair_here, cond_pair], 0)
    ends = item_ends(extra_length)
    here = lax.axis_index("blk")
    places = here * rows + lax.iota(jnp.int32, rows)
    seg_here = segment_ids(ends, places)
    seg_left = segment_ids(ends, places - rows)
    cond_seg = lax.iota(jnp.int32, cond_pair.shape[0]) // 2
    allowed = seg_here[:, None] == jnp.concatenate([seg_left, seg_here, cond_seg])[None, :]
    head_query = split_heads(query)
    head_key = split_heads(pairs[:, :width])
    head_value = split_heads(pairs[:, width:])

    def head_forward(parts):
        query_one, key_one, value_one = parts
        scores = masked_scores(query_one, key_one, allowed)
        top = jnp.max(scores, axis=1, keepdims=True)
        expo = jnp.exp(scores - top)
        total = jnp.sum(expo, axis=1, keepdims=True)
        probs = (expo / total).astype(jnp.bfloat16)
        mixed = jnp.dot(probs, value_one, preferred_element_type=jnp.float32)
        return (mixed, (top + jnp.log(total))[:, 0])

    mixed, logsum = lax.map(head_forward, (head_query, head_key, head_value))
    attended = merge_heads(mixed).astype(jnp.bfloat16)
    middle = base + jnp.dot(attended, out_matrix, preferred_element_type=jnp.float32) + out_offset
    second_in = layer_norm(middle, gain_second, shift_second).astype(jnp.bfloat16)
    before = jnp.dot(second_in, up_matrix, preferred_element_type=jnp.float32) + up_offset
    hidden = jax.nn.gelu(before, approximate=False).astype(jnp.bfloat16)
    output = middle + jnp.dot(hidden, down_matrix, preferred_element_type=jnp.float32) + down_offset
    again = (
        lax.all_gather(skip_weight, "blk", axis=0, tiled=True),
        lax.all_gather(skip_bias, "blk", axis=0, tiled=True),
        lax.all_gather(first_gain, "blk", axis=0, tiled=True),
        lax.all_gather(first_shift, "blk", axis=0, tiled=True),
        lax.all_gather(joint_weight, "blk", axis=0, tiled=True),
        lax.all_gather(out_weight, "blk", axis=0, tiled=True),
        lax.all_gather(out_bias, "blk", axis=0, tiled=True),
        lax.all_gather(second_gain, "blk", axis=0, tiled=True),
        lax.all_gather(second_shift, "blk", axis=0, tiled=True),
        lax.all_gather(up_weight, "blk", axis=0, tiled=True),
        lax.all_gather(up_bias, "blk", axis=0, tiled=True),
        lax.all_gather(down_weight, "blk", axis=0, tiled=True),
        lax.all_gather(down_bias, "blk", axis=0, tiled=True),
    )
    (
        skip_matrix,
        skip_offset,
        gain_first,
        shift_first,
        joint_matrix,
        out_matrix,
        out_offset,
        gain_second,
        shift_second,
        up_matrix,
        up_offset,
        down_matrix,
        down_offset,
    ) = again
    incoming = cotangent.astype(jnp.float32)
    grad_down_offset = jnp.sum(incoming, axis=0)
    grad_down_matrix = contract_rows(hidden, cotangent)
    d_hidden = contract_cols(cotangent, down_matrix)
    gelu_value, gelu_pull = jax.vjp(partial(jax.nn.gelu, approximate=False), before)
    d_before = gelu_pull(d_hidden)[0].astype(jnp.bfloat16)
    grad_up_offset = jnp.sum(d_before.astype(jnp.float32), axis=0)
    grad_up_matrix = contract_rows(second_in, d_before)
    d_second = contract_cols(d_before, up_matrix)
    norm_value, norm_pull = jax.vjp(
        layer_norm, middle, gain_second.astype(jnp.float32), shift_second.astype(jnp.float32)
    )
    d_middle_norm, grad_gain_second, grad_shift_second = norm_pull(d_second)
    d_middle = incoming + d_middle_norm
    d_branch = d_middle.astype(jnp.bfloat16)
    grad_out_offset = jnp.sum(d_branch.astype(jnp.float32), axis=0)
    grad_out_matrix = contract_rows(attended, d_branch)
    d_attended = contract_cols(d_branch, out_matrix).astype(jnp.bfloat16)

    def head_backward(parts):
        query_one, key_one, value_one, grad_one, logsum_one = parts
        scores = masked_scores(query_one, key_one, allowed)
        probs = jnp.exp(scores - logsum_one[:, None])
        d_probs = contract_cols(grad_one, value_one)
        inner = jnp.sum(probs * d_probs, axis=1, keepdims=True)
        d_scores = (probs * (d_probs - inner)).astype(jnp.bfloat16)
        d_query_one = jnp.dot(d_scores, key_one, preferred_element_type=jnp.float32) * scale
        d_key_one = contract_rows(d_scores, query_one) * scale
        d_value_one = contract_rows(probs.astype(jnp.bfloat16), grad_one)
        return (d_query_one, d_key_one, d_value_one)

    d_query_heads, d_key_heads, d_value_heads = lax.map(
        head_backward, (head_query, head_key, head_value, split_heads(d_attended), logsum)
    )
    d_query = merge_heads(d_query_heads)
    d_pairs = jnp.concatenate([merge_heads(d_key_heads), merge_heads(d_value_heads)], 1)
    d_left = d_pairs[:rows]
    d_own = d_pairs[rows : 2 * rows]
    d_cond_part = d_pairs[2 * rows :]
    d_returned = shifted(d_left.astype(jnp.bfloat16), "blk", -1).astype(d_left.dtype)
    d_cond_total = lax.psum(d_cond_part.astype(jnp.bfloat16), "blk")
    d_triple = jnp.concatenate([d_query, d_own + d_returned], 1).astype(jnp.bfloat16)
    leading = (here == 0).astype(jnp.float32)
    cond_term = contract_rows(cond_in, d_cond_total) * leading
    grad_joint_matrix = contract_rows(first_in, d_triple) + jnp.concatenate(
        [jnp.zeros((width, width), jnp.float32), cond_term], 1
    )
    d_first = contract_cols(d_triple, joint_matrix)
    d_cond_in = contract_cols(d_cond_total, joint_matrix[:, width:])
    first_value, first_pull = jax.vjp(
        layer_norm, base, gain_first.astype(jnp.float32), shift_first.astype(jnp.float32)
    )
    d_base_norm, grad_gain_tokens, grad_shift_tokens = first_pull(d_first)
    cond_value, cond_pull = jax.vjp(
        layer_norm, cond_flat, gain_first.astype(jnp.float32), shift_first.astype(jnp.float32)
    )
    d_cond_flat, grad_gain_cond, grad_shift_cond = cond_pull(d_cond_in)
    grad_gain_first = grad_gain_tokens + leading * grad_gain_cond
    grad_shift_first = grad_shift_tokens + leading * grad_shift_cond
    d_base = (d_middle + d_base_norm).astype(jnp.bfloat16)
    grad_skip_offset = jnp.sum(d_base.astype(jnp.float32), axis=0)
    grad_skip_matrix = contract_rows(joined, d_base)
    d_joined = contract_cols(d_base, skip_matrix)
    shares = (
        lax.psum_scatter(
            grad_skip_matrix.astype(jnp.bfloat16), "blk", scatter_dimension=0, tiled=True
        ).astype(jnp.float32),
        lax.psum_scatter(
            grad_skip_offset.astype(jnp.bfloat16), "blk", scatter_dimension=0, tiled=True
        ).astype(jnp.float32),
        lax.psum_scatter(
            grad_gain_first.astype(jnp.bfloat16), "blk", scatter_dimension=0, tiled=True
        ).astype(jnp.float32),
        lax.psum_scatter(
            grad_shift_first.astype(jnp.bfloat16), "blk", scatter_dimension=0, tiled=True
        ).astype(jnp.float32),
        lax.psum_scatter(
            grad_joint_matrix.astype(jnp.bfloat16), "blk", scatter_dimension=0, tiled=True
        ).astype(jnp.float32),
        lax.psum_scatter(
            grad_out_matrix.astype(jnp.bfloat16), "blk", scatter_dimension=0, tiled=True
        ).astype(jnp.float32),
        lax.psum_scatter(
            grad_out_offset.astype(jnp.bfloat16), "blk", scatter_dimension=0, tiled=True
        ).astype(jnp.float32),
        lax.psum_scatter(
            grad_gain_second.astype(jnp.bfloat16), "blk", scatter_dimension=0, tiled=True
        ).astype(jnp.float32),
        lax.psum_scatter(
            grad_shift_second.astype(jnp.bfloat16), "blk", scatter_dimension=0, tiled=True
        ).astype(jnp.float32),
        lax.psum_scatter(
            grad_up_matrix.astype(jnp.bfloat16), "blk", scatter_dimension=0, tiled=True
        ).astype(jnp.float32),
        lax.psum_scatter(
            grad_up_offset.astype(jnp.bfloat16), "blk", scatter_dimension=0, tiled=True
        ).astype(jnp.float32),
        lax.psum_scatter(
            grad_down_matrix.astype(jnp.bfloat16), "blk", scatter_dimension=0, tiled=True
        ).astype(jnp.float32),
        lax.psum_scatter(
            grad_down_offset.astype(jnp.bfloat16), "blk", scatter_dimension=0, tiled=True
        ).astype(jnp.float32),
    )
    (
        share_skip,
        share_skip_offset,
        share_gain_first,
        share_shift_first,
        share_joint,
        share_out,
        share_out_offset,
        share_gain_second,
        share_shift_second,
        share_up,
        share_up_offset,
        share_down,
        share_down_offset,
    ) = shares
    summed = (
        lax.psum(share_skip.astype(jnp.bfloat16), "stream").astype(jnp.float32),
        lax.psum(share_skip_offset.astype(jnp.bfloat16), "stream").astype(jnp.float32),
        lax.psum(share_gain_first.astype(jnp.bfloat16), "stream").astype(jnp.float32),
        lax.psum(share_shift_first.astype(jnp.bfloat16), "stream").astype(jnp.float32),
        lax.psum(share_joint.astype(jnp.bfloat16), "stream").astype(jnp.float32),
        lax.psum(share_out.astype(jnp.bfloat16), "stream").astype(jnp.float32),
        lax.psum(share_out_offset.astype(jnp.bfloat16), "stream").astype(jnp.float32),
        lax.psum(share_gain_second.astype(jnp.bfloat16), "stream").astype(jnp.float32),
        lax.psum(share_shift_second.astype(jnp.bfloat16), "stream").astype(jnp.float32),
        lax.psum(share_up.astype(jnp.bfloat16), "stream").astype(jnp.float32),
        lax.psum(share_up_offset.astype(jnp.bfloat16), "stream").astype(jnp.float32),
        lax.psum(share_down.astype(jnp.bfloat16), "stream").astype(jnp.float32),
        lax.psum(share_down_offset.astype(jnp.bfloat16), "stream").astype(jnp.float32),
    )
    return (
        output.astype(jnp.bfloat16),
        d_joined[:, :width].astype(jnp.bfloat16),
        d_joined[:, width:].astype(jnp.bfloat16),
        d_cond_flat.reshape(cond_tokens.shape).astype(jnp.bfloat16),
        summed[0],
        summed[1],
        summed[2],
        summed[3],
        summed[4],
        summed[5],
        summed[6],
        summed[7],
        summed[8],
        summed[9],
        summed[10],
        summed[11],
        summed[12],
    )


def solution(mesh):
    placed = (
        P(("stream", "blk"), None),
        P(("stream", "blk"), None),
        P("stream", None, None),
        P("stream", None),
        P("blk", None),
        P("blk"),
        P("blk"),
        P("blk"),
        P("blk", None),
        P("blk", None),
        P("blk"),
        P("blk"),
        P("blk"),
        P("blk", None),
        P("blk"),
        P("blk", None),
        P("blk"),
        P(("stream", "blk"), None),
    )
    fits = mesh.shape["stream"] == 4 and mesh.shape["blk"] == 8
    return jax.shard_map(
        quick if fits else plain,
        mesh=mesh,
        in_specs=placed,
        out_specs=(
            P(("stream", "blk"), None),
            P(("stream", "blk"), None),
            P(("stream", "blk"), None),
            P("stream", None, None),
            P("blk", None),
            P("blk"),
            P("blk"),
            P("blk"),
            P("blk", None),
            P("blk", None),
            P("blk"),
            P("blk"),
            P("blk"),
            P("blk", None),
            P("blk"),
            P("blk", None),
            P("blk"),
        ),
        check_vma=False,
    )
```

```python
import functools
from functools import partial

import jax
import jax.numpy as jnp
from jax import lax
from jax.experimental import pallas as pl
from jax.experimental.pallas import tpu as pltpu
from jax.sharding import PartitionSpec as P

HEADS = 16
HEAD = 72
LEN_MIN = 192

MESH = pl.DeviceIdType.MESH
ANY = pl.BlockSpec(memory_space=pl.ANY)
WIDTH = 1152
PART = 144
SMALL = (16, 256)


class Place:
    def __init__(self):
        self.s = lax.axis_index("stream")
        self.b = lax.axis_index("blk")
        self.x = lax.rem(self.s, 2)
        self.y = lax.div(self.s, 2)
        self.c = lax.rem(self.b, 2)
        self.zz = lax.div(self.b, 2)

    def other(self, k):
        low, high = lax.rem(self.zz, 2), lax.div(self.zz, 2)
        return 2 * (1 - high if k & 2 else high) + (1 - low if k & 1 else low)

    def source(self, k):
        zz = self.zz
        table = ((1, 0, 3, 2), (2, 2, 1, 1), (3, 3, 0, 0))[k - 1]
        return jnp.where(zz < 2, jnp.where(zz == 0, table[0], table[1]), jnp.where(zz == 2, table[2], table[3]))

    def at(self, x=None, y=None, zz=None, c=None):
        x = self.x if x is None else x
        y = self.y if y is None else y
        zz = self.zz if zz is None else zz
        c = self.c if c is None else c
        return (2 * y + x, 2 * zz + c)


def greet(place):
    barrier = pltpu.get_barrier_semaphore()
    p = place
    near = [p.at(x=1 - p.x), p.at(y=1 - p.y), p.at(c=1 - p.c)] + [p.at(zz=p.other(k)) for k in (1, 2, 3)]
    for device in near:
        pl.semaphore_signal(barrier, inc=1, device_id=device, device_id_type=MESH)
    up = (p.c == 1) & (p.zz < 3)
    down = (p.c == 0) & (p.zz > 0)
    for go, device in ((up, (p.s, p.b + 1)), (down, (p.s, p.b - 1))):

        @pl.when(go)
        def _():
            pl.semaphore_signal(barrier, inc=1, device_id=device, device_id_type=MESH)

    pl.when(up | down)(lambda: pl.semaphore_wait(barrier, len(near) + 1))
    pl.when(jnp.logical_not(up | down))(lambda: pl.semaphore_wait(barrier, len(near)))


def remote(src, dst, send, recv, device):
    return pltpu.make_async_remote_copy(
        src_ref=src, dst_ref=dst, send_sem=send, recv_sem=recv, device_id=device, device_id_type=MESH
    )


def block(t, ref, b):
    if t in (1, 2):
        return ref.at[b]
    size = 2 if t == 0 else 4
    return ref.at[pl.ds(b * size, size)]


def piece(t, ref, b, x, y):
    if t in (1, 2):
        return ref.at[b, :, pl.ds(pl.multiple_of((2 * y + x) * WIDTH, 128), WIDTH)]
    if t == 3:
        return ref.at[4 * b + 2 * y + x]
    low, size = (0, 80) if y == 0 else (80, 64)
    return ref.at[2 * b + x, pl.ds(low, size)]


KINDS = ("half", "cols", "cols", "rows")


class Gather:
    SEMS = [pltpu.SemaphoreType.DMA((4, 6, 4, 2)), pltpu.SemaphoreType.DMA((12,)), pltpu.SemaphoreType.DMA((2, 8))]

    def __init__(self, place, shards, outs, scratch):
        self.place = place
        self.small_in, self.skip_in, self.joint_in, self.out_in, self.up_in, self.down_in = shards
        self.small = outs[0]
        self.outs = outs[1:]
        self.sems, self.local_sems, self.small_sems = scratch[:3]
        self.stage = scratch[3:]

    def copy(self, t, x, y, zz, c, stage, k, device):
        ref = piece(t, self.outs[t], 2 * zz + c, x, y)
        return remote(ref, ref, self.sems.at[t, stage, k, 0], self.sems.at[t, stage, k, 1], device)

    def each_y(self, t, run):
        if KINDS[t] != "half":
            run(self.place.y)
            return
        for value in (0, 1):
            pl.when(self.place.y == value)(lambda value=value: run(value))

    STAGE = [
        pltpu.VMEM((2, PART, WIDTH), jnp.bfloat16),
        pltpu.VMEM((PART, 4 * WIDTH), jnp.bfloat16),
        pltpu.VMEM((PART, 4 * WIDTH), jnp.bfloat16),
        pltpu.VMEM((4, PART, WIDTH), jnp.bfloat16),
    ]

    def locals(self, t):
        if t == 1:
            return [
                (self.joint_in, self.stage[1].at[:, pl.ds(0, 3 * WIDTH)]),
                (self.out_in, self.stage[1].at[:, pl.ds(3 * WIDTH, WIDTH)]),
            ]
        return [({0: self.skip_in, 2: self.up_in, 3: self.down_in}[t], self.stage[t])]

    def own_start(self, t):
        for i, (src, dst) in enumerate(self.locals(t)):
            pltpu.make_async_copy(src, dst, self.local_sems.at[2 * t + i]).start()

    def own_keep(self, t):
        return pltpu.make_async_copy(self.stage[t], block(t, self.outs[t], self.place.b), self.local_sems.at[8 + t])

    def own_done(self, t):
        for i, (src, dst) in enumerate(self.locals(t)):
            pltpu.make_async_copy(src, dst, self.local_sems.at[2 * t + i]).wait()
        self.own_keep(t).start()

    def own_copy(self, t, c):
        ref = block(t, self.outs[t], 2 * self.place.zz + c)
        src = self.stage[t]
        sems = self.sems.at[t, 4, 0]
        return remote(src, ref, sems.at[0], sems.at[1], self.place.at(c=1 - self.place.c))

    def small_copy(self, i, src, dst, device):
        return remote(src, dst, self.small_sems.at[0, i], self.small_sems.at[1, i], device)

    def small_start(self):
        p = self.place
        for i, device in enumerate([p.at(zz=p.other(k)) for k in (1, 2, 3)] + [p.at(c=1 - p.c)]):
            self.small_copy(i, self.small_in, self.small.at[p.b], device).start()

    def small_pass(self):
        p = self.place
        for i, k in enumerate((1, 2, 3)):
            ref = self.small.at[2 * p.other(k) + p.c]
            self.small_copy(i, ref, ref, p.at()).wait_recv()
            self.small_copy(4 + i, ref, ref, p.at(c=1 - p.c)).start()

    def small_done(self):
        p = self.place
        for i, k in enumerate((0, 1, 2, 3)):
            ref = self.small.at[2 * p.other(k) + 1 - p.c]
            self.small_copy(3 + i, ref, ref, p.at()).wait_recv()
        for i in range(7):
            self.small_copy(i, self.small_in, self.small_in, p.at()).wait_send()

    def stage_piece(self, t, y):
        x = self.place.x
        if t in (1, 2):
            return self.stage[t].at[:, pl.ds(pl.multiple_of((2 * y + x) * WIDTH, 128), WIDTH)]
        if t == 3:
            return self.stage[t].at[2 * y + x]
        low, size = (0, 80) if y == 0 else (80, 64)
        return self.stage[t].at[x, pl.ds(low, size)]

    def z_copies(self, t, y, zz, start, own=False):
        p = self.place
        for step, send in ((1, 0), (-1, 5)):
            go = (zz <= p.zz) & (p.zz < 3) if step == 1 else (zz >= p.zz) & (p.zz > 0)
            ref = piece(t, self.outs[t], 2 * zz + p.c, p.x, y)

            @pl.when(go)
            def _():
                copy = remote(self.stage_piece(t, y) if own else ref, ref, self.sems.at[t, send, zz, 0], self.sems.at[t, 0, zz, 1], p.at(zz=p.zz + step))
                copy.start() if start else copy.wait_send()

    def z_start(self, t):
        p = self.place
        self.each_y(t, lambda y: self.z_copies(t, y, p.zz, True, True))
        self.own_copy(t, p.c).start()

    def z_done(self, t, k):
        p = self.place
        zz = p.source(k)

        def run(y):
            self.copy(t, p.x, y, zz, p.c, 0, zz, p.at()).wait_recv()
            self.z_copies(t, y, zz, True)

        self.each_y(t, run)

    def xy_start(self, t, k):
        p = self.place
        zz = p.source(k)

        def run(y):
            self.copy(t, p.x, y, zz, p.c, 1, k, p.at(x=1 - p.x)).start()
            self.copy(t, p.x, y, zz, p.c, 2, k, p.at(y=1 - p.y)).start()

        self.each_y(t, run)

    def by_x(self, t, k):
        return k == 1 or (k == 2 and t % 2 == 0)

    def xy_done(self, t, k):
        p = self.place

        def run(y):
            zz = p.source(k)
            self.copy(t, 1 - p.x, y, zz, p.c, 1, k, p.at()).wait_recv()
            if self.by_x(t, k):
                self.copy(t, 1 - p.x, y, zz, p.c, 3, k, p.at(y=1 - p.y)).start()
            self.copy(t, p.x, 1 - y, zz, p.c, 2, k, p.at()).wait_recv()
            if not self.by_x(t, k):
                self.copy(t, p.x, 1 - y, zz, p.c, 3, k, p.at(x=1 - p.x)).start()

        self.each_y(t, run)

    def diag_done(self, t, k):
        p = self.place

        def run(y):
            zz = p.source(k)
            self.copy(t, 1 - p.x, 1 - y, zz, p.c, 3, k, p.at()).wait_recv()

        self.each_y(t, run)
        self.pair_copy(t, k, p.c).start()

    def pair_copy(self, t, k, c):
        ref = block(t, self.outs[t], 2 * self.place.source(k) + c)
        sems = self.sems.at[t, 4, k]
        return remote(ref, ref, sems.at[0], sems.at[1], self.place.at(c=1 - self.place.c))

    def ready(self, t):
        p = self.place
        self.own_keep(t).wait()
        self.own_copy(t, 1 - p.c).wait_recv()
        for k in (1, 2, 3):
            self.pair_copy(t, k, 1 - p.c).wait_recv()

    def all_sent(self, t):
        p = self.place
        self.own_copy(t, p.c).wait_send()

        def run(y):
            self.z_copies(t, y, p.zz, False, True)
            for k in (1, 2, 3):
                zz = p.source(k)
                self.z_copies(t, y, zz, False)
                self.copy(t, p.x, y, zz, p.c, 1, k, p.at()).wait_send()
                self.copy(t, p.x, y, zz, p.c, 2, k, p.at()).wait_send()
                if self.by_x(t, k):
                    self.copy(t, 1 - p.x, y, zz, p.c, 3, k, p.at()).wait_send()
                else:
                    self.copy(t, p.x, 1 - y, zz, p.c, 3, k, p.at()).wait_send()

        self.each_y(t, run)
        for k in (1, 2, 3):
            self.pair_copy(t, k, p.c).wait_send()


SIZES = (80, PART, PART, PART)


HALO = 320
COND = 32
TOK = 512
KEYS = HALO + TOK + COND
TILES = ((0, 0), (256, 256))
LOG2E = 1.4426950408889634


def nt(a, b):
    return lax.dot_general(a, b, (((1,), (1,)), ((), ())), preferred_element_type=jnp.float32)


def tn(a, b):
    return lax.dot_general(a, b, (((0,), (0,)), ((), ())), preferred_element_type=jnp.float32)


def nn(a, b):
    return jnp.dot(a, b, preferred_element_type=jnp.float32)


def make_bias(extra, blk, bias):
    row = lax.broadcasted_iota(jnp.int32, (TOK, 1), 0) + blk * TOK
    at = lax.broadcasted_iota(jnp.int32, (1, KEYS), 1)
    key = at + (blk * TOK - HALO)
    item_q, item_k = jnp.zeros_like(row), jnp.zeros_like(key)
    end = 0
    for n in range(extra.shape[1]):
        end = end + extra[0, n] + (LEN_MIN - 1)
        item_q += (row >= end).astype(jnp.int32)
        item_k += (key >= end).astype(jnp.int32)
    item_k = jnp.where(key >= 0, item_k, -1)
    item_k = jnp.where(at >= HALO + TOK, (at - (HALO + TOK)) >> 1, item_k)
    for low in range(0, TOK, 128):
        bias[low : low + 128] = jnp.where(item_q[low : low + 128] == item_k, 0.0, -1e30)


def head(h):
    return slice(HEAD * h, HEAD * (h + 1))


class Names:
    def __init__(self, names, refs):
        for name, ref in zip(names, refs, strict=True):
            setattr(self, name, ref)


def hbm(shape, dtype=jnp.bfloat16):
    return jax.ShapeDtypeStruct(shape, dtype)


GROUP = 4
IN_VMEM = pl.BlockSpec(memory_space=pltpu.VMEM)
IN_SMEM = pl.BlockSpec(memory_space=pltpu.SMEM)
FWD_IN = dict(
    rows=IN_VMEM, extra=IN_SMEM, cond=IN_VMEM, latents=ANY, skip_input=ANY, skip=ANY, joint=ANY, out=ANY, up=ANY, down=ANY,
)
FWD_OUT = dict(
    w_skip=hbm((16, PART, WIDTH)),
    w_joint=hbm((8, PART, 4 * WIDTH)),
    w_up=hbm((8, PART, 4 * WIDTH)),
    w_down=hbm((32, PART, WIDTH)),
    output=hbm((TOK, WIDTH)),
    hidden_t=hbm((8, 4, PART, TOK)),
    slope=hbm((TOK, 4 * WIDTH)),
    second_t=hbm((8, PART, TOK)),
    second_unit=hbm((TOK, WIDTH)),
    att_t=hbm((8, PART, TOK)),
    q=hbm((HEADS, TOK, HEAD)),
    k=hbm((HEADS, KEYS, HEAD)),
    v=hbm((HEADS, KEYS, HEAD)),
    o=hbm((HEADS, TOK, HEAD)),
    logsum=hbm((HEADS, TOK, 1), jnp.float32),
    first_t=hbm((8, PART, TOK)),
    first_unit=hbm((TOK, WIDTH)),
    joined_t=hbm((8, 2 * PART, TOK)),
)
FWD_VM = dict(
    cond_t=hbm((8, PART, 128)),
    second_rstd=hbm((TOK, 1), jnp.float32),
    first_rstd=hbm((TOK, 1), jnp.float32),
    vectors=hbm((16, WIDTH), jnp.float32),
    cond_unit=hbm((COND, WIDTH), jnp.float32),
    cond_rstd=hbm((COND, 1), jnp.float32),
)
FWD_SCRATCH = dict(
    lat=pltpu.VMEM((TOK, WIDTH), jnp.bfloat16),
    ski=pltpu.VMEM((TOK, WIDTH), jnp.bfloat16),
    weight=pltpu.VMEM((2, 8, PART, WIDTH), jnp.bfloat16),
    base=pltpu.VMEM((TOK, WIDTH), jnp.float32),
    acc=pltpu.VMEM((TOK, WIDTH), jnp.float32),
    unit=pltpu.VMEM((TOK, WIDTH), jnp.bfloat16),
    normed=pltpu.VMEM((TOK, WIDTH), jnp.bfloat16),
    pairs=pltpu.VMEM((2, TOK, WIDTH), jnp.bfloat16),
    halo=pltpu.VMEM((2, HALO, WIDTH), jnp.bfloat16),
    cond_in=pltpu.VMEM((COND, WIDTH), jnp.bfloat16),
    qh=pltpu.VMEM((HEADS, TOK, HEAD), jnp.bfloat16),
    kh=pltpu.VMEM((HEADS, KEYS, HEAD), jnp.bfloat16),
    vh=pltpu.VMEM((HEADS, KEYS, HEAD), jnp.bfloat16),
    oh=pltpu.VMEM((HEADS, TOK, HEAD), jnp.bfloat16),
    lh=pltpu.VMEM((GROUP, TOK, 1), jnp.float32),
    bias=pltpu.VMEM((TOK, KEYS), jnp.float32),
    hidden=pltpu.VMEM((4, TOK, WIDTH), jnp.bfloat16),
    turned=pltpu.VMEM((2, WIDTH, TOK), jnp.bfloat16),
    tile=pltpu.VMEM((2, TOK, WIDTH), jnp.bfloat16),
    pack=pltpu.VMEM(SMALL, jnp.float32),
    packs=pltpu.VMEM((8, *SMALL), jnp.float32),
    ups=pltpu.VMEM((4, 1, WIDTH), jnp.float32),
    w_sems=pltpu.SemaphoreType.DMA((2,)),
    t_sems=pltpu.SemaphoreType.DMA((24,)),
    halo_sems=pltpu.SemaphoreType.DMA((2,)),
)
N_GATHER = len(Gather.SEMS) + len(Gather.STAGE)


def forward_kernel(*refs):
    cuts = [len(FWD_IN), len(FWD_OUT), len(FWD_VM), len(FWD_SCRATCH), N_GATHER]
    pieces, at = [], 0
    for cut in cuts:
        pieces.append(refs[at : at + cut])
        at += cut
    i, o, vm, b = (
        Names(names, part) for names, part in zip((FWD_IN, FWD_OUT, FWD_VM, FWD_SCRATCH), pieces)
    )
    f32, bf16 = jnp.float32, jnp.bfloat16
    p = Place()
    g = Gather(
        p, (b.pack, i.skip, i.joint, i.out, i.up, i.down), (b.packs, o.w_skip, o.w_joint, o.w_up, o.w_down), pieces[4]
    )

    def copy(src, dst, sem):
        return pltpu.make_async_copy(src, dst, sem)

    def stream(blocks, body):
        def load(n):
            return copy(blocks[n], b.weight.at[n % 2], b.w_sems.at[n % 2])

        load(0).start()
        for n in range(len(blocks)):
            if n + 1 < len(blocks):
                load(n + 1).start()
            load(n).wait()
            body(n, b.weight[n % 2].reshape(WIDTH, WIDTH))

    def column(ref, q):
        return ref.at[:, :, pl.ds(q * WIDTH, WIDTH)]

    def by_rows(size, body):
        @pl.loop(0, TOK // size)
        def _(n):
            body(pl.ds(pl.multiple_of(n * size, size), size))

    def vector(n):
        return vm.vectors[n : n + 1, :]

    kept = []

    def keep(src, dst, sem):
        one = (src, dst, b.t_sems.at[sem])
        copy(*one).start()
        kept.append(one)

    def flush():
        for one in kept:
            copy(*one).wait()
        kept.clear()

    def norm(values):
        center = values - jnp.mean(values, axis=1, keepdims=True)
        rstd = lax.rsqrt(jnp.mean(center * center, axis=1, keepdims=True) + 1e-05)
        return center * rstd, rstd

    def norm_tokens(gain, shift, rstd_out):
        @functools.partial(by_rows, 64)
        def _(rows):
            unit, rstd = norm(b.base[rows])
            b.unit[rows] = unit.astype(bf16)
            rstd_out[rows] = rstd
            b.normed[rows] = (unit * gain + shift).astype(bf16)

    def turn(slot, src, dst, sem):
        b.turned[slot] = src.T
        keep(b.turned.at[slot], dst, sem)

    loads = [(i.latents, b.lat, b.t_sems.at[0]), (i.skip_input, b.ski, b.t_sems.at[1])]
    for t in range(4):
        g.own_start(t)
    for one in loads:
        copy(*one).start()
    b.pack[...] = jnp.zeros(SMALL, f32)
    b.pack[0:11, 0:PART] = i.rows[...]
    b.packs[p.b] = b.pack[...]
    greet(p)
    g.small_start()
    g.own_done(0)
    g.z_start(0)
    make_bias(i.extra, p.b, b.bias)
    g.small_pass()
    for one in loads:
        copy(*one).wait()

    @pl.when(p.b == 0)
    def _():
        for n in range(HEADS):
            b.kh[n, 0:HALO] = jnp.zeros((HALO, HEAD), bf16)
            b.vh[n, 0:HALO] = jnp.zeros((HALO, HEAD), bf16)

    for k in (1, 2, 3):
        g.z_done(0, k)
        g.xy_start(0, k)
        if k == 2:
            g.own_done(1)
            g.z_start(1)
    g.small_done()
    for n in range(8):
        for row in range(7):
            vm.vectors[row : row + 1, n * PART : (n + 1) * PART] = b.packs[n, row : row + 1, 0:PART]
        for j in range(4):
            at = 4 * n + j
            low = at % 8 * PART
            b.ups[at // 8, :, low : low + PART] = b.packs[n, 7 + j : 8 + j, 0:PART]
    vm.vectors[7:16, :] = jnp.zeros((9, WIDTH), f32)
    for k in (1, 2, 3):
        g.xy_done(0, k)
    g.z_done(1, 1)
    g.xy_start(1, 1)
    for k in (1, 2, 3):
        g.diag_done(0, k)
    g.ready(0)

    def do_base(n, weight):
        made = nn((b.lat, b.ski)[n][...], weight)
        if n == 0:
            b.base[...] = made + vector(0)
        else:
            b.base[...] += made
        g.z_done(1, 2 + n)
        g.xy_start(1, 2 + n)
        if n == 0:
            g.own_done(2)
            g.z_start(2)

    stream([o.w_skip.at[pl.ds(8 * n, 8)] for n in range(2)], do_base)
    norm_tokens(vector(1), vector(2), vm.first_rstd)
    g.z_done(2, 1)
    unit, rstd = norm(i.cond[...].astype(f32))
    vm.cond_unit[...] = unit
    vm.cond_rstd[...] = rstd
    cond_in = (unit * vector(1) + vector(2)).astype(bf16)
    b.cond_in[...] = cond_in
    keep(b.unit, o.first_unit, 2)
    for n in range(2):
        b.turned[n] = (b.lat, b.ski)[n][...].T
        made = b.turned.at[n].reshape(8, PART, TOK)
        for k in range(4):
            keep(made.at[pl.ds(2 * k, 2)].reshape(2 * PART, TOK), o.joined_t.at[4 * n + k], 3 + 4 * n + k)
        if n == 0:
            g.z_done(2, 2)
            g.own_done(3)
            g.z_start(3)
    turned = jnp.concatenate([cond_in.astype(f32)] * 2 + [jnp.zeros((128 - 2 * COND, WIDTH), f32)], 0).T
    vm.cond_t[...] = turned.astype(bf16).reshape(8, PART, 128)
    for k in (1, 2, 3):
        g.xy_done(1, k)
    g.xy_start(2, 1)
    g.z_done(2, 3)
    for k in (1, 2, 3):
        g.diag_done(1, k)
    g.xy_start(2, 2)
    g.xy_start(2, 3)
    g.z_done(3, 1)
    g.ready(1)

    def halo_copy(device):
        src = b.pairs.at[:, pl.ds(TOK - HALO, HALO)]
        return remote(src, b.halo, b.halo_sems.at[0], b.halo_sems.at[1], device)

    def do_triple(n, weight):
        made = nn(b.normed[...], weight).astype(bf16)
        if n < 2:
            b.pairs[n] = made
            few = nn(b.cond_in[...], weight).astype(bf16)
            for h in range(HEADS):
                (b.kh, b.vh)[n][h, HALO + TOK :] = few[:, head(h)]
        else:
            b.tile[0] = made
        if n == 1:
            pl.when(p.b < 7)(lambda: halo_copy((p.s, p.b + 1)).start())
            g.z_done(3, 2)

    stream([column(o.w_joint, n) for n in (1, 2, 0)], do_triple)
    for h in range(HEADS):
        b.qh[h] = b.tile[0, :, head(h)]
        b.kh[h, HALO : HALO + TOK] = b.pairs[0, :, head(h)]
        b.vh[h, HALO : HALO + TOK] = b.pairs[1, :, head(h)]
    g.z_done(3, 3)
    flush()
    turn(0, b.normed[...], o.first_t.reshape(WIDTH, TOK), 2)

    @pl.when(p.b > 0)
    def _():
        halo_copy((p.s, p.b)).wait_recv()
        for h in range(HEADS):
            b.kh[h, 0:HALO] = b.halo[0, :, head(h)]
            b.vh[h, 0:HALO] = b.halo[1, :, head(h)]

    keep(b.qh, o.q, 3)
    keep(b.kh, o.k, 4)
    keep(b.vh, o.v, 5)

    def group(start):
        @pl.loop(0, GROUP)
        def _(n):
            h = start + n
            for row, low in TILES:
                rows, keys = pl.ds(row, 256), pl.ds(low, KEYS - low)
                scores = nt(b.qh[h, rows], b.kh[h, keys]) * (HEAD**-0.5 * LOG2E) + b.bias[rows, keys]
                top = jnp.max(scores, axis=1, keepdims=True)
                expo = jnp.exp2(scores - top)
                total = jnp.sum(expo, axis=1, keepdims=True)
                mixed = nn(expo.astype(bf16), b.vh[h, keys])
                b.oh[h, rows] = (mixed / total).astype(bf16)
                b.lh[n, rows] = top + jnp.log2(total)

        done = copy(b.lh, o.logsum.at[pl.ds(start, GROUP)], b.t_sems.at[6])
        done.start()
        done.wait()

    for k in (1, 2, 3):
        g.xy_done(2, k)
    g.xy_start(3, 1)
    group(0)
    g.xy_start(3, 2)
    group(4)
    g.xy_start(3, 3)
    group(8)
    group(12)
    keep(b.oh, o.o, 7)
    for h in range(HEADS):
        b.tile[0, :, head(h)] = b.oh[h]

    def do_out(_, weight):
        b.base[...] += nn(b.tile[0], weight) + vector(3)

    stream([column(o.w_joint, 3)], do_out)
    norm_tokens(vector(4), vector(5), vm.second_rstd)
    flush()
    keep(b.unit, o.second_unit, 2)
    turn(0, b.tile[0], o.att_t.reshape(WIDTH, TOK), 3)
    turn(1, b.normed[...], o.second_t.reshape(WIDTH, TOK), 4)
    for k in (1, 2, 3):
        g.diag_done(2, k)
    for k in (1, 2, 3):
        g.xy_done(3, k)
    g.ready(2)

    flush()
    hidden_t = o.hidden_t.reshape(4, WIDTH, TOK)

    def wide_keep(q):
        slot = q % 2
        return [
            copy(b.turned.at[slot], hidden_t.at[q], b.t_sems.at[8 + slot]),
            copy(b.tile.at[slot], o.slope.at[:, pl.ds(q * WIDTH, WIDTH)], b.t_sems.at[10 + slot]),
        ]

    def do_up(q, weight):
        slot = q % 2
        b.acc[...] = nn(b.normed[...], weight)
        if q >= 2:
            for one in wide_keep(q - 2):
                one.wait()

        @functools.partial(by_rows, 32)
        def _(rows):
            before = b.acc[rows] + b.ups[q]
            inside = 0.5 + 0.5 * lax.erf(before * 2**-0.5)
            bell = jnp.exp2(before * before * (-0.5 * LOG2E)) * 0.3989422804014327
            b.hidden[q, rows] = (before * inside).astype(bf16)
            b.tile[slot, rows] = (inside + before * bell).astype(bf16)

        b.turned[slot] = b.hidden[q].T
        for one in wide_keep(q):
            one.start()
        if q == 1:
            for k in (1, 2, 3):
                g.diag_done(3, k)

    stream([column(o.w_up, q) for q in range(4)], do_up)
    g.ready(3)

    def do_down(q, weight):
        made = nn(b.hidden[q], weight)
        if q == 0:
            b.base[...] += made + vector(6)
        else:
            b.base[...] += made

    stream([o.w_down.at[pl.ds(8 * q, 8)] for q in range(4)], do_down)
    b.normed[...] = b.base[...].astype(bf16)
    keep(b.normed, o.output, 2)
    for q in (2, 3):
        for one in wide_keep(q):
            one.wait()
    flush()
    pl.when(p.b < 7)(lambda: halo_copy((p.s, p.b + 1)).wait_send())
    for t in range(4):
        g.all_sent(t)


def forward(arrays):
    vm = pl.BlockSpec(memory_space=pltpu.VMEM)
    outs = pl.pallas_call(
        forward_kernel,
        out_shape=[*FWD_OUT.values(), *FWD_VM.values()],
        in_specs=[*FWD_IN.values()],
        out_specs=[ANY] * len(FWD_OUT) + [vm] * len(FWD_VM),
        scratch_shapes=[*FWD_SCRATCH.values()] + Gather.SEMS + Gather.STAGE,
        compiler_params=pltpu.CompilerParams(collective_id=0, has_side_effects=True, vmem_limit_bytes=60 << 20),
    )(*[arrays[name] for name in FWD_IN])
    return dict(zip([*FWD_OUT, *FWD_VM], outs, strict=True))


ORDER = (0, 2, 1, 3)
UNIT = (PART, WIDTH)


def add_into(out, *ins):
    @pl.loop(0, out.shape[0] // 16)
    def _(i):
        rows = pl.ds(pl.multiple_of(i * 16, 16), 16)
        total = ins[0][rows].astype(jnp.float32)
        for ref in ins[1:]:
            total += ref[rows].astype(jnp.float32)
        out[rows] = total.astype(out.dtype)


class Sum:
    SEMS = [
        pltpu.SemaphoreType.DMA((4, 4, 2, 2)),
        pltpu.SemaphoreType.DMA((4, 4, 2)),
        pltpu.SemaphoreType.DMA((4, 4, 2)),
        pltpu.SemaphoreType.DMA((4, 4, 2)),
        pltpu.SemaphoreType.DMA((23,)),
    ]
    SLOTS = [pltpu.VMEM((23, *UNIT), jnp.bfloat16), pltpu.VMEM((4, *UNIT), jnp.bfloat16)]
    LANDS = [
        jax.ShapeDtypeStruct(lead + (size, WIDTH), jnp.bfloat16)
        for size in SIZES
        for lead in ((4, 2), (4,), (4,))
    ]
    PARTS = [
        jax.ShapeDtypeStruct((8, PART, WIDTH), jnp.bfloat16),
        jax.ShapeDtypeStruct((4, PART, 4 * WIDTH), jnp.bfloat16),
        jax.ShapeDtypeStruct((4, PART, 4 * WIDTH), jnp.bfloat16),
        jax.ShapeDtypeStruct((4, 4, PART, WIDTH), jnp.bfloat16),
    ]

    def __init__(self, place, parts, lands, outs, sems, slots):
        self.place, self.parts, self.outs = place, parts, outs
        self.sem1, self.sem2, self.sem3, self.sem4, self.load_sems = sems
        self.slots, self.fins = slots
        self.land1, self.land2, self.land3 = ([lands[3 * t + i] for t in range(4)] for i in range(3))

    def slot(self, t, i):
        return self.slots.at[i, pl.ds(0, SIZES[t])]

    def fin(self, t):
        return self.fins.at[t, pl.ds(0, SIZES[t])]

    def piece(self, t, zz, x, y):
        ref = self.parts[t]
        if t == 0:
            return ref.at[2 * zz + x, pl.ds(pl.multiple_of(64 * y, 16), 80)]
        if t == 3:
            return ref.at[zz, 2 * y + x]
        return ref.at[zz, :, pl.ds(pl.multiple_of((2 * y + x) * WIDTH, 128), WIDTH)]

    def half(self, t, zz, x, y, j):
        return self.piece(t, zz, x, j) if zz < 2 else self.piece(t, zz, j, y)

    def keep(self, zz):
        return self.place.y if zz < 2 else self.place.x

    def first(self, t, zz, j):
        p = self.place
        device = p.at(x=1 - p.x) if zz < 2 else p.at(y=1 - p.y)
        sems = self.sem1.at[t, zz, j]
        src = self.half(t, zz, 1 - p.x, 1 - p.y, j)
        return remote(src, self.land1[t].at[zz, j], sems.at[0], sems.at[1], device)

    def start(self, t, zzs=ORDER):
        for zz in zzs:
            for j in (0, 1):
                self.first(t, zz, j).start()

    def load(self, t, src, i):
        return pltpu.make_async_copy(src, self.slot(t, i), self.load_sems.at[i])

    def second(self, t, zz):
        p = self.place
        device = p.at(y=1 - p.y) if zz < 2 else p.at(x=1 - p.x)
        sems = self.sem2.at[t, zz]
        return remote(self.slot(t, 2 * zz), self.land2[t].at[zz], sems.at[0], sems.at[1], device)

    def pass_on(self, t, after=None):
        p = self.place
        if after is not None:
            for zz in ORDER:
                self.second(after, zz).wait_send()

        def own(zz):
            return self.load(t, self.half(t, zz, p.x, p.y, 1 - self.keep(zz)), 2 * zz)

        def landed(zz):
            return self.load(t, self.land1[t].at[zz, 1 - self.keep(zz)], 2 * zz + 1)

        for zz in ORDER:
            own(zz).start()
        for zz in ORDER:
            for j in (0, 1):
                self.first(t, zz, j).wait_recv()
            landed(zz).start()
        for zz in ORDER:
            own(zz).wait()
            landed(zz).wait()
            add_into(self.slot(t, 2 * zz), self.slot(t, 2 * zz), self.slot(t, 2 * zz + 1))
            self.second(t, zz).start()

    def third(self, t, zz, slot):
        p = self.place
        return remote(
            self.slot(t, 8 + 3 * zz), self.land3[t].at[slot], self.sem3.at[t, zz, 0], self.sem3.at[t, slot, 1],
            p.at(zz=zz),
        )

    def third_sent(self, t):
        for zz in range(4):
            pl.when(zz != self.place.zz)(lambda zz=zz: self.third(t, zz, self.place.zz).wait_send())

    def to_chip(self, t, after=None):
        p = self.place
        if after is not None:
            self.third_sent(after)

        def load(zz, n):
            keep = self.keep(zz)
            if n == 0:
                src = self.half(t, zz, p.x, p.y, keep)
            else:
                src = self.land1[t].at[zz, keep] if n == 1 else self.land2[t].at[zz]
            return self.load(t, src, 8 + 3 * zz + n)

        for zz in ORDER:
            load(zz, 0).start()
            load(zz, 1).start()
        for zz in ORDER:
            self.second(t, zz).wait_recv()
            load(zz, 2).start()
        for zz in ORDER:
            for n in range(3):
                load(zz, n).wait()
            base = 8 + 3 * zz
            mine = self.slot(t, base)
            add_into(mine, mine, self.slot(t, base + 1), self.slot(t, base + 2))

            @pl.when(zz != p.zz)
            def _():
                self.third(t, zz, p.zz).start()

            @pl.when(zz == p.zz)
            def _():
                add_into(self.fin(t), mine)

    def result(self, t, x, y):
        ref = self.outs[t]
        if KINDS[t] == "cols":
            return ref.at[:, pl.ds(pl.multiple_of((2 * y + x) * WIDTH, 128), WIDTH)]
        if KINDS[t] == "rows":
            return ref.at[pl.ds(pl.multiple_of((2 * y + x) * PART, 16), PART)]
        low, size = (0, 80) if y == 0 else (80, 64)
        return ref.at[pl.ds(pl.multiple_of(x * PART + low, 16), size)]

    def fin_part(self, t, y):
        if KINDS[t] != "half" or y == 0:
            return self.fin(t)
        return self.fins.at[t, pl.ds(16, 64)]

    def each_y(self, t, run):
        if KINDS[t] != "half":
            run(self.place.y)
            return
        for value in (0, 1):
            pl.when(self.place.y == value)(lambda value=value: run(value))

    def share(self, t, y, k):
        p = self.place
        sems = self.sem4.at[t, k]
        if k == 1:
            src, dst, device = self.fin_part(t, y), self.result(t, p.x, y), p.at(x=1 - p.x)
        elif k == 2:
            src, dst, device = self.fin_part(t, y), self.result(t, p.x, y), p.at(y=1 - p.y)
        elif t % 2 == 0:
            src = dst = self.result(t, 1 - p.x, y)
            device = p.at(y=1 - p.y)
        else:
            src = dst = self.result(t, p.x, 1 - y)
            device = p.at(x=1 - p.x)
        return remote(src, dst, sems.at[0], sems.at[1], device)

    def arrived(self, t, y, k):
        p = self.place
        ref = self.result(t, 1 - p.x if k & 1 else p.x, 1 - y if k & 2 else y)
        sems = self.sem4.at[t, k]
        return remote(ref, ref, sems.at[0], sems.at[1], p.at())

    def spread(self, t):
        def run(y):
            for k in (1, 2):
                self.share(t, y, k).start()
            pltpu.make_async_copy(self.fin_part(t, y), self.result(t, self.place.x, y), self.sem4.at[t, 0, 0]).start()

        self.each_y(t, run)

    def spread_on(self, t):
        def run(y):
            self.arrived(t, y, 1 if t % 2 == 0 else 2).wait_recv()
            self.share(t, y, 3).start()

        self.each_y(t, run)

    def finish(self, t):
        p = self.place
        for k in (1, 2, 3):
            ref = self.land3[t].at[p.other(k)]
            remote(ref, ref, self.sem3.at[t, p.zz, 0], self.sem3.at[t, p.other(k), 1], p.at()).wait_recv()
            self.load(t, ref, 19 + k).start()
        for k in (1, 2, 3):
            self.load(t, self.land3[t].at[p.other(k)], 19 + k).wait()
        add_into(self.fin(t), self.fin(t), *[self.slot(t, 19 + k) for k in (1, 2, 3)])
        self.spread(t)

    def done(self, t, last):
        p = self.place
        for zz in range(4):
            for j in (0, 1):
                self.first(t, zz, j).wait_send()
            if last:
                self.second(t, zz).wait_send()
        if last:
            self.third_sent(t)

        def run(y):
            self.arrived(t, y, 2 if t % 2 == 0 else 1).wait_recv()
            self.arrived(t, y, 3).wait_recv()
            for k in (1, 2, 3):
                self.share(t, y, k).wait_send()
            pltpu.make_async_copy(self.fin_part(t, y), self.result(t, self.place.x, y), self.sem4.at[t, 0, 0]).wait()

        self.each_y(t, run)


class Vectors:
    SCRATCH = [
        pltpu.VMEM((8, *SMALL), jnp.float32),
        pltpu.VMEM((4, *SMALL), jnp.float32),
        pltpu.VMEM((4, *SMALL), jnp.float32),
        pltpu.VMEM((4, *SMALL), jnp.float32),
        pltpu.VMEM((4, *SMALL), jnp.float32),
        pltpu.VMEM((4, *SMALL), jnp.float32),
        pltpu.VMEM((COND, WIDTH), jnp.float32),
        pltpu.VMEM((COND, WIDTH), jnp.float32),
        pltpu.VMEM((COND, WIDTH), jnp.float32),
        pltpu.VMEM((4, COND, WIDTH), jnp.float32),
        pltpu.SemaphoreType.DMA((16, 2)),
    ]

    def __init__(self, place, small_out, cond_out, scratch):
        self.place, self.small_out, self.cond_out = place, small_out, cond_out
        self.part, self.pair, self.x_in, self.sum1, self.y_in, self.z_in = scratch[:6]
        self.mine, self.cond_pair, self.cond_sum, self.cond_in = scratch[6:10]
        self.sems = scratch[10]

    def copy(self, i, src, dst, device):
        return remote(src, dst, self.sems.at[i, 0], self.sems.at[i, 1], device)

    def small_pair(self, zz):
        p = self.place
        return self.copy(zz, self.part.at[2 * zz + 1 - p.c], self.pair.at[zz], p.at(c=1 - p.c))

    def pair_start(self):
        for zz in range(4):
            self.small_pair(zz).start()
        self.cond_pair_copy().start()

    def cond_pair_copy(self):
        return self.copy(4, self.mine, self.cond_pair, self.place.at(c=1 - self.place.c))

    def pair_end(self):
        p = self.place
        for zz in range(4):
            self.small_pair(zz).wait()
            self.pair[zz] += self.part[2 * zz + p.c]
        self.cond_pair_copy().wait()
        self.cond_sum[...] = self.mine[...] + self.cond_pair[...]
        self.copy(5, self.pair, self.x_in, p.at(x=1 - p.x)).start()
        for k in (1, 2, 3):
            self.copy(6 + k, self.cond_sum, self.cond_in.at[p.zz], p.at(zz=p.other(k))).start()
        self.cond_in[p.zz] = self.cond_sum[...]

    def run_x(self):
        p = self.place
        self.copy(5, self.pair, self.x_in, p.at(x=1 - p.x)).wait()
        self.sum1[...] = self.pair[...] + self.x_in[...]
        self.copy(6, self.sum1, self.y_in, p.at(y=1 - p.y)).start()

    def run_y(self):
        p = self.place
        self.copy(6, self.sum1, self.y_in, p.at(y=1 - p.y)).wait()
        self.sum1[...] += self.y_in[...]
        for k in (1, 2, 3):
            self.copy(9 + k, self.sum1.at[p.other(k)], self.z_in.at[p.zz], p.at(zz=p.other(k))).start()
        self.z_in[p.zz] = self.sum1[p.zz]

    def run_z(self):
        p = self.place
        for k in (1, 2, 3):
            self.copy(9 + k, self.sum1.at[p.other(k)], self.z_in.at[p.zz], p.at(zz=p.other(k))).wait()
            self.copy(6 + k, self.cond_sum, self.cond_in.at[p.zz], p.at(zz=p.other(k))).wait()
        self.small_out[...] = (self.z_in[0] + self.z_in[1]) + (self.z_in[2] + self.z_in[3])
        cond = (self.cond_in[0] + self.cond_in[1]) + (self.cond_in[2] + self.cond_in[3])
        self.cond_out[...] = cond.astype(jnp.bfloat16)


BACK_IN = dict(
    hidden_t=ANY, slope=ANY, cot=ANY, second_t=ANY, second_unit=ANY, att_t=ANY, q=ANY, k=ANY, v=ANY, o=ANY, logsum=ANY,
    first_t=ANY, first_unit=ANY, joined_t=ANY, w_skip=ANY, w_joint=ANY, w_up=ANY, w_down=ANY, cond_t=ANY,
    second_rstd=IN_VMEM, first_rstd=IN_VMEM, vectors=IN_VMEM, cond_unit=IN_VMEM, cond_rstd=IN_VMEM, extra=IN_SMEM,
)
BACK_OUT = dict(
    d_latents=hbm((TOK, WIDTH)),
    d_skip=hbm((TOK, WIDTH)),
    g_skip=hbm((2 * PART, WIDTH)),
    g_joint=hbm((PART, 4 * WIDTH)),
    g_up=hbm((PART, 4 * WIDTH)),
    g_down=hbm((4 * PART, WIDTH)),
    hidden_t2=hbm((4, 4, PART, TOK)),
    second_t2=hbm((4, PART, TOK)),
    att_t2=hbm((4, PART, TOK)),
    first_t2=hbm((4, PART, TOK)),
    joined_t2=hbm((4, 2 * PART, TOK)),
)
BACK_SCRATCH = dict(
    cot_v=pltpu.VMEM((TOK, WIDTH), jnp.bfloat16),
    cot2=pltpu.VMEM((TOK, WIDTH), jnp.bfloat16),
    wide=pltpu.VMEM((4, TOK, WIDTH), jnp.bfloat16),
    before2=pltpu.VMEM((4, TOK, WIDTH), jnp.bfloat16),
    triple2=pltpu.VMEM((3, TOK, WIDTH), jnp.bfloat16),
    branch=pltpu.VMEM((TOK, WIDTH), jnp.bfloat16),
    branch2=pltpu.VMEM((TOK, WIDTH), jnp.bfloat16),
    base_g=pltpu.VMEM((TOK, WIDTH), jnp.bfloat16),
    base2=pltpu.VMEM((TOK, WIDTH), jnp.bfloat16),
    acc=pltpu.VMEM((TOK, WIDTH), jnp.float32),
    d_middle=pltpu.VMEM((TOK, WIDTH), jnp.float32),
    tile=pltpu.VMEM((TOK, WIDTH), jnp.bfloat16),
    weight=pltpu.VMEM((2, 8, PART, WIDTH), jnp.bfloat16),
    left=pltpu.VMEM((2, 2, 4, PART, TOK), jnp.bfloat16),
    made=pltpu.VMEM((2, 4, PART, WIDTH), jnp.bfloat16),
    heads_g=pltpu.VMEM((HEADS, TOK, HEAD), jnp.bfloat16),
    qh=pltpu.VMEM((GROUP, TOK, HEAD), jnp.bfloat16),
    oh=pltpu.VMEM((GROUP, TOK, HEAD), jnp.bfloat16),
    kh=pltpu.VMEM((GROUP, HALO + TOK + COND, HEAD), jnp.bfloat16),
    vh=pltpu.VMEM((GROUP, HALO + TOK + COND, HEAD), jnp.bfloat16),
    lh=pltpu.VMEM((GROUP, TOK, 1), jnp.float32),
    sum_k=pltpu.VMEM((HALO + TOK + COND, HEAD), jnp.float32),
    sum_v=pltpu.VMEM((HALO + TOK + COND, HEAD), jnp.float32),
    bias=pltpu.VMEM((TOK, HALO + TOK + COND), jnp.float32),
    halo2=pltpu.VMEM((2, HALO, WIDTH), jnp.bfloat16),
    d_cond=pltpu.VMEM((128, 2 * WIDTH), jnp.bfloat16),
    cond_left=pltpu.VMEM((4, PART, 128), jnp.bfloat16),
    sums=pltpu.VMEM((16, WIDTH), jnp.float32),
    wide_sum=pltpu.VMEM((1, WIDTH), jnp.float32),
    w_sems=pltpu.SemaphoreType.DMA((2,)),
    l_sems=pltpu.SemaphoreType.DMA((2, 8)),
    m_sems=pltpu.SemaphoreType.DMA((2,)),
    t_sems=pltpu.SemaphoreType.DMA((8,)),
    sib_sems=pltpu.SemaphoreType.DMA((32, 2)),
)
SUM_SKIP, SUM_GAIN1, SUM_SHIFT1, SUM_OUT, SUM_GAIN2, SUM_SHIFT2, SUM_DOWN, SUM_UP = range(8)


def back_kernel(*refs):
    cuts = [len(BACK_IN), len(BACK_OUT), 2, len(Sum.PARTS), len(Sum.LANDS), len(BACK_SCRATCH), len(Sum.SEMS), 2]
    pieces, at = [], 0
    for cut in cuts:
        pieces.append(refs[at : at + cut])
        at += cut
    i, o, b = Names(BACK_IN, pieces[0]), Names(BACK_OUT, pieces[1]), Names(BACK_SCRATCH, pieces[5])
    p = Place()
    total = Sum(p, pieces[3], pieces[4], (o.g_skip, o.g_joint, o.g_up, o.g_down), pieces[6], pieces[7])
    vectors = Vectors(p, *pieces[2], refs[at:])
    f32, bf16 = jnp.float32, jnp.bfloat16

    def copy(src, dst, sem):
        return pltpu.make_async_copy(src, dst, sem)

    def sib(n, src, dst):
        return remote(src, dst, b.sib_sems.at[n, 0], b.sib_sems.at[n, 1], p.at(c=1 - p.c))

    def halves(n, src, dst):
        return [sib(4 * n + zz, src.at[2 * zz + 1 - p.c], dst.at[zz]) for zz in range(4)]

    left_pairs = (
        (i.hidden_t, o.hidden_t2), (i.second_t, o.second_t2), (i.att_t, o.att_t2), (i.first_t, o.first_t2),
        (i.joined_t, o.joined_t2),
    )

    def column(ref, q):
        return ref.at[:, :, pl.ds(q * WIDTH, WIDTH)]

    blocks = [i.w_down.at[pl.ds(8 * q, 8)] for q in range(4)]
    blocks += [column(i.w_up, q) for q in range(4)]
    blocks += [column(i.w_joint, q) for q in (3, 0, 1, 2)]
    blocks += [i.w_skip.at[pl.ds(8 * n, 8)] for n in range(2)]

    def load_weight(n):
        return copy(blocks[n], b.weight.at[n % 2], b.w_sems.at[n % 2])

    def stream(start, count, body):
        for n in range(start, start + count):
            if n + 1 < len(blocks):
                load_weight(n + 1).start()
            load_weight(n).wait()
            body(n - start, b.weight[n % 2].reshape(WIDTH, WIDTH))

    def by_rows(size, body):
        @pl.loop(0, TOK // size)
        def _(n):
            body(pl.ds(pl.multiple_of(n * size, size), size))

    def add_sum(row, value):
        b.sums[row : row + 1, :] += value

    def colsum(value):
        return jnp.sum(value, axis=0, keepdims=True)

    def form(n, dst, own, own2, pairs, extra=None):
        result = nn(own.reshape(4 * PART, TOK), pairs[0]) + nn(own2.reshape(4 * PART, TOK), pairs[1])
        if extra is not None:
            result += extra
        slot = n % 2
        b.made[slot] = result.astype(bf16).reshape(4, PART, WIDTH)
        copy(b.made.at[slot], dst, b.m_sems.at[slot]).start()

    def formed(n, dst):
        copy(b.made.at[n % 2], dst, b.m_sems.at[n % 2]).wait()

    def send_all(copies):
        for one in copies:
            one.start()

    def recv_all(copies):
        for one in copies:
            one.wait_recv()

    def left_copies(n):
        own, other = b.left.at[n % 2, 0], b.left.at[n % 2, 1]
        sems = b.l_sems.at[n % 2]
        if n < 4:
            zz = ORDER[n]
            pairs = [(i.hidden_t.at[2 * zz + p.c], own), (o.hidden_t2.at[zz], other)]
        elif n < 7:
            src, src2 = left_pairs[n - 3]
            pairs = [(src.at[2 * zz + p.c], own.at[zz]) for zz in range(4)] + [(src2, other)]
        else:
            pairs = []
            for k in range(4):
                zz, rows = 2 * (n - 7) + k // 2, pl.ds((k % 2) * PART, PART)
                pairs.append((i.joined_t.at[2 * zz + p.c, rows], own.at[k]))
                pairs.append((o.joined_t2.at[zz, rows], other.at[k]))
        return [copy(src, dst, sems.at[m]) for m, (src, dst) in enumerate(pairs)]

    def left_start(n):
        if n < 4:
            left_sends[0][ORDER[n]].wait_recv()
        elif n < 7:
            recv_all(left_sends[n - 3])
        else:
            recv_all(left_sends[4][2 * (n - 7) : 2 * (n - 7) + 2])
        send_all(left_copies(n))

    def left_done(n):
        for one in left_copies(n):
            one.wait()
        return b.left[n % 2, 0], b.left[n % 2, 1]

    cot_load = copy(i.cot, b.cot_v, b.t_sems.at[0])
    cot_load.start()
    load_weight(0).start()
    greet(p)
    sib_cot = sib(20, i.cot, b.cot2)
    left_sends = [halves(n, src, dst) for n, (src, dst) in enumerate(left_pairs)]
    send_all([left_sends[0][zz] for zz in ORDER])
    sib_cot.start()
    b.sums[...] = jnp.zeros_like(b.sums)
    b.d_cond[2 * COND :] = jnp.zeros((128 - 2 * COND, 2 * WIDTH), bf16)
    vectors.part[...] = jnp.zeros_like(vectors.part)
    make_bias(i.extra, p.b, b.bias)
    cot_load.wait()

    def before_sib(q):
        return sib(21 + q, b.wide.at[q], b.before2.at[q])

    def slope_load(q):
        return copy(i.slope.at[:, pl.ds(q * WIDTH, WIDTH)], b.tile, b.t_sems.at[1])

    def do_before(q, weight):
        slope_load(q).start()
        b.acc[...] = nt(b.cot_v[...], weight)
        slope_load(q).wait()
        b.wide_sum[...] = jnp.zeros_like(b.wide_sum)

        @functools.partial(by_rows, 64)
        def _(rows):
            value = (b.acc[rows] * b.tile[rows].astype(f32)).astype(bf16)
            b.wide[q, rows] = value
            b.wide_sum[...] += colsum(value.astype(f32))

        for n in range(8):
            row = 7 + n % 4
            vectors.part[2 * q + n // 4, row : row + 1, 0:PART] = b.wide_sum[:, n * PART : (n + 1) * PART]
        before_sib(q).start()

    stream(0, 4, do_before)

    for n in (1, 2, 3, 4):
        send_all(left_sends[n])

    sib_cot.wait_recv()
    down_parts = pieces[3][3]
    left_start(0)
    for n, zz in enumerate(ORDER):
        left_start(n + 1)
        form(n, down_parts.at[zz], *left_done(n), (b.cot_v[...], b.cot2[...]))
        if n > 0:
            formed(n - 1, down_parts.at[ORDER[n - 1]])
            total.start(3, (ORDER[n - 1],))

    up_parts = pieces[3][2]
    lefts = left_done(4)
    for q in range(4):
        before_sib(q).wait_recv()
        form(q, column(up_parts, q), *lefts, (b.wide[q], b.before2[q]))
        if q == 0:
            formed(3, down_parts.at[ORDER[3]])
            total.start(3, (ORDER[3],))
        else:
            formed(q - 1, column(up_parts, q - 1))
    left_start(5)

    def do_second(q, weight):
        value = nt(b.wide[q], weight)
        if q == 0:
            b.acc[...] = value
        else:
            b.acc[...] += value

    unit_load = copy(i.second_unit, b.tile, b.t_sems.at[1])
    unit_load.start()
    stream(4, 4, do_second)
    unit_load.wait()
    formed(3, column(up_parts, 3))

    def norm_rows(unit, rstd, gain, grad, gain_row, shift_row):
        scaled = grad * gain
        mean1 = jnp.mean(scaled, axis=1, keepdims=True)
        mean2 = jnp.mean(scaled * unit, axis=1, keepdims=True)
        add_sum(gain_row, colsum(grad * unit))
        add_sum(shift_row, colsum(grad))
        return rstd * (scaled - mean1 - unit * mean2)

    @functools.partial(by_rows, 64)
    def _(rows):
        unit = b.tile[rows].astype(f32)
        back = norm_rows(unit, i.second_rstd[rows], i.vectors[4:5], b.acc[rows], SUM_GAIN2, SUM_SHIFT2)
        g = b.cot_v[rows].astype(f32)
        middle = g + back
        b.d_middle[rows] = middle
        low = middle.astype(bf16)
        b.branch[rows] = low
        add_sum(SUM_OUT, colsum(low.astype(f32)))
        add_sum(SUM_DOWN, colsum(g))

    branch_sib = sib(25, b.branch, b.branch2)
    branch_sib.start()

    def do_attended(_, weight):
        b.tile[...] = nt(b.branch[...], weight).astype(bf16)
        for h in range(HEADS):
            b.heads_g[h] = b.tile[:, head(h)]

    stream(8, 1, do_attended)

    joint_parts = pieces[3][1]
    lefts = left_done(5)
    left_start(6)
    branch_sib.wait_recv()
    form(0, column(joint_parts, 3), *lefts, (b.branch[...], b.branch2[...]))

    total.pass_on(3)
    total.start(2)
    formed(0, column(joint_parts, 3))
    for q in range(4):
        before_sib(q).wait_send()

    scale = HEAD**-0.5
    n_keys = HALO + TOK + COND

    def group_loads(start):
        hs = pl.ds(start, GROUP)
        pairs = ((i.q, b.qh), (i.o, b.oh), (i.k, b.kh), (i.v, b.vh), (i.logsum, b.lh))
        return [copy(src.at[hs], dst, b.t_sems.at[n]) for n, (src, dst) in enumerate(pairs)]

    def group(start):
        send_all(group_loads(start))
        for one in group_loads(start):
            one.wait()

        @pl.loop(0, GROUP)
        def _(h):
            for row, low in TILES:
                rows, keys = pl.ds(row, 256), pl.ds(low, n_keys - low)
                q, k, v, g = b.qh[h, rows], b.kh[h, keys], b.vh[h, keys], b.heads_g[start + h, rows]
                scores = nt(q, k) * (scale * LOG2E) + b.bias[rows, keys]
                probs = jnp.exp2(scores - b.lh[h, rows])
                d_probs = nt(g, v)
                inner = jnp.sum(g.astype(f32) * b.oh[h, rows].astype(f32), axis=1, keepdims=True)
                d_scores = (probs * (d_probs - inner)).astype(bf16)
                d_k, d_v = tn(d_scores, q), tn(probs.astype(bf16), g)
                if row == 0:
                    b.sum_k[...] = d_k
                    b.sum_v[...] = d_v
                else:
                    b.sum_k[keys] += d_k
                    b.sum_v[keys] += d_v
                b.oh[h, rows] = (nn(d_scores, k) * scale).astype(bf16)
            b.kh[h] = (b.sum_k[...] * scale).astype(bf16)
            b.vh[h] = b.sum_v[...].astype(bf16)

        for n in range(GROUP):
            at = head(start + n)
            b.wide[0, :, at] = b.oh[n]
            for j, made in ((0, b.kh), (1, b.vh)):
                wide = slice(j * WIDTH + at.start, j * WIDTH + at.stop)
                b.before2[j, 0:HALO, at] = made[n, 0:HALO]
                b.wide[1 + j, :, at] = made[n, HALO : HALO + TOK]
                b.d_cond[0:COND, wide] = made[n, HALO + TOK :]

    group(0)
    group(4)
    total.to_chip(3)
    group(8)
    group(12)

    def halo_copy(device):
        src = b.before2.at[pl.ds(0, 2), pl.ds(0, HALO)]
        return remote(src, b.halo2, b.sib_sems.at[31, 0], b.sib_sems.at[31, 1], device)

    cond_sib = sib(30, b.d_cond.at[pl.ds(0, COND)], b.d_cond.at[pl.ds(COND, COND)])
    cond_sib.start()
    pl.when(p.b > 0)(lambda: halo_copy((p.s, p.b - 1)).start())

    def triple_sib(j):
        return sib(26 + j, b.wide.at[j], b.triple2.at[j])

    triple_sib(0).start()
    for zz in range(4):
        copy(i.cond_t.at[2 * zz + p.c], b.cond_left.at[zz], b.t_sems.at[4 + zz]).start()
    unit_load = copy(i.first_unit, b.tile, b.t_sems.at[1])
    unit_load.start()

    def do_first(j, weight):
        if j == 1:
            merge_halo()
        value = nt(b.wide[j], weight)
        if j == 0:
            b.acc[...] = value
        else:
            b.acc[...] += value
            cond = nt(b.d_cond[0:COND, (j - 1) * WIDTH : j * WIDTH], weight)
            if j == 1:
                vectors.mine[...] = cond
            else:
                vectors.mine[...] += cond

    def merge_halo():
        @pl.when(p.b < 7)
        def _():
            halo_copy((p.s, p.b)).wait_recv()

            @pl.loop(0, HALO // 64)
            def _(n):
                low = pl.ds(pl.multiple_of(n * 64, 64), 64)
                rows = pl.ds(pl.multiple_of(n * 64 + TOK - HALO, 64), 64)
                for j in (0, 1):
                    extra = b.halo2[j, low].astype(f32)
                    b.wide[1 + j, rows] = (b.wide[1 + j, rows].astype(f32) + extra).astype(bf16)

        triple_sib(1).start()
        triple_sib(2).start()

    stream(9, 3, do_first)
    unit_load.wait()
    total.pass_on(2, after=3)

    @functools.partial(by_rows, 64)
    def _(rows):
        unit = b.tile[rows].astype(f32)
        back = norm_rows(unit, i.first_rstd[rows], i.vectors[1:2], b.acc[rows], SUM_GAIN1, SUM_SHIFT1)
        low = (b.d_middle[rows] + back).astype(bf16)
        b.base_g[rows] = low
        add_sum(SUM_SKIP, colsum(low.astype(f32)))

    base_sib = sib(29, b.base_g, b.base2)
    base_sib.start()
    for zz in range(4):
        copy(i.cond_t.at[2 * zz + p.c], b.cond_left.at[zz], b.t_sems.at[4 + zz]).wait()
    cond_sib.wait_recv()

    lefts = left_done(6)
    left_start(7)
    for j in range(3):
        triple_sib(j).wait_recv()
        extra = None
        if j > 0:
            extra = nn(b.cond_left[...].reshape(4 * PART, 128), b.d_cond[:, (j - 1) * WIDTH : j * WIDTH])
        form(j, column(joint_parts, j), *lefts, (b.wide[j], b.triple2[j]), extra)
        if j > 0:
            formed(j - 1, column(joint_parts, j - 1))
    formed(2, column(joint_parts, 2))
    total.start(1)
    vectors.mine[...] = norm_rows(
        i.cond_unit[...], i.cond_rstd[...], i.vectors[1:2], vectors.mine[...], SUM_GAIN1, SUM_SHIFT1
    )
    for row in range(7):
        for n in range(8):
            vectors.part[n, row : row + 1, 0:PART] = b.sums[row : row + 1, n * PART : (n + 1) * PART]
    vectors.pair_start()
    total.finish(3)

    skip_parts = pieces[3][0]
    base_sib.wait_recv()
    for n in (0, 1):
        lefts = left_done(7 + n)
        if n == 0:
            left_start(8)
        form(n, skip_parts.at[pl.ds(4 * n, 4)], *lefts, (b.base_g[...], b.base2[...]))
    vectors.pair_end()
    total.to_chip(2, after=3)
    for n in (0, 1):
        formed(n, skip_parts.at[pl.ds(4 * n, 4)])

    def do_joined(n, weight):
        made = (b.tile, b.branch)[n]
        made[...] = nt(b.base_g[...], weight).astype(bf16)
        copy(made, (o.d_latents, o.d_skip)[n], b.t_sems.at[n]).start()

    branch_sib.wait_send()
    stream(12, 2, do_joined)
    vectors.run_x()

    total.spread_on(3)
    total.pass_on(1, after=2)
    total.start(0)
    vectors.run_y()
    total.finish(2)
    total.to_chip(1, after=2)
    total.pass_on(0, after=1)
    total.spread_on(2)
    total.finish(1)
    total.to_chip(0, after=1)
    total.spread_on(1)
    total.finish(0)
    total.spread_on(0)
    vectors.run_z()
    for n in (0, 1):
        copy((b.tile, b.branch)[n], (o.d_latents, o.d_skip)[n], b.t_sems.at[n]).wait()
    for group_sends in left_sends:
        for one in group_sends:
            one.wait_send()
    for one in (sib_cot, cond_sib, base_sib, triple_sib(0), triple_sib(1), triple_sib(2)):
        one.wait_send()
    pl.when(p.b > 0)(lambda: halo_copy((p.s, p.b - 1)).wait_send())
    for t in (3, 2, 1, 0):
        total.done(t, t == 0)


def backward(arrays):
    vm = pl.BlockSpec(memory_space=pltpu.VMEM)
    outs = pl.pallas_call(
        back_kernel,
        out_shape=[*BACK_OUT.values()] + [
            jax.ShapeDtypeStruct(SMALL, jnp.float32), jax.ShapeDtypeStruct((COND, WIDTH), jnp.bfloat16)
        ] + Sum.PARTS + Sum.LANDS,
        in_specs=[*BACK_IN.values()],
        out_specs=[ANY] * len(BACK_OUT) + [vm] * 2 + [ANY] * (len(Sum.PARTS) + len(Sum.LANDS)),
        scratch_shapes=[*BACK_SCRATCH.values()] + Sum.SEMS + Sum.SLOTS + Vectors.SCRATCH,
        compiler_params=pltpu.CompilerParams(collective_id=1, has_side_effects=True, vmem_limit_bytes=60 << 20),
    )(*[arrays[name] for name in BACK_IN])
    named = Names(BACK_OUT, outs[: len(BACK_OUT)])
    return named, outs[len(BACK_OUT)], outs[len(BACK_OUT) + 1]


def item_ends(extra_length):
    lengths = extra_length[0] + (LEN_MIN - 1)
    count = lengths.shape[0]
    upto = lax.iota(jnp.int32, count)[None, :] <= lax.iota(jnp.int32, count)[:, None]
    return jnp.sum(jnp.where(upto, lengths[None, :], 0), axis=1)


def quick(
    latents, skip_input, cond_tokens, extra_length, skip_weight, skip_bias, first_gain, first_shift, joint_weight,
    out_weight, out_bias, second_gain, second_shift, up_weight, up_bias, down_weight, down_bias, cotangent,
):
    f32, bf16 = jnp.float32, jnp.bfloat16
    few = (skip_bias, first_gain, first_shift, out_bias, second_gain, second_shift, down_bias)
    rows = jnp.concatenate([jnp.stack(few), up_bias.reshape(4, PART)], 0).astype(f32)
    arrays = dict(
        rows=rows,
        extra=extra_length,
        cond=cond_tokens.reshape(COND, WIDTH),
        latents=latents,
        skip_input=skip_input,
        skip=skip_weight.reshape(2, PART, WIDTH),
        joint=joint_weight,
        out=out_weight,
        up=up_weight,
        down=down_weight.reshape(4, PART, WIDTH),
        cot=cotangent,
    )
    made = forward(arrays)
    grads, sums, cond_sum = backward({**arrays, **made})
    v = [sums[n, :PART] for n in range(7)]
    return (
        made["output"],
        grads.d_latents,
        grads.d_skip,
        cond_sum.reshape(cond_tokens.shape),
        grads.g_skip.astype(f32),
        v[0],
        v[1],
        v[2],
        grads.g_joint[:, : 3 * WIDTH].astype(f32),
        grads.g_joint[:, 3 * WIDTH :].astype(f32),
        v[3],
        v[4],
        v[5],
        grads.g_up.astype(f32),
        sums[7:11, :PART].reshape(-1),
        grads.g_down.astype(f32),
        v[6],
    )


def shifted(value, axis, steps):
    count = lax.axis_size(axis)
    leading, last = (max(0, -steps), min(count, count - steps))
    return lax.ppermute(value, axis, [(source, source + steps) for source in range(leading, last)])


def layer_norm(values, gain, shift):
    center = values - jnp.mean(values, axis=-1, keepdims=True)
    spread = jnp.mean(center * center, axis=-1, keepdims=True)
    return center * lax.rsqrt(spread + 1e-05) * gain + shift


def contract_rows(left, right):
    return lax.dot_general(
        left, right, (((0,), (0,)), ((), ())), preferred_element_type=jnp.float32
    )


def contract_cols(left, right):
    return lax.dot_general(
        left, right, (((1,), (1,)), ((), ())), preferred_element_type=jnp.float32
    )


def segment_ids(ends, places):
    inside = jnp.sum((ends[None, :] <= places[:, None]).astype(jnp.int32), axis=1)
    return jnp.where(places >= 0, inside, -1)


def split_heads(block):
    return block.reshape(block.shape[0], HEADS, HEAD).transpose(1, 0, 2)


def merge_heads(block):
    return block.transpose(1, 0, 2).reshape(block.shape[1], HEADS * HEAD)


def masked_scores(query, keys, allowed):
    scores = contract_cols(query, keys) * HEAD ** (-0.5)
    return jnp.where(allowed, scores, -1e30)


def plain(
    latents,
    skip_input,
    cond_tokens,
    extra_length,
    skip_weight,
    skip_bias,
    first_gain,
    first_shift,
    joint_weight,
    out_weight,
    out_bias,
    second_gain,
    second_shift,
    up_weight,
    up_bias,
    down_weight,
    down_bias,
    cotangent,
):
    whole = (
        lax.all_gather(skip_weight, "blk", axis=0, tiled=True),
        lax.all_gather(skip_bias, "blk", axis=0, tiled=True),
        lax.all_gather(first_gain, "blk", axis=0, tiled=True),
        lax.all_gather(first_shift, "blk", axis=0, tiled=True),
        lax.all_gather(joint_weight, "blk", axis=0, tiled=True),
        lax.all_gather(out_weight, "blk", axis=0, tiled=True),
        lax.all_gather(out_bias, "blk", axis=0, tiled=True),
        lax.all_gather(second_gain, "blk", axis=0, tiled=True),
        lax.all_gather(second_shift, "blk", axis=0, tiled=True),
        lax.all_gather(up_weight, "blk", axis=0, tiled=True),
        lax.all_gather(up_bias, "blk", axis=0, tiled=True),
        lax.all_gather(down_weight, "blk", axis=0, tiled=True),
        lax.all_gather(down_bias, "blk", axis=0, tiled=True),
    )
    (
        skip_matrix,
        skip_offset,
        gain_first,
        shift_first,
        joint_matrix,
        out_matrix,
        out_offset,
        gain_second,
        shift_second,
        up_matrix,
        up_offset,
        down_matrix,
        down_offset,
    ) = whole
    rows = latents.shape[0]
    width = latents.shape[1]
    scale = HEAD ** (-0.5)
    joined = jnp.concatenate([latents, skip_input], 1)
    base = jnp.dot(joined, skip_matrix, preferred_element_type=jnp.float32) + skip_offset
    first_in = layer_norm(base, gain_first, shift_first).astype(jnp.bfloat16)
    triple = jnp.dot(first_in, joint_matrix, preferred_element_type=jnp.float32).astype(
        jnp.bfloat16
    )
    query = triple[:, :width]
    pair_here = triple[:, width:]
    pair_left = shifted(pair_here, "blk", 1)
    cond_flat = cond_tokens.reshape(-1, width).astype(jnp.float32)
    cond_in = layer_norm(cond_flat, gain_first, shift_first).astype(jnp.bfloat16)
    cond_pair = jnp.dot(
        cond_in, joint_matrix[:, width:], preferred_element_type=jnp.float32
    ).astype(jnp.bfloat16)
    pairs = jnp.concatenate([pair_left, pair_here, cond_pair], 0)
    ends = item_ends(extra_length)
    here = lax.axis_index("blk")
    places = here * rows + lax.iota(jnp.int32, rows)
    seg_here = segment_ids(ends, places)
    seg_left = segment_ids(ends, places - rows)
    cond_seg = lax.iota(jnp.int32, cond_pair.shape[0]) // 2
    allowed = seg_here[:, None] == jnp.concatenate([seg_left, seg_here, cond_seg])[None, :]
    head_query = split_heads(query)
    head_key = split_heads(pairs[:, :width])
    head_value = split_heads(pairs[:, width:])

    def head_forward(parts):
        query_one, key_one, value_one = parts
        scores = masked_scores(query_one, key_one, allowed)
        top = jnp.max(scores, axis=1, keepdims=True)
        expo = jnp.exp(scores - top)
        total = jnp.sum(expo, axis=1, keepdims=True)
        probs = (expo / total).astype(jnp.bfloat16)
        mixed = jnp.dot(probs, value_one, preferred_element_type=jnp.float32)
        return (mixed, (top + jnp.log(total))[:, 0])

    mixed, logsum = lax.map(head_forward, (head_query, head_key, head_value))
    attended = merge_heads(mixed).astype(jnp.bfloat16)
    middle = base + jnp.dot(attended, out_matrix, preferred_element_type=jnp.float32) + out_offset
    second_in = layer_norm(middle, gain_second, shift_second).astype(jnp.bfloat16)
    before = jnp.dot(second_in, up_matrix, preferred_element_type=jnp.float32) + up_offset
    hidden = jax.nn.gelu(before, approximate=False).astype(jnp.bfloat16)
    output = middle + jnp.dot(hidden, down_matrix, preferred_element_type=jnp.float32) + down_offset
    again = (
        lax.all_gather(skip_weight, "blk", axis=0, tiled=True),
        lax.all_gather(skip_bias, "blk", axis=0, tiled=True),
        lax.all_gather(first_gain, "blk", axis=0, tiled=True),
        lax.all_gather(first_shift, "blk", axis=0, tiled=True),
        lax.all_gather(joint_weight, "blk", axis=0, tiled=True),
        lax.all_gather(out_weight, "blk", axis=0, tiled=True),
        lax.all_gather(out_bias, "blk", axis=0, tiled=True),
        lax.all_gather(second_gain, "blk", axis=0, tiled=True),
        lax.all_gather(second_shift, "blk", axis=0, tiled=True),
        lax.all_gather(up_weight, "blk", axis=0, tiled=True),
        lax.all_gather(up_bias, "blk", axis=0, tiled=True),
        lax.all_gather(down_weight, "blk", axis=0, tiled=True),
        lax.all_gather(down_bias, "blk", axis=0, tiled=True),
    )
    (
        skip_matrix,
        skip_offset,
        gain_first,
        shift_first,
        joint_matrix,
        out_matrix,
        out_offset,
        gain_second,
        shift_second,
        up_matrix,
        up_offset,
        down_matrix,
        down_offset,
    ) = again
    incoming = cotangent.astype(jnp.float32)
    grad_down_offset = jnp.sum(incoming, axis=0)
    grad_down_matrix = contract_rows(hidden, cotangent)
    d_hidden = contract_cols(cotangent, down_matrix)
    gelu_value, gelu_pull = jax.vjp(partial(jax.nn.gelu, approximate=False), before)
    d_before = gelu_pull(d_hidden)[0].astype(jnp.bfloat16)
    grad_up_offset = jnp.sum(d_before.astype(jnp.float32), axis=0)
    grad_up_matrix = contract_rows(second_in, d_before)
    d_second = contract_cols(d_before, up_matrix)
    norm_value, norm_pull = jax.vjp(
        layer_norm, middle, gain_second.astype(jnp.float32), shift_second.astype(jnp.float32)
    )
    d_middle_norm, grad_gain_second, grad_shift_second = norm_pull(d_second)
    d_middle = incoming + d_middle_norm
    d_branch = d_middle.astype(jnp.bfloat16)
    grad_out_offset = jnp.sum(d_branch.astype(jnp.float32), axis=0)
    grad_out_matrix = contract_rows(attended, d_branch)
    d_attended = contract_cols(d_branch, out_matrix).astype(jnp.bfloat16)

    def head_backward(parts):
        query_one, key_one, value_one, grad_one, logsum_one = parts
        scores = masked_scores(query_one, key_one, allowed)
        probs = jnp.exp(scores - logsum_one[:, None])
        d_probs = contract_cols(grad_one, value_one)
        inner = jnp.sum(probs * d_probs, axis=1, keepdims=True)
        d_scores = (probs * (d_probs - inner)).astype(jnp.bfloat16)
        d_query_one = jnp.dot(d_scores, key_one, preferred_element_type=jnp.float32) * scale
        d_key_one = contract_rows(d_scores, query_one) * scale
        d_value_one = contract_rows(probs.astype(jnp.bfloat16), grad_one)
        return (d_query_one, d_key_one, d_value_one)

    d_query_heads, d_key_heads, d_value_heads = lax.map(
        head_backward, (head_query, head_key, head_value, split_heads(d_attended), logsum)
    )
    d_query = merge_heads(d_query_heads)
    d_pairs = jnp.concatenate([merge_heads(d_key_heads), merge_heads(d_value_heads)], 1)
    d_left = d_pairs[:rows]
    d_own = d_pairs[rows : 2 * rows]
    d_cond_part = d_pairs[2 * rows :]
    d_returned = shifted(d_left.astype(jnp.bfloat16), "blk", -1).astype(d_left.dtype)
    d_cond_total = lax.psum(d_cond_part.astype(jnp.bfloat16), "blk")
    d_triple = jnp.concatenate([d_query, d_own + d_returned], 1).astype(jnp.bfloat16)
    leading = (here == 0).astype(jnp.float32)
    cond_term = contract_rows(cond_in, d_cond_total) * leading
    grad_joint_matrix = contract_rows(first_in, d_triple) + jnp.concatenate(
        [jnp.zeros((width, width), jnp.float32), cond_term], 1
    )
    d_first = contract_cols(d_triple, joint_matrix)
    d_cond_in = contract_cols(d_cond_total, joint_matrix[:, width:])
    first_value, first_pull = jax.vjp(
        layer_norm, base, gain_first.astype(jnp.float32), shift_first.astype(jnp.float32)
    )
    d_base_norm, grad_gain_tokens, grad_shift_tokens = first_pull(d_first)
    cond_value, cond_pull = jax.vjp(
        layer_norm, cond_flat, gain_first.astype(jnp.float32), shift_first.astype(jnp.float32)
    )
    d_cond_flat, grad_gain_cond, grad_shift_cond = cond_pull(d_cond_in)
    grad_gain_first = grad_gain_tokens + leading * grad_gain_cond
    grad_shift_first = grad_shift_tokens + leading * grad_shift_cond
    d_base = (d_middle + d_base_norm).astype(jnp.bfloat16)
    grad_skip_offset = jnp.sum(d_base.astype(jnp.float32), axis=0)
    grad_skip_matrix = contract_rows(joined, d_base)
    d_joined = contract_cols(d_base, skip_matrix)
    shares = (
        lax.psum_scatter(
            grad_skip_matrix.astype(jnp.bfloat16), "blk", scatter_dimension=0, tiled=True
        ).astype(jnp.float32),
        lax.psum_scatter(
            grad_skip_offset.astype(jnp.bfloat16), "blk", scatter_dimension=0, tiled=True
        ).astype(jnp.float32),
        lax.psum_scatter(
            grad_gain_first.astype(jnp.bfloat16), "blk", scatter_dimension=0, tiled=True
        ).astype(jnp.float32),
        lax.psum_scatter(
            grad_shift_first.astype(jnp.bfloat16), "blk", scatter_dimension=0, tiled=True
        ).astype(jnp.float32),
        lax.psum_scatter(
            grad_joint_matrix.astype(jnp.bfloat16), "blk", scatter_dimension=0, tiled=True
        ).astype(jnp.float32),
        lax.psum_scatter(
            grad_out_matrix.astype(jnp.bfloat16), "blk", scatter_dimension=0, tiled=True
        ).astype(jnp.float32),
        lax.psum_scatter(
            grad_out_offset.astype(jnp.bfloat16), "blk", scatter_dimension=0, tiled=True
        ).astype(jnp.float32),
        lax.psum_scatter(
            grad_gain_second.astype(jnp.bfloat16), "blk", scatter_dimension=0, tiled=True
        ).astype(jnp.float32),
        lax.psum_scatter(
            grad_shift_second.astype(jnp.bfloat16), "blk", scatter_dimension=0, tiled=True
        ).astype(jnp.float32),
        lax.psum_scatter(
            grad_up_matrix.astype(jnp.bfloat16), "blk", scatter_dimension=0, tiled=True
        ).astype(jnp.float32),
        lax.psum_scatter(
            grad_up_offset.astype(jnp.bfloat16), "blk", scatter_dimension=0, tiled=True
        ).astype(jnp.float32),
        lax.psum_scatter(
            grad_down_matrix.astype(jnp.bfloat16), "blk", scatter_dimension=0, tiled=True
        ).astype(jnp.float32),
        lax.psum_scatter(
            grad_down_offset.astype(jnp.bfloat16), "blk", scatter_dimension=0, tiled=True
        ).astype(jnp.float32),
    )
    (
        share_skip,
        share_skip_offset,
        share_gain_first,
        share_shift_first,
        share_joint,
        share_out,
        share_out_offset,
        share_gain_second,
        share_shift_second,
        share_up,
        share_up_offset,
        share_down,
        share_down_offset,
    ) = shares
    summed = (
        lax.psum(share_skip.astype(jnp.bfloat16), "stream").astype(jnp.float32),
        lax.psum(share_skip_offset.astype(jnp.bfloat16), "stream").astype(jnp.float32),
        lax.psum(share_gain_first.astype(jnp.bfloat16), "stream").astype(jnp.float32),
        lax.psum(share_shift_first.astype(jnp.bfloat16), "stream").astype(jnp.float32),
        lax.psum(share_joint.astype(jnp.bfloat16), "stream").astype(jnp.float32),
        lax.psum(share_out.astype(jnp.bfloat16), "stream").astype(jnp.float32),
        lax.psum(share_out_offset.astype(jnp.bfloat16), "stream").astype(jnp.float32),
        lax.psum(share_gain_second.astype(jnp.bfloat16), "stream").astype(jnp.float32),
        lax.psum(share_shift_second.astype(jnp.bfloat16), "stream").astype(jnp.float32),
        lax.psum(share_up.astype(jnp.bfloat16), "stream").astype(jnp.float32),
        lax.psum(share_up_offset.astype(jnp.bfloat16), "stream").astype(jnp.float32),
        lax.psum(share_down.astype(jnp.bfloat16), "stream").astype(jnp.float32),
        lax.psum(share_down_offset.astype(jnp.bfloat16), "stream").astype(jnp.float32),
    )
    return (
        output.astype(jnp.bfloat16),
        d_joined[:, :width].astype(jnp.bfloat16),
        d_joined[:, width:].astype(jnp.bfloat16),
        d_cond_flat.reshape(cond_tokens.shape).astype(jnp.bfloat16),
        summed[0],
        summed[1],
        summed[2],
        summed[3],
        summed[4],
        summed[5],
        summed[6],
        summed[7],
        summed[8],
        summed[9],
        summed[10],
        summed[11],
        summed[12],
    )


def solution(mesh):
    placed = (
        P(("stream", "blk"), None),
        P(("stream", "blk"), None),
        P("stream", None, None),
        P("stream", None),
        P("blk", None),
        P("blk"),
        P("blk"),
        P("blk"),
        P("blk", None),
        P("blk", None),
        P("blk"),
        P("blk"),
        P("blk"),
        P("blk", None),
        P("blk"),
        P("blk", None),
        P("blk"),
        P(("stream", "blk"), None),
    )
    fits = mesh.shape["stream"] == 4 and mesh.shape["blk"] == 8
    return jax.shard_map(
        quick if fits else plain,
        mesh=mesh,
        in_specs=placed,
        out_specs=(
            P(("stream", "blk"), None),
            P(("stream", "blk"), None),
            P(("stream", "blk"), None),
            P("stream", None, None),
            P("blk", None),
            P("blk"),
            P("blk"),
            P("blk"),
            P("blk", None),
            P("blk", None),
            P("blk"),
            P("blk"),
            P("blk"),
            P("blk", None),
            P("blk"),
            P("blk", None),
            P("blk"),
        ),
        check_vma=False,
    )
```

```python
import functools
from functools import partial

import jax
import jax.numpy as jnp
from jax import lax
from jax.experimental import pallas as pl
from jax.experimental.pallas import tpu as pltpu
from jax.sharding import PartitionSpec as P

HEADS = 16
HEAD = 72
LEN_MIN = 192

MESH = pl.DeviceIdType.MESH
ANY = pl.BlockSpec(memory_space=pl.ANY)
WIDTH = 1152
PART = 144
SMALL = (16, 256)


class Place:
    def __init__(self):
        self.s = lax.axis_index("stream")
        self.b = lax.axis_index("blk")
        self.x = lax.rem(self.s, 2)
        self.y = lax.div(self.s, 2)
        self.c = lax.rem(self.b, 2)
        self.zz = lax.div(self.b, 2)

    def other(self, k):
        low, high = lax.rem(self.zz, 2), lax.div(self.zz, 2)
        return 2 * (1 - high if k & 2 else high) + (1 - low if k & 1 else low)

    def source(self, k):
        zz = self.zz
        table = ((1, 0, 3, 2), (2, 2, 1, 1), (3, 3, 0, 0))[k - 1]
        return jnp.where(zz < 2, jnp.where(zz == 0, table[0], table[1]), jnp.where(zz == 2, table[2], table[3]))

    def at(self, x=None, y=None, zz=None, c=None):
        x = self.x if x is None else x
        y = self.y if y is None else y
        zz = self.zz if zz is None else zz
        c = self.c if c is None else c
        return (2 * y + x, 2 * zz + c)


def greet(place):
    barrier = pltpu.get_barrier_semaphore()
    p = place
    near = [p.at(x=1 - p.x), p.at(y=1 - p.y), p.at(c=1 - p.c)] + [p.at(zz=p.other(k)) for k in (1, 2, 3)]
    for device in near:
        pl.semaphore_signal(barrier, inc=1, device_id=device, device_id_type=MESH)
    up = (p.c == 1) & (p.zz < 3)
    down = (p.c == 0) & (p.zz > 0)
    for go, device in ((up, (p.s, p.b + 1)), (down, (p.s, p.b - 1))):

        @pl.when(go)
        def _():
            pl.semaphore_signal(barrier, inc=1, device_id=device, device_id_type=MESH)

    pl.when(up | down)(lambda: pl.semaphore_wait(barrier, len(near) + 1))
    pl.when(jnp.logical_not(up | down))(lambda: pl.semaphore_wait(barrier, len(near)))


def remote(src, dst, send, recv, device):
    return pltpu.make_async_remote_copy(
        src_ref=src, dst_ref=dst, send_sem=send, recv_sem=recv, device_id=device, device_id_type=MESH
    )


def block(t, ref, b):
    if t in (1, 2):
        return ref.at[b]
    size = 2 if t == 0 else 4
    return ref.at[pl.ds(b * size, size)]


def piece(t, ref, b, x, y):
    if t in (1, 2):
        return ref.at[b, :, pl.ds(pl.multiple_of((2 * y + x) * WIDTH, 128), WIDTH)]
    if t == 3:
        return ref.at[4 * b + 2 * y + x]
    low, size = (0, 80) if y == 0 else (80, 64)
    return ref.at[2 * b + x, pl.ds(low, size)]


KINDS = ("half", "cols", "cols", "rows")


class Gather:
    SEMS = [pltpu.SemaphoreType.DMA((4, 6, 4, 2)), pltpu.SemaphoreType.DMA((12,)), pltpu.SemaphoreType.DMA((2, 8))]

    def __init__(self, place, shards, outs, scratch):
        self.place = place
        self.small_in, self.skip_in, self.joint_in, self.out_in, self.up_in, self.down_in = shards
        self.small = outs[0]
        self.outs = outs[1:]
        self.sems, self.local_sems, self.small_sems = scratch[:3]
        self.stage = scratch[3:]

    def copy(self, t, x, y, zz, c, stage, k, device):
        ref = piece(t, self.outs[t], 2 * zz + c, x, y)
        return remote(ref, ref, self.sems.at[t, stage, k, 0], self.sems.at[t, stage, k, 1], device)

    def each_y(self, t, run):
        if KINDS[t] != "half":
            run(self.place.y)
            return
        for value in (0, 1):
            pl.when(self.place.y == value)(lambda value=value: run(value))

    STAGE = [
        pltpu.VMEM((2, PART, WIDTH), jnp.bfloat16),
        pltpu.VMEM((PART, 4 * WIDTH), jnp.bfloat16),
        pltpu.VMEM((PART, 4 * WIDTH), jnp.bfloat16),
        pltpu.VMEM((4, PART, WIDTH), jnp.bfloat16),
    ]

    def locals(self, t):
        if t == 1:
            return [
                (self.joint_in, self.stage[1].at[:, pl.ds(0, 3 * WIDTH)]),
                (self.out_in, self.stage[1].at[:, pl.ds(3 * WIDTH, WIDTH)]),
            ]
        return [({0: self.skip_in, 2: self.up_in, 3: self.down_in}[t], self.stage[t])]

    def own_start(self, t):
        for i, (src, dst) in enumerate(self.locals(t)):
            pltpu.make_async_copy(src, dst, self.local_sems.at[2 * t + i]).start()

    def own_keep(self, t):
        return pltpu.make_async_copy(self.stage[t], block(t, self.outs[t], self.place.b), self.local_sems.at[8 + t])

    def own_done(self, t):
        for i, (src, dst) in enumerate(self.locals(t)):
            pltpu.make_async_copy(src, dst, self.local_sems.at[2 * t + i]).wait()
        self.own_keep(t).start()

    def own_copy(self, t, c):
        ref = block(t, self.outs[t], 2 * self.place.zz + c)
        src = self.stage[t]
        sems = self.sems.at[t, 4, 0]
        return remote(src, ref, sems.at[0], sems.at[1], self.place.at(c=1 - self.place.c))

    def small_copy(self, i, src, dst, device):
        return remote(src, dst, self.small_sems.at[0, i], self.small_sems.at[1, i], device)

    def small_start(self):
        p = self.place
        for i, device in enumerate([p.at(zz=p.other(k)) for k in (1, 2, 3)] + [p.at(c=1 - p.c)]):
            self.small_copy(i, self.small_in, self.small.at[p.b], device).start()

    def small_pass(self):
        p = self.place
        for i, k in enumerate((1, 2, 3)):
            ref = self.small.at[2 * p.other(k) + p.c]
            self.small_copy(i, ref, ref, p.at()).wait_recv()
            self.small_copy(4 + i, ref, ref, p.at(c=1 - p.c)).start()

    def small_done(self):
        p = self.place
        for i, k in enumerate((0, 1, 2, 3)):
            ref = self.small.at[2 * p.other(k) + 1 - p.c]
            self.small_copy(3 + i, ref, ref, p.at()).wait_recv()
        for i in range(7):
            self.small_copy(i, self.small_in, self.small_in, p.at()).wait_send()

    def stage_piece(self, t, y):
        x = self.place.x
        if t in (1, 2):
            return self.stage[t].at[:, pl.ds(pl.multiple_of((2 * y + x) * WIDTH, 128), WIDTH)]
        if t == 3:
            return self.stage[t].at[2 * y + x]
        low, size = (0, 80) if y == 0 else (80, 64)
        return self.stage[t].at[x, pl.ds(low, size)]

    def z_copies(self, t, y, zz, start, own=False):
        p = self.place
        for step, send in ((1, 0), (-1, 5)):
            go = (zz <= p.zz) & (p.zz < 3) if step == 1 else (zz >= p.zz) & (p.zz > 0)
            ref = piece(t, self.outs[t], 2 * zz + p.c, p.x, y)

            @pl.when(go)
            def _():
                copy = remote(self.stage_piece(t, y) if own else ref, ref, self.sems.at[t, send, zz, 0], self.sems.at[t, 0, zz, 1], p.at(zz=p.zz + step))
                copy.start() if start else copy.wait_send()

    def z_start(self, t):
        p = self.place
        self.each_y(t, lambda y: self.z_copies(t, y, p.zz, True, True))
        self.own_copy(t, p.c).start()

    def z_wait(self, t, y, zz):
        p = self.place
        self.copy(t, p.x, y, zz, p.c, 0, zz, p.at()).wait_recv()

    def z_done(self, t, k):
        p = self.place
        zz = p.source(k)

        def run(y):
            self.z_wait(t, y, zz)
            self.z_copies(t, y, zz, True)

        pl.when((p.zz > 0) & (p.zz < 3))(lambda: self.each_y(t, run))

    def xy_start(self, t, k):
        p = self.place
        zz = p.source(k)

        def run(y):
            pl.when((p.zz == 0) | (p.zz == 3))(lambda: self.z_wait(t, y, zz))
            self.copy(t, p.x, y, zz, p.c, 1, k, p.at(x=1 - p.x)).start()
            self.copy(t, p.x, y, zz, p.c, 2, k, p.at(y=1 - p.y)).start()

        self.each_y(t, run)

    def by_x(self, t, k):
        return k == 1 or (k == 2 and t % 2 == 0)

    def xy_done(self, t, k):
        p = self.place

        def run(y):
            zz = p.source(k)
            self.copy(t, 1 - p.x, y, zz, p.c, 1, k, p.at()).wait_recv()
            if self.by_x(t, k):
                self.copy(t, 1 - p.x, y, zz, p.c, 3, k, p.at(y=1 - p.y)).start()
            self.copy(t, p.x, 1 - y, zz, p.c, 2, k, p.at()).wait_recv()
            if not self.by_x(t, k):
                self.copy(t, p.x, 1 - y, zz, p.c, 3, k, p.at(x=1 - p.x)).start()

        self.each_y(t, run)

    def diag_done(self, t, k):
        p = self.place

        def run(y):
            zz = p.source(k)
            self.copy(t, 1 - p.x, 1 - y, zz, p.c, 3, k, p.at()).wait_recv()

        self.each_y(t, run)
        self.pair_copy(t, k, p.c).start()

    def pair_copy(self, t, k, c):
        ref = block(t, self.outs[t], 2 * self.place.source(k) + c)
        sems = self.sems.at[t, 4, k]
        return remote(ref, ref, sems.at[0], sems.at[1], self.place.at(c=1 - self.place.c))

    def ready(self, t):
        p = self.place
        self.own_keep(t).wait()
        self.own_copy(t, 1 - p.c).wait_recv()
        for k in (1, 2, 3):
            self.pair_copy(t, k, 1 - p.c).wait_recv()

    def all_sent(self, t):
        p = self.place
        self.own_copy(t, p.c).wait_send()

        def run(y):
            self.z_copies(t, y, p.zz, False, True)
            for k in (1, 2, 3):
                zz = p.source(k)
                self.z_copies(t, y, zz, False)
                self.copy(t, p.x, y, zz, p.c, 1, k, p.at()).wait_send()
                self.copy(t, p.x, y, zz, p.c, 2, k, p.at()).wait_send()
                if self.by_x(t, k):
                    self.copy(t, 1 - p.x, y, zz, p.c, 3, k, p.at()).wait_send()
                else:
                    self.copy(t, p.x, 1 - y, zz, p.c, 3, k, p.at()).wait_send()

        self.each_y(t, run)
        for k in (1, 2, 3):
            self.pair_copy(t, k, p.c).wait_send()


SIZES = (80, PART, PART, PART)


HALO = 320
COND = 32
TOK = 512
KEYS = HALO + TOK + COND
TILES = ((0, 0), (256, 256))
LOG2E = 1.4426950408889634


def nt(a, b):
    return lax.dot_general(a, b, (((1,), (1,)), ((), ())), preferred_element_type=jnp.float32)


def tn(a, b):
    return lax.dot_general(a, b, (((0,), (0,)), ((), ())), preferred_element_type=jnp.float32)


def nn(a, b):
    return jnp.dot(a, b, preferred_element_type=jnp.float32)


def make_bias(extra, blk, bias):
    row = lax.broadcasted_iota(jnp.int32, (TOK, 1), 0) + blk * TOK
    at = lax.broadcasted_iota(jnp.int32, (1, KEYS), 1)
    key = at + (blk * TOK - HALO)
    item_q, item_k = jnp.zeros_like(row), jnp.zeros_like(key)
    end = 0
    for n in range(extra.shape[1]):
        end = end + extra[0, n] + (LEN_MIN - 1)
        item_q += (row >= end).astype(jnp.int32)
        item_k += (key >= end).astype(jnp.int32)
    item_k = jnp.where(key >= 0, item_k, -1)
    item_k = jnp.where(at >= HALO + TOK, (at - (HALO + TOK)) >> 1, item_k)
    for low in range(0, TOK, 128):
        bias[low : low + 128] = jnp.where(item_q[low : low + 128] == item_k, 0.0, -1e30)


def head(h):
    return slice(HEAD * h, HEAD * (h + 1))


class Names:
    def __init__(self, names, refs):
        for name, ref in zip(names, refs, strict=True):
            setattr(self, name, ref)


def hbm(shape, dtype=jnp.bfloat16):
    return jax.ShapeDtypeStruct(shape, dtype)


GROUP = 4
IN_VMEM = pl.BlockSpec(memory_space=pltpu.VMEM)
IN_SMEM = pl.BlockSpec(memory_space=pltpu.SMEM)
FWD_IN = dict(
    skip_bias=IN_VMEM, first_gain=IN_VMEM, first_shift=IN_VMEM, out_bias=IN_VMEM, second_gain=IN_VMEM,
    second_shift=IN_VMEM, down_bias=IN_VMEM, up_bias=IN_VMEM, extra=IN_SMEM, cond=IN_VMEM, latents=ANY, skip_input=ANY, skip=ANY, joint=ANY, out=ANY, up=ANY, down=ANY,
)
FWD_OUT = dict(
    w_skip=hbm((16, PART, WIDTH)),
    w_joint=hbm((8, PART, 4 * WIDTH)),
    w_up=hbm((8, PART, 4 * WIDTH)),
    w_down=hbm((32, PART, WIDTH)),
    output=hbm((TOK, WIDTH)),
    hidden_t=hbm((8, 4, PART, TOK)),
    slope=hbm((TOK, 4 * WIDTH)),
    second_t=hbm((8, PART, TOK)),
    second_unit=hbm((TOK, WIDTH)),
    att_t=hbm((8, PART, TOK)),
    q=hbm((HEADS, TOK, HEAD)),
    k=hbm((HEADS, KEYS, HEAD)),
    v=hbm((HEADS, KEYS, HEAD)),
    o=hbm((HEADS, TOK, HEAD)),
    logsum=hbm((HEADS, TOK, 1), jnp.float32),
    first_t=hbm((8, PART, TOK)),
    first_unit=hbm((TOK, WIDTH)),
    joined_t=hbm((8, 2 * PART, TOK)),
)
FWD_VM = dict(
    cond_t=hbm((8, PART, 128)),
    second_rstd=hbm((TOK, 1), jnp.float32),
    first_rstd=hbm((TOK, 1), jnp.float32),
    vectors=hbm((16, WIDTH), jnp.float32),
    cond_unit=hbm((COND, WIDTH), jnp.float32),
    cond_rstd=hbm((COND, 1), jnp.float32),
)
FWD_SCRATCH = dict(
    lat=pltpu.VMEM((TOK, WIDTH), jnp.bfloat16),
    ski=pltpu.VMEM((TOK, WIDTH), jnp.bfloat16),
    weight=pltpu.VMEM((2, 8, PART, WIDTH), jnp.bfloat16),
    base=pltpu.VMEM((TOK, WIDTH), jnp.float32),
    acc=pltpu.VMEM((TOK, WIDTH), jnp.float32),
    unit=pltpu.VMEM((TOK, WIDTH), jnp.bfloat16),
    normed=pltpu.VMEM((TOK, WIDTH), jnp.bfloat16),
    pairs=pltpu.VMEM((2, TOK, WIDTH), jnp.bfloat16),
    halo=pltpu.VMEM((2, HALO, WIDTH), jnp.bfloat16),
    cond_in=pltpu.VMEM((COND, WIDTH), jnp.bfloat16),
    qh=pltpu.VMEM((HEADS, TOK, HEAD), jnp.bfloat16),
    kh=pltpu.VMEM((HEADS, KEYS, HEAD), jnp.bfloat16),
    vh=pltpu.VMEM((HEADS, KEYS, HEAD), jnp.bfloat16),
    oh=pltpu.VMEM((HEADS, TOK, HEAD), jnp.bfloat16),
    lh=pltpu.VMEM((HEADS // 2, 256, 1), jnp.float32),
    bias=pltpu.VMEM((TOK, KEYS), jnp.float32),
    hidden=pltpu.VMEM((4, TOK, WIDTH), jnp.bfloat16),
    turned=pltpu.VMEM((2, WIDTH, TOK), jnp.bfloat16),
    tile=pltpu.VMEM((2, TOK, WIDTH), jnp.bfloat16),
    pack=pltpu.VMEM(SMALL, jnp.float32),
    packs=pltpu.VMEM((8, *SMALL), jnp.float32),
    ups=pltpu.VMEM((4, 1, WIDTH), jnp.float32),
    w_sems=pltpu.SemaphoreType.DMA((2,)),
    t_sems=pltpu.SemaphoreType.DMA((24,)),
    halo_sems=pltpu.SemaphoreType.DMA((2, 2)),
)
N_GATHER = len(Gather.SEMS) + len(Gather.STAGE)


def forward_kernel(*refs):
    cuts = [len(FWD_IN), len(FWD_OUT), len(FWD_VM), len(FWD_SCRATCH), N_GATHER]
    pieces, at = [], 0
    for cut in cuts:
        pieces.append(refs[at : at + cut])
        at += cut
    i, o, vm, b = (
        Names(names, part) for names, part in zip((FWD_IN, FWD_OUT, FWD_VM, FWD_SCRATCH), pieces)
    )
    f32, bf16 = jnp.float32, jnp.bfloat16
    p = Place()
    g = Gather(
        p, (b.pack, i.skip, i.joint, i.out, i.up, i.down), (b.packs, o.w_skip, o.w_joint, o.w_up, o.w_down), pieces[4]
    )

    def copy(src, dst, sem):
        return pltpu.make_async_copy(src, dst, sem)

    def stream(blocks, body):
        def load(n):
            return copy(blocks[n], b.weight.at[n % 2], b.w_sems.at[n % 2])

        load(0).start()
        for n in range(len(blocks)):
            if n + 1 < len(blocks):
                load(n + 1).start()
            load(n).wait()
            body(n, b.weight[n % 2].reshape(WIDTH, WIDTH))

    def column(ref, q):
        return ref.at[:, :, pl.ds(q * WIDTH, WIDTH)]

    def by_rows(size, body):
        @pl.loop(0, TOK // size)
        def _(n):
            body(pl.ds(pl.multiple_of(n * size, size), size))

    def vector(n):
        return vm.vectors[n : n + 1, :]

    kept = []

    def keep(src, dst, sem):
        one = (src, dst, b.t_sems.at[sem])
        copy(*one).start()
        kept.append(one)

    def flush():
        for one in kept:
            copy(*one).wait()
        kept.clear()

    def norm(values):
        center = values - jnp.mean(values, axis=1, keepdims=True)
        rstd = lax.rsqrt(jnp.mean(center * center, axis=1, keepdims=True) + 1e-05)
        return center * rstd, rstd

    def norm_tokens(gain, shift, rstd_out):
        @functools.partial(by_rows, 64)
        def _(rows):
            unit, rstd = norm(b.base[rows])
            b.unit[rows] = unit.astype(bf16)
            rstd_out[rows] = rstd
            b.normed[rows] = (unit * gain + shift).astype(bf16)

    def turn(slot, src, dst, sem):
        b.turned[slot] = src.T
        keep(b.turned.at[slot], dst, sem)

    loads = [(i.latents, b.lat, b.t_sems.at[0]), (i.skip_input, b.ski, b.t_sems.at[1])]
    for t in range(4):
        g.own_start(t)
    for one in loads:
        copy(*one).start()
    b.pack[...] = jnp.zeros(SMALL, f32)
    few = (i.skip_bias, i.first_gain, i.first_shift, i.out_bias, i.second_gain, i.second_shift, i.down_bias)
    for n, ref in enumerate(few):
        b.pack[n : n + 1, 0:PART] = ref[...].astype(f32).reshape(1, PART)
    wide = i.up_bias[...].astype(f32).reshape(1, 4 * PART)
    for n in range(4):
        b.pack[7 + n : 8 + n, 0:PART] = wide[:, n * PART : (n + 1) * PART]
    b.packs[p.b] = b.pack[...]
    greet(p)
    g.small_start()
    g.own_done(0)
    g.z_start(0)
    make_bias(i.extra, p.b, b.bias)
    g.small_pass()
    for one in loads:
        copy(*one).wait()

    @pl.when(p.b == 0)
    def _():
        for n in range(HEADS):
            b.kh[n, 0:HALO] = jnp.zeros((HALO, HEAD), bf16)
            b.vh[n, 0:HALO] = jnp.zeros((HALO, HEAD), bf16)

    for k in (1, 2, 3):
        g.z_done(0, k)
        g.xy_start(0, k)
        if k == 2:
            g.own_done(1)
            g.z_start(1)
    g.small_done()
    for n in range(8):
        for row in range(7):
            vm.vectors[row : row + 1, n * PART : (n + 1) * PART] = b.packs[n, row : row + 1, 0:PART]
        for j in range(4):
            at = 4 * n + j
            low = at % 8 * PART
            b.ups[at // 8, :, low : low + PART] = b.packs[n, 7 + j : 8 + j, 0:PART]
    vm.vectors[7:16, :] = jnp.zeros((9, WIDTH), f32)
    for k in (1, 2, 3):
        g.xy_done(0, k)
    g.z_done(1, 1)
    g.xy_start(1, 1)
    for k in (1, 2, 3):
        g.diag_done(0, k)
    g.ready(0)

    def do_base(n, weight):
        made = nn((b.lat, b.ski)[n][...], weight)
        if n == 0:
            b.base[...] = made + vector(0)
        else:
            b.base[...] += made
        if n == 0:
            g.z_done(1, 2)
            g.z_done(1, 3)
            g.xy_start(1, 2)
            g.own_done(2)
            g.z_start(2)

    stream([o.w_skip.at[pl.ds(8 * n, 8)] for n in range(2)], do_base)
    norm_tokens(vector(1), vector(2), vm.first_rstd)
    g.xy_start(1, 3)
    g.z_done(2, 1)
    for n in range(COND // 2):
        vm.cond_unit[2 * n : 2 * n + 2] = i.cond[n].astype(f32)
    unit, rstd = norm(vm.cond_unit[...])
    vm.cond_unit[...] = unit
    vm.cond_rstd[...] = rstd
    cond_in = (unit * vector(1) + vector(2)).astype(bf16)
    b.cond_in[...] = cond_in
    keep(b.unit, o.first_unit, 2)
    for n in range(2):
        b.turned[n] = (b.lat, b.ski)[n][...].T
        made = b.turned.at[n].reshape(8, PART, TOK)
        for k in range(4):
            keep(made.at[pl.ds(2 * k, 2)].reshape(2 * PART, TOK), o.joined_t.at[4 * n + k], 3 + 4 * n + k)
        if n == 0:
            g.z_done(2, 2)
            g.own_done(3)
            g.z_start(3)
    turned = jnp.concatenate([cond_in.astype(f32)] * 2 + [jnp.zeros((128 - 2 * COND, WIDTH), f32)], 0).T
    vm.cond_t[...] = turned.astype(bf16).reshape(8, PART, 128)
    for k in (1, 2, 3):
        g.xy_done(1, k)
    g.xy_start(2, 1)
    g.z_done(2, 3)
    for k in (1, 2, 3):
        g.diag_done(1, k)
    g.xy_start(2, 2)
    g.xy_start(2, 3)
    g.z_done(3, 1)
    g.ready(1)

    def halo_copy(n, device):
        low, size = ((HALO - 64, 64), (0, HALO - 64))[n]
        src, dst = b.pairs.at[:, pl.ds(TOK - HALO + low, size)], b.halo.at[:, pl.ds(low, size)]
        return remote(src, dst, b.halo_sems.at[n, 0], b.halo_sems.at[n, 1], device)

    def halo_heads(n):
        low, size = ((HALO - 64, 64), (0, HALO - 64))[n]

        @pl.when(p.b > 0)
        def _():
            halo_copy(n, (p.s, p.b)).wait_recv()
            for h in range(HEADS):
                b.kh[h, low : low + size] = b.halo[0, low : low + size, head(h)]
                b.vh[h, low : low + size] = b.halo[1, low : low + size, head(h)]

    def do_triple(n, weight):
        made = nn(b.normed[...], weight).astype(bf16)
        if n < 2:
            b.pairs[n] = made
            few = nn(b.cond_in[...], weight).astype(bf16)
            for h in range(HEADS):
                (b.kh, b.vh)[n][h, HALO + TOK :] = few[:, head(h)]
        else:
            b.tile[0] = made
        if n == 1:
            for m in (0, 1):
                pl.when(p.b < 7)(lambda m=m: halo_copy(m, (p.s, p.b + 1)).start())
            g.z_done(3, 2)

    stream([column(o.w_joint, n) for n in (1, 2, 0)], do_triple)
    for h in range(HEADS):
        b.qh[h] = b.tile[0, :, head(h)]
        b.kh[h, HALO : HALO + TOK] = b.pairs[0, :, head(h)]
        b.vh[h, HALO : HALO + TOK] = b.pairs[1, :, head(h)]
    g.z_done(3, 3)
    flush()
    turn(0, b.normed[...], o.first_t.reshape(WIDTH, TOK), 2)

    halo_heads(0)
    keep(b.qh, o.q, 3)

    def logsum_copy(half, start):
        dst = o.logsum.at[pl.ds(start, HEADS // 2), pl.ds(TILES[half][0], 256)]
        return copy(b.lh, dst, b.t_sems.at[6])

    def attend(half, start, before):
        row, low = TILES[half]
        rows, keys = pl.ds(row, 256), pl.ds(low, KEYS - low)
        if before is not None:
            logsum_copy(*before).wait()

        @pl.loop(0, HEADS // 2)
        def _(n):
            h = start + n
            scores = nt(b.qh[h, rows], b.kh[h, keys]) * (HEAD**-0.5 * LOG2E) + b.bias[rows, keys]
            top = jnp.max(scores, axis=1, keepdims=True)
            expo = jnp.exp2(scores - top)
            total = jnp.sum(expo, axis=1, keepdims=True)
            mixed = nn(expo.astype(bf16), b.vh[h, keys])
            b.oh[h, rows] = (mixed / total).astype(bf16)
            b.lh[n] = top + jnp.log2(total)

        logsum_copy(half, start).start()

    attend(1, 0, None)
    for k in (1, 2, 3):
        g.xy_done(2, k)
    g.xy_start(3, 1)
    attend(1, 8, (1, 0))
    halo_heads(1)
    keep(b.kh, o.k, 4)
    keep(b.vh, o.v, 5)
    g.xy_start(3, 2)
    attend(0, 0, (1, 8))
    g.xy_start(3, 3)
    attend(0, 8, (0, 0))
    logsum_copy(0, 8).wait()
    keep(b.oh, o.o, 7)
    for h in range(HEADS):
        b.tile[0, :, head(h)] = b.oh[h]

    def do_out(_, weight):
        b.base[...] += nn(b.tile[0], weight) + vector(3)

    stream([column(o.w_joint, 3)], do_out)
    norm_tokens(vector(4), vector(5), vm.second_rstd)
    flush()
    keep(b.unit, o.second_unit, 2)
    turn(0, b.tile[0], o.att_t.reshape(WIDTH, TOK), 3)
    turn(1, b.normed[...], o.second_t.reshape(WIDTH, TOK), 4)
    for k in (1, 2, 3):
        g.diag_done(2, k)
    for k in (1, 2, 3):
        g.xy_done(3, k)
    g.ready(2)

    flush()
    hidden_t = o.hidden_t.reshape(4, WIDTH, TOK)

    def wide_keep(q):
        slot = q % 2
        return [
            copy(b.turned.at[slot], hidden_t.at[q], b.t_sems.at[8 + slot]),
            copy(b.tile.at[slot], o.slope.at[:, pl.ds(q * WIDTH, WIDTH)], b.t_sems.at[10 + slot]),
        ]

    def do_up(q, weight):
        slot = q % 2
        b.acc[...] = nn(b.normed[...], weight)
        if q >= 2:
            for one in wide_keep(q - 2):
                one.wait()

        @functools.partial(by_rows, 32)
        def _(rows):
            before = b.acc[rows] + b.ups[q]
            inside = 0.5 + 0.5 * lax.erf(before * 2**-0.5)
            bell = jnp.exp2(before * before * (-0.5 * LOG2E)) * 0.3989422804014327
            b.hidden[q, rows] = (before * inside).astype(bf16)
            b.tile[slot, rows] = (inside + before * bell).astype(bf16)

        b.turned[slot] = b.hidden[q].T
        for one in wide_keep(q):
            one.start()
        if q == 1:
            for k in (1, 2, 3):
                g.diag_done(3, k)

    stream([column(o.w_up, q) for q in range(4)], do_up)
    g.ready(3)

    def do_down(q, weight):
        made = nn(b.hidden[q], weight)
        if q == 0:
            b.base[...] += made + vector(6)
        else:
            b.base[...] += made

    stream([o.w_down.at[pl.ds(8 * q, 8)] for q in range(4)], do_down)
    b.normed[...] = b.base[...].astype(bf16)
    keep(b.normed, o.output, 2)
    for q in (2, 3):
        for one in wide_keep(q):
            one.wait()
    flush()
    for m in (0, 1):
        pl.when(p.b < 7)(lambda m=m: halo_copy(m, (p.s, p.b + 1)).wait_send())
    for t in range(4):
        g.all_sent(t)


def forward(arrays):
    vm = pl.BlockSpec(memory_space=pltpu.VMEM)
    outs = pl.pallas_call(
        forward_kernel,
        out_shape=[*FWD_OUT.values(), *FWD_VM.values()],
        in_specs=[*FWD_IN.values()],
        out_specs=[ANY] * len(FWD_OUT) + [vm] * len(FWD_VM),
        scratch_shapes=[*FWD_SCRATCH.values()] + Gather.SEMS + Gather.STAGE,
        compiler_params=pltpu.CompilerParams(collective_id=0, has_side_effects=True, vmem_limit_bytes=60 << 20),
    )(*[arrays[name] for name in FWD_IN])
    return dict(zip([*FWD_OUT, *FWD_VM], outs, strict=True))


ORDER = (0, 2, 1, 3)
UNIT = (PART, WIDTH)


def add_into(out, *ins):
    @pl.loop(0, out.shape[0] // 16)
    def _(i):
        rows = pl.ds(pl.multiple_of(i * 16, 16), 16)
        total = ins[0][rows].astype(jnp.float32)
        for ref in ins[1:]:
            total += ref[rows].astype(jnp.float32)
        out[rows] = total.astype(out.dtype)


class Sum:
    SEMS = [
        pltpu.SemaphoreType.DMA((4, 4, 2, 2)),
        pltpu.SemaphoreType.DMA((4, 4, 2)),
        pltpu.SemaphoreType.DMA((4, 4, 2)),
        pltpu.SemaphoreType.DMA((4, 4, 2)),
        pltpu.SemaphoreType.DMA((23,)),
    ]
    SLOTS = [pltpu.VMEM((23, *UNIT), jnp.bfloat16), pltpu.VMEM((4, *UNIT), jnp.bfloat16)]
    LANDS = [
        jax.ShapeDtypeStruct(lead + (size, WIDTH), jnp.bfloat16)
        for size in SIZES
        for lead in ((4, 2), (4,), (4,))
    ]
    PARTS = [
        jax.ShapeDtypeStruct((8, PART, WIDTH), jnp.bfloat16),
        jax.ShapeDtypeStruct((4, PART, 4 * WIDTH), jnp.bfloat16),
        jax.ShapeDtypeStruct((4, PART, 4 * WIDTH), jnp.bfloat16),
        jax.ShapeDtypeStruct((4, 4, PART, WIDTH), jnp.bfloat16),
    ]

    def __init__(self, place, parts, lands, outs, sems, slots):
        self.place, self.parts, self.outs = place, parts, outs
        self.sem1, self.sem2, self.sem3, self.sem4, self.load_sems = sems
        self.slots, self.fins = slots
        self.land1, self.land2, self.land3 = ([lands[3 * t + i] for t in range(4)] for i in range(3))

    def slot(self, t, i):
        return self.slots.at[i, pl.ds(0, SIZES[t])]

    def fin(self, t):
        return self.fins.at[t, pl.ds(0, SIZES[t])]

    def piece(self, t, zz, x, y):
        ref = self.parts[t]
        if t == 0:
            return ref.at[2 * zz + x, pl.ds(pl.multiple_of(64 * y, 16), 80)]
        if t == 3:
            return ref.at[zz, 2 * y + x]
        return ref.at[zz, :, pl.ds(pl.multiple_of((2 * y + x) * WIDTH, 128), WIDTH)]

    def half(self, t, zz, x, y, j):
        return self.piece(t, zz, x, j) if zz < 2 else self.piece(t, zz, j, y)

    def keep(self, zz):
        return self.place.y if zz < 2 else self.place.x

    def first(self, t, zz, j):
        p = self.place
        device = p.at(x=1 - p.x) if zz < 2 else p.at(y=1 - p.y)
        sems = self.sem1.at[t, zz, j]
        src = self.half(t, zz, 1 - p.x, 1 - p.y, j)
        return remote(src, self.land1[t].at[zz, j], sems.at[0], sems.at[1], device)

    def start(self, t, zzs=ORDER):
        for zz in zzs:
            for j in (0, 1):
                self.first(t, zz, j).start()

    def load(self, t, src, i):
        return pltpu.make_async_copy(src, self.slot(t, i), self.load_sems.at[i])

    def second(self, t, zz):
        p = self.place
        device = p.at(y=1 - p.y) if zz < 2 else p.at(x=1 - p.x)
        sems = self.sem2.at[t, zz]
        return remote(self.slot(t, 2 * zz), self.land2[t].at[zz], sems.at[0], sems.at[1], device)

    def pass_on(self, t, after=None):
        p = self.place
        if after is not None:
            for zz in ORDER:
                self.second(after, zz).wait_send()

        def own(zz):
            return self.load(t, self.half(t, zz, p.x, p.y, 1 - self.keep(zz)), 2 * zz)

        def landed(zz):
            return self.load(t, self.land1[t].at[zz, 1 - self.keep(zz)], 2 * zz + 1)

        for zz in ORDER:
            own(zz).start()
        for zz in ORDER:
            for j in (0, 1):
                self.first(t, zz, j).wait_recv()
            landed(zz).start()
        for zz in ORDER:
            own(zz).wait()
            landed(zz).wait()
            add_into(self.slot(t, 2 * zz), self.slot(t, 2 * zz), self.slot(t, 2 * zz + 1))
            self.second(t, zz).start()

    def third(self, t, zz, slot):
        p = self.place
        return remote(
            self.slot(t, 8 + 3 * zz), self.land3[t].at[slot], self.sem3.at[t, zz, 0], self.sem3.at[t, slot, 1],
            p.at(zz=zz),
        )

    def third_sent(self, t):
        for zz in range(4):
            pl.when(zz != self.place.zz)(lambda zz=zz: self.third(t, zz, self.place.zz).wait_send())

    def to_chip(self, t, after=None):
        p = self.place
        if after is not None:
            self.third_sent(after)

        def load(zz, n):
            keep = self.keep(zz)
            if n == 0:
                src = self.half(t, zz, p.x, p.y, keep)
            else:
                src = self.land1[t].at[zz, keep] if n == 1 else self.land2[t].at[zz]
            return self.load(t, src, 8 + 3 * zz + n)

        for zz in ORDER:
            load(zz, 0).start()
            load(zz, 1).start()
        for zz in ORDER:
            self.second(t, zz).wait_recv()
            load(zz, 2).start()
        for zz in ORDER:
            for n in range(3):
                load(zz, n).wait()
            base = 8 + 3 * zz
            mine = self.slot(t, base)
            add_into(mine, mine, self.slot(t, base + 1), self.slot(t, base + 2))

            @pl.when(zz != p.zz)
            def _():
                self.third(t, zz, p.zz).start()

            @pl.when(zz == p.zz)
            def _():
                add_into(self.fin(t), mine)

    def result(self, t, x, y):
        ref = self.outs[t]
        if KINDS[t] == "cols":
            return ref.at[:, pl.ds(pl.multiple_of((2 * y + x) * WIDTH, 128), WIDTH)]
        if KINDS[t] == "rows":
            return ref.at[pl.ds(pl.multiple_of((2 * y + x) * PART, 16), PART)]
        low, size = (0, 80) if y == 0 else (80, 64)
        return ref.at[pl.ds(pl.multiple_of(x * PART + low, 16), size)]

    def fin_part(self, t, y):
        if KINDS[t] != "half" or y == 0:
            return self.fin(t)
        return self.fins.at[t, pl.ds(16, 64)]

    def each_y(self, t, run):
        if KINDS[t] != "half":
            run(self.place.y)
            return
        for value in (0, 1):
            pl.when(self.place.y == value)(lambda value=value: run(value))

    def share(self, t, y, k):
        p = self.place
        sems = self.sem4.at[t, k]
        if k == 1:
            src, dst, device = self.fin_part(t, y), self.result(t, p.x, y), p.at(x=1 - p.x)
        elif k == 2:
            src, dst, device = self.fin_part(t, y), self.result(t, p.x, y), p.at(y=1 - p.y)
        elif t % 2 == 0:
            src = dst = self.result(t, 1 - p.x, y)
            device = p.at(y=1 - p.y)
        else:
            src = dst = self.result(t, p.x, 1 - y)
            device = p.at(x=1 - p.x)
        return remote(src, dst, sems.at[0], sems.at[1], device)

    def arrived(self, t, y, k):
        p = self.place
        ref = self.result(t, 1 - p.x if k & 1 else p.x, 1 - y if k & 2 else y)
        sems = self.sem4.at[t, k]
        return remote(ref, ref, sems.at[0], sems.at[1], p.at())

    def spread(self, t):
        def run(y):
            for k in (1, 2):
                self.share(t, y, k).start()
            pltpu.make_async_copy(self.fin_part(t, y), self.result(t, self.place.x, y), self.sem4.at[t, 0, 0]).start()

        self.each_y(t, run)

    def spread_on(self, t):
        def run(y):
            self.arrived(t, y, 1 if t % 2 == 0 else 2).wait_recv()
            self.share(t, y, 3).start()

        self.each_y(t, run)

    def finish(self, t):
        p = self.place
        for k in (1, 2, 3):
            ref = self.land3[t].at[p.other(k)]
            remote(ref, ref, self.sem3.at[t, p.zz, 0], self.sem3.at[t, p.other(k), 1], p.at()).wait_recv()
            self.load(t, ref, 19 + k).start()
        for k in (1, 2, 3):
            self.load(t, self.land3[t].at[p.other(k)], 19 + k).wait()
        add_into(self.fin(t), self.fin(t), *[self.slot(t, 19 + k) for k in (1, 2, 3)])
        self.spread(t)

    def done(self, t, last):
        p = self.place
        for zz in range(4):
            for j in (0, 1):
                self.first(t, zz, j).wait_send()
            if last:
                self.second(t, zz).wait_send()
        if last:
            self.third_sent(t)

        def run(y):
            self.arrived(t, y, 2 if t % 2 == 0 else 1).wait_recv()
            self.arrived(t, y, 3).wait_recv()
            for k in (1, 2, 3):
                self.share(t, y, k).wait_send()
            pltpu.make_async_copy(self.fin_part(t, y), self.result(t, self.place.x, y), self.sem4.at[t, 0, 0]).wait()

        self.each_y(t, run)


class Vectors:
    SCRATCH = [
        pltpu.VMEM((8, *SMALL), jnp.float32),
        pltpu.VMEM((4, *SMALL), jnp.float32),
        pltpu.VMEM((4, *SMALL), jnp.float32),
        pltpu.VMEM((4, *SMALL), jnp.float32),
        pltpu.VMEM((4, *SMALL), jnp.float32),
        pltpu.VMEM((4, *SMALL), jnp.float32),
        pltpu.VMEM((COND, WIDTH), jnp.float32),
        pltpu.VMEM((COND, WIDTH), jnp.float32),
        pltpu.VMEM((COND, WIDTH), jnp.float32),
        pltpu.VMEM((4, COND, WIDTH), jnp.float32),
        pltpu.SemaphoreType.DMA((16, 2)),
    ]

    def __init__(self, place, small_out, cond_out, scratch):
        self.place, self.small_out, self.cond_out = place, small_out, cond_out
        self.part, self.pair, self.x_in, self.sum1, self.y_in, self.z_in = scratch[:6]
        self.mine, self.cond_pair, self.cond_sum, self.cond_in = scratch[6:10]
        self.sems = scratch[10]

    def copy(self, i, src, dst, device):
        return remote(src, dst, self.sems.at[i, 0], self.sems.at[i, 1], device)

    def small_pair(self, zz):
        p = self.place
        return self.copy(zz, self.part.at[2 * zz + 1 - p.c], self.pair.at[zz], p.at(c=1 - p.c))

    def pair_start(self):
        for zz in range(4):
            self.small_pair(zz).start()
        self.cond_pair_copy().start()

    def cond_pair_copy(self):
        return self.copy(4, self.mine, self.cond_pair, self.place.at(c=1 - self.place.c))

    def pair_end(self):
        p = self.place
        for zz in range(4):
            self.small_pair(zz).wait()
            self.pair[zz] += self.part[2 * zz + p.c]
        self.cond_pair_copy().wait()
        self.cond_sum[...] = self.mine[...] + self.cond_pair[...]
        self.copy(5, self.pair, self.x_in, p.at(x=1 - p.x)).start()
        for k in (1, 2, 3):
            self.copy(6 + k, self.cond_sum, self.cond_in.at[p.zz], p.at(zz=p.other(k))).start()
        self.cond_in[p.zz] = self.cond_sum[...]

    def run_x(self):
        p = self.place
        self.copy(5, self.pair, self.x_in, p.at(x=1 - p.x)).wait()
        self.sum1[...] = self.pair[...] + self.x_in[...]
        self.copy(6, self.sum1, self.y_in, p.at(y=1 - p.y)).start()

    def run_y(self):
        p = self.place
        self.copy(6, self.sum1, self.y_in, p.at(y=1 - p.y)).wait()
        self.sum1[...] += self.y_in[...]
        for k in (1, 2, 3):
            self.copy(9 + k, self.sum1.at[p.other(k)], self.z_in.at[p.zz], p.at(zz=p.other(k))).start()
        self.z_in[p.zz] = self.sum1[p.zz]

    def run_z(self):
        p = self.place
        for k in (1, 2, 3):
            self.copy(9 + k, self.sum1.at[p.other(k)], self.z_in.at[p.zz], p.at(zz=p.other(k))).wait()
            self.copy(6 + k, self.cond_sum, self.cond_in.at[p.zz], p.at(zz=p.other(k))).wait()
        self.small_out[...] = (self.z_in[0] + self.z_in[1]) + (self.z_in[2] + self.z_in[3])
        cond = (self.cond_in[0] + self.cond_in[1]) + (self.cond_in[2] + self.cond_in[3])
        self.cond_out[...] = cond.astype(jnp.bfloat16)


BACK_IN = dict(
    hidden_t=ANY, slope=ANY, cot=ANY, second_t=ANY, second_unit=ANY, att_t=ANY, q=ANY, k=ANY, v=ANY, o=ANY, logsum=ANY,
    first_t=ANY, first_unit=ANY, joined_t=ANY, w_skip=ANY, w_joint=ANY, w_up=ANY, w_down=ANY, cond_t=ANY,
    second_rstd=IN_VMEM, first_rstd=IN_VMEM, vectors=IN_VMEM, cond_unit=IN_VMEM, cond_rstd=IN_VMEM, extra=IN_SMEM,
)
BACK_OUT = dict(
    d_latents=hbm((TOK, WIDTH)),
    d_skip=hbm((TOK, WIDTH)),
    g_skip=hbm((2 * PART, WIDTH)),
    g_joint=hbm((PART, 4 * WIDTH)),
    g_up=hbm((PART, 4 * WIDTH)),
    g_down=hbm((4 * PART, WIDTH)),
    hidden_t2=hbm((4, 4, PART, TOK)),
    second_t2=hbm((4, PART, TOK)),
    att_t2=hbm((4, PART, TOK)),
    first_t2=hbm((4, PART, TOK)),
    joined_t2=hbm((4, 2 * PART, TOK)),
)
BACK_SCRATCH = dict(
    cot_v=pltpu.VMEM((TOK, WIDTH), jnp.bfloat16),
    cot2=pltpu.VMEM((TOK, WIDTH), jnp.bfloat16),
    wide=pltpu.VMEM((4, TOK, WIDTH), jnp.bfloat16),
    before2=pltpu.VMEM((4, TOK, WIDTH), jnp.bfloat16),
    triple2=pltpu.VMEM((3, TOK, WIDTH), jnp.bfloat16),
    branch=pltpu.VMEM((TOK, WIDTH), jnp.bfloat16),
    branch2=pltpu.VMEM((TOK, WIDTH), jnp.bfloat16),
    base_g=pltpu.VMEM((TOK, WIDTH), jnp.bfloat16),
    base2=pltpu.VMEM((TOK, WIDTH), jnp.bfloat16),
    acc=pltpu.VMEM((TOK, WIDTH), jnp.float32),
    d_middle=pltpu.VMEM((TOK, WIDTH), jnp.float32),
    tile=pltpu.VMEM((TOK, WIDTH), jnp.bfloat16),
    weight=pltpu.VMEM((2, 8, PART, WIDTH), jnp.bfloat16),
    left=pltpu.VMEM((2, 2, 4, PART, TOK), jnp.bfloat16),
    made=pltpu.VMEM((2, 4, PART, WIDTH), jnp.bfloat16),
    heads_g=pltpu.VMEM((HEADS, TOK, HEAD), jnp.bfloat16),
    qh=pltpu.VMEM((GROUP, TOK, HEAD), jnp.bfloat16),
    oh=pltpu.VMEM((GROUP, TOK, HEAD), jnp.bfloat16),
    kh=pltpu.VMEM((GROUP, HALO + TOK + COND, HEAD), jnp.bfloat16),
    vh=pltpu.VMEM((GROUP, HALO + TOK + COND, HEAD), jnp.bfloat16),
    lh=pltpu.VMEM((GROUP, TOK, 1), jnp.float32),
    sum_k=pltpu.VMEM((HALO + TOK + COND, HEAD), jnp.float32),
    sum_v=pltpu.VMEM((HALO + TOK + COND, HEAD), jnp.float32),
    bias=pltpu.VMEM((TOK, HALO + TOK + COND), jnp.float32),
    halo2=pltpu.VMEM((2, HALO, WIDTH), jnp.bfloat16),
    d_cond=pltpu.VMEM((128, 2 * WIDTH), jnp.bfloat16),
    cond_left=pltpu.VMEM((4, PART, 128), jnp.bfloat16),
    sums=pltpu.VMEM((16, WIDTH), jnp.float32),
    wide_sum=pltpu.VMEM((4, 1, WIDTH), jnp.float32),
    w_sems=pltpu.SemaphoreType.DMA((2,)),
    l_sems=pltpu.SemaphoreType.DMA((2, 8)),
    m_sems=pltpu.SemaphoreType.DMA((2,)),
    t_sems=pltpu.SemaphoreType.DMA((8,)),
    sib_sems=pltpu.SemaphoreType.DMA((34, 2)),
)
SUM_SKIP, SUM_GAIN1, SUM_SHIFT1, SUM_OUT, SUM_GAIN2, SUM_SHIFT2, SUM_DOWN, SUM_UP = range(8)


def back_kernel(*refs):
    cuts = [len(BACK_IN), len(BACK_OUT), 2, len(Sum.PARTS), len(Sum.LANDS), len(BACK_SCRATCH), len(Sum.SEMS), 2]
    pieces, at = [], 0
    for cut in cuts:
        pieces.append(refs[at : at + cut])
        at += cut
    i, o, b = Names(BACK_IN, pieces[0]), Names(BACK_OUT, pieces[1]), Names(BACK_SCRATCH, pieces[5])
    p = Place()
    total = Sum(p, pieces[3], pieces[4], (o.g_skip, o.g_joint, o.g_up, o.g_down), pieces[6], pieces[7])
    vectors = Vectors(p, *pieces[2], refs[at:])
    f32, bf16 = jnp.float32, jnp.bfloat16

    def copy(src, dst, sem):
        return pltpu.make_async_copy(src, dst, sem)

    def sib(n, src, dst):
        return remote(src, dst, b.sib_sems.at[n, 0], b.sib_sems.at[n, 1], p.at(c=1 - p.c))

    def halves(n, src, dst):
        return [sib(4 * n + zz, src.at[2 * zz + 1 - p.c], dst.at[zz]) for zz in range(4)]

    left_pairs = (
        (i.hidden_t, o.hidden_t2), (i.second_t, o.second_t2), (i.att_t, o.att_t2), (i.first_t, o.first_t2),
        (i.joined_t, o.joined_t2),
    )

    def column(ref, q):
        return ref.at[:, :, pl.ds(q * WIDTH, WIDTH)]

    blocks = [i.w_down.at[pl.ds(8 * q, 8)] for q in range(4)]
    blocks += [column(i.w_up, q) for q in range(4)]
    blocks += [column(i.w_joint, q) for q in (3, 0, 1, 2)]
    blocks += [i.w_skip.at[pl.ds(8 * n, 8)] for n in range(2)]

    def load_weight(n):
        return copy(blocks[n], b.weight.at[n % 2], b.w_sems.at[n % 2])

    def stream(start, count, body):
        for n in range(start, start + count):
            if n + 1 < len(blocks):
                load_weight(n + 1).start()
            load_weight(n).wait()
            body(n - start, b.weight[n % 2].reshape(WIDTH, WIDTH))

    def by_rows(size, body):
        @pl.loop(0, TOK // size)
        def _(n):
            body(pl.ds(pl.multiple_of(n * size, size), size))

    def add_sum(row, value):
        b.sums[row : row + 1, :] += value

    def colsum(value):
        return jnp.sum(value, axis=0, keepdims=True)

    def form(n, dst, own, own2, pairs, extra=None):
        result = nn(own.reshape(4 * PART, TOK), pairs[0]) + nn(own2.reshape(4 * PART, TOK), pairs[1])
        if extra is not None:
            result += extra
        slot = n % 2
        b.made[slot] = result.astype(bf16).reshape(4, PART, WIDTH)
        copy(b.made.at[slot], dst, b.m_sems.at[slot]).start()

    def formed(n, dst):
        copy(b.made.at[n % 2], dst, b.m_sems.at[n % 2]).wait()

    def send_all(copies):
        for one in copies:
            one.start()

    def recv_all(copies):
        for one in copies:
            one.wait_recv()

    def left_copies(n):
        own, other = b.left.at[n % 2, 0], b.left.at[n % 2, 1]
        sems = b.l_sems.at[n % 2]
        if n < 4:
            zz = ORDER[n]
            pairs = [(i.hidden_t.at[2 * zz + p.c], own), (o.hidden_t2.at[zz], other)]
        elif n < 7:
            src, src2 = left_pairs[n - 3]
            pairs = [(src.at[2 * zz + p.c], own.at[zz]) for zz in range(4)] + [(src2, other)]
        else:
            pairs = []
            for k in range(4):
                zz, rows = 2 * (n - 7) + k // 2, pl.ds((k % 2) * PART, PART)
                pairs.append((i.joined_t.at[2 * zz + p.c, rows], own.at[k]))
                pairs.append((o.joined_t2.at[zz, rows], other.at[k]))
        return [copy(src, dst, sems.at[m]) for m, (src, dst) in enumerate(pairs)]

    def left_start(n):
        if n < 4:
            left_sends[0][ORDER[n]].wait_recv()
        elif n < 7:
            recv_all(left_sends[n - 3])
        else:
            recv_all(left_sends[4][2 * (n - 7) : 2 * (n - 7) + 2])
        send_all(left_copies(n))

    def left_done(n):
        for one in left_copies(n):
            one.wait()
        return b.left[n % 2, 0], b.left[n % 2, 1]

    cot_load = copy(i.cot, b.cot_v, b.t_sems.at[0])
    cot_load.start()
    load_weight(0).start()
    greet(p)
    sib_cot = sib(20, i.cot, b.cot2)
    left_sends = [halves(n, src, dst) for n, (src, dst) in enumerate(left_pairs)]
    send_all([left_sends[0][zz] for zz in ORDER])
    sib_cot.start()
    b.sums[...] = jnp.zeros_like(b.sums)
    b.d_cond[2 * COND :] = jnp.zeros((128 - 2 * COND, 2 * WIDTH), bf16)
    vectors.part[...] = jnp.zeros_like(vectors.part)
    make_bias(i.extra, p.b, b.bias)
    cot_load.wait()

    def before_sib(q):
        return sib(21 + q, b.wide.at[q], b.before2.at[q])

    def slope_load(q):
        return copy(i.slope.at[:, pl.ds(q * WIDTH, WIDTH)], b.tile, b.t_sems.at[1])

    def do_before(q, weight):
        slope_load(q).start()
        b.acc[...] = nt(b.cot_v[...], weight)
        slope_load(q).wait()
        b.wide_sum[q] = jnp.zeros((1, WIDTH), f32)

        @functools.partial(by_rows, 64)
        def _(rows):
            value = (b.acc[rows] * b.tile[rows].astype(f32)).astype(bf16)
            b.wide[q, rows] = value
            b.wide_sum[q] += colsum(value.astype(f32))

        before_sib(q).start()

    stream(0, 4, do_before)

    for n in (1, 2, 3, 4):
        send_all(left_sends[n])

    sib_cot.wait_recv()
    down_parts = pieces[3][3]
    left_start(0)
    for n, zz in enumerate(ORDER):
        left_start(n + 1)
        form(n, down_parts.at[zz], *left_done(n), (b.cot_v[...], b.cot2[...]))
        if n > 0:
            formed(n - 1, down_parts.at[ORDER[n - 1]])
            total.start(3, (ORDER[n - 1],))

    up_parts = pieces[3][2]
    lefts = left_done(4)
    for q in range(4):
        before_sib(q).wait_recv()
        form(q, column(up_parts, q), *lefts, (b.wide[q], b.before2[q]))
        if q == 0:
            formed(3, down_parts.at[ORDER[3]])
            total.start(3, (ORDER[3],))
        else:
            formed(q - 1, column(up_parts, q - 1))
    left_start(5)

    def do_second(q, weight):
        value = nt(b.wide[q], weight)
        if q == 0:
            b.acc[...] = value
        else:
            b.acc[...] += value

    unit_load = copy(i.second_unit, b.tile, b.t_sems.at[1])
    unit_load.start()
    stream(4, 4, do_second)
    unit_load.wait()
    formed(3, column(up_parts, 3))

    def norm_rows(unit, rstd, gain, grad, gain_row, shift_row):
        scaled = grad * gain
        mean1 = jnp.mean(scaled, axis=1, keepdims=True)
        mean2 = jnp.mean(scaled * unit, axis=1, keepdims=True)
        add_sum(gain_row, colsum(grad * unit))
        add_sum(shift_row, colsum(grad))
        return rstd * (scaled - mean1 - unit * mean2)

    @functools.partial(by_rows, 64)
    def _(rows):
        unit = b.tile[rows].astype(f32)
        back = norm_rows(unit, i.second_rstd[rows], i.vectors[4:5], b.acc[rows], SUM_GAIN2, SUM_SHIFT2)
        g = b.cot_v[rows].astype(f32)
        middle = g + back
        b.d_middle[rows] = middle
        low = middle.astype(bf16)
        b.branch[rows] = low
        add_sum(SUM_OUT, colsum(low.astype(f32)))
        add_sum(SUM_DOWN, colsum(g))

    branch_sib = sib(25, b.branch, b.branch2)
    branch_sib.start()
    total.pass_on(3)
    total.start(2)

    def do_attended(_, weight):
        b.tile[...] = nt(b.branch[...], weight).astype(bf16)
        for h in range(HEADS):
            b.heads_g[h] = b.tile[:, head(h)]

    stream(8, 1, do_attended)

    joint_parts = pieces[3][1]
    lefts = left_done(5)
    left_start(6)
    branch_sib.wait_recv()
    form(0, column(joint_parts, 3), *lefts, (b.branch[...], b.branch2[...]))

    formed(0, column(joint_parts, 3))
    for q in range(4):
        before_sib(q).wait_send()

    def halo_copy(n, device):
        low, size = ((0, 512), (512, 256), (768, 384))[n]
        columns = pl.ds(low, size)
        src = b.before2.at[pl.ds(0, 2), pl.ds(0, HALO), columns]
        sems = b.sib_sems.at[31 + n]
        return remote(src, b.halo2.at[:, :, columns], sems.at[0], sems.at[1], device)

    def halo_start(n):
        pl.when(p.b > 0)(lambda: halo_copy(n, (p.s, p.b - 1)).start())

    scale = HEAD**-0.5
    n_keys = HALO + TOK + COND

    def group_loads(start):
        hs = pl.ds(start, GROUP)
        pairs = ((i.q, b.qh), (i.o, b.oh), (i.k, b.kh), (i.v, b.vh), (i.logsum, b.lh))
        return [copy(src.at[hs], dst, b.t_sems.at[n]) for n, (src, dst) in enumerate(pairs)]

    def group(start):
        send_all(group_loads(start))
        for one in group_loads(start):
            one.wait()

        @pl.loop(0, GROUP)
        def _(h):
            for row, low in TILES:
                rows, keys = pl.ds(row, 256), pl.ds(low, n_keys - low)
                q, k, v, g = b.qh[h, rows], b.kh[h, keys], b.vh[h, keys], b.heads_g[start + h, rows]
                scores = nt(q, k) * (scale * LOG2E) + b.bias[rows, keys]
                probs = jnp.exp2(scores - b.lh[h, rows])
                d_probs = nt(g, v)
                inner = jnp.sum(g.astype(f32) * b.oh[h, rows].astype(f32), axis=1, keepdims=True)
                d_scores = (probs * (d_probs - inner)).astype(bf16)
                d_k, d_v = tn(d_scores, q), tn(probs.astype(bf16), g)
                if row == 0:
                    b.sum_k[...] = d_k
                    b.sum_v[...] = d_v
                else:
                    b.sum_k[keys] += d_k
                    b.sum_v[keys] += d_v
                b.oh[h, rows] = (nn(d_scores, k) * scale).astype(bf16)
            b.kh[h] = (b.sum_k[...] * scale).astype(bf16)
            b.vh[h] = b.sum_v[...].astype(bf16)

        for n in range(GROUP):
            at = head(start + n)
            b.wide[0, :, at] = b.oh[n]
            for j, made in ((0, b.kh), (1, b.vh)):
                wide = slice(j * WIDTH + at.start, j * WIDTH + at.stop)
                b.before2[j, 0:HALO, at] = made[n, 0:HALO]
                b.wide[1 + j, :, at] = made[n, HALO : HALO + TOK]
                b.d_cond[0:COND, wide] = made[n, HALO + TOK :]

    group(0)
    group(4)
    halo_start(0)
    group(8)
    halo_start(1)
    group(12)
    halo_start(2)

    cond_sib = sib(30, b.d_cond.at[pl.ds(0, COND)], b.d_cond.at[pl.ds(COND, COND)])
    cond_sib.start()

    def triple_sib(j):
        return sib(26 + j, b.wide.at[j], b.triple2.at[j])

    triple_sib(0).start()
    for zz in range(4):
        copy(i.cond_t.at[2 * zz + p.c], b.cond_left.at[zz], b.t_sems.at[4 + zz]).start()
    unit_load = copy(i.first_unit, b.tile, b.t_sems.at[1])
    unit_load.start()

    def do_first(j, weight):
        if j == 1:
            merge_halo()
        value = nt(b.wide[j], weight)
        if j == 0:
            b.acc[...] = value
        else:
            b.acc[...] += value
            cond = nt(b.d_cond[0:COND, (j - 1) * WIDTH : j * WIDTH], weight)
            if j == 1:
                vectors.mine[...] = cond
            else:
                vectors.mine[...] += cond

    def merge_halo():
        @pl.when(p.b < 7)
        def _():
            for n in range(3):
                halo_copy(n, (p.s, p.b)).wait_recv()

            @pl.loop(0, HALO // 64)
            def _(n):
                low = pl.ds(pl.multiple_of(n * 64, 64), 64)
                rows = pl.ds(pl.multiple_of(n * 64 + TOK - HALO, 64), 64)
                for j in (0, 1):
                    extra = b.halo2[j, low].astype(f32)
                    b.wide[1 + j, rows] = (b.wide[1 + j, rows].astype(f32) + extra).astype(bf16)

        triple_sib(1).start()
        triple_sib(2).start()

    total.pass_on(2, after=3)
    stream(9, 3, do_first)
    total.to_chip(3)
    unit_load.wait()

    @functools.partial(by_rows, 64)
    def _(rows):
        unit = b.tile[rows].astype(f32)
        back = norm_rows(unit, i.first_rstd[rows], i.vectors[1:2], b.acc[rows], SUM_GAIN1, SUM_SHIFT1)
        low = (b.d_middle[rows] + back).astype(bf16)
        b.base_g[rows] = low
        add_sum(SUM_SKIP, colsum(low.astype(f32)))

    base_sib = sib(29, b.base_g, b.base2)
    base_sib.start()
    for zz in range(4):
        copy(i.cond_t.at[2 * zz + p.c], b.cond_left.at[zz], b.t_sems.at[4 + zz]).wait()
    cond_sib.wait_recv()

    lefts = left_done(6)
    left_start(7)
    for j in range(3):
        triple_sib(j).wait_recv()
        extra = None
        if j > 0:
            extra = nn(b.cond_left[...].reshape(4 * PART, 128), b.d_cond[:, (j - 1) * WIDTH : j * WIDTH])
        form(j, column(joint_parts, j), *lefts, (b.wide[j], b.triple2[j]), extra)
        if j > 0:
            formed(j - 1, column(joint_parts, j - 1))
    formed(2, column(joint_parts, 2))
    total.start(1)
    vectors.mine[...] = norm_rows(
        i.cond_unit[...], i.cond_rstd[...], i.vectors[1:2], vectors.mine[...], SUM_GAIN1, SUM_SHIFT1
    )
    for row in range(7):
        for n in range(8):
            vectors.part[n, row : row + 1, 0:PART] = b.sums[row : row + 1, n * PART : (n + 1) * PART]
    for n in range(32):
        row, low = 7 + n % 4, n % 8 * PART
        vectors.part[n // 4, row : row + 1, 0:PART] = b.wide_sum[n // 8, :, low : low + PART]
    vectors.pair_start()

    skip_parts = pieces[3][0]
    base_sib.wait_recv()
    for n in (0, 1):
        lefts = left_done(7 + n)
        if n == 0:
            left_start(8)
        form(n, skip_parts.at[pl.ds(4 * n, 4)], *lefts, (b.base_g[...], b.base2[...]))
    vectors.pair_end()
    total.to_chip(2, after=3)
    for n in (0, 1):
        formed(n, skip_parts.at[pl.ds(4 * n, 4)])

    def do_joined(n, weight):
        made = (b.tile, b.branch)[n]
        made[...] = nt(b.base_g[...], weight).astype(bf16)
        copy(made, (o.d_latents, o.d_skip)[n], b.t_sems.at[n]).start()

    branch_sib.wait_send()
    stream(12, 2, do_joined)
    vectors.run_x()
    total.finish(3)

    total.pass_on(1, after=2)
    total.start(0)
    total.spread_on(3)
    vectors.run_y()
    total.finish(2)
    total.to_chip(1, after=2)
    total.pass_on(0, after=1)
    total.spread_on(2)
    total.finish(1)
    total.to_chip(0, after=1)
    total.spread_on(1)
    total.finish(0)
    total.spread_on(0)
    vectors.run_z()
    for n in (0, 1):
        copy((b.tile, b.branch)[n], (o.d_latents, o.d_skip)[n], b.t_sems.at[n]).wait()
    for group_sends in left_sends:
        for one in group_sends:
            one.wait_send()
    for one in (sib_cot, cond_sib, base_sib, triple_sib(0), triple_sib(1), triple_sib(2)):
        one.wait_send()
    for n in range(3):
        pl.when(p.b > 0)(lambda n=n: halo_copy(n, (p.s, p.b - 1)).wait_send())
    for t in (3, 2, 1, 0):
        total.done(t, t == 0)


def backward(arrays):
    vm = pl.BlockSpec(memory_space=pltpu.VMEM)
    outs = pl.pallas_call(
        back_kernel,
        out_shape=[*BACK_OUT.values()] + [
            jax.ShapeDtypeStruct(SMALL, jnp.float32), jax.ShapeDtypeStruct((COND, WIDTH), jnp.bfloat16)
        ] + Sum.PARTS + Sum.LANDS,
        in_specs=[*BACK_IN.values()],
        out_specs=[ANY] * len(BACK_OUT) + [vm] * 2 + [ANY] * (len(Sum.PARTS) + len(Sum.LANDS)),
        scratch_shapes=[*BACK_SCRATCH.values()] + Sum.SEMS + Sum.SLOTS + Vectors.SCRATCH,
        compiler_params=pltpu.CompilerParams(collective_id=1, has_side_effects=True, vmem_limit_bytes=60 << 20),
    )(*[arrays[name] for name in BACK_IN])
    named = Names(BACK_OUT, outs[: len(BACK_OUT)])
    return named, outs[len(BACK_OUT)], outs[len(BACK_OUT) + 1]


def item_ends(extra_length):
    lengths = extra_length[0] + (LEN_MIN - 1)
    count = lengths.shape[0]
    upto = lax.iota(jnp.int32, count)[None, :] <= lax.iota(jnp.int32, count)[:, None]
    return jnp.sum(jnp.where(upto, lengths[None, :], 0), axis=1)


def quick(
    latents, skip_input, cond_tokens, extra_length, skip_weight, skip_bias, first_gain, first_shift, joint_weight,
    out_weight, out_bias, second_gain, second_shift, up_weight, up_bias, down_weight, down_bias, cotangent,
):
    arrays = dict(
        skip_bias=skip_bias,
        first_gain=first_gain,
        first_shift=first_shift,
        out_bias=out_bias,
        second_gain=second_gain,
        second_shift=second_shift,
        down_bias=down_bias,
        up_bias=up_bias,
        extra=extra_length,
        cond=cond_tokens,
        latents=latents,
        skip_input=skip_input,
        skip=skip_weight.reshape(2, PART, WIDTH),
        joint=joint_weight,
        out=out_weight,
        up=up_weight,
        down=down_weight.reshape(4, PART, WIDTH),
        cot=cotangent,
    )
    made = forward(arrays)
    grads, sums, cond_sum = backward({**arrays, **made})
    return settle(made["output"], grads, sums, cond_sum)


SETTLE_STEPS = 3


def settle_kernel(output, d_latents, d_skip, g_skip, g_joint, g_up, g_down, sums, cond, *outs):
    f32 = jnp.float32
    for src, dst in zip((output, d_latents, d_skip), outs[:3]):
        dst[...] = src[...]
    outs[4][...] = g_skip[...].astype(f32)
    outs[8][...] = g_joint[:, : 3 * WIDTH].astype(f32)
    outs[9][...] = g_joint[:, 3 * WIDTH :].astype(f32)
    outs[13][...] = g_up[...].astype(f32)
    outs[15][...] = g_down[...].astype(f32)

    @pl.when(pl.program_id(0) == 0)
    def _():
        pairs = cond[...].astype(f32)
        for n in range(COND // 2):
            outs[3][n] = pairs[2 * n : 2 * n + 2].astype(jnp.bfloat16)
        for row, n in enumerate((5, 6, 7, 10, 11, 12, 16)):
            outs[n][...] = sums[row : row + 1, 0:PART].reshape(PART)
        wide = jnp.concatenate([sums[7 + n : 8 + n, 0:PART] for n in range(4)], axis=1)
        outs[14][...] = wide.reshape(4 * PART)


def settle(output, grads, sums, cond):
    f32, bf16 = jnp.float32, jnp.bfloat16

    def columns(shape, dtype):
        spec = pl.BlockSpec((shape[0], shape[1] // SETTLE_STEPS), lambda n: (0, n))
        return spec, jax.ShapeDtypeStruct(shape, dtype)

    def rows(shape, dtype):
        spec = pl.BlockSpec((shape[0] // SETTLE_STEPS, shape[1]), lambda n: (n, 0))
        return spec, jax.ShapeDtypeStruct(shape, dtype)

    def whole(shape, dtype):
        spec = pl.BlockSpec(shape, lambda n: (0,) * len(shape))
        return spec, jax.ShapeDtypeStruct(shape, dtype)

    token, few = columns((TOK, WIDTH), bf16), whole((PART,), f32)
    outs = [
        token, token, token, whole((COND // 2, 2, WIDTH), bf16), rows((2 * PART, WIDTH), f32), few, few, few,
        rows((PART, 3 * WIDTH), f32), rows((PART, WIDTH), f32), few, few, few, rows((PART, 4 * WIDTH), f32),
        whole((4 * PART,), f32), rows((4 * PART, WIDTH), f32), few,
    ]
    ins = [
        token, token, token, rows((2 * PART, WIDTH), bf16), rows((PART, 4 * WIDTH), bf16), rows((PART, 4 * WIDTH), bf16),
        rows((4 * PART, WIDTH), bf16), whole(SMALL, f32), whole((COND, WIDTH), bf16),
    ]
    return tuple(
        pl.pallas_call(
            settle_kernel,
            grid=(SETTLE_STEPS,),
            out_shape=[shape for _, shape in outs],
            in_specs=[spec for spec, _ in ins],
            out_specs=[spec for spec, _ in outs],
            compiler_params=pltpu.CompilerParams(vmem_limit_bytes=60 << 20),
        )(
            output, grads.d_latents, grads.d_skip, grads.g_skip, grads.g_joint, grads.g_up, grads.g_down, sums, cond,
        )
    )


def shifted(value, axis, steps):
    count = lax.axis_size(axis)
    leading, last = (max(0, -steps), min(count, count - steps))
    return lax.ppermute(value, axis, [(source, source + steps) for source in range(leading, last)])


def layer_norm(values, gain, shift):
    center = values - jnp.mean(values, axis=-1, keepdims=True)
    spread = jnp.mean(center * center, axis=-1, keepdims=True)
    return center * lax.rsqrt(spread + 1e-05) * gain + shift


def contract_rows(left, right):
    return lax.dot_general(
        left, right, (((0,), (0,)), ((), ())), preferred_element_type=jnp.float32
    )


def contract_cols(left, right):
    return lax.dot_general(
        left, right, (((1,), (1,)), ((), ())), preferred_element_type=jnp.float32
    )


def segment_ids(ends, places):
    inside = jnp.sum((ends[None, :] <= places[:, None]).astype(jnp.int32), axis=1)
    return jnp.where(places >= 0, inside, -1)


def split_heads(block):
    return block.reshape(block.shape[0], HEADS, HEAD).transpose(1, 0, 2)


def merge_heads(block):
    return block.transpose(1, 0, 2).reshape(block.shape[1], HEADS * HEAD)


def masked_scores(query, keys, allowed):
    scores = contract_cols(query, keys) * HEAD ** (-0.5)
    return jnp.where(allowed, scores, -1e30)


def plain(
    latents,
    skip_input,
    cond_tokens,
    extra_length,
    skip_weight,
    skip_bias,
    first_gain,
    first_shift,
    joint_weight,
    out_weight,
    out_bias,
    second_gain,
    second_shift,
    up_weight,
    up_bias,
    down_weight,
    down_bias,
    cotangent,
):
    whole = (
        lax.all_gather(skip_weight, "blk", axis=0, tiled=True),
        lax.all_gather(skip_bias, "blk", axis=0, tiled=True),
        lax.all_gather(first_gain, "blk", axis=0, tiled=True),
        lax.all_gather(first_shift, "blk", axis=0, tiled=True),
        lax.all_gather(joint_weight, "blk", axis=0, tiled=True),
        lax.all_gather(out_weight, "blk", axis=0, tiled=True),
        lax.all_gather(out_bias, "blk", axis=0, tiled=True),
        lax.all_gather(second_gain, "blk", axis=0, tiled=True),
        lax.all_gather(second_shift, "blk", axis=0, tiled=True),
        lax.all_gather(up_weight, "blk", axis=0, tiled=True),
        lax.all_gather(up_bias, "blk", axis=0, tiled=True),
        lax.all_gather(down_weight, "blk", axis=0, tiled=True),
        lax.all_gather(down_bias, "blk", axis=0, tiled=True),
    )
    (
        skip_matrix,
        skip_offset,
        gain_first,
        shift_first,
        joint_matrix,
        out_matrix,
        out_offset,
        gain_second,
        shift_second,
        up_matrix,
        up_offset,
        down_matrix,
        down_offset,
    ) = whole
    rows = latents.shape[0]
    width = latents.shape[1]
    scale = HEAD ** (-0.5)
    joined = jnp.concatenate([latents, skip_input], 1)
    base = jnp.dot(joined, skip_matrix, preferred_element_type=jnp.float32) + skip_offset
    first_in = layer_norm(base, gain_first, shift_first).astype(jnp.bfloat16)
    triple = jnp.dot(first_in, joint_matrix, preferred_element_type=jnp.float32).astype(
        jnp.bfloat16
    )
    query = triple[:, :width]
    pair_here = triple[:, width:]
    pair_left = shifted(pair_here, "blk", 1)
    cond_flat = cond_tokens.reshape(-1, width).astype(jnp.float32)
    cond_in = layer_norm(cond_flat, gain_first, shift_first).astype(jnp.bfloat16)
    cond_pair = jnp.dot(
        cond_in, joint_matrix[:, width:], preferred_element_type=jnp.float32
    ).astype(jnp.bfloat16)
    pairs = jnp.concatenate([pair_left, pair_here, cond_pair], 0)
    ends = item_ends(extra_length)
    here = lax.axis_index("blk")
    places = here * rows + lax.iota(jnp.int32, rows)
    seg_here = segment_ids(ends, places)
    seg_left = segment_ids(ends, places - rows)
    cond_seg = lax.iota(jnp.int32, cond_pair.shape[0]) // 2
    allowed = seg_here[:, None] == jnp.concatenate([seg_left, seg_here, cond_seg])[None, :]
    head_query = split_heads(query)
    head_key = split_heads(pairs[:, :width])
    head_value = split_heads(pairs[:, width:])

    def head_forward(parts):
        query_one, key_one, value_one = parts
        scores = masked_scores(query_one, key_one, allowed)
        top = jnp.max(scores, axis=1, keepdims=True)
        expo = jnp.exp(scores - top)
        total = jnp.sum(expo, axis=1, keepdims=True)
        probs = (expo / total).astype(jnp.bfloat16)
        mixed = jnp.dot(probs, value_one, preferred_element_type=jnp.float32)
        return (mixed, (top + jnp.log(total))[:, 0])

    mixed, logsum = lax.map(head_forward, (head_query, head_key, head_value))
    attended = merge_heads(mixed).astype(jnp.bfloat16)
    middle = base + jnp.dot(attended, out_matrix, preferred_element_type=jnp.float32) + out_offset
    second_in = layer_norm(middle, gain_second, shift_second).astype(jnp.bfloat16)
    before = jnp.dot(second_in, up_matrix, preferred_element_type=jnp.float32) + up_offset
    hidden = jax.nn.gelu(before, approximate=False).astype(jnp.bfloat16)
    output = middle + jnp.dot(hidden, down_matrix, preferred_element_type=jnp.float32) + down_offset
    again = (
        lax.all_gather(skip_weight, "blk", axis=0, tiled=True),
        lax.all_gather(skip_bias, "blk", axis=0, tiled=True),
        lax.all_gather(first_gain, "blk", axis=0, tiled=True),
        lax.all_gather(first_shift, "blk", axis=0, tiled=True),
        lax.all_gather(joint_weight, "blk", axis=0, tiled=True),
        lax.all_gather(out_weight, "blk", axis=0, tiled=True),
        lax.all_gather(out_bias, "blk", axis=0, tiled=True),
        lax.all_gather(second_gain, "blk", axis=0, tiled=True),
        lax.all_gather(second_shift, "blk", axis=0, tiled=True),
        lax.all_gather(up_weight, "blk", axis=0, tiled=True),
        lax.all_gather(up_bias, "blk", axis=0, tiled=True),
        lax.all_gather(down_weight, "blk", axis=0, tiled=True),
        lax.all_gather(down_bias, "blk", axis=0, tiled=True),
    )
    (
        skip_matrix,
        skip_offset,
        gain_first,
        shift_first,
        joint_matrix,
        out_matrix,
        out_offset,
        gain_second,
        shift_second,
        up_matrix,
        up_offset,
        down_matrix,
        down_offset,
    ) = again
    incoming = cotangent.astype(jnp.float32)
    grad_down_offset = jnp.sum(incoming, axis=0)
    grad_down_matrix = contract_rows(hidden, cotangent)
    d_hidden = contract_cols(cotangent, down_matrix)
    gelu_value, gelu_pull = jax.vjp(partial(jax.nn.gelu, approximate=False), before)
    d_before = gelu_pull(d_hidden)[0].astype(jnp.bfloat16)
    grad_up_offset = jnp.sum(d_before.astype(jnp.float32), axis=0)
    grad_up_matrix = contract_rows(second_in, d_before)
    d_second = contract_cols(d_before, up_matrix)
    norm_value, norm_pull = jax.vjp(
        layer_norm, middle, gain_second.astype(jnp.float32), shift_second.astype(jnp.float32)
    )
    d_middle_norm, grad_gain_second, grad_shift_second = norm_pull(d_second)
    d_middle = incoming + d_middle_norm
    d_branch = d_middle.astype(jnp.bfloat16)
    grad_out_offset = jnp.sum(d_branch.astype(jnp.float32), axis=0)
    grad_out_matrix = contract_rows(attended, d_branch)
    d_attended = contract_cols(d_branch, out_matrix).astype(jnp.bfloat16)

    def head_backward(parts):
        query_one, key_one, value_one, grad_one, logsum_one = parts
        scores = masked_scores(query_one, key_one, allowed)
        probs = jnp.exp(scores - logsum_one[:, None])
        d_probs = contract_cols(grad_one, value_one)
        inner = jnp.sum(probs * d_probs, axis=1, keepdims=True)
        d_scores = (probs * (d_probs - inner)).astype(jnp.bfloat16)
        d_query_one = jnp.dot(d_scores, key_one, preferred_element_type=jnp.float32) * scale
        d_key_one = contract_rows(d_scores, query_one) * scale
        d_value_one = contract_rows(probs.astype(jnp.bfloat16), grad_one)
        return (d_query_one, d_key_one, d_value_one)

    d_query_heads, d_key_heads, d_value_heads = lax.map(
        head_backward, (head_query, head_key, head_value, split_heads(d_attended), logsum)
    )
    d_query = merge_heads(d_query_heads)
    d_pairs = jnp.concatenate([merge_heads(d_key_heads), merge_heads(d_value_heads)], 1)
    d_left = d_pairs[:rows]
    d_own = d_pairs[rows : 2 * rows]
    d_cond_part = d_pairs[2 * rows :]
    d_returned = shifted(d_left.astype(jnp.bfloat16), "blk", -1).astype(d_left.dtype)
    d_cond_total = lax.psum(d_cond_part.astype(jnp.bfloat16), "blk")
    d_triple = jnp.concatenate([d_query, d_own + d_returned], 1).astype(jnp.bfloat16)
    leading = (here == 0).astype(jnp.float32)
    cond_term = contract_rows(cond_in, d_cond_total) * leading
    grad_joint_matrix = contract_rows(first_in, d_triple) + jnp.concatenate(
        [jnp.zeros((width, width), jnp.float32), cond_term], 1
    )
    d_first = contract_cols(d_triple, joint_matrix)
    d_cond_in = contract_cols(d_cond_total, joint_matrix[:, width:])
    first_value, first_pull = jax.vjp(
        layer_norm, base, gain_first.astype(jnp.float32), shift_first.astype(jnp.float32)
    )
    d_base_norm, grad_gain_tokens, grad_shift_tokens = first_pull(d_first)
    cond_value, cond_pull = jax.vjp(
        layer_norm, cond_flat, gain_first.astype(jnp.float32), shift_first.astype(jnp.float32)
    )
    d_cond_flat, grad_gain_cond, grad_shift_cond = cond_pull(d_cond_in)
    grad_gain_first = grad_gain_tokens + leading * grad_gain_cond
    grad_shift_first = grad_shift_tokens + leading * grad_shift_cond
    d_base = (d_middle + d_base_norm).astype(jnp.bfloat16)
    grad_skip_offset = jnp.sum(d_base.astype(jnp.float32), axis=0)
    grad_skip_matrix = contract_rows(joined, d_base)
    d_joined = contract_cols(d_base, skip_matrix)
    shares = (
        lax.psum_scatter(
            grad_skip_matrix.astype(jnp.bfloat16), "blk", scatter_dimension=0, tiled=True
        ).astype(jnp.float32),
        lax.psum_scatter(
            grad_skip_offset.astype(jnp.bfloat16), "blk", scatter_dimension=0, tiled=True
        ).astype(jnp.float32),
        lax.psum_scatter(
            grad_gain_first.astype(jnp.bfloat16), "blk", scatter_dimension=0, tiled=True
        ).astype(jnp.float32),
        lax.psum_scatter(
            grad_shift_first.astype(jnp.bfloat16), "blk", scatter_dimension=0, tiled=True
        ).astype(jnp.float32),
        lax.psum_scatter(
            grad_joint_matrix.astype(jnp.bfloat16), "blk", scatter_dimension=0, tiled=True
        ).astype(jnp.float32),
        lax.psum_scatter(
            grad_out_matrix.astype(jnp.bfloat16), "blk", scatter_dimension=0, tiled=True
        ).astype(jnp.float32),
        lax.psum_scatter(
            grad_out_offset.astype(jnp.bfloat16), "blk", scatter_dimension=0, tiled=True
        ).astype(jnp.float32),
        lax.psum_scatter(
            grad_gain_second.astype(jnp.bfloat16), "blk", scatter_dimension=0, tiled=True
        ).astype(jnp.float32),
        lax.psum_scatter(
            grad_shift_second.astype(jnp.bfloat16), "blk", scatter_dimension=0, tiled=True
        ).astype(jnp.float32),
        lax.psum_scatter(
            grad_up_matrix.astype(jnp.bfloat16), "blk", scatter_dimension=0, tiled=True
        ).astype(jnp.float32),
        lax.psum_scatter(
            grad_up_offset.astype(jnp.bfloat16), "blk", scatter_dimension=0, tiled=True
        ).astype(jnp.float32),
        lax.psum_scatter(
            grad_down_matrix.astype(jnp.bfloat16), "blk", scatter_dimension=0, tiled=True
        ).astype(jnp.float32),
        lax.psum_scatter(
            grad_down_offset.astype(jnp.bfloat16), "blk", scatter_dimension=0, tiled=True
        ).astype(jnp.float32),
    )
    (
        share_skip,
        share_skip_offset,
        share_gain_first,
        share_shift_first,
        share_joint,
        share_out,
        share_out_offset,
        share_gain_second,
        share_shift_second,
        share_up,
        share_up_offset,
        share_down,
        share_down_offset,
    ) = shares
    summed = (
        lax.psum(share_skip.astype(jnp.bfloat16), "stream").astype(jnp.float32),
        lax.psum(share_skip_offset.astype(jnp.bfloat16), "stream").astype(jnp.float32),
        lax.psum(share_gain_first.astype(jnp.bfloat16), "stream").astype(jnp.float32),
        lax.psum(share_shift_first.astype(jnp.bfloat16), "stream").astype(jnp.float32),
        lax.psum(share_joint.astype(jnp.bfloat16), "stream").astype(jnp.float32),
        lax.psum(share_out.astype(jnp.bfloat16), "stream").astype(jnp.float32),
        lax.psum(share_out_offset.astype(jnp.bfloat16), "stream").astype(jnp.float32),
        lax.psum(share_gain_second.astype(jnp.bfloat16), "stream").astype(jnp.float32),
        lax.psum(share_shift_second.astype(jnp.bfloat16), "stream").astype(jnp.float32),
        lax.psum(share_up.astype(jnp.bfloat16), "stream").astype(jnp.float32),
        lax.psum(share_up_offset.astype(jnp.bfloat16), "stream").astype(jnp.float32),
        lax.psum(share_down.astype(jnp.bfloat16), "stream").astype(jnp.float32),
        lax.psum(share_down_offset.astype(jnp.bfloat16), "stream").astype(jnp.float32),
    )
    return (
        output.astype(jnp.bfloat16),
        d_joined[:, :width].astype(jnp.bfloat16),
        d_joined[:, width:].astype(jnp.bfloat16),
        d_cond_flat.reshape(cond_tokens.shape).astype(jnp.bfloat16),
        summed[0],
        summed[1],
        summed[2],
        summed[3],
        summed[4],
        summed[5],
        summed[6],
        summed[7],
        summed[8],
        summed[9],
        summed[10],
        summed[11],
        summed[12],
    )


def solution(mesh):
    placed = (
        P(("stream", "blk"), None),
        P(("stream", "blk"), None),
        P("stream", None, None),
        P("stream", None),
        P("blk", None),
        P("blk"),
        P("blk"),
        P("blk"),
        P("blk", None),
        P("blk", None),
        P("blk"),
        P("blk"),
        P("blk"),
        P("blk", None),
        P("blk"),
        P("blk", None),
        P("blk"),
        P(("stream", "blk"), None),
    )
    fits = mesh.shape["stream"] == 4 and mesh.shape["blk"] == 8
    return jax.shard_map(
        quick if fits else plain,
        mesh=mesh,
        in_specs=placed,
        out_specs=(
            P(("stream", "blk"), None),
            P(("stream", "blk"), None),
            P(("stream", "blk"), None),
            P("stream", None, None),
            P("blk", None),
            P("blk"),
            P("blk"),
            P("blk"),
            P("blk", None),
            P("blk", None),
            P("blk"),
            P("blk"),
            P("blk"),
            P("blk", None),
            P("blk"),
            P("blk", None),
            P("blk"),
        ),
        check_vma=False,
    )
```

```python
import functools
from functools import partial

import jax
import jax.numpy as jnp
from jax import lax
from jax.experimental import pallas as pl
from jax.experimental.pallas import tpu as pltpu
from jax.sharding import PartitionSpec as P

HEADS = 16
HEAD = 72
LEN_MIN = 192

MESH = pl.DeviceIdType.MESH
ANY = pl.BlockSpec(memory_space=pl.ANY)
WIDTH = 1152
PART = 144
SMALL = (16, 256)


class Place:
    def __init__(self):
        self.s = lax.axis_index("stream")
        self.b = lax.axis_index("blk")
        self.x = lax.rem(self.s, 2)
        self.y = lax.div(self.s, 2)
        self.c = lax.rem(self.b, 2)
        self.zz = lax.div(self.b, 2)

    def other(self, k):
        low, high = lax.rem(self.zz, 2), lax.div(self.zz, 2)
        return 2 * (1 - high if k & 2 else high) + (1 - low if k & 1 else low)

    def source(self, k):
        zz = self.zz
        table = ((1, 0, 3, 2), (2, 2, 1, 1), (3, 3, 0, 0))[k - 1]
        return jnp.where(zz < 2, jnp.where(zz == 0, table[0], table[1]), jnp.where(zz == 2, table[2], table[3]))

    def at(self, x=None, y=None, zz=None, c=None):
        x = self.x if x is None else x
        y = self.y if y is None else y
        zz = self.zz if zz is None else zz
        c = self.c if c is None else c
        return (2 * y + x, 2 * zz + c)


def greet(place):
    barrier = pltpu.get_barrier_semaphore()
    p = place
    near = [p.at(x=1 - p.x), p.at(y=1 - p.y), p.at(c=1 - p.c)] + [p.at(zz=p.other(k)) for k in (1, 2, 3)]
    for device in near:
        pl.semaphore_signal(barrier, inc=1, device_id=device, device_id_type=MESH)
    up = (p.c == 1) & (p.zz < 3)
    down = (p.c == 0) & (p.zz > 0)
    for go, device in ((up, (p.s, p.b + 1)), (down, (p.s, p.b - 1))):

        @pl.when(go)
        def _():
            pl.semaphore_signal(barrier, inc=1, device_id=device, device_id_type=MESH)

    pl.when(up | down)(lambda: pl.semaphore_wait(barrier, len(near) + 1))
    pl.when(jnp.logical_not(up | down))(lambda: pl.semaphore_wait(barrier, len(near)))


def remote(src, dst, send, recv, device):
    return pltpu.make_async_remote_copy(
        src_ref=src, dst_ref=dst, send_sem=send, recv_sem=recv, device_id=device, device_id_type=MESH
    )


def block(t, ref, b):
    if t in (1, 2):
        return ref.at[b]
    size = 2 if t == 0 else 4
    return ref.at[pl.ds(b * size, size)]


def piece(t, ref, b, x, y):
    if t in (1, 2):
        return ref.at[b, :, pl.ds(pl.multiple_of((2 * y + x) * WIDTH, 128), WIDTH)]
    if t == 3:
        return ref.at[4 * b + 2 * y + x]
    low, size = (0, 80) if y == 0 else (80, 64)
    return ref.at[2 * b + x, pl.ds(low, size)]


KINDS = ("half", "cols", "cols", "rows")


class Gather:
    SEMS = [pltpu.SemaphoreType.DMA((4, 6, 4, 2)), pltpu.SemaphoreType.DMA((12,)), pltpu.SemaphoreType.DMA((2, 8))]

    def __init__(self, place, shards, outs, scratch):
        self.place = place
        self.small_in, self.skip_in, self.joint_in, self.out_in, self.up_in, self.down_in = shards
        self.small = outs[0]
        self.outs = outs[1:]
        self.sems, self.local_sems, self.small_sems = scratch[:3]
        self.stage = scratch[3:]

    def copy(self, t, x, y, zz, c, stage, k, device):
        ref = piece(t, self.outs[t], 2 * zz + c, x, y)
        return remote(ref, ref, self.sems.at[t, stage, k, 0], self.sems.at[t, stage, k, 1], device)

    def each_y(self, t, run):
        if KINDS[t] != "half":
            run(self.place.y)
            return
        for value in (0, 1):
            pl.when(self.place.y == value)(lambda value=value: run(value))

    STAGE = [
        pltpu.VMEM((2, PART, WIDTH), jnp.bfloat16),
        pltpu.VMEM((PART, 4 * WIDTH), jnp.bfloat16),
        pltpu.VMEM((PART, 4 * WIDTH), jnp.bfloat16),
        pltpu.VMEM((4, PART, WIDTH), jnp.bfloat16),
    ]

    def locals(self, t):
        if t == 1:
            return [
                (self.joint_in, self.stage[1].at[:, pl.ds(0, 3 * WIDTH)]),
                (self.out_in, self.stage[1].at[:, pl.ds(3 * WIDTH, WIDTH)]),
            ]
        return [({0: self.skip_in, 2: self.up_in, 3: self.down_in}[t], self.stage[t])]

    def own_start(self, t):
        for i, (src, dst) in enumerate(self.locals(t)):
            pltpu.make_async_copy(src, dst, self.local_sems.at[2 * t + i]).start()

    def own_keep(self, t):
        return pltpu.make_async_copy(self.stage[t], block(t, self.outs[t], self.place.b), self.local_sems.at[8 + t])

    def own_done(self, t):
        for i, (src, dst) in enumerate(self.locals(t)):
            pltpu.make_async_copy(src, dst, self.local_sems.at[2 * t + i]).wait()
        self.own_keep(t).start()

    def own_copy(self, t, c):
        ref = block(t, self.outs[t], 2 * self.place.zz + c)
        src = self.stage[t]
        sems = self.sems.at[t, 4, 0]
        return remote(src, ref, sems.at[0], sems.at[1], self.place.at(c=1 - self.place.c))

    def small_copy(self, i, src, dst, device):
        return remote(src, dst, self.small_sems.at[0, i], self.small_sems.at[1, i], device)

    def small_start(self):
        p = self.place
        for i, device in enumerate([p.at(zz=p.other(k)) for k in (1, 2, 3)] + [p.at(c=1 - p.c)]):
            self.small_copy(i, self.small_in, self.small.at[p.b], device).start()

    def small_pass(self):
        p = self.place
        for i, k in enumerate((1, 2, 3)):
            ref = self.small.at[2 * p.other(k) + p.c]
            self.small_copy(i, ref, ref, p.at()).wait_recv()
            self.small_copy(4 + i, ref, ref, p.at(c=1 - p.c)).start()

    def small_done(self):
        p = self.place
        for i, k in enumerate((0, 1, 2, 3)):
            ref = self.small.at[2 * p.other(k) + 1 - p.c]
            self.small_copy(3 + i, ref, ref, p.at()).wait_recv()
        for i in range(7):
            self.small_copy(i, self.small_in, self.small_in, p.at()).wait_send()

    def stage_piece(self, t, y):
        x = self.place.x
        if t in (1, 2):
            return self.stage[t].at[:, pl.ds(pl.multiple_of((2 * y + x) * WIDTH, 128), WIDTH)]
        if t == 3:
            return self.stage[t].at[2 * y + x]
        low, size = (0, 80) if y == 0 else (80, 64)
        return self.stage[t].at[x, pl.ds(low, size)]

    def z_copies(self, t, y, zz, start, own=False):
        p = self.place
        for step, send in ((1, 0), (-1, 5)):
            go = (zz <= p.zz) & (p.zz < 3) if step == 1 else (zz >= p.zz) & (p.zz > 0)
            ref = piece(t, self.outs[t], 2 * zz + p.c, p.x, y)

            @pl.when(go)
            def _():
                copy = remote(self.stage_piece(t, y) if own else ref, ref, self.sems.at[t, send, zz, 0], self.sems.at[t, 0, zz, 1], p.at(zz=p.zz + step))
                copy.start() if start else copy.wait_send()

    def z_start(self, t):
        p = self.place
        self.each_y(t, lambda y: self.z_copies(t, y, p.zz, True, True))
        self.own_copy(t, p.c).start()

    def z_wait(self, t, y, zz):
        p = self.place
        self.copy(t, p.x, y, zz, p.c, 0, zz, p.at()).wait_recv()

    def z_done(self, t, k):
        p = self.place
        zz = p.source(k)

        def run(y):
            self.z_wait(t, y, zz)
            self.z_copies(t, y, zz, True)

        pl.when((p.zz > 0) & (p.zz < 3))(lambda: self.each_y(t, run))

    def xy_start(self, t, k):
        p = self.place
        zz = p.source(k)

        def run(y):
            pl.when((p.zz == 0) | (p.zz == 3))(lambda: self.z_wait(t, y, zz))
            self.copy(t, p.x, y, zz, p.c, 1, k, p.at(x=1 - p.x)).start()
            self.copy(t, p.x, y, zz, p.c, 2, k, p.at(y=1 - p.y)).start()

        self.each_y(t, run)

    def by_x(self, t, k):
        return k == 1 or (k == 2 and t % 2 == 0)

    def xy_done(self, t, k):
        p = self.place

        def run(y):
            zz = p.source(k)
            self.copy(t, 1 - p.x, y, zz, p.c, 1, k, p.at()).wait_recv()
            if self.by_x(t, k):
                self.copy(t, 1 - p.x, y, zz, p.c, 3, k, p.at(y=1 - p.y)).start()
            self.copy(t, p.x, 1 - y, zz, p.c, 2, k, p.at()).wait_recv()
            if not self.by_x(t, k):
                self.copy(t, p.x, 1 - y, zz, p.c, 3, k, p.at(x=1 - p.x)).start()

        self.each_y(t, run)

    def diag_done(self, t, k):
        p = self.place

        def run(y):
            zz = p.source(k)
            self.copy(t, 1 - p.x, 1 - y, zz, p.c, 3, k, p.at()).wait_recv()

        self.each_y(t, run)
        self.pair_copy(t, k, p.c).start()

    def pair_copy(self, t, k, c):
        ref = block(t, self.outs[t], 2 * self.place.source(k) + c)
        sems = self.sems.at[t, 4, k]
        return remote(ref, ref, sems.at[0], sems.at[1], self.place.at(c=1 - self.place.c))

    def ready(self, t):
        p = self.place
        self.own_keep(t).wait()
        self.own_copy(t, 1 - p.c).wait_recv()
        for k in (1, 2, 3):
            self.pair_copy(t, k, 1 - p.c).wait_recv()

    def all_sent(self, t):
        p = self.place
        self.own_copy(t, p.c).wait_send()

        def run(y):
            self.z_copies(t, y, p.zz, False, True)
            for k in (1, 2, 3):
                zz = p.source(k)
                self.z_copies(t, y, zz, False)
                self.copy(t, p.x, y, zz, p.c, 1, k, p.at()).wait_send()
                self.copy(t, p.x, y, zz, p.c, 2, k, p.at()).wait_send()
                if self.by_x(t, k):
                    self.copy(t, 1 - p.x, y, zz, p.c, 3, k, p.at()).wait_send()
                else:
                    self.copy(t, p.x, 1 - y, zz, p.c, 3, k, p.at()).wait_send()

        self.each_y(t, run)
        for k in (1, 2, 3):
            self.pair_copy(t, k, p.c).wait_send()


SIZES = (80, PART, PART, PART)


HALO = 320
COND = 32
TOK = 512
KEYS = HALO + TOK + COND
TILES = ((0, 0), (256, 256))
LOG2E = 1.4426950408889634


def nt(a, b):
    return lax.dot_general(a, b, (((1,), (1,)), ((), ())), preferred_element_type=jnp.float32)


def tn(a, b):
    return lax.dot_general(a, b, (((0,), (0,)), ((), ())), preferred_element_type=jnp.float32)


def nn(a, b):
    return jnp.dot(a, b, preferred_element_type=jnp.float32)


def make_bias(extra, blk, bias):
    row = lax.broadcasted_iota(jnp.int32, (TOK, 1), 0) + blk * TOK
    at = lax.broadcasted_iota(jnp.int32, (1, KEYS), 1)
    key = at + (blk * TOK - HALO)
    item_q, item_k = jnp.zeros_like(row), jnp.zeros_like(key)
    end = 0
    for n in range(extra.shape[1]):
        end = end + extra[0, n] + (LEN_MIN - 1)
        item_q += (row >= end).astype(jnp.int32)
        item_k += (key >= end).astype(jnp.int32)
    item_k = jnp.where(key >= 0, item_k, -1)
    item_k = jnp.where(at >= HALO + TOK, (at - (HALO + TOK)) >> 1, item_k)
    for low in range(0, TOK, 128):
        bias[low : low + 128] = jnp.where(item_q[low : low + 128] == item_k, 0.0, -1e30)


def head(h):
    return slice(HEAD * h, HEAD * (h + 1))


class Names:
    def __init__(self, names, refs):
        for name, ref in zip(names, refs, strict=True):
            setattr(self, name, ref)


def hbm(shape, dtype=jnp.bfloat16):
    return jax.ShapeDtypeStruct(shape, dtype)


GROUP = 4
IN_VMEM = pl.BlockSpec(memory_space=pltpu.VMEM)
IN_SMEM = pl.BlockSpec(memory_space=pltpu.SMEM)
FWD_IN = dict(
    skip_bias=IN_VMEM, first_gain=IN_VMEM, first_shift=IN_VMEM, out_bias=IN_VMEM, second_gain=IN_VMEM,
    second_shift=IN_VMEM, down_bias=IN_VMEM, up_bias=IN_VMEM, extra=IN_SMEM, cond=IN_VMEM, latents=ANY, skip_input=ANY, skip=ANY, joint=ANY, out=ANY, up=ANY, down=ANY,
)
FWD_OUT = dict(
    w_skip=hbm((16, PART, WIDTH)),
    w_joint=hbm((8, PART, 4 * WIDTH)),
    w_up=hbm((8, PART, 4 * WIDTH)),
    w_down=hbm((32, PART, WIDTH)),
    output=hbm((TOK, WIDTH)),
    hidden_t=hbm((8, 4, PART, TOK)),
    slope=hbm((TOK, 4 * WIDTH)),
    second_t=hbm((8, PART, TOK)),
    second_unit=hbm((TOK, WIDTH)),
    att_t=hbm((8, PART, TOK)),
    q=hbm((HEADS, TOK, HEAD)),
    k=hbm((HEADS, KEYS, HEAD)),
    v=hbm((HEADS, KEYS, HEAD)),
    o=hbm((HEADS, TOK, HEAD)),
    logsum=hbm((HEADS, TOK, 1), jnp.float32),
    first_t=hbm((8, PART, TOK)),
    first_unit=hbm((TOK, WIDTH)),
    joined_t=hbm((8, 2 * PART, TOK)),
)
FWD_VM = dict(
    cond_t=hbm((8, PART, 128)),
    second_rstd=hbm((TOK, 1), jnp.float32),
    first_rstd=hbm((TOK, 1), jnp.float32),
    vectors=hbm((16, WIDTH), jnp.float32),
    cond_unit=hbm((COND, WIDTH), jnp.float32),
    cond_rstd=hbm((COND, 1), jnp.float32),
)
FWD_SCRATCH = dict(
    lat=pltpu.VMEM((TOK, WIDTH), jnp.bfloat16),
    ski=pltpu.VMEM((TOK, WIDTH), jnp.bfloat16),
    weight=pltpu.VMEM((2, 8, PART, WIDTH), jnp.bfloat16),
    base=pltpu.VMEM((TOK, WIDTH), jnp.float32),
    acc=pltpu.VMEM((TOK, WIDTH), jnp.float32),
    unit=pltpu.VMEM((TOK, WIDTH), jnp.bfloat16),
    normed=pltpu.VMEM((TOK, WIDTH), jnp.bfloat16),
    pairs=pltpu.VMEM((2, TOK, WIDTH), jnp.bfloat16),
    halo=pltpu.VMEM((2, HALO, WIDTH), jnp.bfloat16),
    cond_in=pltpu.VMEM((COND, WIDTH), jnp.bfloat16),
    qh=pltpu.VMEM((HEADS, TOK, HEAD), jnp.bfloat16),
    kh=pltpu.VMEM((HEADS, KEYS, HEAD), jnp.bfloat16),
    vh=pltpu.VMEM((HEADS, KEYS, HEAD), jnp.bfloat16),
    oh=pltpu.VMEM((HEADS, TOK, HEAD), jnp.bfloat16),
    lh=pltpu.VMEM((HEADS // 2, 256, 1), jnp.float32),
    bias=pltpu.VMEM((TOK, KEYS), jnp.float32),
    hidden=pltpu.VMEM((4, TOK, WIDTH), jnp.bfloat16),
    turned=pltpu.VMEM((2, WIDTH, TOK), jnp.bfloat16),
    tile=pltpu.VMEM((2, TOK, WIDTH), jnp.bfloat16),
    pack=pltpu.VMEM(SMALL, jnp.float32),
    packs=pltpu.VMEM((8, *SMALL), jnp.float32),
    ups=pltpu.VMEM((4, 1, WIDTH), jnp.float32),
    w_sems=pltpu.SemaphoreType.DMA((2,)),
    t_sems=pltpu.SemaphoreType.DMA((24,)),
    halo_sems=pltpu.SemaphoreType.DMA((2, 2)),
)
N_GATHER = len(Gather.SEMS) + len(Gather.STAGE)


def forward_kernel(*refs):
    cuts = [len(FWD_IN), len(FWD_OUT), len(FWD_VM), len(FWD_SCRATCH), N_GATHER]
    pieces, at = [], 0
    for cut in cuts:
        pieces.append(refs[at : at + cut])
        at += cut
    i, o, vm, b = (
        Names(names, part) for names, part in zip((FWD_IN, FWD_OUT, FWD_VM, FWD_SCRATCH), pieces)
    )
    f32, bf16 = jnp.float32, jnp.bfloat16
    p = Place()
    g = Gather(
        p, (b.pack, i.skip, i.joint, i.out, i.up, i.down), (b.packs, o.w_skip, o.w_joint, o.w_up, o.w_down), pieces[4]
    )

    def copy(src, dst, sem):
        return pltpu.make_async_copy(src, dst, sem)

    def stream(blocks, body):
        def load(n):
            return copy(blocks[n], b.weight.at[n % 2], b.w_sems.at[n % 2])

        load(0).start()
        for n in range(len(blocks)):
            if n + 1 < len(blocks):
                load(n + 1).start()
            load(n).wait()
            body(n, b.weight[n % 2].reshape(WIDTH, WIDTH))

    def column(ref, q):
        return ref.at[:, :, pl.ds(q * WIDTH, WIDTH)]

    def by_rows(size, body):
        @pl.loop(0, TOK // size)
        def _(n):
            body(pl.ds(pl.multiple_of(n * size, size), size))

    def vector(n):
        return vm.vectors[n : n + 1, :]

    kept = []

    def keep(src, dst, sem):
        one = (src, dst, b.t_sems.at[sem])
        copy(*one).start()
        kept.append(one)

    def flush():
        for one in kept:
            copy(*one).wait()
        kept.clear()

    def norm(values):
        center = values - jnp.mean(values, axis=1, keepdims=True)
        rstd = lax.rsqrt(jnp.mean(center * center, axis=1, keepdims=True) + 1e-05)
        return center * rstd, rstd

    def norm_tokens(gain, shift, rstd_out):
        @functools.partial(by_rows, 64)
        def _(rows):
            unit, rstd = norm(b.base[rows])
            b.unit[rows] = unit.astype(bf16)
            rstd_out[rows] = rstd
            b.normed[rows] = (unit * gain + shift).astype(bf16)

    def turn(slot, src, dst, sem):
        b.turned[slot] = src.T
        keep(b.turned.at[slot], dst, sem)

    loads = [(i.latents, b.lat, b.t_sems.at[0]), (i.skip_input, b.ski, b.t_sems.at[1])]
    for t in range(4):
        g.own_start(t)
    for one in loads:
        copy(*one).start()
    b.pack[...] = jnp.zeros(SMALL, f32)
    few = (i.skip_bias, i.first_gain, i.first_shift, i.out_bias, i.second_gain, i.second_shift, i.down_bias)
    for n, ref in enumerate(few):
        b.pack[n : n + 1, 0:PART] = ref[...].astype(f32).reshape(1, PART)
    wide = i.up_bias[...].astype(f32).reshape(1, 4 * PART)
    for n in range(4):
        b.pack[7 + n : 8 + n, 0:PART] = wide[:, n * PART : (n + 1) * PART]
    b.packs[p.b] = b.pack[...]
    greet(p)
    g.small_start()
    g.own_done(0)
    g.z_start(0)
    make_bias(i.extra, p.b, b.bias)
    g.small_pass()
    for one in loads:
        copy(*one).wait()

    @pl.when(p.b == 0)
    def _():
        for n in range(HEADS):
            b.kh[n, 0:HALO] = jnp.zeros((HALO, HEAD), bf16)
            b.vh[n, 0:HALO] = jnp.zeros((HALO, HEAD), bf16)

    for k in (1, 2, 3):
        g.z_done(0, k)
        g.xy_start(0, k)
        if k == 2:
            g.own_done(1)
            g.z_start(1)
    g.small_done()
    for n in range(8):
        for row in range(7):
            vm.vectors[row : row + 1, n * PART : (n + 1) * PART] = b.packs[n, row : row + 1, 0:PART]
        for j in range(4):
            at = 4 * n + j
            low = at % 8 * PART
            b.ups[at // 8, :, low : low + PART] = b.packs[n, 7 + j : 8 + j, 0:PART]
    vm.vectors[7:16, :] = jnp.zeros((9, WIDTH), f32)
    for k in (1, 2, 3):
        g.xy_done(0, k)
    g.z_done(1, 1)
    g.xy_start(1, 1)
    for k in (1, 2, 3):
        g.diag_done(0, k)
    g.ready(0)

    def do_base(n, weight):
        made = nn((b.lat, b.ski)[n][...], weight)
        if n == 0:
            b.base[...] = made + vector(0)
        else:
            b.base[...] += made
        if n == 0:
            g.z_done(1, 2)
            g.z_done(1, 3)
            g.xy_start(1, 2)
            g.own_done(2)
            g.z_start(2)

    stream([o.w_skip.at[pl.ds(8 * n, 8)] for n in range(2)], do_base)
    norm_tokens(vector(1), vector(2), vm.first_rstd)
    g.xy_start(1, 3)
    g.z_done(2, 1)
    for n in range(COND // 2):
        vm.cond_unit[2 * n : 2 * n + 2] = i.cond[n].astype(f32)
    unit, rstd = norm(vm.cond_unit[...])
    vm.cond_unit[...] = unit
    vm.cond_rstd[...] = rstd
    cond_in = (unit * vector(1) + vector(2)).astype(bf16)
    b.cond_in[...] = cond_in
    keep(b.unit, o.first_unit, 2)
    for n in range(2):
        b.turned[n] = (b.lat, b.ski)[n][...].T
        made = b.turned.at[n].reshape(8, PART, TOK)
        for k in range(4):
            keep(made.at[pl.ds(2 * k, 2)].reshape(2 * PART, TOK), o.joined_t.at[4 * n + k], 3 + 4 * n + k)
        if n == 0:
            g.z_done(2, 2)
            g.own_done(3)
            g.z_start(3)
    turned = jnp.concatenate([cond_in.astype(f32)] * 2 + [jnp.zeros((128 - 2 * COND, WIDTH), f32)], 0).T
    vm.cond_t[...] = turned.astype(bf16).reshape(8, PART, 128)
    for k in (1, 2, 3):
        g.xy_done(1, k)
    g.xy_start(2, 1)
    g.z_done(2, 3)
    for k in (1, 2, 3):
        g.diag_done(1, k)
    g.xy_start(2, 2)
    g.xy_start(2, 3)
    g.z_done(3, 1)
    g.ready(1)

    def halo_copy(n, device):
        low, size = ((HALO - 64, 64), (0, HALO - 64))[n]
        src, dst = b.pairs.at[:, pl.ds(TOK - HALO + low, size)], b.halo.at[:, pl.ds(low, size)]
        return remote(src, dst, b.halo_sems.at[n, 0], b.halo_sems.at[n, 1], device)

    def halo_heads(n):
        low, size = ((HALO - 64, 64), (0, HALO - 64))[n]

        @pl.when(p.b > 0)
        def _():
            halo_copy(n, (p.s, p.b)).wait_recv()
            for h in range(HEADS):
                b.kh[h, low : low + size] = b.halo[0, low : low + size, head(h)]
                b.vh[h, low : low + size] = b.halo[1, low : low + size, head(h)]

    def do_triple(n, weight):
        made = nn(b.normed[...], weight).astype(bf16)
        if n < 2:
            b.pairs[n] = made
            few = nn(b.cond_in[...], weight).astype(bf16)
            for h in range(HEADS):
                (b.kh, b.vh)[n][h, HALO + TOK :] = few[:, head(h)]
        else:
            b.tile[0] = made
        if n == 1:
            for m in (0, 1):
                pl.when(p.b < 7)(lambda m=m: halo_copy(m, (p.s, p.b + 1)).start())
            g.z_done(3, 2)

    stream([column(o.w_joint, n) for n in (1, 2, 0)], do_triple)
    for h in range(HEADS):
        b.qh[h] = b.tile[0, :, head(h)]
        b.kh[h, HALO : HALO + TOK] = b.pairs[0, :, head(h)]
        b.vh[h, HALO : HALO + TOK] = b.pairs[1, :, head(h)]
    g.z_done(3, 3)
    flush()
    turn(0, b.normed[...], o.first_t.reshape(WIDTH, TOK), 2)

    halo_heads(0)
    keep(b.qh, o.q, 3)

    def logsum_copy(half, start):
        dst = o.logsum.at[pl.ds(start, HEADS // 2), pl.ds(TILES[half][0], 256)]
        return copy(b.lh, dst, b.t_sems.at[6])

    def attend(half, start, before):
        row, low = TILES[half]
        rows, keys = pl.ds(row, 256), pl.ds(low, KEYS - low)
        if before is not None:
            logsum_copy(*before).wait()

        @pl.loop(0, HEADS // 2)
        def _(n):
            h = start + n
            scores = nt(b.qh[h, rows], b.kh[h, keys]) * (HEAD**-0.5 * LOG2E) + b.bias[rows, keys]
            top = jnp.max(scores, axis=1, keepdims=True)
            expo = jnp.exp2(scores - top)
            total = jnp.sum(expo, axis=1, keepdims=True)
            mixed = nn(expo.astype(bf16), b.vh[h, keys])
            b.oh[h, rows] = (mixed / total).astype(bf16)
            b.lh[n] = top + jnp.log2(total)

        logsum_copy(half, start).start()

    attend(1, 0, None)
    for k in (1, 2, 3):
        g.xy_done(2, k)
    g.xy_start(3, 1)
    attend(1, 8, (1, 0))
    halo_heads(1)
    keep(b.kh, o.k, 4)
    keep(b.vh, o.v, 5)
    g.xy_start(3, 2)
    attend(0, 0, (1, 8))
    g.xy_start(3, 3)
    attend(0, 8, (0, 0))
    logsum_copy(0, 8).wait()
    keep(b.oh, o.o, 7)
    for h in range(HEADS):
        b.tile[0, :, head(h)] = b.oh[h]

    def do_out(_, weight):
        b.base[...] += nn(b.tile[0], weight) + vector(3)

    stream([column(o.w_joint, 3)], do_out)
    norm_tokens(vector(4), vector(5), vm.second_rstd)
    flush()
    keep(b.unit, o.second_unit, 2)
    turn(0, b.tile[0], o.att_t.reshape(WIDTH, TOK), 3)
    turn(1, b.normed[...], o.second_t.reshape(WIDTH, TOK), 4)
    for k in (1, 2, 3):
        g.diag_done(2, k)
    for k in (1, 2, 3):
        g.xy_done(3, k)
    g.ready(2)

    flush()
    hidden_t = o.hidden_t.reshape(4, WIDTH, TOK)

    def wide_keep(q):
        slot = q % 2
        return [
            copy(b.turned.at[slot], hidden_t.at[q], b.t_sems.at[8 + slot]),
            copy(b.tile.at[slot], o.slope.at[:, pl.ds(q * WIDTH, WIDTH)], b.t_sems.at[10 + slot]),
        ]

    def do_up(q, weight):
        slot = q % 2
        b.acc[...] = nn(b.normed[...], weight)
        if q >= 2:
            for one in wide_keep(q - 2):
                one.wait()

        @functools.partial(by_rows, 32)
        def _(rows):
            before = b.acc[rows] + b.ups[q]
            inside = 0.5 + 0.5 * lax.erf(before * 2**-0.5)
            bell = jnp.exp2(before * before * (-0.5 * LOG2E)) * 0.3989422804014327
            b.hidden[q, rows] = (before * inside).astype(bf16)
            b.tile[slot, rows] = (inside + before * bell).astype(bf16)

        b.turned[slot] = b.hidden[q].T
        for one in wide_keep(q):
            one.start()
        if q == 1:
            for k in (1, 2, 3):
                g.diag_done(3, k)

    stream([column(o.w_up, q) for q in range(4)], do_up)
    g.ready(3)

    def do_down(q, weight):
        made = nn(b.hidden[q], weight)
        if q == 0:
            b.base[...] += made + vector(6)
        else:
            b.base[...] += made

    stream([o.w_down.at[pl.ds(8 * q, 8)] for q in range(4)], do_down)
    b.normed[...] = b.base[...].astype(bf16)
    keep(b.normed, o.output, 2)
    for q in (2, 3):
        for one in wide_keep(q):
            one.wait()
    flush()
    for m in (0, 1):
        pl.when(p.b < 7)(lambda m=m: halo_copy(m, (p.s, p.b + 1)).wait_send())
    for t in range(4):
        g.all_sent(t)


def forward(arrays):
    vm = pl.BlockSpec(memory_space=pltpu.VMEM)
    outs = pl.pallas_call(
        forward_kernel,
        out_shape=[*FWD_OUT.values(), *FWD_VM.values()],
        in_specs=[*FWD_IN.values()],
        out_specs=[ANY] * len(FWD_OUT) + [vm] * len(FWD_VM),
        scratch_shapes=[*FWD_SCRATCH.values()] + Gather.SEMS + Gather.STAGE,
        compiler_params=pltpu.CompilerParams(collective_id=0, has_side_effects=True, vmem_limit_bytes=60 << 20),
    )(*[arrays[name] for name in FWD_IN])
    return dict(zip([*FWD_OUT, *FWD_VM], outs, strict=True))


ORDER = (0, 2, 1, 3)
UNIT = (PART, WIDTH)


def add_into(out, *ins):
    @pl.loop(0, out.shape[0] // 16)
    def _(i):
        rows = pl.ds(pl.multiple_of(i * 16, 16), 16)
        total = ins[0][rows].astype(jnp.float32)
        for ref in ins[1:]:
            total += ref[rows].astype(jnp.float32)
        out[rows] = total.astype(out.dtype)


class Sum:
    SEMS = [
        pltpu.SemaphoreType.DMA((4, 4, 2, 2)),
        pltpu.SemaphoreType.DMA((4, 4, 2)),
        pltpu.SemaphoreType.DMA((4, 4, 2)),
        pltpu.SemaphoreType.DMA((4, 4, 2)),
        pltpu.SemaphoreType.DMA((23,)),
    ]
    SLOTS = [pltpu.VMEM((23, *UNIT), jnp.bfloat16), pltpu.VMEM((4, *UNIT), jnp.bfloat16)]
    LANDS = [
        jax.ShapeDtypeStruct(lead + (size, WIDTH), jnp.bfloat16)
        for size in SIZES
        for lead in ((4, 2), (4,), (4,))
    ]
    PARTS = [
        jax.ShapeDtypeStruct((8, PART, WIDTH), jnp.bfloat16),
        jax.ShapeDtypeStruct((4, PART, 4 * WIDTH), jnp.bfloat16),
        jax.ShapeDtypeStruct((4, PART, 4 * WIDTH), jnp.bfloat16),
        jax.ShapeDtypeStruct((4, 4, PART, WIDTH), jnp.bfloat16),
    ]

    def __init__(self, place, parts, lands, outs, sems, slots):
        self.place, self.parts, self.outs = place, parts, outs
        self.sem1, self.sem2, self.sem3, self.sem4, self.load_sems = sems
        self.slots, self.fins = slots
        self.land1, self.land2, self.land3 = ([lands[3 * t + i] for t in range(4)] for i in range(3))

    def slot(self, t, i):
        return self.slots.at[i, pl.ds(0, SIZES[t])]

    def fin(self, t):
        return self.fins.at[t, pl.ds(0, SIZES[t])]

    def piece(self, t, zz, x, y):
        ref = self.parts[t]
        if t == 0:
            return ref.at[2 * zz + x, pl.ds(pl.multiple_of(64 * y, 16), 80)]
        if t == 3:
            return ref.at[zz, 2 * y + x]
        return ref.at[zz, :, pl.ds(pl.multiple_of((2 * y + x) * WIDTH, 128), WIDTH)]

    def half(self, t, zz, x, y, j):
        return self.piece(t, zz, x, j) if zz < 2 else self.piece(t, zz, j, y)

    def keep(self, zz):
        return self.place.y if zz < 2 else self.place.x

    def first(self, t, zz, j):
        p = self.place
        device = p.at(x=1 - p.x) if zz < 2 else p.at(y=1 - p.y)
        sems = self.sem1.at[t, zz, j]
        src = self.half(t, zz, 1 - p.x, 1 - p.y, j)
        return remote(src, self.land1[t].at[zz, j], sems.at[0], sems.at[1], device)

    def start(self, t, zzs=ORDER):
        for zz in zzs:
            for j in (0, 1):
                self.first(t, zz, j).start()

    def load(self, t, src, i):
        return pltpu.make_async_copy(src, self.slot(t, i), self.load_sems.at[i])

    def second(self, t, zz):
        p = self.place
        device = p.at(y=1 - p.y) if zz < 2 else p.at(x=1 - p.x)
        sems = self.sem2.at[t, zz]
        return remote(self.slot(t, 2 * zz), self.land2[t].at[zz], sems.at[0], sems.at[1], device)

    def pass_on(self, t, after=None):
        p = self.place
        if after is not None:
            for zz in ORDER:
                self.second(after, zz).wait_send()

        def own(zz):
            return self.load(t, self.half(t, zz, p.x, p.y, 1 - self.keep(zz)), 2 * zz)

        def landed(zz):
            return self.load(t, self.land1[t].at[zz, 1 - self.keep(zz)], 2 * zz + 1)

        for zz in ORDER:
            own(zz).start()
        for zz in ORDER:
            for j in (0, 1):
                self.first(t, zz, j).wait_recv()
            landed(zz).start()
        for zz in ORDER:
            own(zz).wait()
            landed(zz).wait()
            add_into(self.slot(t, 2 * zz), self.slot(t, 2 * zz), self.slot(t, 2 * zz + 1))
            self.second(t, zz).start()

    def third(self, t, zz, slot):
        p = self.place
        return remote(
            self.slot(t, 8 + 3 * zz), self.land3[t].at[slot], self.sem3.at[t, zz, 0], self.sem3.at[t, slot, 1],
            p.at(zz=zz),
        )

    def third_sent(self, t):
        for zz in range(4):
            pl.when(zz != self.place.zz)(lambda zz=zz: self.third(t, zz, self.place.zz).wait_send())

    def to_chip(self, t, after=None):
        p = self.place
        if after is not None:
            self.third_sent(after)

        def load(zz, n):
            keep = self.keep(zz)
            if n == 0:
                src = self.half(t, zz, p.x, p.y, keep)
            else:
                src = self.land1[t].at[zz, keep] if n == 1 else self.land2[t].at[zz]
            return self.load(t, src, 8 + 3 * zz + n)

        for zz in ORDER:
            load(zz, 0).start()
            load(zz, 1).start()
        for zz in ORDER:
            self.second(t, zz).wait_recv()
            load(zz, 2).start()
        for zz in ORDER:
            for n in range(3):
                load(zz, n).wait()
            base = 8 + 3 * zz
            mine = self.slot(t, base)
            add_into(mine, mine, self.slot(t, base + 1), self.slot(t, base + 2))

            @pl.when(zz != p.zz)
            def _():
                self.third(t, zz, p.zz).start()

            @pl.when(zz == p.zz)
            def _():
                add_into(self.fin(t), mine)

    def result(self, t, x, y):
        ref = self.outs[t]
        if KINDS[t] == "cols":
            return ref.at[:, pl.ds(pl.multiple_of((2 * y + x) * WIDTH, 128), WIDTH)]
        if KINDS[t] == "rows":
            return ref.at[pl.ds(pl.multiple_of((2 * y + x) * PART, 16), PART)]
        low, size = (0, 80) if y == 0 else (80, 64)
        return ref.at[pl.ds(pl.multiple_of(x * PART + low, 16), size)]

    def fin_part(self, t, y):
        if KINDS[t] != "half" or y == 0:
            return self.fin(t)
        return self.fins.at[t, pl.ds(16, 64)]

    def each_y(self, t, run):
        if KINDS[t] != "half":
            run(self.place.y)
            return
        for value in (0, 1):
            pl.when(self.place.y == value)(lambda value=value: run(value))

    def share(self, t, y, k):
        p = self.place
        sems = self.sem4.at[t, k]
        if k == 1:
            src, dst, device = self.fin_part(t, y), self.result(t, p.x, y), p.at(x=1 - p.x)
        elif k == 2:
            src, dst, device = self.fin_part(t, y), self.result(t, p.x, y), p.at(y=1 - p.y)
        elif t % 2 == 0:
            src = dst = self.result(t, 1 - p.x, y)
            device = p.at(y=1 - p.y)
        else:
            src = dst = self.result(t, p.x, 1 - y)
            device = p.at(x=1 - p.x)
        return remote(src, dst, sems.at[0], sems.at[1], device)

    def arrived(self, t, y, k):
        p = self.place
        ref = self.result(t, 1 - p.x if k & 1 else p.x, 1 - y if k & 2 else y)
        sems = self.sem4.at[t, k]
        return remote(ref, ref, sems.at[0], sems.at[1], p.at())

    def spread(self, t):
        def run(y):
            for k in (1, 2):
                self.share(t, y, k).start()
            pltpu.make_async_copy(self.fin_part(t, y), self.result(t, self.place.x, y), self.sem4.at[t, 0, 0]).start()

        self.each_y(t, run)

    def spread_on(self, t):
        def run(y):
            self.arrived(t, y, 1 if t % 2 == 0 else 2).wait_recv()
            self.share(t, y, 3).start()

        self.each_y(t, run)

    def finish(self, t):
        p = self.place
        for k in (1, 2, 3):
            ref = self.land3[t].at[p.other(k)]
            remote(ref, ref, self.sem3.at[t, p.zz, 0], self.sem3.at[t, p.other(k), 1], p.at()).wait_recv()
            self.load(t, ref, 19 + k).start()
        for k in (1, 2, 3):
            self.load(t, self.land3[t].at[p.other(k)], 19 + k).wait()
        add_into(self.fin(t), self.fin(t), *[self.slot(t, 19 + k) for k in (1, 2, 3)])
        self.spread(t)

    def done(self, t, last):
        p = self.place
        for zz in range(4):
            for j in (0, 1):
                self.first(t, zz, j).wait_send()
            if last:
                self.second(t, zz).wait_send()
        if last:
            self.third_sent(t)

        def run(y):
            self.arrived(t, y, 2 if t % 2 == 0 else 1).wait_recv()
            self.arrived(t, y, 3).wait_recv()
            for k in (1, 2, 3):
                self.share(t, y, k).wait_send()
            pltpu.make_async_copy(self.fin_part(t, y), self.result(t, self.place.x, y), self.sem4.at[t, 0, 0]).wait()

        self.each_y(t, run)


class Vectors:
    SCRATCH = [
        pltpu.VMEM((8, *SMALL), jnp.float32),
        pltpu.VMEM((4, *SMALL), jnp.float32),
        pltpu.VMEM((4, *SMALL), jnp.float32),
        pltpu.VMEM((4, *SMALL), jnp.float32),
        pltpu.VMEM((4, *SMALL), jnp.float32),
        pltpu.VMEM((4, *SMALL), jnp.float32),
        pltpu.VMEM((COND, WIDTH), jnp.float32),
        pltpu.VMEM((COND, WIDTH), jnp.float32),
        pltpu.VMEM((COND, WIDTH), jnp.float32),
        pltpu.VMEM((4, COND, WIDTH), jnp.float32),
        pltpu.SemaphoreType.DMA((16, 2)),
    ]

    def __init__(self, place, small_out, cond_out, scratch):
        self.place, self.small_out, self.cond_out = place, small_out, cond_out
        self.part, self.pair, self.x_in, self.sum1, self.y_in, self.z_in = scratch[:6]
        self.mine, self.cond_pair, self.cond_sum, self.cond_in = scratch[6:10]
        self.sems = scratch[10]

    def copy(self, i, src, dst, device):
        return remote(src, dst, self.sems.at[i, 0], self.sems.at[i, 1], device)

    def small_pair(self, zz):
        p = self.place
        return self.copy(zz, self.part.at[2 * zz + 1 - p.c], self.pair.at[zz], p.at(c=1 - p.c))

    def pair_start(self):
        for zz in range(4):
            self.small_pair(zz).start()
        self.cond_pair_copy().start()

    def cond_pair_copy(self):
        return self.copy(4, self.mine, self.cond_pair, self.place.at(c=1 - self.place.c))

    def pair_end(self):
        p = self.place
        for zz in range(4):
            self.small_pair(zz).wait()
            self.pair[zz] += self.part[2 * zz + p.c]
        self.cond_pair_copy().wait()
        self.cond_sum[...] = self.mine[...] + self.cond_pair[...]
        self.copy(5, self.pair, self.x_in, p.at(x=1 - p.x)).start()
        for k in (1, 2, 3):
            self.copy(6 + k, self.cond_sum, self.cond_in.at[p.zz], p.at(zz=p.other(k))).start()
        self.cond_in[p.zz] = self.cond_sum[...]

    def run_x(self):
        p = self.place
        self.copy(5, self.pair, self.x_in, p.at(x=1 - p.x)).wait()
        self.sum1[...] = self.pair[...] + self.x_in[...]
        self.copy(6, self.sum1, self.y_in, p.at(y=1 - p.y)).start()

    def run_y(self):
        p = self.place
        self.copy(6, self.sum1, self.y_in, p.at(y=1 - p.y)).wait()
        self.sum1[...] += self.y_in[...]
        for k in (1, 2, 3):
            self.copy(9 + k, self.sum1.at[p.other(k)], self.z_in.at[p.zz], p.at(zz=p.other(k))).start()
        self.z_in[p.zz] = self.sum1[p.zz]

    def run_z(self):
        p = self.place
        for k in (1, 2, 3):
            self.copy(9 + k, self.sum1.at[p.other(k)], self.z_in.at[p.zz], p.at(zz=p.other(k))).wait()
            self.copy(6 + k, self.cond_sum, self.cond_in.at[p.zz], p.at(zz=p.other(k))).wait()
        self.small_out[...] = (self.z_in[0] + self.z_in[1]) + (self.z_in[2] + self.z_in[3])
        cond = (self.cond_in[0] + self.cond_in[1]) + (self.cond_in[2] + self.cond_in[3])
        self.cond_out[...] = cond.astype(jnp.bfloat16)


BACK_IN = dict(
    hidden_t=ANY, slope=ANY, cot=ANY, second_t=ANY, second_unit=ANY, att_t=ANY, q=ANY, k=ANY, v=ANY, o=ANY, logsum=ANY,
    first_t=ANY, first_unit=ANY, joined_t=ANY, w_skip=ANY, w_joint=ANY, w_up=ANY, w_down=ANY, cond_t=ANY,
    second_rstd=IN_VMEM, first_rstd=IN_VMEM, vectors=IN_VMEM, cond_unit=IN_VMEM, cond_rstd=IN_VMEM, extra=IN_SMEM,
)
BACK_OUT = dict(
    d_latents=hbm((TOK, WIDTH)),
    d_skip=hbm((TOK, WIDTH)),
    g_skip=hbm((2 * PART, WIDTH)),
    g_joint=hbm((PART, 4 * WIDTH)),
    g_up=hbm((PART, 4 * WIDTH)),
    g_down=hbm((4 * PART, WIDTH)),
    hidden_t2=hbm((4, 4, PART, TOK)),
    second_t2=hbm((4, PART, TOK)),
    att_t2=hbm((4, PART, TOK)),
    first_t2=hbm((4, PART, TOK)),
    joined_t2=hbm((4, 2 * PART, TOK)),
)
BACK_SCRATCH = dict(
    cot_v=pltpu.VMEM((TOK, WIDTH), jnp.bfloat16),
    cot2=pltpu.VMEM((TOK, WIDTH), jnp.bfloat16),
    wide=pltpu.VMEM((4, TOK, WIDTH), jnp.bfloat16),
    before2=pltpu.VMEM((4, TOK, WIDTH), jnp.bfloat16),
    triple2=pltpu.VMEM((3, TOK, WIDTH), jnp.bfloat16),
    branch=pltpu.VMEM((TOK, WIDTH), jnp.bfloat16),
    branch2=pltpu.VMEM((TOK, WIDTH), jnp.bfloat16),
    base_g=pltpu.VMEM((TOK, WIDTH), jnp.bfloat16),
    base2=pltpu.VMEM((TOK, WIDTH), jnp.bfloat16),
    acc=pltpu.VMEM((TOK, WIDTH), jnp.float32),
    d_middle=pltpu.VMEM((TOK, WIDTH), jnp.float32),
    tile=pltpu.VMEM((TOK, WIDTH), jnp.bfloat16),
    weight=pltpu.VMEM((2, 8, PART, WIDTH), jnp.bfloat16),
    left=pltpu.VMEM((2, 2, 4, PART, TOK), jnp.bfloat16),
    made=pltpu.VMEM((2, 4, PART, WIDTH), jnp.bfloat16),
    heads_g=pltpu.VMEM((HEADS, TOK, HEAD), jnp.bfloat16),
    qh=pltpu.VMEM((GROUP, TOK, HEAD), jnp.bfloat16),
    oh=pltpu.VMEM((GROUP, TOK, HEAD), jnp.bfloat16),
    kh=pltpu.VMEM((GROUP, HALO + TOK + COND, HEAD), jnp.bfloat16),
    vh=pltpu.VMEM((GROUP, HALO + TOK + COND, HEAD), jnp.bfloat16),
    lh=pltpu.VMEM((GROUP, TOK, 1), jnp.float32),
    sum_k=pltpu.VMEM((HALO + TOK + COND, HEAD), jnp.float32),
    sum_v=pltpu.VMEM((HALO + TOK + COND, HEAD), jnp.float32),
    bias=pltpu.VMEM((TOK, HALO + TOK + COND), jnp.float32),
    halo2=pltpu.VMEM((2, HALO, WIDTH), jnp.bfloat16),
    d_cond=pltpu.VMEM((128, 2 * WIDTH), jnp.bfloat16),
    cond_left=pltpu.VMEM((4, PART, 128), jnp.bfloat16),
    sums=pltpu.VMEM((16, WIDTH), jnp.float32),
    wide_sum=pltpu.VMEM((4, 1, WIDTH), jnp.float32),
    w_sems=pltpu.SemaphoreType.DMA((2,)),
    l_sems=pltpu.SemaphoreType.DMA((2, 8)),
    m_sems=pltpu.SemaphoreType.DMA((2,)),
    t_sems=pltpu.SemaphoreType.DMA((8,)),
    sib_sems=pltpu.SemaphoreType.DMA((34, 2)),
)
SUM_SKIP, SUM_GAIN1, SUM_SHIFT1, SUM_OUT, SUM_GAIN2, SUM_SHIFT2, SUM_DOWN, SUM_UP = range(8)


def back_kernel(*refs):
    cuts = [len(BACK_IN), len(BACK_OUT), 2, len(Sum.PARTS), len(Sum.LANDS), len(BACK_SCRATCH), len(Sum.SEMS), 2]
    pieces, at = [], 0
    for cut in cuts:
        pieces.append(refs[at : at + cut])
        at += cut
    i, o, b = Names(BACK_IN, pieces[0]), Names(BACK_OUT, pieces[1]), Names(BACK_SCRATCH, pieces[5])
    p = Place()
    total = Sum(p, pieces[3], pieces[4], (o.g_skip, o.g_joint, o.g_up, o.g_down), pieces[6], pieces[7])
    vectors = Vectors(p, *pieces[2], refs[at:])
    f32, bf16 = jnp.float32, jnp.bfloat16

    def copy(src, dst, sem):
        return pltpu.make_async_copy(src, dst, sem)

    def sib(n, src, dst):
        return remote(src, dst, b.sib_sems.at[n, 0], b.sib_sems.at[n, 1], p.at(c=1 - p.c))

    def halves(n, src, dst):
        return [sib(4 * n + zz, src.at[2 * zz + 1 - p.c], dst.at[zz]) for zz in range(4)]

    left_pairs = (
        (i.hidden_t, o.hidden_t2), (i.second_t, o.second_t2), (i.att_t, o.att_t2), (i.first_t, o.first_t2),
        (i.joined_t, o.joined_t2),
    )

    def column(ref, q):
        return ref.at[:, :, pl.ds(q * WIDTH, WIDTH)]

    blocks = [i.w_down.at[pl.ds(8 * q, 8)] for q in range(4)]
    blocks += [column(i.w_up, q) for q in range(4)]
    blocks += [column(i.w_joint, q) for q in (3, 0, 1, 2)]
    blocks += [i.w_skip.at[pl.ds(8 * n, 8)] for n in range(2)]

    def load_weight(n):
        return copy(blocks[n], b.weight.at[n % 2], b.w_sems.at[n % 2])

    def stream(start, count, body):
        for n in range(start, start + count):
            if n + 1 < len(blocks):
                load_weight(n + 1).start()
            load_weight(n).wait()
            body(n - start, b.weight[n % 2].reshape(WIDTH, WIDTH))

    def by_rows(size, body):
        @pl.loop(0, TOK // size)
        def _(n):
            body(pl.ds(pl.multiple_of(n * size, size), size))

    def add_sum(row, value):
        b.sums[row : row + 1, :] += value

    def colsum(value):
        return jnp.sum(value, axis=0, keepdims=True)

    def form(n, dst, own, own2, pairs, extra=None):
        result = nn(own.reshape(4 * PART, TOK), pairs[0]) + nn(own2.reshape(4 * PART, TOK), pairs[1])
        if extra is not None:
            result += extra
        slot = n % 2
        b.made[slot] = result.astype(bf16).reshape(4, PART, WIDTH)
        copy(b.made.at[slot], dst, b.m_sems.at[slot]).start()

    def formed(n, dst):
        copy(b.made.at[n % 2], dst, b.m_sems.at[n % 2]).wait()

    def send_all(copies):
        for one in copies:
            one.start()

    def recv_all(copies):
        for one in copies:
            one.wait_recv()

    def left_copies(n):
        own, other = b.left.at[n % 2, 0], b.left.at[n % 2, 1]
        sems = b.l_sems.at[n % 2]
        if n < 4:
            zz = ORDER[n]
            pairs = [(i.hidden_t.at[2 * zz + p.c], own), (o.hidden_t2.at[zz], other)]
        elif n < 7:
            src, src2 = left_pairs[n - 3]
            pairs = [(src.at[2 * zz + p.c], own.at[zz]) for zz in range(4)] + [(src2, other)]
        else:
            pairs = []
            for k in range(4):
                zz, rows = 2 * (n - 7) + k // 2, pl.ds((k % 2) * PART, PART)
                pairs.append((i.joined_t.at[2 * zz + p.c, rows], own.at[k]))
                pairs.append((o.joined_t2.at[zz, rows], other.at[k]))
        return [copy(src, dst, sems.at[m]) for m, (src, dst) in enumerate(pairs)]

    def left_start(n):
        if n < 4:
            left_sends[0][ORDER[n]].wait_recv()
        elif n < 7:
            recv_all(left_sends[n - 3])
        else:
            recv_all(left_sends[4][2 * (n - 7) : 2 * (n - 7) + 2])
        send_all(left_copies(n))

    def left_done(n):
        for one in left_copies(n):
            one.wait()
        return b.left[n % 2, 0], b.left[n % 2, 1]

    cot_load = copy(i.cot, b.cot_v, b.t_sems.at[0])
    cot_load.start()
    load_weight(0).start()
    greet(p)
    sib_cot = sib(20, i.cot, b.cot2)
    left_sends = [halves(n, src, dst) for n, (src, dst) in enumerate(left_pairs)]
    send_all([left_sends[0][zz] for zz in ORDER])
    sib_cot.start()
    b.sums[...] = jnp.zeros_like(b.sums)
    b.d_cond[2 * COND :] = jnp.zeros((128 - 2 * COND, 2 * WIDTH), bf16)
    vectors.part[...] = jnp.zeros_like(vectors.part)
    make_bias(i.extra, p.b, b.bias)
    cot_load.wait()

    def before_sib(q):
        return sib(21 + q, b.wide.at[q], b.before2.at[q])

    def slope_load(q):
        return copy(i.slope.at[:, pl.ds(q * WIDTH, WIDTH)], b.tile, b.t_sems.at[1])

    def do_before(q, weight):
        slope_load(q).start()
        b.acc[...] = nt(b.cot_v[...], weight)
        slope_load(q).wait()
        b.wide_sum[q] = jnp.zeros((1, WIDTH), f32)

        @functools.partial(by_rows, 64)
        def _(rows):
            value = (b.acc[rows] * b.tile[rows].astype(f32)).astype(bf16)
            b.wide[q, rows] = value
            b.wide_sum[q] += colsum(value.astype(f32))

        before_sib(q).start()

    stream(0, 4, do_before)

    for n in (1, 2, 3, 4):
        send_all(left_sends[n])

    sib_cot.wait_recv()
    down_parts = pieces[3][3]
    left_start(0)
    for n, zz in enumerate(ORDER):
        left_start(n + 1)
        form(n, down_parts.at[zz], *left_done(n), (b.cot_v[...], b.cot2[...]))
        if n > 0:
            formed(n - 1, down_parts.at[ORDER[n - 1]])
            total.start(3, (ORDER[n - 1],))

    up_parts = pieces[3][2]
    lefts = left_done(4)
    for q in range(4):
        before_sib(q).wait_recv()
        form(q, column(up_parts, q), *lefts, (b.wide[q], b.before2[q]))
        if q == 0:
            formed(3, down_parts.at[ORDER[3]])
            total.start(3, (ORDER[3],))
        else:
            formed(q - 1, column(up_parts, q - 1))
    left_start(5)

    def do_second(q, weight):
        value = nt(b.wide[q], weight)
        if q == 0:
            b.acc[...] = value
        else:
            b.acc[...] += value

    unit_load = copy(i.second_unit, b.tile, b.t_sems.at[1])
    unit_load.start()
    stream(4, 4, do_second)
    unit_load.wait()
    formed(3, column(up_parts, 3))

    def norm_rows(unit, rstd, gain, grad, gain_row, shift_row):
        scaled = grad * gain
        mean1 = jnp.mean(scaled, axis=1, keepdims=True)
        mean2 = jnp.mean(scaled * unit, axis=1, keepdims=True)
        add_sum(gain_row, colsum(grad * unit))
        add_sum(shift_row, colsum(grad))
        return rstd * (scaled - mean1 - unit * mean2)

    @functools.partial(by_rows, 64)
    def _(rows):
        unit = b.tile[rows].astype(f32)
        back = norm_rows(unit, i.second_rstd[rows], i.vectors[4:5], b.acc[rows], SUM_GAIN2, SUM_SHIFT2)
        g = b.cot_v[rows].astype(f32)
        middle = g + back
        b.d_middle[rows] = middle
        low = middle.astype(bf16)
        b.branch[rows] = low
        add_sum(SUM_OUT, colsum(low.astype(f32)))
        add_sum(SUM_DOWN, colsum(g))

    branch_sib = sib(25, b.branch, b.branch2)
    branch_sib.start()
    total.pass_on(3)
    total.start(2)

    def do_attended(_, weight):
        b.tile[...] = nt(b.branch[...], weight).astype(bf16)
        for h in range(HEADS):
            b.heads_g[h] = b.tile[:, head(h)]

    stream(8, 1, do_attended)

    joint_parts = pieces[3][1]
    lefts = left_done(5)
    left_start(6)
    branch_sib.wait_recv()
    form(0, column(joint_parts, 3), *lefts, (b.branch[...], b.branch2[...]))

    formed(0, column(joint_parts, 3))
    for q in range(4):
        before_sib(q).wait_send()

    def halo_copy(n, device):
        low, size = ((0, 512), (512, 256), (768, 384))[n]
        columns = pl.ds(low, size)
        src = b.before2.at[pl.ds(0, 2), pl.ds(0, HALO), columns]
        sems = b.sib_sems.at[31 + n]
        return remote(src, b.halo2.at[:, :, columns], sems.at[0], sems.at[1], device)

    def halo_start(n):
        pl.when(p.b > 0)(lambda: halo_copy(n, (p.s, p.b - 1)).start())

    scale = HEAD**-0.5
    n_keys = HALO + TOK + COND

    def group_loads(start):
        hs = pl.ds(start, GROUP)
        pairs = ((i.q, b.qh), (i.o, b.oh), (i.k, b.kh), (i.v, b.vh), (i.logsum, b.lh))
        return [copy(src.at[hs], dst, b.t_sems.at[n]) for n, (src, dst) in enumerate(pairs)]

    def group(start):
        send_all(group_loads(start))
        for one in group_loads(start):
            one.wait()

        @pl.loop(0, GROUP)
        def _(h):
            for row, low in TILES:
                rows, keys = pl.ds(row, 256), pl.ds(low, n_keys - low)
                q, k, v, g = b.qh[h, rows], b.kh[h, keys], b.vh[h, keys], b.heads_g[start + h, rows]
                scores = nt(q, k) * (scale * LOG2E) + b.bias[rows, keys]
                probs = jnp.exp2(scores - b.lh[h, rows])
                d_probs = nt(g, v)
                inner = jnp.sum(g.astype(f32) * b.oh[h, rows].astype(f32), axis=1, keepdims=True)
                d_scores = (probs * (d_probs - inner)).astype(bf16)
                d_k, d_v = tn(d_scores, q), tn(probs.astype(bf16), g)
                if row == 0:
                    b.sum_k[...] = d_k
                    b.sum_v[...] = d_v
                else:
                    b.sum_k[keys] += d_k
                    b.sum_v[keys] += d_v
                b.oh[h, rows] = (nn(d_scores, k) * scale).astype(bf16)
            b.kh[h] = (b.sum_k[...] * scale).astype(bf16)
            b.vh[h] = b.sum_v[...].astype(bf16)

        for n in range(GROUP):
            at = head(start + n)
            b.wide[0, :, at] = b.oh[n]
            for j, made in ((0, b.kh), (1, b.vh)):
                wide = slice(j * WIDTH + at.start, j * WIDTH + at.stop)
                b.before2[j, 0:HALO, at] = made[n, 0:HALO]
                b.wide[1 + j, :, at] = made[n, HALO : HALO + TOK]
                b.d_cond[0:COND, wide] = made[n, HALO + TOK :]

    group(0)
    group(4)
    halo_start(0)
    group(8)
    halo_start(1)
    group(12)
    halo_start(2)

    cond_sib = sib(30, b.d_cond.at[pl.ds(0, COND)], b.d_cond.at[pl.ds(COND, COND)])
    cond_sib.start()

    def triple_sib(j):
        return sib(26 + j, b.wide.at[j], b.triple2.at[j])

    triple_sib(0).start()
    for zz in range(4):
        copy(i.cond_t.at[2 * zz + p.c], b.cond_left.at[zz], b.t_sems.at[4 + zz]).start()
    unit_load = copy(i.first_unit, b.tile, b.t_sems.at[1])
    unit_load.start()

    def do_first(j, weight):
        if j == 1:
            merge_halo()
        value = nt(b.wide[j], weight)
        if j == 0:
            b.acc[...] = value
        else:
            b.acc[...] += value
            cond = nt(b.d_cond[0:COND, (j - 1) * WIDTH : j * WIDTH], weight)
            if j == 1:
                vectors.mine[...] = cond
            else:
                vectors.mine[...] += cond

    def merge_halo():
        @pl.when(p.b < 7)
        def _():
            for n in range(3):
                halo_copy(n, (p.s, p.b)).wait_recv()

            @pl.loop(0, HALO // 64)
            def _(n):
                low = pl.ds(pl.multiple_of(n * 64, 64), 64)
                rows = pl.ds(pl.multiple_of(n * 64 + TOK - HALO, 64), 64)
                for j in (0, 1):
                    extra = b.halo2[j, low].astype(f32)
                    b.wide[1 + j, rows] = (b.wide[1 + j, rows].astype(f32) + extra).astype(bf16)

        triple_sib(1).start()
        triple_sib(2).start()

    total.pass_on(2, after=3)
    total.to_chip(3)
    stream(9, 3, do_first)
    unit_load.wait()

    @functools.partial(by_rows, 64)
    def _(rows):
        unit = b.tile[rows].astype(f32)
        back = norm_rows(unit, i.first_rstd[rows], i.vectors[1:2], b.acc[rows], SUM_GAIN1, SUM_SHIFT1)
        low = (b.d_middle[rows] + back).astype(bf16)
        b.base_g[rows] = low
        add_sum(SUM_SKIP, colsum(low.astype(f32)))

    base_sib = sib(29, b.base_g, b.base2)
    base_sib.start()
    for zz in range(4):
        copy(i.cond_t.at[2 * zz + p.c], b.cond_left.at[zz], b.t_sems.at[4 + zz]).wait()
    cond_sib.wait_recv()

    lefts = left_done(6)
    left_start(7)
    for j in range(3):
        triple_sib(j).wait_recv()
        extra = None
        if j > 0:
            extra = nn(b.cond_left[...].reshape(4 * PART, 128), b.d_cond[:, (j - 1) * WIDTH : j * WIDTH])
        form(j, column(joint_parts, j), *lefts, (b.wide[j], b.triple2[j]), extra)
        if j > 0:
            formed(j - 1, column(joint_parts, j - 1))
    formed(2, column(joint_parts, 2))
    total.start(1)
    vectors.mine[...] = norm_rows(
        i.cond_unit[...], i.cond_rstd[...], i.vectors[1:2], vectors.mine[...], SUM_GAIN1, SUM_SHIFT1
    )
    for row in range(7):
        for n in range(8):
            vectors.part[n, row : row + 1, 0:PART] = b.sums[row : row + 1, n * PART : (n + 1) * PART]
    for n in range(32):
        row, low = 7 + n % 4, n % 8 * PART
        vectors.part[n // 4, row : row + 1, 0:PART] = b.wide_sum[n // 8, :, low : low + PART]
    vectors.pair_start()

    skip_parts = pieces[3][0]
    base_sib.wait_recv()
    for n in (0, 1):
        lefts = left_done(7 + n)
        if n == 0:
            left_start(8)
        form(n, skip_parts.at[pl.ds(4 * n, 4)], *lefts, (b.base_g[...], b.base2[...]))
    vectors.pair_end()
    total.to_chip(2, after=3)
    for n in (0, 1):
        formed(n, skip_parts.at[pl.ds(4 * n, 4)])

    def do_joined(n, weight):
        made = (b.tile, b.branch)[n]
        made[...] = nt(b.base_g[...], weight).astype(bf16)
        copy(made, (o.d_latents, o.d_skip)[n], b.t_sems.at[n]).start()

    branch_sib.wait_send()
    stream(12, 2, do_joined)
    vectors.run_x()
    total.finish(3)

    total.pass_on(1, after=2)
    total.start(0)
    total.spread_on(3)
    vectors.run_y()
    total.finish(2)
    total.to_chip(1, after=2)
    total.pass_on(0, after=1)
    total.spread_on(2)
    total.finish(1)
    total.to_chip(0, after=1)
    total.spread_on(1)
    total.finish(0)
    total.spread_on(0)
    vectors.run_z()
    for n in (0, 1):
        copy((b.tile, b.branch)[n], (o.d_latents, o.d_skip)[n], b.t_sems.at[n]).wait()
    for group_sends in left_sends:
        for one in group_sends:
            one.wait_send()
    for one in (sib_cot, cond_sib, base_sib, triple_sib(0), triple_sib(1), triple_sib(2)):
        one.wait_send()
    for n in range(3):
        pl.when(p.b > 0)(lambda n=n: halo_copy(n, (p.s, p.b - 1)).wait_send())
    for t in (3, 2, 1, 0):
        total.done(t, t == 0)


def backward(arrays):
    vm = pl.BlockSpec(memory_space=pltpu.VMEM)
    outs = pl.pallas_call(
        back_kernel,
        out_shape=[*BACK_OUT.values()] + [
            jax.ShapeDtypeStruct(SMALL, jnp.float32), jax.ShapeDtypeStruct((COND, WIDTH), jnp.bfloat16)
        ] + Sum.PARTS + Sum.LANDS,
        in_specs=[*BACK_IN.values()],
        out_specs=[ANY] * len(BACK_OUT) + [vm] * 2 + [ANY] * (len(Sum.PARTS) + len(Sum.LANDS)),
        scratch_shapes=[*BACK_SCRATCH.values()] + Sum.SEMS + Sum.SLOTS + Vectors.SCRATCH,
        compiler_params=pltpu.CompilerParams(collective_id=1, has_side_effects=True, vmem_limit_bytes=60 << 20),
    )(*[arrays[name] for name in BACK_IN])
    named = Names(BACK_OUT, outs[: len(BACK_OUT)])
    return named, outs[len(BACK_OUT)], outs[len(BACK_OUT) + 1]


def item_ends(extra_length):
    lengths = extra_length[0] + (LEN_MIN - 1)
    count = lengths.shape[0]
    upto = lax.iota(jnp.int32, count)[None, :] <= lax.iota(jnp.int32, count)[:, None]
    return jnp.sum(jnp.where(upto, lengths[None, :], 0), axis=1)


def quick(
    latents, skip_input, cond_tokens, extra_length, skip_weight, skip_bias, first_gain, first_shift, joint_weight,
    out_weight, out_bias, second_gain, second_shift, up_weight, up_bias, down_weight, down_bias, cotangent,
):
    arrays = dict(
        skip_bias=skip_bias,
        first_gain=first_gain,
        first_shift=first_shift,
        out_bias=out_bias,
        second_gain=second_gain,
        second_shift=second_shift,
        down_bias=down_bias,
        up_bias=up_bias,
        extra=extra_length,
        cond=cond_tokens,
        latents=latents,
        skip_input=skip_input,
        skip=skip_weight.reshape(2, PART, WIDTH),
        joint=joint_weight,
        out=out_weight,
        up=up_weight,
        down=down_weight.reshape(4, PART, WIDTH),
        cot=cotangent,
    )
    made = forward(arrays)
    grads, sums, cond_sum = backward({**arrays, **made})
    return settle(made["output"], grads, sums, cond_sum)


SETTLE_STEPS = 3


def settle_kernel(output, d_latents, d_skip, g_skip, g_joint, g_up, g_down, sums, cond, *outs):
    f32 = jnp.float32
    for src, dst in zip((output, d_latents, d_skip), outs[:3]):
        dst[...] = src[...]
    outs[4][...] = g_skip[...].astype(f32)
    outs[8][...] = g_joint[:, : 3 * WIDTH].astype(f32)
    outs[9][...] = g_joint[:, 3 * WIDTH :].astype(f32)
    outs[13][...] = g_up[...].astype(f32)
    outs[15][...] = g_down[...].astype(f32)

    @pl.when(pl.program_id(0) == 0)
    def _():
        pairs = cond[...].astype(f32)
        for n in range(COND // 2):
            outs[3][n] = pairs[2 * n : 2 * n + 2].astype(jnp.bfloat16)
        for row, n in enumerate((5, 6, 7, 10, 11, 12, 16)):
            outs[n][...] = sums[row : row + 1, 0:PART].reshape(PART)
        wide = jnp.concatenate([sums[7 + n : 8 + n, 0:PART] for n in range(4)], axis=1)
        outs[14][...] = wide.reshape(4 * PART)


def settle(output, grads, sums, cond):
    f32, bf16 = jnp.float32, jnp.bfloat16

    def columns(shape, dtype):
        spec = pl.BlockSpec((shape[0], shape[1] // SETTLE_STEPS), lambda n: (0, n))
        return spec, jax.ShapeDtypeStruct(shape, dtype)

    def rows(shape, dtype):
        spec = pl.BlockSpec((shape[0] // SETTLE_STEPS, shape[1]), lambda n: (n, 0))
        return spec, jax.ShapeDtypeStruct(shape, dtype)

    def whole(shape, dtype):
        spec = pl.BlockSpec(shape, lambda n: (0,) * len(shape))
        return spec, jax.ShapeDtypeStruct(shape, dtype)

    token, few = columns((TOK, WIDTH), bf16), whole((PART,), f32)
    outs = [
        token, token, token, whole((COND // 2, 2, WIDTH), bf16), rows((2 * PART, WIDTH), f32), few, few, few,
        rows((PART, 3 * WIDTH), f32), rows((PART, WIDTH), f32), few, few, few, rows((PART, 4 * WIDTH), f32),
        whole((4 * PART,), f32), rows((4 * PART, WIDTH), f32), few,
    ]
    ins = [
        token, token, token, rows((2 * PART, WIDTH), bf16), rows((PART, 4 * WIDTH), bf16), rows((PART, 4 * WIDTH), bf16),
        rows((4 * PART, WIDTH), bf16), whole(SMALL, f32), whole((COND, WIDTH), bf16),
    ]
    return tuple(
        pl.pallas_call(
            settle_kernel,
            grid=(SETTLE_STEPS,),
            out_shape=[shape for _, shape in outs],
            in_specs=[spec for spec, _ in ins],
            out_specs=[spec for spec, _ in outs],
            compiler_params=pltpu.CompilerParams(vmem_limit_bytes=60 << 20),
        )(
            output, grads.d_latents, grads.d_skip, grads.g_skip, grads.g_joint, grads.g_up, grads.g_down, sums, cond,
        )
    )


def shifted(value, axis, steps):
    count = lax.axis_size(axis)
    leading, last = (max(0, -steps), min(count, count - steps))
    return lax.ppermute(value, axis, [(source, source + steps) for source in range(leading, last)])


def layer_norm(values, gain, shift):
    center = values - jnp.mean(values, axis=-1, keepdims=True)
    spread = jnp.mean(center * center, axis=-1, keepdims=True)
    return center * lax.rsqrt(spread + 1e-05) * gain + shift


def contract_rows(left, right):
    return lax.dot_general(
        left, right, (((0,), (0,)), ((), ())), preferred_element_type=jnp.float32
    )


def contract_cols(left, right):
    return lax.dot_general(
        left, right, (((1,), (1,)), ((), ())), preferred_element_type=jnp.float32
    )


def segment_ids(ends, places):
    inside = jnp.sum((ends[None, :] <= places[:, None]).astype(jnp.int32), axis=1)
    return jnp.where(places >= 0, inside, -1)


def split_heads(block):
    return block.reshape(block.shape[0], HEADS, HEAD).transpose(1, 0, 2)


def merge_heads(block):
    return block.transpose(1, 0, 2).reshape(block.shape[1], HEADS * HEAD)


def masked_scores(query, keys, allowed):
    scores = contract_cols(query, keys) * HEAD ** (-0.5)
    return jnp.where(allowed, scores, -1e30)


def plain(
    latents,
    skip_input,
    cond_tokens,
    extra_length,
    skip_weight,
    skip_bias,
    first_gain,
    first_shift,
    joint_weight,
    out_weight,
    out_bias,
    second_gain,
    second_shift,
    up_weight,
    up_bias,
    down_weight,
    down_bias,
    cotangent,
):
    whole = (
        lax.all_gather(skip_weight, "blk", axis=0, tiled=True),
        lax.all_gather(skip_bias, "blk", axis=0, tiled=True),
        lax.all_gather(first_gain, "blk", axis=0, tiled=True),
        lax.all_gather(first_shift, "blk", axis=0, tiled=True),
        lax.all_gather(joint_weight, "blk", axis=0, tiled=True),
        lax.all_gather(out_weight, "blk", axis=0, tiled=True),
        lax.all_gather(out_bias, "blk", axis=0, tiled=True),
        lax.all_gather(second_gain, "blk", axis=0, tiled=True),
        lax.all_gather(second_shift, "blk", axis=0, tiled=True),
        lax.all_gather(up_weight, "blk", axis=0, tiled=True),
        lax.all_gather(up_bias, "blk", axis=0, tiled=True),
        lax.all_gather(down_weight, "blk", axis=0, tiled=True),
        lax.all_gather(down_bias, "blk", axis=0, tiled=True),
    )
    (
        skip_matrix,
        skip_offset,
        gain_first,
        shift_first,
        joint_matrix,
        out_matrix,
        out_offset,
        gain_second,
        shift_second,
        up_matrix,
        up_offset,
        down_matrix,
        down_offset,
    ) = whole
    rows = latents.shape[0]
    width = latents.shape[1]
    scale = HEAD ** (-0.5)
    joined = jnp.concatenate([latents, skip_input], 1)
    base = jnp.dot(joined, skip_matrix, preferred_element_type=jnp.float32) + skip_offset
    first_in = layer_norm(base, gain_first, shift_first).astype(jnp.bfloat16)
    triple = jnp.dot(first_in, joint_matrix, preferred_element_type=jnp.float32).astype(
        jnp.bfloat16
    )
    query = triple[:, :width]
    pair_here = triple[:, width:]
    pair_left = shifted(pair_here, "blk", 1)
    cond_flat = cond_tokens.reshape(-1, width).astype(jnp.float32)
    cond_in = layer_norm(cond_flat, gain_first, shift_first).astype(jnp.bfloat16)
    cond_pair = jnp.dot(
        cond_in, joint_matrix[:, width:], preferred_element_type=jnp.float32
    ).astype(jnp.bfloat16)
    pairs = jnp.concatenate([pair_left, pair_here, cond_pair], 0)
    ends = item_ends(extra_length)
    here = lax.axis_index("blk")
    places = here * rows + lax.iota(jnp.int32, rows)
    seg_here = segment_ids(ends, places)
    seg_left = segment_ids(ends, places - rows)
    cond_seg = lax.iota(jnp.int32, cond_pair.shape[0]) // 2
    allowed = seg_here[:, None] == jnp.concatenate([seg_left, seg_here, cond_seg])[None, :]
    head_query = split_heads(query)
    head_key = split_heads(pairs[:, :width])
    head_value = split_heads(pairs[:, width:])

    def head_forward(parts):
        query_one, key_one, value_one = parts
        scores = masked_scores(query_one, key_one, allowed)
        top = jnp.max(scores, axis=1, keepdims=True)
        expo = jnp.exp(scores - top)
        total = jnp.sum(expo, axis=1, keepdims=True)
        probs = (expo / total).astype(jnp.bfloat16)
        mixed = jnp.dot(probs, value_one, preferred_element_type=jnp.float32)
        return (mixed, (top + jnp.log(total))[:, 0])

    mixed, logsum = lax.map(head_forward, (head_query, head_key, head_value))
    attended = merge_heads(mixed).astype(jnp.bfloat16)
    middle = base + jnp.dot(attended, out_matrix, preferred_element_type=jnp.float32) + out_offset
    second_in = layer_norm(middle, gain_second, shift_second).astype(jnp.bfloat16)
    before = jnp.dot(second_in, up_matrix, preferred_element_type=jnp.float32) + up_offset
    hidden = jax.nn.gelu(before, approximate=False).astype(jnp.bfloat16)
    output = middle + jnp.dot(hidden, down_matrix, preferred_element_type=jnp.float32) + down_offset
    again = (
        lax.all_gather(skip_weight, "blk", axis=0, tiled=True),
        lax.all_gather(skip_bias, "blk", axis=0, tiled=True),
        lax.all_gather(first_gain, "blk", axis=0, tiled=True),
        lax.all_gather(first_shift, "blk", axis=0, tiled=True),
        lax.all_gather(joint_weight, "blk", axis=0, tiled=True),
        lax.all_gather(out_weight, "blk", axis=0, tiled=True),
        lax.all_gather(out_bias, "blk", axis=0, tiled=True),
        lax.all_gather(second_gain, "blk", axis=0, tiled=True),
        lax.all_gather(second_shift, "blk", axis=0, tiled=True),
        lax.all_gather(up_weight, "blk", axis=0, tiled=True),
        lax.all_gather(up_bias, "blk", axis=0, tiled=True),
        lax.all_gather(down_weight, "blk", axis=0, tiled=True),
        lax.all_gather(down_bias, "blk", axis=0, tiled=True),
    )
    (
        skip_matrix,
        skip_offset,
        gain_first,
        shift_first,
        joint_matrix,
        out_matrix,
        out_offset,
        gain_second,
        shift_second,
        up_matrix,
        up_offset,
        down_matrix,
        down_offset,
    ) = again
    incoming = cotangent.astype(jnp.float32)
    grad_down_offset = jnp.sum(incoming, axis=0)
    grad_down_matrix = contract_rows(hidden, cotangent)
    d_hidden = contract_cols(cotangent, down_matrix)
    gelu_value, gelu_pull = jax.vjp(partial(jax.nn.gelu, approximate=False), before)
    d_before = gelu_pull(d_hidden)[0].astype(jnp.bfloat16)
    grad_up_offset = jnp.sum(d_before.astype(jnp.float32), axis=0)
    grad_up_matrix = contract_rows(second_in, d_before)
    d_second = contract_cols(d_before, up_matrix)
    norm_value, norm_pull = jax.vjp(
        layer_norm, middle, gain_second.astype(jnp.float32), shift_second.astype(jnp.float32)
    )
    d_middle_norm, grad_gain_second, grad_shift_second = norm_pull(d_second)
    d_middle = incoming + d_middle_norm
    d_branch = d_middle.astype(jnp.bfloat16)
    grad_out_offset = jnp.sum(d_branch.astype(jnp.float32), axis=0)
    grad_out_matrix = contract_rows(attended, d_branch)
    d_attended = contract_cols(d_branch, out_matrix).astype(jnp.bfloat16)

    def head_backward(parts):
        query_one, key_one, value_one, grad_one, logsum_one = parts
        scores = masked_scores(query_one, key_one, allowed)
        probs = jnp.exp(scores - logsum_one[:, None])
        d_probs = contract_cols(grad_one, value_one)
        inner = jnp.sum(probs * d_probs, axis=1, keepdims=True)
        d_scores = (probs * (d_probs - inner)).astype(jnp.bfloat16)
        d_query_one = jnp.dot(d_scores, key_one, preferred_element_type=jnp.float32) * scale
        d_key_one = contract_rows(d_scores, query_one) * scale
        d_value_one = contract_rows(probs.astype(jnp.bfloat16), grad_one)
        return (d_query_one, d_key_one, d_value_one)

    d_query_heads, d_key_heads, d_value_heads = lax.map(
        head_backward, (head_query, head_key, head_value, split_heads(d_attended), logsum)
    )
    d_query = merge_heads(d_query_heads)
    d_pairs = jnp.concatenate([merge_heads(d_key_heads), merge_heads(d_value_heads)], 1)
    d_left = d_pairs[:rows]
    d_own = d_pairs[rows : 2 * rows]
    d_cond_part = d_pairs[2 * rows :]
    d_returned = shifted(d_left.astype(jnp.bfloat16), "blk", -1).astype(d_left.dtype)
    d_cond_total = lax.psum(d_cond_part.astype(jnp.bfloat16), "blk")
    d_triple = jnp.concatenate([d_query, d_own + d_returned], 1).astype(jnp.bfloat16)
    leading = (here == 0).astype(jnp.float32)
    cond_term = contract_rows(cond_in, d_cond_total) * leading
    grad_joint_matrix = contract_rows(first_in, d_triple) + jnp.concatenate(
        [jnp.zeros((width, width), jnp.float32), cond_term], 1
    )
    d_first = contract_cols(d_triple, joint_matrix)
    d_cond_in = contract_cols(d_cond_total, joint_matrix[:, width:])
    first_value, first_pull = jax.vjp(
        layer_norm, base, gain_first.astype(jnp.float32), shift_first.astype(jnp.float32)
    )
    d_base_norm, grad_gain_tokens, grad_shift_tokens = first_pull(d_first)
    cond_value, cond_pull = jax.vjp(
        layer_norm, cond_flat, gain_first.astype(jnp.float32), shift_first.astype(jnp.float32)
    )
    d_cond_flat, grad_gain_cond, grad_shift_cond = cond_pull(d_cond_in)
    grad_gain_first = grad_gain_tokens + leading * grad_gain_cond
    grad_shift_first = grad_shift_tokens + leading * grad_shift_cond
    d_base = (d_middle + d_base_norm).astype(jnp.bfloat16)
    grad_skip_offset = jnp.sum(d_base.astype(jnp.float32), axis=0)
    grad_skip_matrix = contract_rows(joined, d_base)
    d_joined = contract_cols(d_base, skip_matrix)
    shares = (
        lax.psum_scatter(
            grad_skip_matrix.astype(jnp.bfloat16), "blk", scatter_dimension=0, tiled=True
        ).astype(jnp.float32),
        lax.psum_scatter(
            grad_skip_offset.astype(jnp.bfloat16), "blk", scatter_dimension=0, tiled=True
        ).astype(jnp.float32),
        lax.psum_scatter(
            grad_gain_first.astype(jnp.bfloat16), "blk", scatter_dimension=0, tiled=True
        ).astype(jnp.float32),
        lax.psum_scatter(
            grad_shift_first.astype(jnp.bfloat16), "blk", scatter_dimension=0, tiled=True
        ).astype(jnp.float32),
        lax.psum_scatter(
            grad_joint_matrix.astype(jnp.bfloat16), "blk", scatter_dimension=0, tiled=True
        ).astype(jnp.float32),
        lax.psum_scatter(
            grad_out_matrix.astype(jnp.bfloat16), "blk", scatter_dimension=0, tiled=True
        ).astype(jnp.float32),
        lax.psum_scatter(
            grad_out_offset.astype(jnp.bfloat16), "blk", scatter_dimension=0, tiled=True
        ).astype(jnp.float32),
        lax.psum_scatter(
            grad_gain_second.astype(jnp.bfloat16), "blk", scatter_dimension=0, tiled=True
        ).astype(jnp.float32),
        lax.psum_scatter(
            grad_shift_second.astype(jnp.bfloat16), "blk", scatter_dimension=0, tiled=True
        ).astype(jnp.float32),
        lax.psum_scatter(
            grad_up_matrix.astype(jnp.bfloat16), "blk", scatter_dimension=0, tiled=True
        ).astype(jnp.float32),
        lax.psum_scatter(
            grad_up_offset.astype(jnp.bfloat16), "blk", scatter_dimension=0, tiled=True
        ).astype(jnp.float32),
        lax.psum_scatter(
            grad_down_matrix.astype(jnp.bfloat16), "blk", scatter_dimension=0, tiled=True
        ).astype(jnp.float32),
        lax.psum_scatter(
            grad_down_offset.astype(jnp.bfloat16), "blk", scatter_dimension=0, tiled=True
        ).astype(jnp.float32),
    )
    (
        share_skip,
        share_skip_offset,
        share_gain_first,
        share_shift_first,
        share_joint,
        share_out,
        share_out_offset,
        share_gain_second,
        share_shift_second,
        share_up,
        share_up_offset,
        share_down,
        share_down_offset,
    ) = shares
    summed = (
        lax.psum(share_skip.astype(jnp.bfloat16), "stream").astype(jnp.float32),
        lax.psum(share_skip_offset.astype(jnp.bfloat16), "stream").astype(jnp.float32),
        lax.psum(share_gain_first.astype(jnp.bfloat16), "stream").astype(jnp.float32),
        lax.psum(share_shift_first.astype(jnp.bfloat16), "stream").astype(jnp.float32),
        lax.psum(share_joint.astype(jnp.bfloat16), "stream").astype(jnp.float32),
        lax.psum(share_out.astype(jnp.bfloat16), "stream").astype(jnp.float32),
        lax.psum(share_out_offset.astype(jnp.bfloat16), "stream").astype(jnp.float32),
        lax.psum(share_gain_second.astype(jnp.bfloat16), "stream").astype(jnp.float32),
        lax.psum(share_shift_second.astype(jnp.bfloat16), "stream").astype(jnp.float32),
        lax.psum(share_up.astype(jnp.bfloat16), "stream").astype(jnp.float32),
        lax.psum(share_up_offset.astype(jnp.bfloat16), "stream").astype(jnp.float32),
        lax.psum(share_down.astype(jnp.bfloat16), "stream").astype(jnp.float32),
        lax.psum(share_down_offset.astype(jnp.bfloat16), "stream").astype(jnp.float32),
    )
    return (
        output.astype(jnp.bfloat16),
        d_joined[:, :width].astype(jnp.bfloat16),
        d_joined[:, width:].astype(jnp.bfloat16),
        d_cond_flat.reshape(cond_tokens.shape).astype(jnp.bfloat16),
        summed[0],
        summed[1],
        summed[2],
        summed[3],
        summed[4],
        summed[5],
        summed[6],
        summed[7],
        summed[8],
        summed[9],
        summed[10],
        summed[11],
        summed[12],
    )


def solution(mesh):
    placed = (
        P(("stream", "blk"), None),
        P(("stream", "blk"), None),
        P("stream", None, None),
        P("stream", None),
        P("blk", None),
        P("blk"),
        P("blk"),
        P("blk"),
        P("blk", None),
        P("blk", None),
        P("blk"),
        P("blk"),
        P("blk"),
        P("blk", None),
        P("blk"),
        P("blk", None),
        P("blk"),
        P(("stream", "blk"), None),
    )
    fits = mesh.shape["stream"] == 4 and mesh.shape["blk"] == 8
    return jax.shard_map(
        quick if fits else plain,
        mesh=mesh,
        in_specs=placed,
        out_specs=(
            P(("stream", "blk"), None),
            P(("stream", "blk"), None),
            P(("stream", "blk"), None),
            P("stream", None, None),
            P("blk", None),
            P("blk"),
            P("blk"),
            P("blk"),
            P("blk", None),
            P("blk", None),
            P("blk"),
            P("blk"),
            P("blk"),
            P("blk", None),
            P("blk"),
            P("blk", None),
            P("blk"),
        ),
        check_vma=False,
    )
```
